32 devices in a mesh: groups: 2 (over y), user: 4 (over z), item: 2 (over x), rep: 2 (over core).
Axes of the slice: x: 2, y: 2, z: 4, core: 2. Of those that a mesh axis runs over, the one named last changes fastest.
Arguments:
- user_emb: bfloat16 [64, 16384], P(None, ('groups', 'user')), parts along dimension 1, may hold values from -2 to 2
- item_emb: bfloat16 [64, 8192], P(None, ('groups', 'item')), parts along dimension 1, may hold values from -2 to 2
- user_deg: int32 [16384], P(('groups', 'user')), parts along dimension 0, may hold values from 16 to 256
- item_deg: int32 [8192], P(('groups', 'item')), parts along dimension 0, may hold values from 16 to 256
- block_vals: bfloat16 [9216, 128, 128], P(('groups', 'user', 'item', 'rep')), parts along dimension 0, may hold values from 0 to 1
- block_row: int32 [9216], P(('groups', 'user', 'item', 'rep')), parts along dimension 0, may hold values from 0 to 15
- block_col: int32 [9216], P(('groups', 'user', 'item', 'rep')), parts along dimension 0, may hold values from 0 to 15
- block_count: int32 [32], P(('groups', 'user', 'item', 'rep')), parts along dimension 0, may hold values from 36 to 288, as said below
- trip_user: int32 [8192], P(('groups', 'user', 'item', 'rep')), parts along dimension 0, may hold values from 0 to 2047
- trip_pos: int32 [8192], P(('groups', 'user', 'item', 'rep')), parts along dimension 0, may hold values from 0 to 2047
- trip_neg: int32 [8192], P(('groups', 'user', 'item', 'rep')), parts along dimension 0, may hold values from 0 to 2047
Outputs:
- grad_user: float32 [64, 16384], P(None, ('groups', 'user')), parts along dimension 1
- grad_item: float32 [64, 8192], P(None, ('groups', 'item')), parts along dimension 1
The draws below stay inside these ranges and needn't reach their ends.
There are 2 independent parts, one for each index of `groups`. The reference program is written for one: setup_inputs(seed, part) draws one part's arguments, and reference() takes and returns one part's arrays. A program takes and returns all parts, laid end to end along the dimension named above; each array names one. Nothing has to cross between parts.
Inputs may be any that keep to these rules, and one draw needn't show every extreme that they name: `block_count`: every draw has a device with exactly 288 live slots; slots at or past a device's count hold arbitrary values and are left out of R.
All inputs are finite; a program needn't handle non-finite values.
Results may differ from the reference program's by a relative error of at most 0.00076.
Values sent between devices are 32-bit elements; how exact they have to be, the bound alone decides.
No kernel may reach another device: no remote copies, remote signals or barrier semaphores. Data moves between devices by JAX's collectives and lax.ppermute only.
A program may use at most 128 MiB of HBM per device.

```python
import math
import jax
import jax.numpy as jnp
import numpy as np
from jax import lax

K = 64
BLOCK = 128
UB_DEV = 16
IB_DEV = 16
NBLK = 288
TRIP_DEV = 256
PLACES = 16
NU = 8192
NI = 4096
BLOCKS = 4608
TRIPS = 4096
N_ITEM = 2
N_REP = 2


def draw_block_count(key, part):
    key = jax.random.fold_in(key, 11)
    first_key, second_key = jax.random.split(key)
    counts = jax.random.randint(first_key, (PLACES,), max(1, NBLK // 8), NBLK // 2 + 1)
    fullest = jax.random.randint(second_key, (), 0, PLACES)
    return jnp.where(jnp.arange(PLACES) == fullest, NBLK, counts).astype(jnp.int32)


def touch_ends(result, stream_key, low, largest):
    place = [jax.random.randint(jax.random.fold_in(stream_key, axis), (), 0, length) for axis, length in enumerate(result.shape)]
    widest = result.shape.index(max(result.shape))
    next_to = place[:widest] + [(place[widest] + 1) % result.shape[widest]] + place[widest + 1:]
    return result.at[tuple(place)].set(low).at[tuple(next_to)].set(largest)


def block_levels(own_key, dims, pieces, smallest, high):
    gain = 1.0
    for axis_at, parts in pieces:
        draws = jax.random.uniform(jax.random.fold_in(jax.random.fold_in(own_key, 6), axis_at), (parts,), jnp.float32, smallest / len(pieces), high / len(pieces))
        gain = gain * jnp.repeat(jnp.exp(draws), dims[axis_at] // parts).reshape((-1,) + (1,) * (len(dims) - 1 - axis_at))
    return gain


def rank_table(count, lean):
    portions = [(1 << 20) // math.isqrt(standing ** lean) + 1 for standing in range(1, count + 1)]
    spread = 1 + sum(portions) // (1 << 30)
    return np.cumsum(np.array([max(1, weight // spread) for weight in portions]))


def skewed_ids(key, dims, amount, skew):
    grid = rank_table(amount, skew)
    pick = jax.random.randint(jax.random.fold_in(key, 1), dims, 0, int(grid[amount - 1]))
    standing = jnp.searchsorted(jnp.asarray(grid, jnp.int32), pick, side="right")
    return jax.random.permutation(jax.random.fold_in(key, 2), amount)[standing].astype(jnp.int32)


def normal_values(rng, dims, deviation, reach, pieces=(), kind=jnp.bfloat16):
    loudness = block_levels(rng, dims, pieces, -0.22, 0.18) if pieces else 1.0
    values = jax.random.normal(rng, dims, jnp.float32) * deviation * loudness
    return jnp.minimum(jnp.maximum(values, -reach), reach).astype(kind)


def setup_inputs(seed: int = 0, part: int = 0) -> dict:
    streams_of = jax.random.split(jax.random.key(seed), 12)
    part_keys = jax.random.split(jax.random.fold_in(streams_of[11], part), 12)
    user_emb = normal_values(part_keys[0], (K, NU), 0.3, 2.0, ((1, 4),))
    item_emb = normal_values(part_keys[1], (K, NI), 0.3, 2.0, ((1, 2),))
    user_deg = touch_ends(jax.random.randint(part_keys[2], (NU,), 16, 257), jax.random.fold_in(part_keys[2], 1), 16, 256).astype(jnp.int32)
    item_deg = touch_ends(jax.random.randint(part_keys[3], (NI,), 16, 257), jax.random.fold_in(part_keys[3], 1), 16, 256).astype(jnp.int32)
    block_vals = jnp.clip(1.0 * jax.random.uniform(part_keys[4], (BLOCKS, BLOCK, BLOCK), jnp.float32) ** block_levels(part_keys[4], (BLOCKS, BLOCK, BLOCK), ((0, 16),), -0.2, 0.2), 0.0, 1.0).astype(jnp.bfloat16)
    block_row = touch_ends(skewed_ids(part_keys[5], (BLOCKS,), UB_DEV, 2), jax.random.fold_in(part_keys[5], 3), 0, UB_DEV - 1).astype(jnp.int32)
    block_col = touch_ends(jax.random.randint(part_keys[6], (BLOCKS,), 0, IB_DEV), jax.random.fold_in(part_keys[6], 1), 0, IB_DEV - 1).astype(jnp.int32)
    block_count = draw_block_count(jax.random.fold_in(jax.random.fold_in(streams_of[11], part), 71), part)
    trip_user = touch_ends(jax.random.randint(part_keys[8], (TRIPS,), 0, UB_DEV * BLOCK), jax.random.fold_in(part_keys[8], 1), 0, (UB_DEV * BLOCK) - 1).astype(jnp.int32)
    trip_pos = touch_ends(jax.random.randint(part_keys[9], (TRIPS,), 0, IB_DEV * BLOCK), jax.random.fold_in(part_keys[9], 1), 0, (IB_DEV * BLOCK) - 1).astype(jnp.int32)
    trip_neg = touch_ends(jax.random.randint(part_keys[10], (TRIPS,), 0, IB_DEV * BLOCK), jax.random.fold_in(part_keys[10], 1), 0, (IB_DEV * BLOCK) - 1).astype(jnp.int32)
    return {"user_emb": user_emb, "item_emb": item_emb, "user_deg": user_deg, "item_deg": item_deg, "block_vals": block_vals, "block_row": block_row, "block_col": block_col, "block_count": block_count, "trip_user": trip_user, "trip_pos": trip_pos, "trip_neg": trip_neg}


def propagate(to_users, to_items, block_vals, global_rows, global_cols, live):
    user_blocks = NU // BLOCK
    item_blocks = NI // BLOCK
    item_source = to_users.reshape(K, item_blocks, BLOCK)
    user_source = to_items.reshape(K, user_blocks, BLOCK)
    values = block_vals.reshape(PLACES, NBLK, BLOCK, BLOCK)

    def one_place(carry, inputs):
        user_total, item_total = carry
        place_vals, rows_here, cols_here, live_here = inputs
        weights = place_vals.astype(jnp.float32)
        gathered_items = item_source[:, cols_here].astype(jnp.float32)
        gathered_users = user_source[:, rows_here].astype(jnp.float32)
        user_terms = jnp.einsum('kbj,bij->kbi', gathered_items, weights) * live_here[None, :, None]
        item_terms = jnp.einsum('kbi,bij->kbj', gathered_users, weights) * live_here[None, :, None]
        user_total = user_total.at[:, rows_here].add(user_terms)
        item_total = item_total.at[:, cols_here].add(item_terms)
        return ((user_total, item_total), None)
    start = (jnp.zeros((K, user_blocks, BLOCK), jnp.float32), jnp.zeros((K, item_blocks, BLOCK), jnp.float32))
    (user_total, item_total), _ = lax.scan(one_place, start, (values, global_rows, global_cols, live))
    return (user_total.reshape(K, NU), item_total.reshape(K, NI))

def reference(user_emb, item_emb, user_deg, item_deg, block_vals, block_row, block_col, block_count, trip_user, trip_pos, trip_neg):
    user_scale = lax.rsqrt(user_deg.astype(jnp.float32))
    item_scale = lax.rsqrt(item_deg.astype(jnp.float32))
    user_base = user_emb.astype(jnp.float32)
    item_base = item_emb.astype(jnp.float32)
    places = jnp.arange(PLACES, dtype=jnp.int32)
    place_user = places // (N_ITEM * N_REP)
    place_item = places // N_REP % N_ITEM
    global_rows = block_row.reshape(PLACES, NBLK) + (place_user * UB_DEV)[:, None]
    global_cols = block_col.reshape(PLACES, NBLK) + (place_item * IB_DEV)[:, None]
    live = (jnp.arange(NBLK, dtype=jnp.int32)[None, :] < block_count[:, None]).astype(jnp.float32)
    scaled_items = (item_scale[None, :] * item_base).astype(jnp.bfloat16)
    scaled_users = (user_scale[None, :] * user_base).astype(jnp.bfloat16)
    user_sum, item_sum = propagate(scaled_items, scaled_users, block_vals, global_rows, global_cols, live)
    user_final = 0.5 * (user_base + user_scale[None, :] * user_sum)
    item_final = 0.5 * (item_base + item_scale[None, :] * item_sum)
    trip_place = jnp.arange(TRIPS, dtype=jnp.int32) // TRIP_DEV
    users_global = trip_user + trip_place // (N_ITEM * N_REP) * (UB_DEV * BLOCK)
    item_offset = trip_place // N_REP % N_ITEM * (IB_DEV * BLOCK)
    pos_global = trip_pos + item_offset
    neg_global = trip_neg + item_offset
    user_rows = user_final[:, users_global]
    difference = item_final[:, pos_global] - item_final[:, neg_global]
    margin = lax.optimization_barrier(jnp.sum(user_rows * difference, axis=0))
    slope = -jax.nn.sigmoid(-margin)
    user_grad_final = jnp.zeros((K, NU), jnp.float32).at[:, users_global].add(slope[None, :] * difference)
    pushed = slope[None, :] * user_rows
    item_grad_final = jnp.zeros((K, NI), jnp.float32).at[:, pos_global].add(pushed).at[:, neg_global].add(-pushed)
    back_users = (user_scale[None, :] * user_grad_final * 0.5).astype(jnp.bfloat16)
    back_items = (item_scale[None, :] * item_grad_final * 0.5).astype(jnp.bfloat16)
    user_back, item_back = propagate(back_items, back_users, block_vals, global_rows, global_cols, live)
    grad_user = 0.5 * user_grad_final + user_scale[None, :] * user_back
    grad_item = 0.5 * item_grad_final + item_scale[None, :] * item_back
    return (grad_user, grad_item)
```

```python
import functools

import jax
import jax.numpy as jnp
from jax import lax
from jax.experimental import pallas as pl
from jax.experimental.pallas import tpu as pltpu
from jax.sharding import PartitionSpec as P

F32 = jnp.float32
BF16 = jnp.bfloat16
GROUP = 8
CHUNK = 32

VMEM = pl.BlockSpec(memory_space=pltpu.VMEM)
SMEM = pl.BlockSpec(memory_space=pltpu.SMEM)
ANY = pl.BlockSpec(memory_space=pl.ANY)


def call(kernel, outs, ins, specs, scratch=(), flops=0, moved=0):
    return pl.pallas_call(
        kernel,
        out_shape=outs,
        in_specs=specs,
        out_specs=jax.tree.map(lambda _: VMEM, outs),
        scratch_shapes=list(scratch),
        cost_estimate=pl.CostEstimate(flops=flops, bytes_accessed=moved, transcendentals=0),
        compiler_params=pltpu.CompilerParams(vmem_limit_bytes=48 * 1024 * 1024),
    )(*ins)


def shape(*dims):
    return jax.ShapeDtypeStruct(dims, F32)


def split3(values):
    high = values.astype(BF16)
    rest = values - high.astype(F32)
    middle = rest.astype(BF16)
    low = (rest - middle.astype(F32)).astype(BF16)
    return high, middle, low


def scale_of(deg_ref, block):
    return lax.rsqrt(deg_ref[pl.ds(block, 1), :].astype(F32))


def hot(ids, start, rows):
    place = lax.broadcasted_iota(jnp.int32, (rows, ids.shape[1]), 0) + start
    return jnp.where(place == ids, 1.0, 0.0)


def start_blocks(count, vals, buf, sems):
    for part in range(vals.shape[0] // CHUNK):
        @pl.when(part * CHUNK < count)
        def _():
            span = pl.ds(part * CHUNK, CHUNK)
            pltpu.make_async_copy(vals.at[span], buf.at[span], sems.at[part]).start()


def multiply_blocks(count, source_ids, target_ids, vals, buf, sems, source, total, across):
    trash = total.shape[0] - 1
    total[...] = jnp.zeros_like(total)
    contract = (((1,), (1,)), ((), ())) if across else (((1,), (0,)), ((), ()))

    def group(index, _):
        first = index * GROUP
        targets, terms = [], []
        for step in range(GROUP):
            slot = first + step
            live = slot < count
            origin = jnp.where(live, source_ids[slot], 0)
            targets.append(jnp.where(live, target_ids[slot], trash))
            terms.append(
                lax.dot_general(source[origin], buf[slot], contract, preferred_element_type=F32)
            )
        for target, term in zip(targets, terms):
            total[target] += term
        return 0

    per = CHUNK // GROUP
    for part in range(vals.shape[0] // CHUNK):
        @pl.when(part * CHUNK < count)
        def _():
            span = pl.ds(part * CHUNK, CHUNK)
            pltpu.make_async_copy(vals.at[span], buf.at[span], sems.at[part]).wait()
            groups = jnp.minimum(per, (count - part * CHUNK + GROUP - 1) // GROUP)
            lax.fori_loop(part * per, part * per + groups, group, 0)


def product_scratch(slots, size, width, sources, targets):
    return [
        pltpu.VMEM((slots, size, size), BF16),
        pltpu.SemaphoreType.DMA((slots // CHUNK,)),
        pltpu.VMEM((sources, width, size), BF16),
        pltpu.VMEM((targets + 1, width, size), F32),
    ]


def first_pass(across, count, source_ids, target_ids, emb, source_deg, target_deg, vals, out,
               buf, sems, source, total):
    start_blocks(count[0], vals, buf, sems)
    size = source.shape[2]
    for block in range(source.shape[0]):
        piece = emb[:, block * size:(block + 1) * size].astype(F32)
        source[block] = (scale_of(source_deg, block) * piece).astype(BF16)
    multiply_blocks(count[0], source_ids, target_ids, vals, buf, sems, source, total, across)
    for block in range(out.shape[0]):
        out[block] = scale_of(target_deg, block) * total[block]


def table_of(blocks, table):
    count, width, size = blocks.shape
    for block in range(count):
        span = slice(block * size, (block + 1) * size)
        for part, piece in enumerate(split3(blocks[block])):
            table[part * width:(part + 1) * width, span] = piece


def fold(stacked, width):
    return (
        stacked[:width] + stacked[width:2 * width] + stacked[2 * width:3 * width]
    )


def pick(table, ids_ref, peer, rows, tile):
    total = None
    for start in range(0, table.shape[1], tile):
        chosen = hot(ids_ref[peer, pl.ds(rows[0], 1), :], start, tile)
        if len(rows) == 2:
            chosen = chosen - hot(ids_ref[peer, pl.ds(rows[1], 1), :], start, tile)
        term = jnp.dot(
            table[:, start:start + tile], chosen.astype(BF16), preferred_element_type=F32
        )
        total = term if total is None else total + term
    return total


def gather(rows, blocks, ids, keep, send, table):
    width = blocks.shape[1]
    tile = 2 * blocks.shape[2]
    table_of(blocks, table)

    def one(peer, _):
        keep[peer] = fold(pick(table, ids, peer, rows, tile), width)
        send[peer] = fold(pick(table, ids, peer, [row + 3 for row in rows], tile), width)
        return 0

    lax.fori_loop(0, ids.shape[0], one, 0)


def gather_base(user_emb, item_emb, ids, user_out, item_out):
    user_out[...] = pick(user_emb, ids, 0, [0], 256)
    item_out[...] = pick(item_emb, ids, 0, [1, 2], 256)


def add_split(peers, keep, received, *outs):
    for peer in range(peers):
        outs[peer][...] = keep[peer] + received[peer]


def add_all(refs):
    total = refs[0][...]
    for ref in refs[1:]:
        total = total + ref[...]
    return total


def slopes(user_parts, item_parts, *refs):
    users, items = refs[:user_parts], refs[user_parts:user_parts + item_parts]
    pieces, pushed = refs[user_parts + item_parts:]
    user_rows = 0.5 * add_all(users)
    difference = 0.5 * add_all(items)
    margin = jnp.sum(user_rows * difference, axis=0, keepdims=True)
    slope = -jax.nn.sigmoid(-margin)
    pieces[...] = slope * difference
    pushed[...] = slope * user_rows


def second_pass(across, rows, chunks, count, source_ids, target_ids, ids, source_deg, target_deg,
                vals, *refs):
    pieces = refs[:len(chunks)]
    half_grad, keep, send, buf, sems, source, total, table = refs[len(chunks):]
    start_blocks(count[0], vals, buf, sems)
    blocks, width, size = source.shape
    tile = 2 * size
    trips = ids.shape[2]
    for place, piece in enumerate(pieces):
        for part, value in enumerate(split3(piece[...])):
            table[place, part * width:(part + 1) * width, :] = value
    for start in range(0, blocks * size, tile):
        total_here = jnp.zeros((3 * width, tile), F32)
        for place, (peer, other) in enumerate(chunks):
            chosen = hot(ids[peer, pl.ds(rows[0] + 3 * other, 1), :], start, tile)
            if len(rows) == 2:
                chosen = chosen - hot(ids[peer, pl.ds(rows[1] + 3 * other, 1), :], start, tile)
            total_here = total_here + lax.dot_general(
                table[place], chosen.astype(BF16), (((1,), (1,)), ((), ())),
                preferred_element_type=F32,
            )
        grad = fold(total_here, width)
        for offset in range(0, tile, size):
            block = (start + offset) // size
            mine = grad[:, offset:offset + size]
            half_grad[block] = 0.5 * mine
            source[block] = (scale_of(source_deg, block) * mine * 0.5).astype(BF16)
    multiply_blocks(count[0], source_ids, target_ids, vals, buf, sems, source, total, across)
    me = lax.axis_index("rep")
    half = keep.shape[1]
    for block in range(keep.shape[0]):
        scale = scale_of(target_deg, block)
        keep[block] = scale * total[block, pl.ds(pl.multiple_of(me * half, half), half), :]
        send[block] = scale * total[block, pl.ds(pl.multiple_of((1 - me) * half, half), half), :]


def add_deal(peers, keep, received, *outs):
    me = lax.axis_index("user")
    per = outs[0].shape[0]
    for offset in range(peers):
        there = lax.rem(me + offset, peers) * per
        for block in range(per):
            outs[offset][block] = keep[there + block] + received[there + block]


def add_two(keep, received, out):
    out[...] = keep[...] + received[...]


def sum_parts(*refs):
    refs[-1][...] = add_all(refs[:-1])


def finish_users(parts, half_grad, *refs):
    mine, other = refs[:parts], refs[parts:2 * parts]
    out = refs[-1]
    me = lax.axis_index("rep")
    blocks, width, size = half_grad.shape
    half = width // 2
    for block in range(blocks):
        span = slice(block * size, (block + 1) * size)
        for rank, group in ((me, mine), (1 - me, other)):
            rows = pl.ds(pl.multiple_of(rank * half, half), half)
            total = half_grad[block, rows, :]
            for ref in group:
                total = total + ref[block]
            out[rows, span] = total


def finish_items(peers, half_grad, *refs):
    mine, other = refs[:peers], refs[peers:2 * peers]
    out = refs[-1]
    me = lax.axis_index("rep")
    place = lax.axis_index("user")
    blocks, width, size = half_grad.shape
    half = width // 2
    per = blocks // peers
    for offset in range(peers):
        there = lax.rem(place + offset, peers) * per
        for block in range(per):
            span = pl.ds(pl.multiple_of((there + block) * size, size), size)
            for rank, group in ((me, mine), (1 - me, other)):
                rows = pl.ds(pl.multiple_of(rank * half, half), half)
                out[rows, span] = half_grad[there + block, rows, :] + group[offset][block]


def shift(values, axis, count, offset):
    return lax.ppermute(values, axis, [(i, (i + offset) % count) for i in range(count)])


def on_device(users, items, user_emb, item_emb, user_deg, item_deg, block_vals, block_row,
              block_col, block_count, trip_user, trip_pos, trip_neg):
    width = user_emb.shape[0]
    slots, size, _ = block_vals.shape
    user_blocks = user_emb.shape[1] // size
    item_blocks = item_emb.shape[1] // size
    trips = trip_user.shape[0]
    half = width // 2
    swap = functools.partial(shift, axis="rep", count=2, offset=1)
    user_deg = user_deg.reshape(user_blocks, size)
    item_deg = item_deg.reshape(item_blocks, size)

    ids = jnp.stack([trip_user, trip_pos, trip_neg])
    ids = jnp.concatenate([ids, swap(ids)])
    ids_user = jnp.stack([ids] + [shift(ids, "item", items, -o) for o in range(1, items)])
    ids_item = jnp.stack([ids] + [shift(ids, "user", users, -o) for o in range(1, users)])

    product_flops = 2 * slots * size * size * width
    product_bytes = slots * size * size * 2

    def first(across, emb, source_deg, target_deg, source_ids, target_ids, sources, targets):
        return call(
            functools.partial(first_pass, across),
            shape(targets, width, size),
            (block_count, source_ids, target_ids, emb, source_deg, target_deg, block_vals),
            [SMEM, SMEM, SMEM, VMEM, VMEM, VMEM, ANY],
            product_scratch(slots, size, width, sources, targets),
            product_flops, product_bytes,
        )

    def picked(rows, table, peer_ids):
        peers = peer_ids.shape[0]
        blocks = table.shape[0]
        return call(
            functools.partial(gather, rows),
            [shape(peers, width, trips)] * 2,
            (table, peer_ids),
            [VMEM, VMEM],
            [pltpu.VMEM((3 * width, blocks * size), BF16)],
            2 * peers * 2 * 3 * width * blocks * size * trips, 4 * blocks * width * size,
        )

    def reduced(rows, table, peer_ids, axis):
        peers = peer_ids.shape[0]
        keep, send = picked(rows, table, peer_ids)
        received = swap(send)
        dealt = call(
            functools.partial(add_split, peers),
            [shape(width, trips)] * peers,
            (keep, received), [VMEM, VMEM],
            moved=12 * peers * width * trips,
        )
        return [dealt[0]] + [shift(dealt[o], axis, peers, o) for o in range(1, peers)]

    item_table = first(False, user_emb, user_deg, item_deg, block_row, block_col,
                       user_blocks, item_blocks)
    item_parts = reduced([1, 2], item_table, ids_item, "user")
    user_table = first(True, item_emb, item_deg, user_deg, block_col, block_row,
                       item_blocks, user_blocks)
    user_parts = reduced([0], user_table, ids_user, "item")
    user_base, item_base = call(
        gather_base, [shape(width, trips)] * 2, (user_emb, item_emb, ids_item),
        [VMEM, VMEM, VMEM], (), 4 * width * trips * size * (user_blocks + item_blocks),
        2 * width * size * (user_blocks + item_blocks),
    )
    user_parts.append(user_base)
    item_parts.append(item_base)
    pieces, pushed = call(
        functools.partial(slopes, len(user_parts), len(item_parts)),
        [shape(width, trips)] * 2,
        (*user_parts, *item_parts), [VMEM] * (len(user_parts) + len(item_parts)),
        moved=4 * width * trips * (len(user_parts) + len(item_parts) + 2),
    )

    def shared(own, axis, peers):
        arrays, chunks = [own, swap(own)], [(0, 0), (0, 1)]
        for offset in range(1, peers):
            come = shift(own, axis, peers, offset)
            arrays += [come, swap(come)]
            chunks += [(peers - offset, 0), (peers - offset, 1)]
        return arrays, chunks

    def second(across, rows, own, axis, peer_ids, source_deg, target_deg, source_ids, target_ids,
               sources, targets):
        arrays, chunks = shared(own, axis, peer_ids.shape[0])
        return call(
            functools.partial(second_pass, across, rows, chunks),
            [shape(sources, width, size), shape(targets, half, size), shape(targets, half, size)],
            (block_count, source_ids, target_ids, peer_ids, source_deg, target_deg, block_vals,
             *arrays),
            [SMEM, SMEM, SMEM, VMEM, VMEM, VMEM, ANY] + [VMEM] * len(arrays),
            product_scratch(slots, size, width, sources, targets)
            + [pltpu.VMEM((len(arrays), 3 * width, trips), BF16)],
            product_flops + 2 * len(arrays) * 3 * width * trips * sources * size, product_bytes,
        )

    user_half_grad, item_keep, item_send = second(
        False, [0], pieces, "item", ids_user, user_deg, item_deg, block_row, block_col,
        user_blocks, item_blocks)
    item_half_grad, user_keep, user_send = second(
        True, [1, 2], pushed, "user", ids_item, item_deg, user_deg, block_col, block_row,
        item_blocks, user_blocks)

    per = item_blocks // users
    dealt = call(
        functools.partial(add_deal, users), [shape(per, half, size)] * users,
        (item_keep, swap(item_send)), [VMEM, VMEM], moved=12 * item_blocks * half * size,
    )
    parts = [dealt[0]] + [shift(dealt[o], "user", users, o) for o in range(1, users)]
    own = call(sum_parts, shape(per, half, size), tuple(parts), [VMEM] * users,
               moved=4 * (users + 1) * per * half * size)
    mine = [own] + [shift(own, "user", users, -o) for o in range(1, users)]
    other = [swap(part) for part in mine]
    grad_item = call(
        functools.partial(finish_items, users), shape(width, item_blocks * size),
        (item_half_grad, *mine, *other), [VMEM] * (2 * users + 1),
        moved=12 * item_blocks * width * size,
    )

    own = call(add_two, shape(user_blocks, half, size), (user_keep, swap(user_send)),
               [VMEM, VMEM], moved=12 * user_blocks * half * size)
    mine = [own] + [shift(own, "item", items, o) for o in range(1, items)]
    other = [swap(part) for part in mine]
    grad_user = call(
        functools.partial(finish_users, items), shape(width, user_blocks * size),
        (user_half_grad, *mine, *other), [VMEM] * (2 * items + 1),
        moved=12 * user_blocks * width * size,
    )
    return (grad_user, grad_item)


def solution(mesh):
    return jax.shard_map(
        functools.partial(on_device, mesh.shape["user"], mesh.shape["item"]),
        mesh=mesh,
        in_specs=(
            P(None, ("groups", "user")),
            P(None, ("groups", "item")),
            P(("groups", "user")),
            P(("groups", "item")),
            P(("groups", "user", "item", "rep"), None, None),
            P(("groups", "user", "item", "rep")),
            P(("groups", "user", "item", "rep")),
            P(("groups", "user", "item", "rep")),
            P(("groups", "user", "item", "rep")),
            P(("groups", "user", "item", "rep")),
            P(("groups", "user", "item", "rep")),
        ),
        out_specs=(P(None, ("groups", "user")), P(None, ("groups", "item"))),
        check_vma=False,
    )
```

```python
import functools

import jax
import jax.numpy as jnp
from jax import lax
from jax.experimental import pallas as pl
from jax.experimental.pallas import tpu as pltpu
from jax.sharding import PartitionSpec as P

F32 = jnp.float32
BF16 = jnp.bfloat16
PACK = 4
GROUP = 4

VMEM = pl.BlockSpec(memory_space=pltpu.VMEM)
SMEM = pl.BlockSpec(memory_space=pltpu.SMEM)
ANY = pl.BlockSpec(memory_space=pl.ANY)
HBM = pl.BlockSpec(memory_space=pltpu.HBM)


def call(kernel, outs, ins, specs, scratch=(), flops=0, moved=0, room=24):
    return pl.pallas_call(
        kernel,
        out_shape=outs,
        in_specs=specs,
        out_specs=jax.tree.map(lambda _: VMEM, outs),
        scratch_shapes=list(scratch),
        cost_estimate=pl.CostEstimate(flops=flops, bytes_accessed=moved, transcendentals=0),
        compiler_params=pltpu.CompilerParams(vmem_limit_bytes=room * 1024 * 1024),
    )(*ins)


def shape(*dims):
    return jax.ShapeDtypeStruct(dims, F32)


def split3(values):
    high = values.astype(BF16)
    rest = values - high.astype(F32)
    middle = rest.astype(BF16)
    low = (rest - middle.astype(F32)).astype(BF16)
    return high, middle, low


def hot(ids, start, rows):
    place = lax.broadcasted_iota(jnp.int32, (rows, ids.shape[1]), 0) + start
    return jnp.where(place == ids, 1.0, 0.0)


def sort_slots(keys, sources, count, blocks):
    lanes = keys.shape[1]
    rows = 2 * blocks
    place = lax.broadcasted_iota(jnp.int32, (1, lanes), 1)
    live = place < count
    mine = (lax.broadcasted_iota(jnp.int32, (rows, lanes), 0) == keys) & live
    mine = jnp.where(mine, 1.0, 0.0)
    earlier = lax.broadcasted_iota(jnp.int32, (lanes, lanes), 0) < lax.broadcasted_iota(
        jnp.int32, (lanes, lanes), 1)
    before = jnp.dot(mine.astype(BF16), jnp.where(earlier, 1.0, 0.0).astype(BF16),
                     preferred_element_type=F32)
    packs = jnp.floor((jnp.sum(mine, axis=1, keepdims=True) + (PACK - 1)) * (1.0 / PACK))
    packs = jnp.broadcast_to(packs, (rows, 128))
    lower = lax.broadcasted_iota(jnp.int32, (rows, rows), 1) < lax.broadcasted_iota(
        jnp.int32, (rows, rows), 0)
    first = jnp.dot(jnp.where(lower, 1.0, 0.0).astype(BF16), packs.astype(BF16),
                    preferred_element_type=F32)
    position = jnp.sum(mine * (first[:, :1] * PACK + before), axis=0, keepdims=True)
    position = jnp.where(live, position.astype(jnp.int32), -1)
    match = lax.broadcasted_iota(jnp.int32, (lanes, lanes), 0) == position
    row = lax.broadcasted_iota(jnp.int32, (16, lanes), 0)
    values = jnp.where(row == 0, place // 16, jnp.where(row == 1, place % 16, jnp.where(
        row == 2, sources, jnp.where(row == 3, keys, jnp.where(row == 4, 1, 0)))))
    values = jnp.where(live, values, 0).astype(F32)
    found = lax.dot_general(values.astype(BF16), jnp.where(match, 1.0, 0.0).astype(BF16),
                            (((1,), (1,)), ((), ())), preferred_element_type=F32)
    found = found.astype(jnp.int32)
    valid = found[4:5] > 0
    total = jnp.broadcast_to(jnp.sum(packs[:, :1], axis=0, keepdims=True), (1, lanes))
    row = lax.broadcasted_iota(jnp.int32, (8, lanes), 0)
    slot = found[0:1] * 16 + found[1:2]
    source = jnp.where(valid, found[2:3], blocks)
    target = jnp.where(valid, found[3:4], blocks)
    return jnp.where(row == 0, slot, jnp.where(row == 1, source, jnp.where(
        row == 2, target, total.astype(jnp.int32))))


def multiply_blocks(order, vals, source, total, across):
    total[...] = jnp.zeros_like(total)
    contract = (((1,), (1,)), ((), ())) if across else (((1,), (0,)), ((), ()))

    def group(index, _):
        targets, terms = [], []
        for step in range(GROUP):
            places = [(index * GROUP + step) * PACK + each for each in range(PACK)]
            left = jnp.concatenate([source[order[1, place]] for place in places], axis=1)
            right = jnp.concatenate([vals[order[0, place]] for place in places],
                                    axis=1 if across else 0)
            targets.append(order[2, places[0]])
            terms.append(lax.dot_general(left, right, contract, preferred_element_type=F32))
        for target, term in zip(targets, terms):
            total[target] += term
        return 0

    lax.fori_loop(0, (order[3, 0] + GROUP - 1) // GROUP, group, 0)


def begin(out):
    out[...] = jnp.zeros_like(out)


def stack_ids(user, positive, negative, after, out):
    for row, ids in enumerate((user, positive, negative)):
        out[row:row + 1, :] = ids[...]


def prepare(count, rows, columns, user_emb, item_emb, user_deg, item_deg, after,
            user_source, item_source, user_scale, item_scale, item_order, user_order, keys):
    live = count[0]
    slots = rows.shape[0]
    keys[...] = jnp.zeros_like(keys)
    keys[0:1, 0:slots] = rows[...].reshape(1, slots)
    keys[1:2, 0:slots] = columns[...].reshape(1, slots)
    users, items = keys[0:1, :], keys[1:2, :]
    item_order[...] = sort_slots(items, users, live, item_scale.shape[0])
    user_order[...] = sort_slots(users, items, live, user_scale.shape[0])
    for emb, deg, scale, into in ((user_emb, user_deg, user_scale, user_source),
                                  (item_emb, item_deg, item_scale, item_source)):
        scale[...] = lax.rsqrt(deg[...].astype(F32))
        blocks, size = scale.shape
        for block in range(blocks):
            piece = emb[:, block * size:(block + 1) * size].astype(F32)
            into[block] = (scale[block:block + 1, :] * piece).astype(BF16)
        into[blocks] = jnp.zeros(into.shape[1:], BF16)


def first_pass(across, order, vals, source, total):
    multiply_blocks(order, vals, source, total, across)


def table_of(blocks, scale, table):
    _, width, size = blocks.shape
    for block in range(scale.shape[0]):
        span = slice(block * size, (block + 1) * size)
        for part, piece in enumerate(split3(scale[block:block + 1, :] * blocks[block])):
            table[part * width:(part + 1) * width, span] = piece


def fold(stacked, width):
    return (
        stacked[:width] + stacked[width:2 * width] + stacked[2 * width:3 * width]
    )


def pick(table, ids_ref, peer, rows, tile):
    total = None
    for start in range(0, table.shape[1], tile):
        chosen = hot(ids_ref[peer, pl.ds(rows[0], 1), :], start, tile)
        if len(rows) == 2:
            chosen = chosen - hot(ids_ref[peer, pl.ds(rows[1], 1), :], start, tile)
        term = jnp.dot(
            table[:, start:start + tile], chosen.astype(BF16), preferred_element_type=F32
        )
        total = term if total is None else total + term
    return total


def gather(rows, blocks, scale, ids, keep, send, table):
    width = blocks.shape[1]
    tile = 2 * blocks.shape[2]
    table_of(blocks, scale, table)

    def one(peer, _):
        keep[peer] = fold(pick(table, ids, peer, rows, tile), width)
        send[peer] = fold(pick(table, ids, peer, [row + 3 for row in rows], tile), width)
        return 0

    lax.fori_loop(0, ids.shape[0], one, 0)


def gather_base(user_emb, item_emb, ids, user_out, item_out):
    user_out[...] = pick(user_emb, ids, 0, [0], 256)
    item_out[...] = pick(item_emb, ids, 0, [1, 2], 256)


def add_split(peers, keep, received, *outs):
    for peer in range(peers):
        outs[peer][...] = keep[peer] + received[peer]


def add_all(refs):
    total = refs[0][...]
    for ref in refs[1:]:
        total = total + ref[...]
    return total


def slopes(user_parts, item_parts, *refs):
    users, items = refs[:user_parts], refs[user_parts:user_parts + item_parts]
    pieces, pushed = refs[user_parts + item_parts:]
    user_rows = 0.5 * add_all(users)
    difference = 0.5 * add_all(items)
    margin = jnp.sum(user_rows * difference, axis=0, keepdims=True)
    slope = -jax.nn.sigmoid(-margin)
    pieces[...] = slope * difference
    pushed[...] = slope * user_rows


def second_pass(across, rows, chunks, order, ids, source_scale, target_scale, vals, after, *refs):
    pieces = refs[:len(chunks)]
    half_grad, keep, send, source, total, table = refs[len(chunks):]
    blocks, width, size = half_grad.shape
    tile = 2 * size
    for place, piece in enumerate(pieces):
        for part, value in enumerate(split3(piece[...])):
            table[place, part * width:(part + 1) * width, :] = value
    for start in range(0, blocks * size, tile):
        total_here = jnp.zeros((3 * width, tile), F32)
        for place, (peer, other) in enumerate(chunks):
            chosen = hot(ids[peer, pl.ds(rows[0] + 3 * other, 1), :], start, tile)
            if len(rows) == 2:
                chosen = chosen - hot(ids[peer, pl.ds(rows[1] + 3 * other, 1), :], start, tile)
            total_here = total_here + lax.dot_general(
                table[place], chosen.astype(BF16), (((1,), (1,)), ((), ())),
                preferred_element_type=F32,
            )
        grad = fold(total_here, width)
        for offset in range(0, tile, size):
            block = (start + offset) // size
            mine = grad[:, offset:offset + size]
            half_grad[block] = 0.5 * mine
            source[block] = (source_scale[block:block + 1, :] * mine * 0.5).astype(BF16)
    source[blocks] = jnp.zeros((width, size), BF16)
    multiply_blocks(order, vals, source, total, across)
    me = lax.axis_index("rep")
    half = keep.shape[1]
    for block in range(keep.shape[0]):
        scale = target_scale[block:block + 1, :]
        keep[block] = scale * total[block, pl.ds(pl.multiple_of(me * half, half), half), :]
        send[block] = scale * total[block, pl.ds(pl.multiple_of((1 - me) * half, half), half), :]


def add_deal(peers, keep, received, *outs):
    me = lax.axis_index("user")
    per = outs[0].shape[0]
    for offset in range(peers):
        there = lax.rem(me + offset, peers) * per
        for block in range(per):
            outs[offset][block] = keep[there + block] + received[there + block]


def add_two(keep, received, out):
    out[...] = keep[...] + received[...]


def sum_parts(*refs):
    refs[-1][...] = add_all(refs[:-1])


def finish_users(parts, half_grad, *refs):
    mine, other = refs[:parts], refs[parts:2 * parts]
    out = refs[-1]
    me = lax.axis_index("rep")
    blocks, width, size = half_grad.shape
    half = width // 2
    for block in range(blocks):
        span = slice(block * size, (block + 1) * size)
        for rank, group in ((me, mine), (1 - me, other)):
            rows = pl.ds(pl.multiple_of(rank * half, half), half)
            total = half_grad[block, rows, :]
            for ref in group:
                total = total + ref[block]
            out[rows, span] = total


def finish_items(peers, half_grad, *refs):
    mine, other = refs[:peers], refs[peers:2 * peers]
    out = refs[-1]
    me = lax.axis_index("rep")
    place = lax.axis_index("user")
    blocks, width, size = half_grad.shape
    half = width // 2
    per = blocks // peers
    for offset in range(peers):
        there = lax.rem(place + offset, peers) * per
        for block in range(per):
            span = pl.ds(pl.multiple_of((there + block) * size, size), size)
            for rank, group in ((me, mine), (1 - me, other)):
                rows = pl.ds(pl.multiple_of(rank * half, half), half)
                out[rows, span] = half_grad[there + block, rows, :] + group[offset][block]


def shift(values, axis, count, offset):
    return lax.ppermute(values, axis, [(i, (i + offset) % count) for i in range(count)])


def on_device(users, items, user_emb, item_emb, user_deg, item_deg, block_vals, block_row,
              block_col, block_count, trip_user, trip_pos, trip_neg):
    width = user_emb.shape[0]
    slots, size, _ = block_vals.shape
    user_blocks = user_emb.shape[1] // size
    item_blocks = item_emb.shape[1] // size
    trips = trip_user.shape[0]
    half = width // 2
    swap = functools.partial(shift, axis="rep", count=2, offset=1)
    user_deg = user_deg.reshape(user_blocks, size)
    item_deg = item_deg.reshape(item_blocks, size)

    product_flops = 2 * slots * size * size * width
    product_bytes = slots * size * size * 2
    started = call(begin, shape(8, size), (), [], (), 16 * product_flops, product_bytes)
    ids = call(
        stack_ids, jax.ShapeDtypeStruct((3, trips), jnp.int32),
        [each.reshape(1, trips) for each in (trip_user, trip_pos, trip_neg)] + [started],
        [VMEM, VMEM, VMEM, ANY],
    )
    both = jnp.concatenate([ids, swap(ids)])
    ids_user = jnp.stack([both] + [shift(both, "item", items, -o) for o in range(1, items)])
    ids_item = jnp.stack([both] + [shift(both, "user", users, -o) for o in range(1, users)])

    lanes = -(-slots // size) * size

    order_shape = jax.ShapeDtypeStruct((8, lanes), jnp.int32)
    def source_shape(blocks):
        return jax.ShapeDtypeStruct((blocks + 1, width, size), BF16)

    (user_source, item_source, user_scale, item_scale, item_order, user_order) = call(
        prepare,
        [source_shape(user_blocks), source_shape(item_blocks), shape(user_blocks, size),
         shape(item_blocks, size), order_shape, order_shape],
        (block_count, block_row, block_col, user_emb, item_emb, user_deg, item_deg, ids),
        [SMEM, VMEM, VMEM, VMEM, VMEM, VMEM, VMEM, ANY],
        [pltpu.VMEM((8, lanes), jnp.int32)], product_flops, product_bytes,
    )
    item_table = call(
        functools.partial(first_pass, False), shape(item_blocks + 1, width, size),
        (item_order, block_vals, user_source), [SMEM, VMEM, VMEM], (),
        product_flops, product_bytes,
    )
    user_table = call(
        functools.partial(first_pass, True), shape(user_blocks + 1, width, size),
        (user_order, block_vals, item_source), [SMEM, VMEM, VMEM], (),
        product_flops, product_bytes,
    )

    def picked(rows, table, scale, peer_ids):
        peers = peer_ids.shape[0]
        blocks = scale.shape[0]
        return call(
            functools.partial(gather, rows),
            [shape(peers, width, trips)] * 2,
            (table, scale, peer_ids),
            [VMEM, VMEM, VMEM],
            [pltpu.VMEM((3 * width, blocks * size), BF16)],
            2 * peers * 2 * 3 * width * blocks * size * trips, 4 * blocks * width * size,
        )

    def reduced(rows, table, scale, peer_ids, axis):
        peers = peer_ids.shape[0]
        keep, send = picked(rows, table, scale, peer_ids)
        received = swap(send)
        dealt = call(
            functools.partial(add_split, peers),
            [shape(width, trips)] * peers,
            (keep, received), [VMEM, VMEM],
            moved=12 * peers * width * trips,
        )
        return [dealt[0]] + [shift(dealt[o], axis, peers, o) for o in range(1, peers)]

    item_parts = reduced([1, 2], item_table, item_scale, ids_item, "user")
    user_parts = reduced([0], user_table, user_scale, ids_user, "item")
    user_base, item_base = call(
        gather_base, [shape(width, trips)] * 2, (user_emb, item_emb, ids_item),
        [VMEM, VMEM, VMEM], (), 4 * width * trips * size * (user_blocks + item_blocks),
        2 * width * size * (user_blocks + item_blocks),
    )
    user_parts.append(user_base)
    item_parts.append(item_base)
    pieces, pushed = call(
        functools.partial(slopes, len(user_parts), len(item_parts)),
        [shape(width, trips)] * 2,
        (*user_parts, *item_parts), [VMEM] * (len(user_parts) + len(item_parts)),
        moved=4 * width * trips * (len(user_parts) + len(item_parts) + 2),
    )

    def shared(own, axis, peers):
        arrays, chunks = [own, swap(own)], [(0, 0), (0, 1)]
        for offset in range(1, peers):
            come = shift(own, axis, peers, offset)
            arrays += [come, swap(come)]
            chunks += [(peers - offset, 0), (peers - offset, 1)]
        return arrays, chunks

    def second(across, rows, own, axis, peer_ids, order, source_scale, target_scale, after):
        arrays, chunks = shared(own, axis, peer_ids.shape[0])
        sources, targets = source_scale.shape[0], target_scale.shape[0]
        return call(
            functools.partial(second_pass, across, rows, chunks),
            [shape(sources, width, size), shape(targets, half, size), shape(targets, half, size)],
            (order, peer_ids, source_scale, target_scale, block_vals, after, *arrays),
            [SMEM, VMEM, VMEM, VMEM, VMEM, ANY] + [VMEM] * len(arrays),
            [pltpu.VMEM((sources + 1, width, size), BF16),
             pltpu.VMEM((targets + 1, width, size), F32),
             pltpu.VMEM((len(arrays), 3 * width, trips), BF16)],
            product_flops + 2 * len(arrays) * 3 * width * trips * sources * size, product_bytes,
        )

    user_half_grad, item_keep, item_send = second(
        False, [0], pieces, "item", ids_user, item_order, user_scale, item_scale, pieces)
    item_half_grad, user_keep, user_send = second(
        True, [1, 2], pushed, "user", ids_item, user_order, item_scale, user_scale, item_send)

    per = item_blocks // users
    dealt = call(
        functools.partial(add_deal, users), [shape(per, half, size)] * users,
        (item_keep, swap(item_send)), [VMEM, VMEM], moved=12 * item_blocks * half * size,
    )
    parts = [dealt[0]] + [shift(dealt[o], "user", users, o) for o in range(1, users)]
    own = call(sum_parts, shape(per, half, size), tuple(parts), [VMEM] * users,
               moved=4 * (users + 1) * per * half * size)
    mine = [own] + [shift(own, "user", users, -o) for o in range(1, users)]
    other = [swap(part) for part in mine]
    grad_item = call(
        functools.partial(finish_items, users), shape(width, item_blocks * size),
        (item_half_grad, *mine, *other), [VMEM] * (2 * users + 1),
        moved=12 * item_blocks * width * size,
    )

    own = call(add_two, shape(user_blocks, half, size), (user_keep, swap(user_send)),
               [VMEM, VMEM], moved=12 * user_blocks * half * size)
    mine = [own] + [shift(own, "item", items, o) for o in range(1, items)]
    other = [swap(part) for part in mine]
    grad_user = call(
        functools.partial(finish_users, items), shape(width, user_blocks * size),
        (user_half_grad, *mine, *other), [VMEM] * (2 * items + 1),
        moved=12 * user_blocks * width * size,
    )
    return (grad_user, grad_item)


def solution(mesh):
    return jax.shard_map(
        functools.partial(on_device, mesh.shape["user"], mesh.shape["item"]),
        mesh=mesh,
        in_specs=(
            P(None, ("groups", "user")),
            P(None, ("groups", "item")),
            P(("groups", "user")),
            P(("groups", "item")),
            P(("groups", "user", "item", "rep"), None, None),
            P(("groups", "user", "item", "rep")),
            P(("groups", "user", "item", "rep")),
            P(("groups", "user", "item", "rep")),
            P(("groups", "user", "item", "rep")),
            P(("groups", "user", "item", "rep")),
            P(("groups", "user", "item", "rep")),
        ),
        out_specs=(P(None, ("groups", "user")), P(None, ("groups", "item"))),
        check_vma=False,
    )
```

```python
import functools

import jax
import jax.numpy as jnp
from jax import lax
from jax.experimental import pallas as pl
from jax.experimental.pallas import tpu as pltpu
from jax.sharding import PartitionSpec as P

F32 = jnp.float32
BF16 = jnp.bfloat16
PACK = 4
GROUP = 4

VMEM = pl.BlockSpec(memory_space=pltpu.VMEM)
SMEM = pl.BlockSpec(memory_space=pltpu.SMEM)
ANY = pl.BlockSpec(memory_space=pl.ANY)
HBM = pl.BlockSpec(memory_space=pltpu.HBM)


def call(kernel, outs, ins, specs, scratch=(), flops=0, moved=0, room=24):
    return pl.pallas_call(
        kernel,
        out_shape=outs,
        in_specs=specs,
        out_specs=jax.tree.map(lambda _: VMEM, outs),
        scratch_shapes=list(scratch),
        cost_estimate=pl.CostEstimate(flops=flops, bytes_accessed=moved, transcendentals=0),
        compiler_params=pltpu.CompilerParams(vmem_limit_bytes=room * 1024 * 1024),
    )(*ins)


def shape(*dims):
    return jax.ShapeDtypeStruct(dims, F32)


def split3(values):
    high = values.astype(BF16)
    rest = values - high.astype(F32)
    middle = rest.astype(BF16)
    low = (rest - middle.astype(F32)).astype(BF16)
    return high, middle, low


def hot(ids_ref, rows, start, tile):
    ids = [ids_ref[row:row + 1, :] for row in rows]
    if len(rows) == 2:
        same = ids[0] == ids[1]
        ids = [jnp.where(same, -1, each) for each in ids]
    ids = [each.astype(jnp.int16) for each in ids]
    place = lax.broadcasted_iota(jnp.int16, (tile, ids[0].shape[1]), 0) + jnp.int16(start)
    chosen = jnp.zeros(place.shape, BF16)
    for each, sign in zip(ids, (1, -1)):
        chosen = jnp.where(place == each, jnp.asarray(sign, BF16), chosen)
    return chosen


def sort_slots(keys, sources, count, blocks):
    lanes = keys.shape[1]
    rows = 2 * blocks
    place = lax.broadcasted_iota(jnp.int32, (1, lanes), 1)
    live = place < count
    mine = (lax.broadcasted_iota(jnp.int32, (rows, lanes), 0) == keys) & live
    mine = jnp.where(mine, 1.0, 0.0)
    earlier = lax.broadcasted_iota(jnp.int32, (lanes, lanes), 0) < lax.broadcasted_iota(
        jnp.int32, (lanes, lanes), 1)
    before = jnp.dot(mine.astype(BF16), jnp.where(earlier, 1.0, 0.0).astype(BF16),
                     preferred_element_type=F32)
    packs = jnp.floor((jnp.sum(mine, axis=1, keepdims=True) + (PACK - 1)) * (1.0 / PACK))
    packs = jnp.broadcast_to(packs, (rows, 128))
    lower = lax.broadcasted_iota(jnp.int32, (rows, rows), 1) < lax.broadcasted_iota(
        jnp.int32, (rows, rows), 0)
    first = jnp.dot(jnp.where(lower, 1.0, 0.0).astype(BF16), packs.astype(BF16),
                    preferred_element_type=F32)
    position = jnp.sum(mine * (first[:, :1] * PACK + before), axis=0, keepdims=True)
    position = jnp.where(live, position.astype(jnp.int32), -1)
    match = lax.broadcasted_iota(jnp.int32, (lanes, lanes), 0) == position
    row = lax.broadcasted_iota(jnp.int32, (16, lanes), 0)
    values = jnp.where(row == 0, place // 16, jnp.where(row == 1, place % 16, jnp.where(
        row == 2, sources, jnp.where(row == 3, keys, jnp.where(row == 4, 1, 0)))))
    values = jnp.where(live, values, 0).astype(F32)
    found = lax.dot_general(values.astype(BF16), jnp.where(match, 1.0, 0.0).astype(BF16),
                            (((1,), (1,)), ((), ())), preferred_element_type=F32)
    found = found.astype(jnp.int32)
    valid = found[4:5] > 0
    total = jnp.broadcast_to(jnp.sum(packs[:, :1], axis=0, keepdims=True), (1, lanes))
    row = lax.broadcasted_iota(jnp.int32, (8, lanes), 0)
    slot = found[0:1] * 16 + found[1:2]
    source = jnp.where(valid, found[2:3], blocks)
    target = jnp.where(valid, found[3:4], 0)
    return jnp.where(row == 0, slot, jnp.where(row == 1, source, jnp.where(
        row == 2, target, total.astype(jnp.int32))))


def multiply_blocks(order, vals, source, total, across):
    total[...] = jnp.zeros_like(total)
    contract = (((1,), (1,)), ((), ())) if across else (((1,), (0,)), ((), ()))

    def group(index, _):
        targets, terms = [], []
        for step in range(GROUP):
            places = [(index * GROUP + step) * PACK + each for each in range(PACK)]
            left = jnp.concatenate([source[order[1, place]] for place in places], axis=1)
            right = jnp.concatenate([vals[order[0, place]] for place in places],
                                    axis=1 if across else 0)
            targets.append(order[2, places[0]])
            terms.append(lax.dot_general(left, right, contract, preferred_element_type=F32))
        for target, term in zip(targets, terms):
            total[target] += term
        return 0

    lax.fori_loop(0, (order[3, 0] + GROUP - 1) // GROUP, group, 0)


def begin(out):
    out[...] = jnp.zeros_like(out)


def stack_ids(user, positive, negative, after, out):
    for row, ids in enumerate((user, positive, negative)):
        out[row:row + 1, :] = ids[...]


def prepare(count, rows, columns, user_emb, item_emb, user_deg, item_deg, after,
            user_source, item_source, user_scale, item_scale, item_order, user_order, keys):
    live = count[0]
    slots = rows.shape[0]
    keys[...] = jnp.zeros_like(keys)
    keys[0:1, 0:slots] = rows[...].reshape(1, slots)
    keys[1:2, 0:slots] = columns[...].reshape(1, slots)
    users, items = keys[0:1, :], keys[1:2, :]
    item_order[...] = sort_slots(items, users, live, item_scale.shape[0])
    user_order[...] = sort_slots(users, items, live, user_scale.shape[0])
    for emb, deg, scale, into in ((user_emb, user_deg, user_scale, user_source),
                                  (item_emb, item_deg, item_scale, item_source)):
        scale[...] = lax.rsqrt(deg[...].astype(F32))
        blocks, size = scale.shape
        for block in range(blocks):
            piece = emb[:, block * size:(block + 1) * size].astype(F32)
            into[block] = (scale[block:block + 1, :] * piece).astype(BF16)
        into[blocks] = jnp.zeros(into.shape[1:], BF16)


def first_pass(across, order, vals, source, after, total):
    multiply_blocks(order, vals, source, total, across)


def fold(stacked, width):
    return (
        stacked[:width] + stacked[width:2 * width] + stacked[2 * width:3 * width]
    )


def pick(table, ids_ref, rows, tile):
    total = None
    for start in range(0, table.shape[1], tile):
        term = jnp.dot(
            table[:, start:start + tile], hot(ids_ref, rows, start, tile),
            preferred_element_type=F32,
        )
        total = term if total is None else total + term
    return total


def gather(rows, peers, mine, other, scale, *refs):
    ids, outs, table = refs[:peers], refs[peers:2 * peers], refs[2 * peers]
    blocks, width, size = mine.shape
    for block in range(blocks):
        span = slice(block * size, (block + 1) * size)
        here = scale[block:block + 1, :] * (mine[block] + other[block])
        for part, piece in enumerate(split3(here)):
            table[part * width:(part + 1) * width, span] = piece
    for peer in range(peers):
        outs[peer][...] = fold(pick(table, ids[peer], rows, 2 * size), width)


def scatter(rows, peers, after, *refs):
    pieces, ids, out, table = refs[:peers], refs[peers:2 * peers], refs[2 * peers], refs[-1]
    blocks, width, size = out.shape
    tile = 2 * size
    for place, piece in enumerate(pieces):
        for part, value in enumerate(split3(piece[...])):
            table[place, part * width:(part + 1) * width, :] = value
    for start in range(0, blocks * size, tile):
        total = None
        for place in range(peers):
            term = lax.dot_general(
                table[place], hot(ids[place], rows, start, tile), (((1,), (1,)), ((), ())),
                preferred_element_type=F32,
            )
            total = term if total is None else total + term
        total = fold(total, width)
        for offset in range(0, tile, size):
            out[(start + offset) // size] = total[:, offset:offset + size]


def gather_base(user_emb, item_emb, ids, user_out, item_out):
    tile = ids.shape[1]
    user_out[...] = pick(user_emb, ids, [0], tile)
    item_out[...] = pick(item_emb, ids, [1, 2], tile)


def add_all(refs):
    total = refs[0][...]
    for ref in refs[1:]:
        total = total + ref[...]
    return total


def slopes(user_parts, item_parts, *refs):
    users, items = refs[:user_parts], refs[user_parts:user_parts + item_parts]
    pieces, pushed = refs[user_parts + item_parts:]
    user_rows = 0.5 * add_all(users)
    difference = 0.5 * add_all(items)
    margin = jnp.sum(user_rows * difference, axis=0, keepdims=True)
    slope = -jax.nn.sigmoid(-margin)
    pieces[...] = slope * difference
    pushed[...] = slope * user_rows


def second_pass(across, order, mine, other, source_scale, target_scale, vals, after,
                half_grad, keep, send, source, total):
    blocks, width, size = mine.shape
    for block in range(blocks):
        grad = mine[block] + other[block]
        half_grad[block] = 0.5 * grad
        source[block] = (source_scale[block:block + 1, :] * grad * 0.5).astype(BF16)
    source[blocks] = jnp.zeros((width, size), BF16)
    multiply_blocks(order, vals, source, total, across)
    me = lax.axis_index("rep")
    half = keep.shape[1]
    for block in range(keep.shape[0]):
        scale = target_scale[block:block + 1, :]
        keep[block] = scale * total[block, pl.ds(pl.multiple_of(me * half, half), half), :]
        send[block] = scale * total[block, pl.ds(pl.multiple_of((1 - me) * half, half), half), :]


def add_deal(peers, keep, received, *outs):
    me = lax.axis_index("user")
    per = outs[0].shape[0]
    for offset in range(peers):
        there = lax.rem(me + offset, peers) * per
        for block in range(per):
            outs[offset][block] = keep[there + block] + received[there + block]


def sum_parts(*refs):
    refs[-1][...] = add_all(refs[:-1])


def pack(*refs):
    for place, ref in enumerate(refs[:-1]):
        refs[-1][place] = ref[...]


def finish_users(half_grad, mine, other, out):
    me = lax.axis_index("rep")
    blocks, width, size = half_grad.shape
    half = width // 2
    for block in range(blocks):
        span = slice(block * size, (block + 1) * size)
        for rank, part in ((me, mine), (1 - me, other)):
            rows = pl.ds(pl.multiple_of(rank * half, half), half)
            out[rows, span] = half_grad[block, rows, :] + part[block]


def finish_items(peers, half_grad, mine, other, out):
    me = lax.axis_index("rep")
    place = lax.axis_index("user")
    blocks, width, size = half_grad.shape
    half = width // 2
    per = blocks // peers
    for offset in range(peers):
        there = lax.rem(place + offset, peers) * per
        for block in range(per):
            span = pl.ds(pl.multiple_of((there + block) * size, size), size)
            for rank, part in ((me, mine), (1 - me, other)):
                rows = pl.ds(pl.multiple_of(rank * half, half), half)
                out[rows, span] = half_grad[there + block, rows, :] + part[offset, block]


def shift(values, axis, count, offset):
    return lax.ppermute(values, axis, [(i, (i + offset) % count) for i in range(count)])


def on_device(users, items, user_emb, item_emb, user_deg, item_deg, block_vals, block_row,
              block_col, block_count, trip_user, trip_pos, trip_neg):
    width = user_emb.shape[0]
    slots, size, _ = block_vals.shape
    user_blocks = user_emb.shape[1] // size
    item_blocks = item_emb.shape[1] // size
    trips = trip_user.shape[0]
    half = width // 2
    swap = functools.partial(shift, axis="rep", count=2, offset=1)
    user_deg = user_deg.reshape(user_blocks, size)
    item_deg = item_deg.reshape(item_blocks, size)

    product_flops = 2 * slots * size * size * width
    product_bytes = slots * size * size * 2
    started = call(begin, shape(8, size), (), [], (), 16 * product_flops, product_bytes)
    ids = call(
        stack_ids, jax.ShapeDtypeStruct((3, trips), jnp.int32),
        [each.reshape(1, trips) for each in (trip_user, trip_pos, trip_neg)] + [started],
        [VMEM, VMEM, VMEM, ANY],
    )
    ids_user = [ids] + [shift(ids, "item", items, -o) for o in range(1, items)]
    ids_item = [ids] + [shift(ids, "user", users, -o) for o in range(1, users)]
    lanes = -(-slots // size) * size

    order_shape = jax.ShapeDtypeStruct((8, lanes), jnp.int32)
    def source_shape(blocks):
        return jax.ShapeDtypeStruct((blocks + 1, width, size), BF16)

    (user_source, item_source, user_scale, item_scale, item_order, user_order) = call(
        prepare,
        [source_shape(user_blocks), source_shape(item_blocks), shape(user_blocks, size),
         shape(item_blocks, size), order_shape, order_shape],
        (block_count, block_row, block_col, user_emb, item_emb, user_deg, item_deg, ids),
        [SMEM, VMEM, VMEM, VMEM, VMEM, VMEM, VMEM, ANY],
        [pltpu.VMEM((8, lanes), jnp.int32)], product_flops, product_bytes,
    )
    item_table = call(
        functools.partial(first_pass, False), shape(item_blocks, width, size),
        (item_order, block_vals, user_source, ids), [SMEM, VMEM, VMEM, ANY], (),
        product_flops, product_bytes,
    )
    user_table = call(
        functools.partial(first_pass, True), shape(user_blocks, width, size),
        (user_order, block_vals, item_source, item_table), [SMEM, VMEM, VMEM, ANY], (),
        product_flops, product_bytes,
    )

    hot_flops = 2 * 3 * width * trips * size

    def reduced(rows, table, scale, peer_ids, axis):
        peers, blocks = len(peer_ids), scale.shape[0]
        dealt = call(
            functools.partial(gather, rows, peers), [shape(width, trips)] * peers,
            (table, swap(table), scale, *peer_ids), [VMEM] * (3 + peers),
            [pltpu.VMEM((3 * width, blocks * size), BF16)],
            peers * blocks * hot_flops, 8 * blocks * width * size,
        )
        return [dealt[0]] + [shift(dealt[o], axis, peers, o) for o in range(1, peers)]

    item_parts = reduced([1, 2], item_table, item_scale, ids_item, "user")
    user_parts = reduced([0], user_table, user_scale, ids_user, "item")
    user_base, item_base = call(
        gather_base, [shape(width, trips)] * 2, (user_emb, item_emb, ids),
        [VMEM, VMEM, VMEM], (), 4 * width * trips * size * (user_blocks + item_blocks),
        2 * width * size * (user_blocks + item_blocks),
    )
    user_parts.append(user_base)
    item_parts.append(item_base)
    pieces, pushed = call(
        functools.partial(slopes, len(user_parts), len(item_parts)),
        [shape(width, trips)] * 2,
        (*user_parts, *item_parts), [VMEM] * (len(user_parts) + len(item_parts)),
        moved=4 * width * trips * (len(user_parts) + len(item_parts) + 2),
    )

    def added(rows, own, axis, peer_ids, blocks, after):
        peers = len(peer_ids)
        arrays = [own] + [shift(own, axis, peers, -o) for o in range(1, peers)]
        return call(
            functools.partial(scatter, rows, peers), shape(blocks, width, size),
            (after, *arrays, *peer_ids), [ANY] + [VMEM] * (2 * peers),
            [pltpu.VMEM((peers, 3 * width, trips), BF16)],
            peers * blocks * hot_flops, 4 * blocks * width * size,
        )

    def second(across, grad, order, source_scale, target_scale, after):
        sources, targets = source_scale.shape[0], target_scale.shape[0]
        return call(
            functools.partial(second_pass, across),
            [shape(sources, width, size), shape(targets, half, size), shape(targets, half, size)],
            (order, grad, swap(grad), source_scale, target_scale, block_vals, after),
            [SMEM, VMEM, VMEM, VMEM, VMEM, VMEM, ANY],
            [pltpu.VMEM((sources + 1, width, size), BF16),
             pltpu.VMEM((targets, width, size), F32)],
            product_flops, product_bytes,
        )

    user_grad = added([0], pieces, "item", ids_user, user_blocks, pieces)
    user_half_grad, item_keep, item_send = second(
        False, user_grad, item_order, user_scale, item_scale, pieces)
    item_grad = added([1, 2], pushed, "user", ids_item, item_blocks, item_send)

    per = item_blocks // users
    dealt = call(
        functools.partial(add_deal, users), [shape(per, half, size)] * users,
        (item_keep, swap(item_send)), [VMEM, VMEM], moved=12 * item_blocks * half * size,
    )
    item_half_grad, user_keep, user_send = second(
        True, item_grad, user_order, item_scale, user_scale, dealt[0])
    parts = [dealt[0]] + [shift(dealt[o], "user", users, o) for o in range(1, users)]
    own = call(sum_parts, shape(per, half, size), tuple(parts), [VMEM] * users,
               moved=4 * (users + 1) * per * half * size)
    mine = call(pack, shape(users, per, half, size),
                (own, *[shift(own, "user", users, -o) for o in range(1, users)]),
                [VMEM] * users, moved=8 * item_blocks * half * size)
    grad_item = call(
        functools.partial(finish_items, users), shape(width, item_blocks * size),
        (item_half_grad, mine, swap(mine)), [VMEM] * 3, moved=12 * item_blocks * width * size,
    )

    own = call(sum_parts, shape(user_blocks, half, size), (user_keep, swap(user_send)),
               [VMEM, VMEM], moved=12 * user_blocks * half * size)
    mine = call(sum_parts, shape(user_blocks, half, size),
                (own, *[shift(own, "item", items, o) for o in range(1, items)]),
                [VMEM] * items, moved=12 * user_blocks * half * size)
    grad_user = call(
        finish_users, shape(width, user_blocks * size), (user_half_grad, mine, swap(mine)),
        [VMEM] * 3, moved=12 * user_blocks * width * size,
    )
    return (grad_user, grad_item)


def solution(mesh):
    return jax.shard_map(
        functools.partial(on_device, mesh.shape["user"], mesh.shape["item"]),
        mesh=mesh,
        in_specs=(
            P(None, ("groups", "user")),
            P(None, ("groups", "item")),
            P(("groups", "user")),
            P(("groups", "item")),
            P(("groups", "user", "item", "rep"), None, None),
            P(("groups", "user", "item", "rep")),
            P(("groups", "user", "item", "rep")),
            P(("groups", "user", "item", "rep")),
            P(("groups", "user", "item", "rep")),
            P(("groups", "user", "item", "rep")),
            P(("groups", "user", "item", "rep")),
        ),
        out_specs=(P(None, ("groups", "user")), P(None, ("groups", "item"))),
        check_vma=False,
    )
```

```python
import functools

import jax
import jax.numpy as jnp
from jax import lax
from jax.experimental import pallas as pl
from jax.experimental.pallas import tpu as pltpu
from jax.sharding import PartitionSpec as P

F32 = jnp.float32
BF16 = jnp.bfloat16
PACK = 4
GROUP = 4

VMEM = pl.BlockSpec(memory_space=pltpu.VMEM)
SMEM = pl.BlockSpec(memory_space=pltpu.SMEM)
ANY = pl.BlockSpec(memory_space=pl.ANY)
HBM = pl.BlockSpec(memory_space=pltpu.HBM)


def call(kernel, outs, ins, specs, scratch=(), flops=0, moved=0, room=24):
    return pl.pallas_call(
        kernel,
        out_shape=outs,
        in_specs=specs,
        out_specs=jax.tree.map(lambda _: VMEM, outs),
        scratch_shapes=list(scratch),
        cost_estimate=pl.CostEstimate(flops=flops, bytes_accessed=moved, transcendentals=0),
        compiler_params=pltpu.CompilerParams(vmem_limit_bytes=room * 1024 * 1024),
    )(*ins)


def shape(*dims):
    return jax.ShapeDtypeStruct(dims, F32)


def split3(values):
    high = values.astype(BF16)
    rest = values - high.astype(F32)
    middle = rest.astype(BF16)
    low = (rest - middle.astype(F32)).astype(BF16)
    return high, middle, low


def hot(ids_ref, rows, start, tile):
    ids = [ids_ref[row:row + 1, :] for row in rows]
    if len(rows) == 2:
        same = ids[0] == ids[1]
        ids = [jnp.where(same, -1, each) for each in ids]
    ids = [each.astype(jnp.int16) for each in ids]
    place = lax.broadcasted_iota(jnp.int16, (tile, ids[0].shape[1]), 0) + jnp.int16(start)
    chosen = jnp.zeros(place.shape, BF16)
    for each, sign in zip(ids, (1, -1)):
        chosen = jnp.where(place == each, jnp.asarray(sign, BF16), chosen)
    return chosen


def sort_slots(keys, sources, count, blocks):
    lanes = keys.shape[1]
    rows = 2 * blocks
    place = lax.broadcasted_iota(jnp.int32, (1, lanes), 1)
    live = place < count
    mine = (lax.broadcasted_iota(jnp.int32, (rows, lanes), 0) == keys) & live
    mine = jnp.where(mine, 1.0, 0.0)
    earlier = lax.broadcasted_iota(jnp.int32, (lanes, lanes), 0) < lax.broadcasted_iota(
        jnp.int32, (lanes, lanes), 1)
    before = jnp.dot(mine.astype(BF16), jnp.where(earlier, 1.0, 0.0).astype(BF16),
                     preferred_element_type=F32)
    packs = jnp.floor((jnp.sum(mine, axis=1, keepdims=True) + (PACK - 1)) * (1.0 / PACK))
    packs = jnp.broadcast_to(packs, (rows, 128))
    lower = lax.broadcasted_iota(jnp.int32, (rows, rows), 1) < lax.broadcasted_iota(
        jnp.int32, (rows, rows), 0)
    first = jnp.dot(jnp.where(lower, 1.0, 0.0).astype(BF16), packs.astype(BF16),
                    preferred_element_type=F32)
    position = jnp.sum(mine * (first[:, :1] * PACK + before), axis=0, keepdims=True)
    position = jnp.where(live, position.astype(jnp.int32), -1)
    match = lax.broadcasted_iota(jnp.int32, (lanes, lanes), 0) == position
    row = lax.broadcasted_iota(jnp.int32, (16, lanes), 0)
    values = jnp.where(row == 0, place // 16, jnp.where(row == 1, place % 16, jnp.where(
        row == 2, sources, jnp.where(row == 3, keys, jnp.where(row == 4, 1, 0)))))
    values = jnp.where(live, values, 0).astype(F32)
    found = lax.dot_general(values.astype(BF16), jnp.where(match, 1.0, 0.0).astype(BF16),
                            (((1,), (1,)), ((), ())), preferred_element_type=F32)
    found = found.astype(jnp.int32)
    valid = found[4:5] > 0
    total = jnp.broadcast_to(jnp.sum(packs[:, :1], axis=0, keepdims=True), (1, lanes))
    row = lax.broadcasted_iota(jnp.int32, (8, lanes), 0)
    slot = found[0:1] * 16 + found[1:2]
    source = jnp.where(valid, found[2:3], blocks)
    target = jnp.where(valid, found[3:4], 0)
    return jnp.where(row == 0, slot, jnp.where(row == 1, source, jnp.where(
        row == 2, target, total.astype(jnp.int32))))


def multiply_blocks(order, vals, source, total, across):
    total[...] = jnp.zeros_like(total)
    contract = (((1,), (1,)), ((), ())) if across else (((1,), (0,)), ((), ()))

    def group(index, _):
        targets, terms = [], []
        for step in range(GROUP):
            places = [(index * GROUP + step) * PACK + each for each in range(PACK)]
            left = jnp.concatenate([source[order[1, place]] for place in places], axis=1)
            right = jnp.concatenate([vals[order[0, place]] for place in places],
                                    axis=1 if across else 0)
            targets.append(order[2, places[0]])
            terms.append(lax.dot_general(left, right, contract, preferred_element_type=F32))
        for target, term in zip(targets, terms):
            total[target] += term
        return 0

    lax.fori_loop(0, (order[3, 0] + GROUP - 1) // GROUP, group, 0)


def begin(out):
    out[...] = jnp.zeros_like(out)


def stack_ids(user, positive, negative, after, *outs):
    for out in outs:
        for place in range(out.shape[0]):
            for row, ids in enumerate((user, positive, negative)):
                out[place, row:row + 1, :] = ids[...]


def prepare(count, rows, columns, user_emb, item_emb, user_deg, item_deg, after,
            user_source, item_source, user_scale, item_scale, item_order, user_order, keys):
    live = count[0]
    slots = rows.shape[0]
    keys[...] = jnp.zeros_like(keys)
    keys[0:1, 0:slots] = rows[...].reshape(1, slots)
    keys[1:2, 0:slots] = columns[...].reshape(1, slots)
    users, items = keys[0:1, :], keys[1:2, :]
    item_order[...] = sort_slots(items, users, live, item_scale.shape[0])
    user_order[...] = sort_slots(users, items, live, user_scale.shape[0])
    for emb, deg, scale, into in ((user_emb, user_deg, user_scale, user_source),
                                  (item_emb, item_deg, item_scale, item_source)):
        scale[...] = lax.rsqrt(deg[...].astype(F32))
        blocks, size = scale.shape
        for block in range(blocks):
            piece = emb[:, block * size:(block + 1) * size].astype(F32)
            into[block] = (scale[block:block + 1, :] * piece).astype(BF16)
        into[blocks] = jnp.zeros(into.shape[1:], BF16)


def first_pass(across, order, vals, source, after, total):
    multiply_blocks(order, vals, source, total, across)


def fold(stacked, width):
    return (
        stacked[:width] + stacked[width:2 * width] + stacked[2 * width:3 * width]
    )


def pick(table, ids_ref, rows, tile):
    total = None
    for start in range(0, table.shape[1], tile):
        term = jnp.dot(
            table[:, start:start + tile], hot(ids_ref, rows, start, tile),
            preferred_element_type=F32,
        )
        total = term if total is None else total + term
    return total


def gather(rows, peers, mine, other, scale, ids, after, out, table):
    blocks, width, size = mine.shape
    for block in range(blocks):
        span = slice(block * size, (block + 1) * size)
        here = scale[block:block + 1, :] * (mine[block] + other[block])
        for part, piece in enumerate(split3(here)):
            table[part * width:(part + 1) * width, span] = piece
    for peer in range(peers):
        out[peer] = fold(pick(table, ids.at[peer], rows, 2 * size), width)


def scatter(rows, peers, pieces, ids, after, out, table):
    blocks, width, size = out.shape
    tile = 2 * size
    for place in range(peers):
        for part, value in enumerate(split3(pieces[place])):
            table[place, part * width:(part + 1) * width, :] = value
    for start in range(0, blocks * size, tile):
        total = None
        for place in range(peers):
            term = lax.dot_general(
                table[place], hot(ids.at[place], rows, start, tile), (((1,), (1,)), ((), ())),
                preferred_element_type=F32,
            )
            total = term if total is None else total + term
        total = fold(total, width)
        for offset in range(0, tile, size):
            out[(start + offset) // size] = total[:, offset:offset + size]


def gather_base(user_emb, item_emb, ids, user_out, item_out):
    tile = ids.shape[2]
    user_out[...] = pick(user_emb, ids.at[0], [0], tile)
    item_out[...] = pick(item_emb, ids.at[0], [1, 2], tile)


def add_parts(parts, start, peers):
    total = parts[start]
    for place in range(start + 1, start + peers):
        total = total + parts[place]
    return total


def slopes(users, items, user_base, item_base, pieces, pushed):
    user_rows = 0.5 * (add_parts(users, 0, users.shape[0]) + user_base[...])
    difference = 0.5 * (add_parts(items, 0, items.shape[0]) + item_base[...])
    margin = jnp.sum(user_rows * difference, axis=0, keepdims=True)
    slope = -jax.nn.sigmoid(-margin)
    for out, value in ((pieces, slope * difference), (pushed, slope * user_rows)):
        for place in range(out.shape[0]):
            out[place] = value


def second_pass(across, order, mine, other, source_scale, target_scale, vals, after,
                half_grad, keep, send, source, total):
    blocks, width, size = mine.shape
    for block in range(blocks):
        grad = mine[block] + other[block]
        half_grad[block] = 0.5 * grad
        source[block] = (source_scale[block:block + 1, :] * grad * 0.5).astype(BF16)
    source[blocks] = jnp.zeros((width, size), BF16)
    multiply_blocks(order, vals, source, total, across)
    me = lax.axis_index("rep")
    half = keep.shape[1]
    for block in range(keep.shape[0]):
        scale = target_scale[block:block + 1, :]
        keep[block] = scale * total[block, pl.ds(pl.multiple_of(me * half, half), half), :]
        send[block] = scale * total[block, pl.ds(pl.multiple_of((1 - me) * half, half), half), :]


def add_two(mine, other, after, out):
    out[...] = mine[...] + other[...]


def add_copies(peers, parts, out):
    per = parts.shape[0] // peers
    for block in range(per):
        total = parts[block]
        for peer in range(1, peers):
            total = total + parts[peer * per + block]
        for peer in range(peers):
            out[peer * per + block] = total


def add_list(*refs):
    total = refs[0][...]
    for ref in refs[1:-1]:
        total = total + ref[...]
    refs[-1][...] = total


def finish(half_grad, mine, other, out):
    me = lax.axis_index("rep")
    blocks, width, size = half_grad.shape
    half = width // 2
    for block in range(blocks):
        span = slice(block * size, (block + 1) * size)
        for rank, part in ((me, mine), (1 - me, other)):
            rows = pl.ds(pl.multiple_of(rank * half, half), half)
            out[rows, span] = half_grad[block, rows, :] + part[block]


def swap(values):
    return lax.ppermute(values, "rep", [(0, 1), (1, 0)])


def exchange(values, axis):
    return lax.all_to_all(values, axis, 0, 0, tiled=True)


def on_device(users, items, user_emb, item_emb, user_deg, item_deg, block_vals, block_row,
              block_col, block_count, trip_user, trip_pos, trip_neg):
    width = user_emb.shape[0]
    slots, size, _ = block_vals.shape
    user_blocks = user_emb.shape[1] // size
    item_blocks = item_emb.shape[1] // size
    trips = trip_user.shape[0]
    half = width // 2
    user_deg = user_deg.reshape(user_blocks, size)
    item_deg = item_deg.reshape(item_blocks, size)

    product_flops = 2 * slots * size * size * width
    product_bytes = slots * size * size * 2
    started = call(begin, shape(8, size), (), [], (), 16 * product_flops, product_bytes)
    ids_item, ids_user = call(
        stack_ids, [jax.ShapeDtypeStruct((peers, 3, trips), jnp.int32) for peers in (users, items)],
        [each.reshape(1, trips) for each in (trip_user, trip_pos, trip_neg)] + [started],
        [VMEM, VMEM, VMEM, ANY],
    )
    ids = ids_user
    ids_item, ids_user = exchange(ids_item, "user"), exchange(ids_user, "item")
    lanes = -(-slots // size) * size

    order_shape = jax.ShapeDtypeStruct((8, lanes), jnp.int32)
    def source_shape(blocks):
        return jax.ShapeDtypeStruct((blocks + 1, width, size), BF16)

    (user_source, item_source, user_scale, item_scale, item_order, user_order) = call(
        prepare,
        [source_shape(user_blocks), source_shape(item_blocks), shape(user_blocks, size),
         shape(item_blocks, size), order_shape, order_shape],
        (block_count, block_row, block_col, user_emb, item_emb, user_deg, item_deg, ids),
        [SMEM, VMEM, VMEM, VMEM, VMEM, VMEM, VMEM, ANY],
        [pltpu.VMEM((8, lanes), jnp.int32)], product_flops, product_bytes,
    )
    item_table = call(
        functools.partial(first_pass, False), shape(item_blocks, width, size),
        (item_order, block_vals, user_source, ids), [SMEM, VMEM, VMEM, ANY], (),
        product_flops, product_bytes,
    )
    user_table = call(
        functools.partial(first_pass, True), shape(user_blocks, width, size),
        (user_order, block_vals, item_source, item_table), [SMEM, VMEM, VMEM, ANY], (),
        product_flops, product_bytes,
    )

    hot_flops = 2 * 3 * width * trips * size

    def reduced(rows, table, scale, peer_ids, axis, after):
        peers, blocks = peer_ids.shape[0], scale.shape[0]
        return call(
            functools.partial(gather, rows, peers), shape(peers, width, trips),
            (table, swap(table), scale, peer_ids, after), [VMEM] * 4 + [ANY],
            [pltpu.VMEM((3 * width, blocks * size), BF16)],
            peers * blocks * hot_flops, 8 * blocks * width * size,
        )

    item_parts = reduced([1, 2], item_table, item_scale, ids_item, "user", ids)
    user_parts = reduced([0], user_table, user_scale, ids_user, "item", item_parts)
    user_base, item_base = call(
        gather_base, [shape(width, trips)] * 2, (user_emb, item_emb, ids),
        [VMEM, VMEM, VMEM], (), 4 * width * trips * size * (user_blocks + item_blocks),
        2 * width * size * (user_blocks + item_blocks),
    )
    pieces, pushed = call(
        slopes, [shape(items, width, trips), shape(users, width, trips)],
        (exchange(user_parts, "item"), exchange(item_parts, "user"), user_base, item_base),
        [VMEM] * 4, moved=8 * width * trips * (users + items + 1),
    )

    def added(rows, own, axis, peer_ids, blocks, after):
        peers = peer_ids.shape[0]
        return call(
            functools.partial(scatter, rows, peers), shape(blocks, width, size),
            (exchange(own, axis), peer_ids, after), [VMEM, VMEM, ANY],
            [pltpu.VMEM((peers, 3 * width, trips), BF16)],
            peers * blocks * hot_flops, 4 * blocks * width * size,
        )

    def second(across, grad, order, source_scale, target_scale, after):
        sources, targets = source_scale.shape[0], target_scale.shape[0]
        return call(
            functools.partial(second_pass, across),
            [shape(sources, width, size), shape(targets, half, size), shape(targets, half, size)],
            (order, grad, swap(grad), source_scale, target_scale, block_vals, after),
            [SMEM, VMEM, VMEM, VMEM, VMEM, VMEM, ANY],
            [pltpu.VMEM((sources + 1, width, size), BF16),
             pltpu.VMEM((targets, width, size), F32)],
            product_flops, product_bytes,
        )

    user_grad = added([0], pieces, "item", ids_user, user_blocks, pieces)
    user_half_grad, item_keep, item_send = second(
        False, user_grad, item_order, user_scale, item_scale, pieces)
    item_grad = added([1, 2], pushed, "user", ids_item, item_blocks, item_send)

    dealt = call(add_two, shape(item_blocks, half, size), (item_keep, swap(item_send), item_grad),
                 [VMEM, VMEM, ANY], moved=12 * item_blocks * half * size)
    item_half_grad, user_keep, user_send = second(
        True, item_grad, user_order, item_scale, user_scale, dealt)
    copies = call(
        functools.partial(add_copies, users), shape(item_blocks, half, size),
        (exchange(dealt, "user"),), [VMEM], moved=8 * item_blocks * half * size,
    )
    own = call(add_two, shape(user_blocks, half, size), (user_keep, swap(user_send), copies),
               [VMEM, VMEM, ANY], moved=12 * user_blocks * half * size)
    mine = exchange(copies, "user")
    grad_item = call(
        finish, shape(width, item_blocks * size), (item_half_grad, mine, swap(mine)),
        [VMEM] * 3, moved=12 * item_blocks * width * size,
    )
    come = [lax.ppermute(own, "item", [(i, (i + o) % items) for i in range(items)])
            for o in range(1, items)]
    mine = call(add_list, shape(user_blocks, half, size), (own, *come), [VMEM] * items,
                moved=12 * user_blocks * half * size)
    grad_user = call(
        finish, shape(width, user_blocks * size), (user_half_grad, mine, swap(mine)),
        [VMEM] * 3, moved=12 * user_blocks * width * size,
    )
    return (grad_user, grad_item)


def solution(mesh):
    return jax.shard_map(
        functools.partial(on_device, mesh.shape["user"], mesh.shape["item"]),
        mesh=mesh,
        in_specs=(
            P(None, ("groups", "user")),
            P(None, ("groups", "item")),
            P(("groups", "user")),
            P(("groups", "item")),
            P(("groups", "user", "item", "rep"), None, None),
            P(("groups", "user", "item", "rep")),
            P(("groups", "user", "item", "rep")),
            P(("groups", "user", "item", "rep")),
            P(("groups", "user", "item", "rep")),
            P(("groups", "user", "item", "rep")),
            P(("groups", "user", "item", "rep")),
        ),
        out_specs=(P(None, ("groups", "user")), P(None, ("groups", "item"))),
        check_vma=False,
    )
```

```python
import functools

import jax
import jax.numpy as jnp
from jax import lax
from jax.experimental import pallas as pl
from jax.experimental.pallas import tpu as pltpu
from jax.sharding import PartitionSpec as P

F32 = jnp.float32
BF16 = jnp.bfloat16
PACK = 4
GROUP = 4

VMEM = pl.BlockSpec(memory_space=pltpu.VMEM)
SMEM = pl.BlockSpec(memory_space=pltpu.SMEM)
ANY = pl.BlockSpec(memory_space=pl.ANY)
HBM = pl.BlockSpec(memory_space=pltpu.HBM)


def call(kernel, outs, ins, specs, scratch=(), flops=0, moved=0, room=24):
    return pl.pallas_call(
        kernel,
        out_shape=outs,
        in_specs=specs,
        out_specs=jax.tree.map(lambda _: VMEM, outs),
        scratch_shapes=list(scratch),
        cost_estimate=pl.CostEstimate(flops=flops, bytes_accessed=moved, transcendentals=0),
        compiler_params=pltpu.CompilerParams(vmem_limit_bytes=room * 1024 * 1024),
    )(*ins)


def shape(*dims):
    return jax.ShapeDtypeStruct(dims, F32)


def split3(values):
    high = values.astype(BF16)
    rest = values - high.astype(F32)
    middle = rest.astype(BF16)
    low = (rest - middle.astype(F32)).astype(BF16)
    return high, middle, low


def hot(ids_ref, rows, start, tile):
    ids = [ids_ref[row:row + 1, :] for row in rows]
    if len(rows) == 2:
        same = ids[0] == ids[1]
        ids = [jnp.where(same, -1, each) for each in ids]
    ids = [each.astype(jnp.int16) for each in ids]
    place = lax.broadcasted_iota(jnp.int16, (tile, ids[0].shape[1]), 0) + jnp.int16(start)
    chosen = jnp.zeros(place.shape, BF16)
    for each, sign in zip(ids, (1, -1)):
        chosen = jnp.where(place == each, jnp.asarray(sign, BF16), chosen)
    return chosen


def sort_slots(keys, sources, count, blocks):
    lanes = keys.shape[1]
    rows = 2 * blocks
    place = lax.broadcasted_iota(jnp.int32, (1, lanes), 1)
    live = place < count
    mine = (lax.broadcasted_iota(jnp.int32, (rows, lanes), 0) == keys) & live
    mine = jnp.where(mine, 1.0, 0.0)
    earlier = lax.broadcasted_iota(jnp.int32, (lanes, lanes), 0) < lax.broadcasted_iota(
        jnp.int32, (lanes, lanes), 1)
    before = jnp.dot(mine.astype(BF16), jnp.where(earlier, 1.0, 0.0).astype(BF16),
                     preferred_element_type=F32)
    packs = jnp.floor((jnp.sum(mine, axis=1, keepdims=True) + (PACK - 1)) * (1.0 / PACK))
    packs = jnp.broadcast_to(packs, (rows, 128))
    lower = lax.broadcasted_iota(jnp.int32, (rows, rows), 1) < lax.broadcasted_iota(
        jnp.int32, (rows, rows), 0)
    first = jnp.dot(jnp.where(lower, 1.0, 0.0).astype(BF16), packs.astype(BF16),
                    preferred_element_type=F32)
    position = jnp.sum(mine * (first[:, :1] * PACK + before), axis=0, keepdims=True)
    position = jnp.where(live, position.astype(jnp.int32), -1)
    match = lax.broadcasted_iota(jnp.int32, (lanes, lanes), 0) == position
    row = lax.broadcasted_iota(jnp.int32, (16, lanes), 0)
    values = jnp.where(row == 0, place // 16, jnp.where(row == 1, place % 16, jnp.where(
        row == 2, sources, jnp.where(row == 3, keys, jnp.where(row == 4, 1, 0)))))
    values = jnp.where(live, values, 0).astype(F32)
    found = lax.dot_general(values.astype(BF16), jnp.where(match, 1.0, 0.0).astype(BF16),
                            (((1,), (1,)), ((), ())), preferred_element_type=F32)
    found = found.astype(jnp.int32)
    valid = found[4:5] > 0
    total = jnp.broadcast_to(jnp.sum(packs[:, :1], axis=0, keepdims=True), (1, lanes))
    row = lax.broadcasted_iota(jnp.int32, (8, lanes), 0)
    slot = found[0:1] * 16 + found[1:2]
    source = jnp.where(valid, found[2:3], blocks)
    target = jnp.where(valid, found[3:4], 0)
    return jnp.where(row == 0, slot, jnp.where(row == 1, source, jnp.where(
        row == 2, target, total.astype(jnp.int32))))


def multiply_blocks(order, vals, source, total, across):
    _, width, size = source.shape
    total[...] = jnp.zeros_like(total)
    contract = (((1,), (1,)), ((), ())) if across else (((1,), (0,)), ((), ()))

    def group(index, _):
        targets, terms = [], []
        for step in range(GROUP):
            left, right = [], []
            for half in range(2):
                first = ((index * GROUP + step) * 2 + half) * PACK
                places = [first + each for each in range(PACK)]
                left.append(jnp.concatenate([source[order[1, each]] for each in places], axis=1))
                right.append(jnp.concatenate([vals[order[0, each]] for each in places],
                                             axis=1 if across else 0))
                targets.append(order[2, first])
            both = lax.dot_general(
                jnp.concatenate(left, axis=0), jnp.concatenate(right, axis=0 if across else 1),
                contract, preferred_element_type=F32,
            )
            terms += [both[:width, :size], both[width:, size:]]
        for target, term in zip(targets, terms):
            total[target] += term
        return 0

    lax.fori_loop(0, (order[3, 0] + 2 * GROUP - 1) // (2 * GROUP), group, 0)


def begin(out):
    out[...] = jnp.zeros_like(out)


def stack_ids(user, positive, negative, after, out):
    for row, ids in enumerate((user, positive, negative)):
        out[row:row + 1, :] = ids[...]


def prepare(count, rows, columns, user_emb, item_emb, user_deg, item_deg, after,
            user_source, item_source, user_scale, item_scale, item_order, user_order, keys):
    live = count[0]
    slots = rows.shape[0]
    keys[...] = jnp.zeros_like(keys)
    keys[0:1, 0:slots] = rows[...].reshape(1, slots)
    keys[1:2, 0:slots] = columns[...].reshape(1, slots)
    users, items = keys[0:1, :], keys[1:2, :]
    item_order[...] = sort_slots(items, users, live, item_scale.shape[0])
    user_order[...] = sort_slots(users, items, live, user_scale.shape[0])
    for emb, deg, scale, into in ((user_emb, user_deg, user_scale, user_source),
                                  (item_emb, item_deg, item_scale, item_source)):
        scale[...] = lax.rsqrt(deg[...].astype(F32))
        blocks, size = scale.shape
        for block in range(blocks):
            piece = emb[:, block * size:(block + 1) * size].astype(F32)
            into[block] = (scale[block:block + 1, :] * piece).astype(BF16)
        into[blocks] = jnp.zeros(into.shape[1:], BF16)


def first_pass(across, order, vals, source, *refs):
    multiply_blocks(order, vals, source, refs[-1], across)


def fold(stacked, width):
    return (
        stacked[:width] + stacked[width:2 * width] + stacked[2 * width:3 * width]
    )


def pick(table, ids_ref, rows, tile):
    total = None
    for start in range(0, table.shape[1], tile):
        term = jnp.dot(
            table[:, start:start + tile], hot(ids_ref, rows, start, tile),
            preferred_element_type=F32,
        )
        total = term if total is None else total + term
    return total


def gather(rows, peers, mine, other, scale, after, *refs):
    ids, outs, table = refs[:peers], refs[peers:2 * peers], refs[2 * peers]
    blocks, width, size = mine.shape
    for block in range(blocks):
        span = slice(block * size, (block + 1) * size)
        here = scale[block:block + 1, :] * (mine[block] + other[block])
        for part, piece in enumerate(split3(here)):
            table[part * width:(part + 1) * width, span] = piece
    for peer in range(peers):
        outs[peer][...] = fold(pick(table, ids[peer], rows, 2 * size), width)


def scatter(rows, peers, after, *refs):
    pieces, ids, out, table = refs[:peers], refs[peers:2 * peers], refs[2 * peers], refs[-1]
    blocks, width, size = out.shape
    tile = 2 * size
    for place, piece in enumerate(pieces):
        for part, value in enumerate(split3(piece[...])):
            table[place, part * width:(part + 1) * width, :] = value
    for start in range(0, blocks * size, tile):
        total = None
        for place in range(peers):
            term = lax.dot_general(
                table[place], hot(ids[place], rows, start, tile), (((1,), (1,)), ((), ())),
                preferred_element_type=F32,
            )
            total = term if total is None else total + term
        total = fold(total, width)
        for offset in range(0, tile, size):
            out[(start + offset) // size] = total[:, offset:offset + size]


def gather_base(user_emb, item_emb, ids, user_out, item_out):
    tile = ids.shape[1]
    user_out[...] = pick(user_emb, ids, [0], tile)
    item_out[...] = pick(item_emb, ids, [1, 2], tile)


def add_all(refs):
    total = refs[0][...]
    for ref in refs[1:]:
        total = total + ref[...]
    return total


def slopes(user_parts, item_parts, *refs):
    users, items = refs[:user_parts], refs[user_parts:user_parts + item_parts]
    pieces, pushed = refs[user_parts + item_parts:]
    user_rows = 0.5 * add_all(users)
    difference = 0.5 * add_all(items)
    margin = jnp.sum(user_rows * difference, axis=0, keepdims=True)
    slope = -jax.nn.sigmoid(-margin)
    pieces[...] = slope * difference
    pushed[...] = slope * user_rows


def halves(total, keep, send):
    me = lax.axis_index("rep")
    half = keep.shape[1]
    for block in range(keep.shape[0]):
        keep[block] = total[block, pl.ds(pl.multiple_of(me * half, half), half), :]
        send[block] = total[block, pl.ds(pl.multiple_of((1 - me) * half, half), half), :]


def second_pass(across, order, mine, other, source_scale, target_scale, vals, after,
                half_grad, *refs):
    outs, (source, total) = refs[:-2], refs[-2:]
    blocks, width, size = mine.shape
    for block in range(blocks):
        grad = mine[block] + other[block]
        half_grad[block] = 0.5 * grad
        source[block] = (source_scale[block:block + 1, :] * grad * 0.5).astype(BF16)
    source[blocks] = jnp.zeros((width, size), BF16)
    multiply_blocks(order, vals, source, total, across)
    scaled = outs[0] if len(outs) == 1 else total
    for block in range(total.shape[0]):
        scaled[block] = target_scale[block:block + 1, :] * total[block]
    if len(outs) == 2:
        halves(total, *outs)


def halves_after(total, after, keep, send):
    halves(total, keep, send)


def add_deal(peers, keep, received, after, *outs):
    me = lax.axis_index("user")
    per = outs[0].shape[0]
    for offset in range(peers):
        there = lax.rem(me + offset, peers) * per
        for block in range(per):
            outs[offset][block] = keep[there + block] + received[there + block]


def sum_parts(*refs):
    refs[-1][...] = add_all(refs[:-1])


def sum_after(after, *refs):
    sum_parts(*refs)


def pack(*refs):
    for place, ref in enumerate(refs[:-1]):
        refs[-1][place] = ref[...]


def finish_users(half_grad, mine, other, out):
    me = lax.axis_index("rep")
    blocks, width, size = half_grad.shape
    half = width // 2
    for block in range(blocks):
        span = slice(block * size, (block + 1) * size)
        for rank, part in ((me, mine), (1 - me, other)):
            rows = pl.ds(pl.multiple_of(rank * half, half), half)
            out[rows, span] = half_grad[block, rows, :] + part[block]


def finish_items(peers, half_grad, mine, other, out):
    me = lax.axis_index("rep")
    place = lax.axis_index("user")
    blocks, width, size = half_grad.shape
    half = width // 2
    per = blocks // peers
    for offset in range(peers):
        there = lax.rem(place + offset, peers) * per
        for block in range(per):
            span = pl.ds(pl.multiple_of((there + block) * size, size), size)
            for rank, part in ((me, mine), (1 - me, other)):
                rows = pl.ds(pl.multiple_of(rank * half, half), half)
                out[rows, span] = half_grad[there + block, rows, :] + part[offset, block]


def shift(values, axis, count, offset):
    return lax.ppermute(values, axis, [(i, (i + offset) % count) for i in range(count)])


def on_device(users, items, user_emb, item_emb, user_deg, item_deg, block_vals, block_row,
              block_col, block_count, trip_user, trip_pos, trip_neg):
    width = user_emb.shape[0]
    slots, size, _ = block_vals.shape
    user_blocks = user_emb.shape[1] // size
    item_blocks = item_emb.shape[1] // size
    trips = trip_user.shape[0]
    half = width // 2
    swap = functools.partial(shift, axis="rep", count=2, offset=1)
    user_deg = user_deg.reshape(user_blocks, size)
    item_deg = item_deg.reshape(item_blocks, size)

    product_flops = 2 * slots * size * size * width
    product_bytes = slots * size * size * 2
    started = call(begin, shape(8, size), (), [], (), 16 * product_flops, product_bytes)
    ids = call(
        stack_ids, jax.ShapeDtypeStruct((3, trips), jnp.int32),
        [each.reshape(1, trips) for each in (trip_user, trip_pos, trip_neg)] + [started],
        [VMEM, VMEM, VMEM, ANY],
    )
    ids_user = [ids] + [shift(ids, "item", items, -o) for o in range(1, items)]
    ids_item = [ids] + [shift(ids, "user", users, -o) for o in range(1, users)]
    lanes = -(-slots // size) * size

    order_shape = jax.ShapeDtypeStruct((8, lanes), jnp.int32)
    def source_shape(blocks):
        return jax.ShapeDtypeStruct((blocks + 1, width, size), BF16)

    (user_source, item_source, user_scale, item_scale, item_order, user_order) = call(
        prepare,
        [source_shape(user_blocks), source_shape(item_blocks), shape(user_blocks, size),
         shape(item_blocks, size), order_shape, order_shape],
        (block_count, block_row, block_col, user_emb, item_emb, user_deg, item_deg, ids),
        [SMEM, VMEM, VMEM, VMEM, VMEM, VMEM, VMEM, ANY],
        [pltpu.VMEM((8, lanes), jnp.int32)], product_flops, product_bytes,
    )
    item_table = call(
        functools.partial(first_pass, False), shape(item_blocks, width, size),
        (item_order, block_vals, user_source, ids), [SMEM, VMEM, VMEM, ANY], (),
        product_flops, product_bytes,
    )
    ids_here = [*ids_item[1:], *ids_user[1:]]
    user_table = call(
        functools.partial(first_pass, True), shape(user_blocks, width, size),
        (user_order, block_vals, item_source, item_table, *ids_here),
        [SMEM, VMEM, VMEM] + [ANY] * (1 + len(ids_here)), (),
        product_flops, product_bytes,
    )

    hot_flops = 2 * 3 * width * trips * size

    def reduced(rows, table, scale, peer_ids, axis, after):
        peers, blocks = len(peer_ids), scale.shape[0]
        dealt = call(
            functools.partial(gather, rows, peers), [shape(width, trips)] * peers,
            (table, swap(table), scale, after, *peer_ids), [VMEM] * 3 + [ANY] + [VMEM] * peers,
            [pltpu.VMEM((3 * width, blocks * size), BF16)],
            peers * blocks * hot_flops, 8 * blocks * width * size,
        )
        return [dealt[0]] + [shift(dealt[o], axis, peers, o) for o in range(1, peers)]

    item_parts = reduced([1, 2], item_table, item_scale, ids_item, "user", ids)
    user_parts = reduced([0], user_table, user_scale, ids_user, "item", item_parts[0])
    user_base, item_base = call(
        gather_base, [shape(width, trips)] * 2, (user_emb, item_emb, ids),
        [VMEM, VMEM, VMEM], (), 4 * width * trips * size * (user_blocks + item_blocks),
        2 * width * size * (user_blocks + item_blocks),
    )
    user_parts.append(user_base)
    item_parts.append(item_base)
    pieces, pushed = call(
        functools.partial(slopes, len(user_parts), len(item_parts)),
        [shape(width, trips)] * 2,
        (*user_parts, *item_parts), [VMEM] * (len(user_parts) + len(item_parts)),
        moved=4 * width * trips * (len(user_parts) + len(item_parts) + 2),
    )

    def added(rows, own, axis, peer_ids, blocks, after):
        peers = len(peer_ids)
        arrays = [own] + [shift(own, axis, peers, -o) for o in range(1, peers)]
        return call(
            functools.partial(scatter, rows, peers), shape(blocks, width, size),
            (after, *arrays, *peer_ids), [ANY] + [VMEM] * (2 * peers),
            [pltpu.VMEM((peers, 3 * width, trips), BF16)],
            peers * blocks * hot_flops, 4 * blocks * width * size,
        )

    def second(across, grad, order, source_scale, target_scale, after, divided):
        sources, targets = source_scale.shape[0], target_scale.shape[0]
        return call(
            functools.partial(second_pass, across),
            [shape(sources, width, size)]
            + ([shape(targets, half, size)] * 2 if divided else [shape(targets, width, size)]),
            (order, grad, swap(grad), source_scale, target_scale, block_vals, after),
            [SMEM, VMEM, VMEM, VMEM, VMEM, VMEM, ANY],
            [pltpu.VMEM((sources + 1, width, size), BF16),
             pltpu.VMEM((targets, width, size), F32)],
            product_flops, product_bytes,
        )

    user_grad = added([0], pieces, "item", ids_user, user_blocks, pieces)
    user_grad = added([0], pieces, "item", ids_user, user_blocks, pieces)
    def divided(total, after):
        blocks = total.shape[0]
        return call(halves, [shape(blocks, half, size)] * 2, (total, after), [VMEM, ANY],
                    moved=8 * blocks * width * size)

    user_grad = added([0], pieces, "item", ids_user, user_blocks, pieces)
    user_half_grad, item_keep, item_send = second(
        False, user_grad, item_order, user_scale, item_scale, pieces, True)
    item_grad = added([1, 2], pushed, "user", ids_item, item_blocks, item_send)

    per = item_blocks // users
    dealt = call(
        functools.partial(add_deal, users), [shape(per, half, size)] * users,
        (item_keep, swap(item_send), item_grad), [VMEM, VMEM, ANY],
        moved=12 * item_blocks * half * size,
    )
    item_half_grad, user_back = second(
        True, item_grad, user_order, item_scale, user_scale, dealt[0], False)
    parts = [dealt[0]] + [shift(dealt[o], "user", users, o) for o in range(1, users)]
    item_own = call(sum_after, shape(per, half, size), (user_back, *parts),
                    [ANY] + [VMEM] * users,
               moved=4 * (users + 1) * per * half * size)
    mine = call(pack, shape(users, per, half, size),
                (item_own, *[shift(item_own, "user", users, -o) for o in range(1, users)]),
                [VMEM] * users, moved=8 * item_blocks * half * size)
    grad_item = call(
        functools.partial(finish_items, users), shape(width, item_blocks * size),
        (item_half_grad, mine, swap(mine)), [VMEM] * 3, moved=12 * item_blocks * width * size,
    )

    user_keep, user_send = call(
        halves_after, [shape(user_blocks, half, size)] * 2, (user_back, item_own), [VMEM, ANY],
        moved=8 * user_blocks * width * size,
    )
    own = call(sum_parts, shape(user_blocks, half, size), (user_keep, swap(user_send)),
               [VMEM, VMEM], moved=12 * user_blocks * half * size)
    mine = call(sum_parts, shape(user_blocks, half, size),
                (own, *[shift(own, "item", items, o) for o in range(1, items)]),
                [VMEM] * items, moved=12 * user_blocks * half * size)
    grad_user = call(
        finish_users, shape(width, user_blocks * size), (user_half_grad, mine, swap(mine)),
        [VMEM] * 3, moved=12 * user_blocks * width * size,
    )
    return (grad_user, grad_item)


def solution(mesh):
    return jax.shard_map(
        functools.partial(on_device, mesh.shape["user"], mesh.shape["item"]),
        mesh=mesh,
        in_specs=(
            P(None, ("groups", "user")),
            P(None, ("groups", "item")),
            P(("groups", "user")),
            P(("groups", "item")),
            P(("groups", "user", "item", "rep"), None, None),
            P(("groups", "user", "item", "rep")),
            P(("groups", "user", "item", "rep")),
            P(("groups", "user", "item", "rep")),
            P(("groups", "user", "item", "rep")),
            P(("groups", "user", "item", "rep")),
            P(("groups", "user", "item", "rep")),
        ),
        out_specs=(P(None, ("groups", "user")), P(None, ("groups", "item"))),
        check_vma=False,
    )
```

```python
import functools

import jax
import jax.numpy as jnp
from jax import lax
from jax.experimental import pallas as pl
from jax.experimental.pallas import tpu as pltpu
from jax.sharding import PartitionSpec as P

F32 = jnp.float32
BF16 = jnp.bfloat16
PACK = 4
GROUP = 4
ID_ROWS = 64

VMEM = pl.BlockSpec(memory_space=pltpu.VMEM)
SMEM = pl.BlockSpec(memory_space=pltpu.SMEM)
ANY = pl.BlockSpec(memory_space=pl.ANY)
HBM = pl.BlockSpec(memory_space=pltpu.HBM)


def call(kernel, outs, ins, specs, scratch=(), flops=0, moved=0, room=24):
    return pl.pallas_call(
        kernel,
        out_shape=outs,
        in_specs=specs,
        out_specs=jax.tree.map(lambda _: VMEM, outs),
        scratch_shapes=list(scratch),
        cost_estimate=pl.CostEstimate(flops=flops, bytes_accessed=moved, transcendentals=0),
        compiler_params=pltpu.CompilerParams(vmem_limit_bytes=room * 1024 * 1024),
    )(*ins)


def shape(*dims):
    return jax.ShapeDtypeStruct(dims, F32)


def split3(values):
    high = values.astype(BF16)
    rest = values - high.astype(F32)
    middle = rest.astype(BF16)
    low = (rest - middle.astype(F32)).astype(BF16)
    return high, middle, low


def hot(ids_ref, rows, start, tile):
    ids = [ids_ref[row:row + 1, :] for row in rows]
    if len(rows) == 2:
        same = ids[0] == ids[1]
        ids = [jnp.where(same, -1, each) for each in ids]
    ids = [each.astype(jnp.int16) for each in ids]
    place = lax.broadcasted_iota(jnp.int16, (tile, ids[0].shape[1]), 0) + jnp.int16(start)
    chosen = jnp.zeros(place.shape, BF16)
    for each, sign in zip(ids, (1, -1)):
        chosen = jnp.where(place == each, jnp.asarray(sign, BF16), chosen)
    return chosen


def sort_slots(keys, sources, count, blocks):
    lanes = keys.shape[1]
    rows = 2 * blocks
    place = lax.broadcasted_iota(jnp.int32, (1, lanes), 1)
    live = place < count
    mine = (lax.broadcasted_iota(jnp.int32, (rows, lanes), 0) == keys) & live
    mine = jnp.where(mine, 1.0, 0.0)
    earlier = lax.broadcasted_iota(jnp.int32, (lanes, lanes), 0) < lax.broadcasted_iota(
        jnp.int32, (lanes, lanes), 1)
    before = jnp.dot(mine.astype(BF16), jnp.where(earlier, 1.0, 0.0).astype(BF16),
                     preferred_element_type=F32)
    packs = jnp.floor((jnp.sum(mine, axis=1, keepdims=True) + (PACK - 1)) * (1.0 / PACK))
    packs = jnp.broadcast_to(packs, (rows, 128))
    lower = lax.broadcasted_iota(jnp.int32, (rows, rows), 1) < lax.broadcasted_iota(
        jnp.int32, (rows, rows), 0)
    first = jnp.dot(jnp.where(lower, 1.0, 0.0).astype(BF16), packs.astype(BF16),
                    preferred_element_type=F32)
    position = jnp.sum(mine * (first[:, :1] * PACK + before), axis=0, keepdims=True)
    position = jnp.where(live, position.astype(jnp.int32), -1)
    match = lax.broadcasted_iota(jnp.int32, (lanes, lanes), 0) == position
    row = lax.broadcasted_iota(jnp.int32, (16, lanes), 0)
    values = jnp.where(row == 0, place // 16, jnp.where(row == 1, place % 16, jnp.where(
        row == 2, sources, jnp.where(row == 3, keys, jnp.where(row == 4, 1, 0)))))
    values = jnp.where(live, values, 0).astype(F32)
    found = lax.dot_general(values.astype(BF16), jnp.where(match, 1.0, 0.0).astype(BF16),
                            (((1,), (1,)), ((), ())), preferred_element_type=F32)
    found = found.astype(jnp.int32)
    valid = found[4:5] > 0
    total = jnp.broadcast_to(jnp.sum(packs[:, :1], axis=0, keepdims=True), (1, lanes))
    row = lax.broadcasted_iota(jnp.int32, (8, lanes), 0)
    slot = found[0:1] * 16 + found[1:2]
    source = jnp.where(valid, found[2:3], blocks)
    target = jnp.where(valid, found[3:4], 0)
    return jnp.where(row == 0, slot, jnp.where(row == 1, source, jnp.where(
        row == 2, target, total.astype(jnp.int32))))


def multiply_blocks(order, vals, source, total, across):
    _, width, size = source.shape
    total[...] = jnp.zeros_like(total)
    contract = (((1,), (1,)), ((), ())) if across else (((1,), (0,)), ((), ()))

    def group(index, _):
        targets, terms = [], []
        for step in range(GROUP):
            left, right = [], []
            for half in range(2):
                first = ((index * GROUP + step) * 2 + half) * PACK
                places = [first + each for each in range(PACK)]
                left.append(jnp.concatenate([source[order[1, each]] for each in places], axis=1))
                right.append(jnp.concatenate([vals[order[0, each]] for each in places],
                                             axis=1 if across else 0))
                targets.append(order[2, first])
            both = lax.dot_general(
                jnp.concatenate(left, axis=0), jnp.concatenate(right, axis=0 if across else 1),
                contract, preferred_element_type=F32,
            )
            terms += [both[:width, :size], both[width:, size:]]
        for target, term in zip(targets, terms):
            total[target] += term
        return 0

    lax.fori_loop(0, (order[3, 0] + 2 * GROUP - 1) // (2 * GROUP), group, 0)


def begin(out):
    out[...] = jnp.zeros_like(out)


def stack_ids(user, positive, negative, after, out):
    out[...] = jnp.zeros_like(out)
    for row, ids in enumerate((user, positive, negative)):
        out[row:row + 1, :] = ids[...]


def prepare(count, rows, columns, user_emb, item_emb, user_deg, item_deg, after,
            user_source, item_source, user_scale, item_scale, item_order, user_order, keys):
    live = count[0]
    slots = rows.shape[0]
    keys[...] = jnp.zeros_like(keys)
    keys[0:1, 0:slots] = rows[...].reshape(1, slots)
    keys[1:2, 0:slots] = columns[...].reshape(1, slots)
    users, items = keys[0:1, :], keys[1:2, :]
    item_order[...] = sort_slots(items, users, live, item_scale.shape[0])
    user_order[...] = sort_slots(users, items, live, user_scale.shape[0])
    for emb, deg, scale, into in ((user_emb, user_deg, user_scale, user_source),
                                  (item_emb, item_deg, item_scale, item_source)):
        scale[...] = lax.rsqrt(deg[...].astype(F32))
        blocks, size = scale.shape
        for block in range(blocks):
            piece = emb[:, block * size:(block + 1) * size].astype(F32)
            into[block] = (scale[block:block + 1, :] * piece).astype(BF16)
        into[blocks] = jnp.zeros(into.shape[1:], BF16)


def first_pass(across, order, vals, source, *refs):
    multiply_blocks(order, vals, source, refs[-1], across)


def fold(stacked, width):
    return (
        stacked[:width] + stacked[width:2 * width] + stacked[2 * width:3 * width]
    )


def pick(table, ids_ref, rows, tile):
    total = None
    for start in range(0, table.shape[1], tile):
        term = jnp.dot(
            table[:, start:start + tile], hot(ids_ref, rows, start, tile),
            preferred_element_type=F32,
        )
        total = term if total is None else total + term
    return total


def gather(rows, peers, mine, other, scale, after, *refs):
    ids, outs, table = refs[:peers], refs[peers:2 * peers], refs[2 * peers]
    blocks, width, size = mine.shape
    for block in range(blocks):
        span = slice(block * size, (block + 1) * size)
        here = scale[block:block + 1, :] * (mine[block] + other[block])
        for part, piece in enumerate(split3(here)):
            table[part * width:(part + 1) * width, span] = piece
    for peer in range(peers):
        outs[peer][...] = fold(pick(table, ids[peer], rows, 2 * size), width)


def scatter(rows, peers, after, *refs):
    pieces, ids, out, table = refs[:peers], refs[peers:2 * peers], refs[2 * peers], refs[-1]
    blocks, width, size = out.shape
    tile = 2 * size
    for place, piece in enumerate(pieces):
        for part, value in enumerate(split3(piece[...])):
            table[place, part * width:(part + 1) * width, :] = value
    for start in range(0, blocks * size, tile):
        total = None
        for place in range(peers):
            term = lax.dot_general(
                table[place], hot(ids[place], rows, start, tile), (((1,), (1,)), ((), ())),
                preferred_element_type=F32,
            )
            total = term if total is None else total + term
        total = fold(total, width)
        for offset in range(0, tile, size):
            out[(start + offset) // size] = total[:, offset:offset + size]


def gather_base(user_emb, item_emb, ids, user_out, item_out):
    tile = ids.shape[1]
    user_out[...] = pick(user_emb, ids, [0], tile)
    item_out[...] = pick(item_emb, ids, [1, 2], tile)


def add_all(refs):
    total = refs[0][...]
    for ref in refs[1:]:
        total = total + ref[...]
    return total


def slopes(user_parts, item_parts, *refs):
    users, items = refs[:user_parts], refs[user_parts:user_parts + item_parts]
    pieces, pushed = refs[user_parts + item_parts:]
    user_rows = 0.5 * add_all(users)
    difference = 0.5 * add_all(items)
    margin = jnp.sum(user_rows * difference, axis=0, keepdims=True)
    slope = -jax.nn.sigmoid(-margin)
    pieces[...] = slope * difference
    pushed[...] = slope * user_rows


def halves(total, keep, send):
    me = lax.axis_index("rep")
    half = keep.shape[1]
    for block in range(keep.shape[0]):
        keep[block] = total[block, pl.ds(pl.multiple_of(me * half, half), half), :]
        send[block] = total[block, pl.ds(pl.multiple_of((1 - me) * half, half), half), :]


def second_pass(across, order, mine, other, source_scale, target_scale, vals, after,
                half_grad, *refs):
    outs, (source, total) = refs[:-2], refs[-2:]
    blocks, width, size = mine.shape
    for block in range(blocks):
        grad = mine[block] + other[block]
        half_grad[block] = 0.5 * grad
        source[block] = (source_scale[block:block + 1, :] * grad * 0.5).astype(BF16)
    source[blocks] = jnp.zeros((width, size), BF16)
    multiply_blocks(order, vals, source, total, across)
    scaled = outs[0] if len(outs) == 1 else total
    for block in range(total.shape[0]):
        scaled[block] = target_scale[block:block + 1, :] * total[block]
    if len(outs) == 2:
        halves(total, *outs)


def halves_after(total, after, keep, send):
    halves(total, keep, send)


def add_deal(peers, keep, received, after, *outs):
    me = lax.axis_index("user")
    per = outs[0].shape[0]
    for offset in range(peers):
        there = (me ^ offset) * per
        for block in range(per):
            outs[offset][block] = keep[there + block] + received[there + block]


def sum_parts(*refs):
    refs[-1][...] = add_all(refs[:-1])


def sum_after(after, *refs):
    sum_parts(*refs)


def pack(*refs):
    for place, ref in enumerate(refs[:-1]):
        refs[-1][place] = ref[...]


def finish(peers, user_half_grad, user_mine, user_other, item_half_grad, item_mine, item_other,
           user_out, item_out):
    finish_users(user_half_grad, user_mine, user_other, user_out)
    finish_items(peers, item_half_grad, item_mine, item_other, item_out)


def finish_users(half_grad, mine, other, out):
    me = lax.axis_index("rep")
    blocks, width, size = half_grad.shape
    half = width // 2
    for block in range(blocks):
        span = slice(block * size, (block + 1) * size)
        for rank, part in ((me, mine), (1 - me, other)):
            rows = pl.ds(pl.multiple_of(rank * half, half), half)
            out[rows, span] = half_grad[block, rows, :] + part[block]


def finish_items(peers, half_grad, mine, other, out):
    me = lax.axis_index("rep")
    place = lax.axis_index("user")
    blocks, width, size = half_grad.shape
    half = width // 2
    per = blocks // peers
    for offset in range(peers):
        there = (place ^ offset) * per
        for block in range(per):
            span = pl.ds(pl.multiple_of((there + block) * size, size), size)
            for rank, part in ((me, mine), (1 - me, other)):
                rows = pl.ds(pl.multiple_of(rank * half, half), half)
                out[rows, span] = half_grad[there + block, rows, :] + part[offset, block]


def swap(values, axis="rep", peers=2, offset=1):
    return lax.ppermute(values, axis, [(i, i ^ offset) for i in range(peers)])


def on_device(users, items, user_emb, item_emb, user_deg, item_deg, block_vals, block_row,
              block_col, block_count, trip_user, trip_pos, trip_neg):
    width = user_emb.shape[0]
    slots, size, _ = block_vals.shape
    user_blocks = user_emb.shape[1] // size
    item_blocks = item_emb.shape[1] // size
    trips = trip_user.shape[0]
    half = width // 2
    user_deg = user_deg.reshape(user_blocks, size)
    item_deg = item_deg.reshape(item_blocks, size)

    product_flops = 2 * slots * size * size * width
    product_bytes = slots * size * size * 2
    started = call(begin, shape(8, size), (), [], (), 16 * product_flops, product_bytes)
    ids = call(
        stack_ids, jax.ShapeDtypeStruct((ID_ROWS, trips), jnp.int32),
        [each.reshape(1, trips) for each in (trip_user, trip_pos, trip_neg)] + [started],
        [VMEM, VMEM, VMEM, ANY],
    )
    ids_user = [ids] + [swap(ids, "item", items, o) for o in range(1, items)]
    ids_item = [ids] + [swap(ids, "user", users, o) for o in range(1, users)]
    lanes = -(-slots // size) * size

    order_shape = jax.ShapeDtypeStruct((8, lanes), jnp.int32)
    def source_shape(blocks):
        return jax.ShapeDtypeStruct((blocks + 1, width, size), BF16)

    (user_source, item_source, user_scale, item_scale, item_order, user_order) = call(
        prepare,
        [source_shape(user_blocks), source_shape(item_blocks), shape(user_blocks, size),
         shape(item_blocks, size), order_shape, order_shape],
        (block_count, block_row, block_col, user_emb, item_emb, user_deg, item_deg, ids),
        [SMEM, VMEM, VMEM, VMEM, VMEM, VMEM, VMEM, ANY],
        [pltpu.VMEM((8, lanes), jnp.int32)], product_flops, product_bytes,
    )
    item_table = call(
        functools.partial(first_pass, False), shape(item_blocks, width, size),
        (item_order, block_vals, user_source, ids), [SMEM, VMEM, VMEM, ANY], (),
        product_flops, product_bytes,
    )
    ids_here = [*ids_item[1:], *ids_user[1:]]
    user_table = call(
        functools.partial(first_pass, True), shape(user_blocks, width, size),
        (user_order, block_vals, item_source, item_table, *ids_here),
        [SMEM, VMEM, VMEM] + [ANY] * (1 + len(ids_here)), (),
        product_flops, product_bytes,
    )

    hot_flops = 2 * 3 * width * trips * size

    def reduced(rows, table, scale, peer_ids, axis, after):
        peers, blocks = len(peer_ids), scale.shape[0]
        dealt = call(
            functools.partial(gather, rows, peers), [shape(width, trips)] * peers,
            (table, swap(table), scale, after, *peer_ids), [VMEM] * 3 + [ANY] + [VMEM] * peers,
            [pltpu.VMEM((3 * width, blocks * size), BF16)],
            peers * blocks * hot_flops, 8 * blocks * width * size,
        )
        return [dealt[0]] + [swap(dealt[o], axis, peers, o) for o in range(1, peers)]

    item_parts = reduced([1, 2], item_table, item_scale, ids_item, "user", ids)
    user_parts = reduced([0], user_table, user_scale, ids_user, "item", item_parts[0])
    user_base, item_base = call(
        gather_base, [shape(width, trips)] * 2, (user_emb, item_emb, ids),
        [VMEM, VMEM, VMEM], (), 4 * width * trips * size * (user_blocks + item_blocks),
        2 * width * size * (user_blocks + item_blocks),
    )
    user_parts.append(user_base)
    item_parts.append(item_base)
    pieces, pushed = call(
        functools.partial(slopes, len(user_parts), len(item_parts)),
        [shape(width, trips)] * 2,
        (*user_parts, *item_parts), [VMEM] * (len(user_parts) + len(item_parts)),
        moved=4 * width * trips * (len(user_parts) + len(item_parts) + 2),
    )

    def added(rows, own, axis, peer_ids, blocks, after):
        peers = len(peer_ids)
        arrays = [own] + [swap(own, axis, peers, o) for o in range(1, peers)]
        return call(
            functools.partial(scatter, rows, peers), shape(blocks, width, size),
            (after, *arrays, *peer_ids), [ANY] + [VMEM] * (2 * peers),
            [pltpu.VMEM((peers, 3 * width, trips), BF16)],
            peers * blocks * hot_flops, 4 * blocks * width * size,
        )

    def second(across, grad, order, source_scale, target_scale, after, divided):
        sources, targets = source_scale.shape[0], target_scale.shape[0]
        return call(
            functools.partial(second_pass, across),
            [shape(sources, width, size)]
            + ([shape(targets, half, size)] * 2 if divided else [shape(targets, width, size)]),
            (order, grad, swap(grad), source_scale, target_scale, block_vals, after),
            [SMEM, VMEM, VMEM, VMEM, VMEM, VMEM, ANY],
            [pltpu.VMEM((sources + 1, width, size), BF16),
             pltpu.VMEM((targets, width, size), F32)],
            product_flops, product_bytes,
        )

    user_grad = added([0], pieces, "item", ids_user, user_blocks, pieces)
    user_grad = added([0], pieces, "item", ids_user, user_blocks, pieces)
    def divided(total, after):
        blocks = total.shape[0]
        return call(halves, [shape(blocks, half, size)] * 2, (total, after), [VMEM, ANY],
                    moved=8 * blocks * width * size)

    user_grad = added([0], pieces, "item", ids_user, user_blocks, pieces)
    user_half_grad, item_keep, item_send = second(
        False, user_grad, item_order, user_scale, item_scale, pieces, True)
    item_grad = added([1, 2], pushed, "user", ids_item, item_blocks, item_send)

    per = item_blocks // users
    dealt = call(
        functools.partial(add_deal, users), [shape(per, half, size)] * users,
        (item_keep, swap(item_send), item_grad), [VMEM, VMEM, ANY],
        moved=12 * item_blocks * half * size,
    )
    item_half_grad, user_back = second(
        True, item_grad, user_order, item_scale, user_scale, dealt[0], False)
    parts = [dealt[0]] + [swap(dealt[o], "user", users, o) for o in range(1, users)]
    item_own = call(sum_after, shape(per, half, size), (user_back, *parts),
                    [ANY] + [VMEM] * users,
               moved=4 * (users + 1) * per * half * size)
    item_mine = call(pack, shape(users, per, half, size),
                     (item_own, *[swap(item_own, "user", users, o) for o in range(1, users)]),
                     [VMEM] * users, moved=8 * item_blocks * half * size)
    item_other = swap(item_mine)

    user_keep, user_send = call(
        halves_after, [shape(user_blocks, half, size)] * 2, (user_back, item_own), [VMEM, ANY],
        moved=8 * user_blocks * width * size,
    )
    own = call(sum_parts, shape(user_blocks, half, size), (user_keep, swap(user_send)),
               [VMEM, VMEM], moved=12 * user_blocks * half * size)
    mine = call(sum_parts, shape(user_blocks, half, size),
                (own, *[swap(own, "item", items, o) for o in range(1, items)]),
                [VMEM] * items, moved=12 * user_blocks * half * size)
    return call(
        functools.partial(finish, users),
        (shape(width, user_blocks * size), shape(width, item_blocks * size)),
        (user_half_grad, mine, swap(mine), item_half_grad, item_mine, item_other),
        [VMEM] * 6, moved=12 * (user_blocks + item_blocks) * width * size,
    )


def solution(mesh):
    return jax.shard_map(
        functools.partial(on_device, mesh.shape["user"], mesh.shape["item"]),
        mesh=mesh,
        in_specs=(
            P(None, ("groups", "user")),
            P(None, ("groups", "item")),
            P(("groups", "user")),
            P(("groups", "item")),
            P(("groups", "user", "item", "rep"), None, None),
            P(("groups", "user", "item", "rep")),
            P(("groups", "user", "item", "rep")),
            P(("groups", "user", "item", "rep")),
            P(("groups", "user", "item", "rep")),
            P(("groups", "user", "item", "rep")),
            P(("groups", "user", "item", "rep")),
        ),
        out_specs=(P(None, ("groups", "user")), P(None, ("groups", "item"))),
        check_vma=False,
    )
```

```python
import functools

import jax
import jax.numpy as jnp
from jax import lax
from jax.experimental import pallas as pl
from jax.experimental.pallas import tpu as pltpu
from jax.sharding import PartitionSpec as P

F32 = jnp.float32
BF16 = jnp.bfloat16
PACK = 4
GROUP = 4
ID_ROWS = 64
LIGHT = 0
HEAVY = 10 ** 11

VMEM = pl.BlockSpec(memory_space=pltpu.VMEM)
SMEM = pl.BlockSpec(memory_space=pltpu.SMEM)
ANY = pl.BlockSpec(memory_space=pl.ANY)
HBM = pl.BlockSpec(memory_space=pltpu.HBM)


def call(kernel, outs, ins, specs, scratch=(), flops=0, moved=0, room=24):
    return pl.pallas_call(
        kernel,
        out_shape=outs,
        in_specs=specs,
        out_specs=jax.tree.map(lambda _: VMEM, outs),
        scratch_shapes=list(scratch),
        cost_estimate=pl.CostEstimate(flops=flops, bytes_accessed=moved, transcendentals=0),
        compiler_params=pltpu.CompilerParams(vmem_limit_bytes=room * 1024 * 1024),
    )(*ins)


def shape(*dims):
    return jax.ShapeDtypeStruct(dims, F32)


def split3(values):
    high = values.astype(BF16)
    rest = values - high.astype(F32)
    middle = rest.astype(BF16)
    low = (rest - middle.astype(F32)).astype(BF16)
    return high, middle, low


def hot(ids_ref, rows, start, tile):
    ids = [ids_ref[row:row + 1, :] for row in rows]
    if len(rows) == 2:
        same = ids[0] == ids[1]
        ids = [jnp.where(same, -1, each) for each in ids]
    ids = [each.astype(jnp.int16) for each in ids]
    place = lax.broadcasted_iota(jnp.int16, (tile, ids[0].shape[1]), 0) + jnp.int16(start)
    chosen = jnp.zeros(place.shape, BF16)
    for each, sign in zip(ids, (1, -1)):
        chosen = jnp.where(place == each, jnp.asarray(sign, BF16), chosen)
    return chosen


def sort_slots(keys, sources, count, blocks):
    lanes = keys.shape[1]
    rows = 2 * blocks
    place = lax.broadcasted_iota(jnp.int32, (1, lanes), 1)
    live = place < count
    mine = (lax.broadcasted_iota(jnp.int32, (rows, lanes), 0) == keys) & live
    mine = jnp.where(mine, 1.0, 0.0)
    earlier = lax.broadcasted_iota(jnp.int32, (lanes, lanes), 0) < lax.broadcasted_iota(
        jnp.int32, (lanes, lanes), 1)
    before = jnp.dot(mine.astype(BF16), jnp.where(earlier, 1.0, 0.0).astype(BF16),
                     preferred_element_type=F32)
    packs = jnp.floor((jnp.sum(mine, axis=1, keepdims=True) + (PACK - 1)) * (1.0 / PACK))
    packs = jnp.broadcast_to(packs, (rows, 128))
    lower = lax.broadcasted_iota(jnp.int32, (rows, rows), 1) < lax.broadcasted_iota(
        jnp.int32, (rows, rows), 0)
    first = jnp.dot(jnp.where(lower, 1.0, 0.0).astype(BF16), packs.astype(BF16),
                    preferred_element_type=F32)
    position = jnp.sum(mine * (first[:, :1] * PACK + before), axis=0, keepdims=True)
    position = jnp.where(live, position.astype(jnp.int32), -1)
    match = lax.broadcasted_iota(jnp.int32, (lanes, lanes), 0) == position
    row = lax.broadcasted_iota(jnp.int32, (16, lanes), 0)
    values = jnp.where(row == 0, place // 16, jnp.where(row == 1, place % 16, jnp.where(
        row == 2, sources, jnp.where(row == 3, keys, jnp.where(row == 4, 1, 0)))))
    values = jnp.where(live, values, 0).astype(F32)
    found = lax.dot_general(values.astype(BF16), jnp.where(match, 1.0, 0.0).astype(BF16),
                            (((1,), (1,)), ((), ())), preferred_element_type=F32)
    found = found.astype(jnp.int32)
    valid = found[4:5] > 0
    total = jnp.broadcast_to(jnp.sum(packs[:, :1], axis=0, keepdims=True), (1, lanes))
    row = lax.broadcasted_iota(jnp.int32, (8, lanes), 0)
    slot = found[0:1] * 16 + found[1:2]
    source = jnp.where(valid, found[2:3], blocks)
    target = jnp.where(valid, found[3:4], 0)
    return jnp.where(row == 0, slot, jnp.where(row == 1, source, jnp.where(
        row == 2, target, total.astype(jnp.int32))))


def multiply_blocks(order, vals, source, total, across):
    _, width, size = source.shape
    total[...] = jnp.zeros_like(total)
    contract = (((1,), (1,)), ((), ())) if across else (((1,), (0,)), ((), ()))

    def group(index, _):
        targets, terms = [], []
        for step in range(GROUP):
            left, right = [], []
            for half in range(2):
                first = ((index * GROUP + step) * 2 + half) * PACK
                places = [first + each for each in range(PACK)]
                left.append(jnp.concatenate([source[order[1, each]] for each in places], axis=1))
                right.append(jnp.concatenate([vals[order[0, each]] for each in places],
                                             axis=1 if across else 0))
                targets.append(order[2, first])
            both = lax.dot_general(
                jnp.concatenate(left, axis=0), jnp.concatenate(right, axis=0 if across else 1),
                contract, preferred_element_type=F32,
            )
            terms += [both[:width, :size], both[width:, size:]]
        for target, term in zip(targets, terms):
            total[target] += term
        return 0

    lax.fori_loop(0, (order[3, 0] + 2 * GROUP - 1) // (2 * GROUP), group, 0)


def begin(out):
    out[...] = jnp.zeros_like(out)


def stack_ids(user, positive, negative, after, out):
    out[...] = jnp.zeros_like(out)
    for row, ids in enumerate((user, positive, negative)):
        out[row:row + 1, :] = ids[...]


def prepare(count, rows, columns, user_emb, item_emb, user_deg, item_deg, after,
            user_source, item_source, user_scale, item_scale, item_order, user_order, keys):
    live = count[0]
    slots = rows.shape[0]
    keys[...] = jnp.zeros_like(keys)
    keys[0:1, 0:slots] = rows[...].reshape(1, slots)
    keys[1:2, 0:slots] = columns[...].reshape(1, slots)
    users, items = keys[0:1, :], keys[1:2, :]
    item_order[...] = sort_slots(items, users, live, item_scale.shape[0])
    user_order[...] = sort_slots(users, items, live, user_scale.shape[0])
    for emb, deg, scale, into in ((user_emb, user_deg, user_scale, user_source),
                                  (item_emb, item_deg, item_scale, item_source)):
        scale[...] = lax.rsqrt(deg[...].astype(F32))
        blocks, size = scale.shape
        for block in range(blocks):
            piece = emb[:, block * size:(block + 1) * size].astype(F32)
            into[block] = (scale[block:block + 1, :] * piece).astype(BF16)
        into[blocks] = jnp.zeros(into.shape[1:], BF16)


def first_pass(across, order, vals, source, *refs):
    multiply_blocks(order, vals, source, refs[-1], across)


def fold(stacked, width):
    return (
        stacked[:width] + stacked[width:2 * width] + stacked[2 * width:3 * width]
    )


def pick(table, ids_ref, rows, tile):
    total = None
    for start in range(0, table.shape[1], tile):
        term = jnp.dot(
            table[:, start:start + tile], hot(ids_ref, rows, start, tile),
            preferred_element_type=F32,
        )
        total = term if total is None else total + term
    return total


def gather(rows, peers, mine, other, scale, after, *refs):
    ids, outs, table = refs[:peers], refs[peers:2 * peers], refs[2 * peers]
    blocks, width, size = mine.shape
    for block in range(blocks):
        span = slice(block * size, (block + 1) * size)
        here = scale[block:block + 1, :] * (mine[block] + other[block])
        for part, piece in enumerate(split3(here)):
            table[part * width:(part + 1) * width, span] = piece
    for peer in range(peers):
        outs[peer][...] = fold(pick(table, ids[peer], rows, 2 * size), width)


def scatter(rows, peers, *refs):
    pieces, ids, out, table = refs[:peers], refs[peers:2 * peers], refs[2 * peers], refs[-1]
    blocks, width, size = out.shape
    tile = 2 * size
    for place, piece in enumerate(pieces):
        for part, value in enumerate(split3(piece[...])):
            table[place, part * width:(part + 1) * width, :] = value
    for start in range(0, blocks * size, tile):
        total = None
        for place in range(peers):
            term = lax.dot_general(
                table[place], hot(ids[place], rows, start, tile), (((1,), (1,)), ((), ())),
                preferred_element_type=F32,
            )
            total = term if total is None else total + term
        total = fold(total, width)
        for offset in range(0, tile, size):
            out[(start + offset) // size] = total[:, offset:offset + size]


def gather_base(user_emb, item_emb, ids, user_out, item_out):
    tile = ids.shape[1]
    user_out[...] = pick(user_emb, ids, [0], tile)
    item_out[...] = pick(item_emb, ids, [1, 2], tile)


def add_all(refs):
    total = refs[0][...]
    for ref in refs[1:]:
        total = total + ref[...]
    return total


def slopes(user_parts, item_parts, *refs):
    users, items = refs[:user_parts], refs[user_parts:user_parts + item_parts]
    pieces, pushed = refs[user_parts + item_parts:]
    user_rows = 0.5 * add_all(users)
    difference = 0.5 * add_all(items)
    margin = jnp.sum(user_rows * difference, axis=0, keepdims=True)
    slope = -jax.nn.sigmoid(-margin)
    pieces[...] = slope * difference
    pushed[...] = slope * user_rows


def halves(total, keep, send):
    me = lax.axis_index("rep")
    half = keep.shape[1]
    for block in range(keep.shape[0]):
        keep[block] = total[block, pl.ds(pl.multiple_of(me * half, half), half), :]
        send[block] = total[block, pl.ds(pl.multiple_of((1 - me) * half, half), half), :]


def second_pass(across, order, mine, other, source_scale, target_scale, vals, after,
                half_grad, *refs):
    outs, (source, total) = refs[:-2], refs[-2:]
    blocks, width, size = mine.shape
    for block in range(blocks):
        grad = mine[block] + other[block]
        half_grad[block] = 0.5 * grad
        source[block] = (source_scale[block:block + 1, :] * grad * 0.5).astype(BF16)
    source[blocks] = jnp.zeros((width, size), BF16)
    multiply_blocks(order, vals, source, total, across)
    scaled = outs[0] if len(outs) == 1 else total
    for block in range(total.shape[0]):
        scaled[block] = target_scale[block:block + 1, :] * total[block]
    if len(outs) == 2:
        halves(total, *outs)


def halves_after(total, after, keep, send):
    halves(total, keep, send)


def add_deal(peers, keep, received, after, *outs):
    me = lax.axis_index("user")
    per = outs[0].shape[0]
    for offset in range(peers):
        there = (me ^ offset) * per
        for block in range(per):
            outs[offset][block] = keep[there + block] + received[there + block]


def sum_parts(*refs):
    refs[-1][...] = add_all(refs[:-1])


def sum_after(after, *refs):
    sum_parts(*refs)


def pack(*refs):
    for place, ref in enumerate(refs[:-1]):
        refs[-1][place] = ref[...]


def finish(peers, user_half_grad, user_mine, user_other, item_half_grad, item_mine, item_other,
           user_out, item_out):
    finish_users(user_half_grad, user_mine, user_other, user_out)
    finish_items(peers, item_half_grad, item_mine, item_other, item_out)


def finish_users(half_grad, mine, other, out):
    me = lax.axis_index("rep")
    blocks, width, size = half_grad.shape
    half = width // 2
    for block in range(blocks):
        span = slice(block * size, (block + 1) * size)
        for rank, part in ((me, mine), (1 - me, other)):
            rows = pl.ds(pl.multiple_of(rank * half, half), half)
            out[rows, span] = half_grad[block, rows, :] + part[block]


def finish_items(peers, half_grad, mine, other, out):
    me = lax.axis_index("rep")
    place = lax.axis_index("user")
    blocks, width, size = half_grad.shape
    half = width // 2
    per = blocks // peers
    for offset in range(peers):
        there = (place ^ offset) * per
        for block in range(per):
            span = pl.ds(pl.multiple_of((there + block) * size, size), size)
            for rank, part in ((me, mine), (1 - me, other)):
                rows = pl.ds(pl.multiple_of(rank * half, half), half)
                out[rows, span] = half_grad[there + block, rows, :] + part[offset, block]


def swap(values, axis="rep", peers=2, offset=1):
    return lax.ppermute(values, axis, [(i, i ^ offset) for i in range(peers)])


def on_device(users, items, user_emb, item_emb, user_deg, item_deg, block_vals, block_row,
              block_col, block_count, trip_user, trip_pos, trip_neg):
    width = user_emb.shape[0]
    slots, size, _ = block_vals.shape
    user_blocks = user_emb.shape[1] // size
    item_blocks = item_emb.shape[1] // size
    trips = trip_user.shape[0]
    half = width // 2
    user_deg = user_deg.reshape(user_blocks, size)
    item_deg = item_deg.reshape(item_blocks, size)

    product_flops = 2 * slots * size * size * width
    product_bytes = slots * size * size * 2
    started = call(begin, shape(8, size), (), [], (), 16 * product_flops, product_bytes)
    ids = call(
        stack_ids, jax.ShapeDtypeStruct((ID_ROWS, trips), jnp.int32),
        [each.reshape(1, trips) for each in (trip_user, trip_pos, trip_neg)] + [started],
        [VMEM, VMEM, VMEM, ANY],
    )
    ids_user = [ids] + [swap(ids, "item", items, o) for o in range(1, items)]
    ids_item = [ids] + [swap(ids, "user", users, o) for o in range(1, users)]
    lanes = -(-slots // size) * size

    order_shape = jax.ShapeDtypeStruct((8, lanes), jnp.int32)
    def source_shape(blocks):
        return jax.ShapeDtypeStruct((blocks + 1, width, size), BF16)

    (user_source, item_source, user_scale, item_scale, item_order, user_order) = call(
        prepare,
        [source_shape(user_blocks), source_shape(item_blocks), shape(user_blocks, size),
         shape(item_blocks, size), order_shape, order_shape],
        (block_count, block_row, block_col, user_emb, item_emb, user_deg, item_deg, ids),
        [SMEM, VMEM, VMEM, VMEM, VMEM, VMEM, VMEM, ANY],
        [pltpu.VMEM((8, lanes), jnp.int32)], product_flops, product_bytes,
    )
    item_table = call(
        functools.partial(first_pass, False), shape(item_blocks, width, size),
        (item_order, block_vals, user_source, ids), [SMEM, VMEM, VMEM, ANY], (),
        product_flops, product_bytes,
    )
    ids_here = [*ids_item[1:], *ids_user[1:]]
    user_table = call(
        functools.partial(first_pass, True), shape(user_blocks, width, size),
        (user_order, block_vals, item_source, item_table, *ids_here),
        [SMEM, VMEM, VMEM] + [ANY] * (1 + len(ids_here)), (),
        product_flops, product_bytes,
    )

    hot_flops = 2 * 3 * width * trips * size

    def reduced(rows, table, scale, peer_ids, axis, after):
        peers, blocks = len(peer_ids), scale.shape[0]
        dealt = call(
            functools.partial(gather, rows, peers), [shape(width, trips)] * peers,
            (table, swap(table), scale, after, *peer_ids), [VMEM] * 3 + [ANY] + [VMEM] * peers,
            [pltpu.VMEM((3 * width, blocks * size), BF16)],
            peers * blocks * hot_flops, 8 * blocks * width * size,
        )
        return [dealt[0]] + [swap(dealt[o], axis, peers, o) for o in range(1, peers)]

    item_parts = reduced([1, 2], item_table, item_scale, ids_item, "user", ids)
    user_parts = reduced([0], user_table, user_scale, ids_user, "item", item_parts[0])
    user_base, item_base = call(
        gather_base, [shape(width, trips)] * 2, (user_emb, item_emb, ids),
        [VMEM, VMEM, VMEM], (), 4 * width * trips * size * (user_blocks + item_blocks),
        2 * width * size * (user_blocks + item_blocks),
    )
    user_parts.append(user_base)
    item_parts.append(item_base)
    pieces, pushed = call(
        functools.partial(slopes, len(user_parts), len(item_parts)),
        [shape(width, trips)] * 2,
        (*user_parts, *item_parts), [VMEM] * (len(user_parts) + len(item_parts)),
        moved=4 * width * trips * (len(user_parts) + len(item_parts) + 2),
    )

    def added(rows, own, axis, peer_ids, blocks, weight):
        peers = len(peer_ids)
        arrays = [own] + [swap(own, axis, peers, o) for o in range(1, peers)]
        return call(
            functools.partial(scatter, rows, peers), shape(blocks, width, size),
            (*arrays, *peer_ids), [VMEM] * (2 * peers),
            [pltpu.VMEM((peers, 3 * width, trips), BF16)], weight, 0,
        )

    def second(across, grad, order, source_scale, target_scale, after, divided):
        sources, targets = source_scale.shape[0], target_scale.shape[0]
        return call(
            functools.partial(second_pass, across),
            [shape(sources, width, size)]
            + ([shape(targets, half, size)] * 2 if divided else [shape(targets, width, size)]),
            (order, grad, swap(grad), source_scale, target_scale, block_vals, after),
            [SMEM, VMEM, VMEM, VMEM, VMEM, VMEM, ANY],
            [pltpu.VMEM((sources + 1, width, size), BF16),
             pltpu.VMEM((targets, width, size), F32)],
            product_flops, product_bytes,
        )

    user_grad = added([0], pieces, "item", ids_user, user_blocks, LIGHT)
    item_grad = added([1, 2], pushed, "user", ids_item, item_blocks, HEAVY)
    user_half_grad, item_keep, item_send = second(
        False, user_grad, item_order, user_scale, item_scale, item_grad, True)

    per = item_blocks // users
    dealt = call(
        functools.partial(add_deal, users), [shape(per, half, size)] * users,
        (item_keep, swap(item_send), pieces), [VMEM, VMEM, ANY],
        moved=12 * item_blocks * half * size,
    )
    item_half_grad, user_back = second(
        True, item_grad, user_order, item_scale, user_scale, dealt[0], False)
    parts = [dealt[0]] + [swap(dealt[o], "user", users, o) for o in range(1, users)]
    item_own = call(sum_after, shape(per, half, size), (user_back, *parts),
                    [ANY] + [VMEM] * users,
               moved=4 * (users + 1) * per * half * size)
    item_mine = call(pack, shape(users, per, half, size),
                     (item_own, *[swap(item_own, "user", users, o) for o in range(1, users)]),
                     [VMEM] * users, moved=8 * item_blocks * half * size)
    item_other = swap(item_mine)

    user_keep, user_send = call(
        halves_after, [shape(user_blocks, half, size)] * 2, (user_back, item_own), [VMEM, ANY],
        moved=8 * user_blocks * width * size,
    )
    own = call(sum_parts, shape(user_blocks, half, size), (user_keep, swap(user_send)),
               [VMEM, VMEM], moved=12 * user_blocks * half * size)
    mine = call(sum_parts, shape(user_blocks, half, size),
                (own, *[swap(own, "item", items, o) for o in range(1, items)]),
                [VMEM] * items, moved=12 * user_blocks * half * size)
    return call(
        functools.partial(finish, users),
        (shape(width, user_blocks * size), shape(width, item_blocks * size)),
        (user_half_grad, mine, swap(mine), item_half_grad, item_mine, item_other),
        [VMEM] * 6, moved=12 * (user_blocks + item_blocks) * width * size,
    )


def solution(mesh):
    return jax.shard_map(
        functools.partial(on_device, mesh.shape["user"], mesh.shape["item"]),
        mesh=mesh,
        in_specs=(
            P(None, ("groups", "user")),
            P(None, ("groups", "item")),
            P(("groups", "user")),
            P(("groups", "item")),
            P(("groups", "user", "item", "rep"), None, None),
            P(("groups", "user", "item", "rep")),
            P(("groups", "user", "item", "rep")),
            P(("groups", "user", "item", "rep")),
            P(("groups", "user", "item", "rep")),
            P(("groups", "user", "item", "rep")),
            P(("groups", "user", "item", "rep")),
        ),
        out_specs=(P(None, ("groups", "user")), P(None, ("groups", "item"))),
        check_vma=False,
    )
```

```python
import functools

import jax
import jax.numpy as jnp
from jax import lax
from jax.experimental import pallas as pl
from jax.experimental.pallas import tpu as pltpu
from jax.sharding import PartitionSpec as P

F32 = jnp.float32
BF16 = jnp.bfloat16
PACK = 4
GROUP = 4
FIELD = 32
ID_ROWS = 64
HEAVY = 10 ** 11

VMEM = pl.BlockSpec(memory_space=pltpu.VMEM)
SMEM = pl.BlockSpec(memory_space=pltpu.SMEM)
ANY = pl.BlockSpec(memory_space=pl.ANY)
HBM = pl.BlockSpec(memory_space=pltpu.HBM)


def call(kernel, outs, ins, specs, scratch=(), flops=0, moved=0, room=24):
    return pl.pallas_call(
        kernel,
        out_shape=outs,
        in_specs=specs,
        out_specs=jax.tree.map(lambda _: VMEM, outs),
        scratch_shapes=list(scratch),
        cost_estimate=pl.CostEstimate(flops=flops, bytes_accessed=moved, transcendentals=0),
        compiler_params=pltpu.CompilerParams(vmem_limit_bytes=room * 1024 * 1024),
    )(*ins)


def shape(*dims):
    return jax.ShapeDtypeStruct(dims, F32)


def split3(values):
    high = values.astype(BF16)
    rest = values - high.astype(F32)
    middle = rest.astype(BF16)
    low = (rest - middle.astype(F32)).astype(BF16)
    return high, middle, low


def hot(ids, start, tile):
    if len(ids) == 2:
        same = ids[0] == ids[1]
        ids = [jnp.where(same, -1, each) for each in ids]
    ids = [each.astype(jnp.int16) for each in ids]
    place = lax.broadcasted_iota(jnp.int16, (tile, ids[0].shape[1]), 0) + jnp.int16(start)
    chosen = jnp.zeros(place.shape, BF16)
    for each, sign in zip(ids, (1, -1)):
        chosen = jnp.where(place == each, jnp.asarray(sign, BF16), chosen)
    return chosen


def sort_slots(keys, sources, count, blocks):
    lanes = keys.shape[1]
    rows = 2 * blocks
    place = lax.broadcasted_iota(jnp.int32, (1, lanes), 1)
    live = place < count
    mine = (lax.broadcasted_iota(jnp.int32, (rows, lanes), 0) == keys) & live
    mine = jnp.where(mine, 1.0, 0.0)
    earlier = lax.broadcasted_iota(jnp.int32, (lanes, lanes), 0) < lax.broadcasted_iota(
        jnp.int32, (lanes, lanes), 1)
    before = jnp.dot(mine.astype(BF16), jnp.where(earlier, 1.0, 0.0).astype(BF16),
                     preferred_element_type=F32)
    packs = jnp.floor((jnp.sum(mine, axis=1, keepdims=True) + (PACK - 1)) * (1.0 / PACK))
    packs = jnp.broadcast_to(packs, (rows, 128))
    lower = lax.broadcasted_iota(jnp.int32, (rows, rows), 1) < lax.broadcasted_iota(
        jnp.int32, (rows, rows), 0)
    first = jnp.dot(jnp.where(lower, 1.0, 0.0).astype(BF16), packs.astype(BF16),
                    preferred_element_type=F32)
    position = jnp.sum(mine * (first[:, :1] * PACK + before), axis=0, keepdims=True)
    position = jnp.where(live, position.astype(jnp.int32), -1)
    match = lax.broadcasted_iota(jnp.int32, (lanes, lanes), 0) == position
    row = lax.broadcasted_iota(jnp.int32, (16, lanes), 0)
    values = jnp.where(row == 0, place // 16, jnp.where(row == 1, place % 16, jnp.where(
        row == 2, sources, jnp.where(row == 3, keys, jnp.where(row == 4, 1, 0)))))
    values = jnp.where(live, values, 0).astype(F32)
    found = lax.dot_general(values.astype(BF16), jnp.where(match, 1.0, 0.0).astype(BF16),
                            (((1,), (1,)), ((), ())), preferred_element_type=F32)
    found = found.astype(jnp.int32)
    valid = found[4:5] > 0
    total = jnp.broadcast_to(jnp.sum(packs[:, :1], axis=0, keepdims=True), (1, lanes))
    row = lax.broadcasted_iota(jnp.int32, (2, lanes), 0)
    slot = found[0:1] * 16 + found[1:2]
    source = jnp.where(valid, found[2:3], blocks)
    target = jnp.where(valid, found[3:4], 0)
    return jnp.where(row == 0, (slot * FIELD + source) * FIELD + target, total.astype(jnp.int32))


def multiply_blocks(order, vals, source, total, across):
    _, width, size = source.shape
    total[...] = jnp.zeros_like(total)
    contract = (((1,), (1,)), ((), ())) if across else (((1,), (0,)), ((), ()))

    def group(index, _):
        targets, terms = [], []
        for step in range(GROUP):
            left, right = [], []
            for half in range(2):
                first = ((index * GROUP + step) * 2 + half) * PACK
                places = [first + each for each in range(PACK)]
                words = [order[0, each] for each in places]
                left.append(jnp.concatenate(
                    [source[lax.rem(word // FIELD, FIELD)] for word in words], axis=1))
                right.append(jnp.concatenate([vals[word // FIELD ** 2] for word in words],
                                             axis=1 if across else 0))
                targets.append(lax.rem(words[0], FIELD))
            both = lax.dot_general(
                jnp.concatenate(left, axis=0), jnp.concatenate(right, axis=0 if across else 1),
                contract, preferred_element_type=F32,
            )
            terms += [both[:width, :size], both[width:, size:]]
        for target, term in zip(targets, terms):
            total[target] += term
        return 0

    lax.fori_loop(0, (order[1, 0] + 2 * GROUP - 1) // (2 * GROUP), group, 0)


def begin(out):
    out[...] = jnp.zeros_like(out)


def stack_ids(user, positive, negative, after, out):
    out[...] = jnp.zeros_like(out)
    for row, ids in enumerate((user, positive, negative)):
        out[row:row + 1, :] = ids[...]


def prepare(count, rows, columns, user_emb, item_emb, user_deg, item_deg, after,
            user_source, item_source, user_scale, item_scale, item_order, user_order, keys):
    live = count[0]
    slots = rows.shape[0]
    keys[...] = jnp.zeros_like(keys)
    keys[0:1, 0:slots] = rows[...].reshape(1, slots)
    keys[1:2, 0:slots] = columns[...].reshape(1, slots)
    users, items = keys[0:1, :], keys[1:2, :]
    item_order[...] = sort_slots(items, users, live, item_scale.shape[0])
    user_order[...] = sort_slots(users, items, live, user_scale.shape[0])
    for emb, deg, scale, into in ((user_emb, user_deg, user_scale, user_source),
                                  (item_emb, item_deg, item_scale, item_source)):
        scale[...] = lax.rsqrt(deg[...].astype(F32))
        blocks, size = scale.shape
        for block in range(blocks):
            piece = emb[:, block * size:(block + 1) * size].astype(F32)
            into[block] = (scale[block:block + 1, :] * piece).astype(BF16)
        into[blocks] = jnp.zeros(into.shape[1:], BF16)


def first_pass(across, order, vals, source, *refs):
    multiply_blocks(order, vals, source, refs[-1], across)


def fold(stacked, width):
    return (
        stacked[:width] + stacked[width:2 * width] + stacked[2 * width:3 * width]
    )


def rows_of(ref, rows):
    return [ref[row:row + 1, :] for row in rows]


def pick(table, ids, tile):
    total = None
    for start in range(0, table.shape[1], tile):
        term = jnp.dot(
            table[:, start:start + tile], hot(ids, start, tile),
            preferred_element_type=F32,
        )
        total = term if total is None else total + term
    return total


def gather(rows, peers, mine, other, scale, after, *refs):
    ids, outs, table = refs[:peers], refs[peers:2 * peers], refs[2 * peers]
    blocks, width, size = mine.shape
    for block in range(blocks):
        span = slice(block * size, (block + 1) * size)
        here = scale[block:block + 1, :] * (mine[block] + other[block])
        for part, piece in enumerate(split3(here)):
            table[part * width:(part + 1) * width, span] = piece
    for peer in range(peers):
        outs[peer][...] = fold(pick(table, rows_of(ids[peer], rows), 2 * size), width)


def scatter(pieces, ids, table, blocks, size, put):
    width = table.shape[1] // 3
    tile = 2 * size
    for place, piece in enumerate(pieces):
        for part, value in enumerate(split3(piece[:width, :])):
            table[place, part * width:(part + 1) * width, :] = value
    for start in range(0, blocks * size, tile):
        total = None
        for place, rows in enumerate(ids):
            term = lax.dot_general(
                table[place], hot(rows, start, tile), (((1,), (1,)), ((), ())),
                preferred_element_type=F32,
            )
            total = term if total is None else total + term
        total = fold(total, width)
        for offset in range(0, tile, size):
            put((start + offset) // size, total[:, offset:offset + size])


def scatter_items(peers, after, *refs):
    pieces, ids, out, table = refs[:peers], refs[peers:2 * peers], refs[2 * peers], refs[-1]
    blocks, _, size = out.shape

    def put(block, value):
        out[block] = value

    scatter(pieces, [rows_of(ref, [1, 2]) for ref in ids], table, blocks, size, put)


def gather_base(user_emb, item_emb, ids, user_out, item_out):
    tile = ids.shape[1]
    user_out[...] = pick(user_emb, rows_of(ids, [0]), tile)
    item_out[...] = pick(item_emb, rows_of(ids, [1, 2]), tile)


def add_all(refs):
    total = refs[0][...]
    for ref in refs[1:]:
        total = total + ref[...]
    return total


def slopes(user_parts, item_parts, ids, *refs):
    users, items = refs[:user_parts], refs[user_parts:user_parts + item_parts]
    pieces, pushed = refs[user_parts + item_parts:]
    width = pushed.shape[0]
    user_rows = 0.5 * add_all(users)
    difference = 0.5 * add_all(items)
    margin = jnp.sum(user_rows * difference, axis=0, keepdims=True)
    slope = -jax.nn.sigmoid(-margin)
    pieces[:width, :] = slope * difference
    pieces[width:, :] = jnp.broadcast_to(ids[0:1, :].astype(F32), (8, ids.shape[1]))
    pushed[...] = slope * user_rows


def halves(total, keep, send):
    me = lax.axis_index("rep")
    half = keep.shape[1]
    for block in range(keep.shape[0]):
        keep[block] = total[block, pl.ds(pl.multiple_of(me * half, half), half), :]
        send[block] = total[block, pl.ds(pl.multiple_of((1 - me) * half, half), half), :]


def second_items(parts, order, source_scale, target_scale, vals, *refs):
    pieces = refs[:parts]
    half_grad, keep, send, source, total, table = refs[parts:]
    blocks, width, size = half_grad.shape

    def put(block, grad):
        half_grad[block] = 0.5 * grad
        source[block] = (source_scale[block:block + 1, :] * grad * 0.5).astype(BF16)

    ids = [[piece[width:width + 1, :].astype(jnp.int32)] for piece in pieces]
    scatter(pieces, ids, table, blocks, size, put)
    source[blocks] = jnp.zeros((width, size), BF16)
    multiply_blocks(order, vals, source, total, False)
    for block in range(total.shape[0]):
        total[block] = target_scale[block:block + 1, :] * total[block]
    halves(total, keep, send)


def second_users(order, mine, other, source_scale, target_scale, vals, after,
                 half_grad, out, source, total):
    blocks, width, size = mine.shape
    for block in range(blocks):
        grad = mine[block] + other[block]
        half_grad[block] = 0.5 * grad
        source[block] = (source_scale[block:block + 1, :] * grad * 0.5).astype(BF16)
    source[blocks] = jnp.zeros((width, size), BF16)
    multiply_blocks(order, vals, source, total, True)
    for block in range(out.shape[0]):
        out[block] = target_scale[block:block + 1, :] * total[block]


def halves_after(total, after, keep, send):
    halves(total, keep, send)


def add_deal(offsets, keep, received, after, *outs):
    me = lax.axis_index("user")
    per = outs[0].shape[0]
    for out, offset in zip(outs, offsets):
        there = (me ^ offset) * per
        for block in range(per):
            out[block] = keep[there + block] + received[there + block]


def sum_parts(*refs):
    refs[-1][...] = add_all(refs[:-1])


def sum_after(after, *refs):
    sum_parts(*refs)


def pack(*refs):
    for place, ref in enumerate(refs[:-1]):
        refs[-1][place] = ref[...]


def finish(offsets, user_half_grad, user_mine, user_other, item_half_grad, item_mine, item_other,
           user_out, item_out):
    finish_users(user_half_grad, user_mine, user_other, user_out)
    finish_items(offsets, item_half_grad, item_mine, item_other, item_out)


def finish_users(half_grad, mine, other, out):
    me = lax.axis_index("rep")
    blocks, width, size = half_grad.shape
    half = width // 2
    for block in range(blocks):
        span = slice(block * size, (block + 1) * size)
        for rank, part in ((me, mine), (1 - me, other)):
            rows = pl.ds(pl.multiple_of(rank * half, half), half)
            out[rows, span] = half_grad[block, rows, :] + part[block]


def finish_items(offsets, half_grad, mine, other, out):
    me = lax.axis_index("rep")
    place = lax.axis_index("user")
    blocks, width, size = half_grad.shape
    half = width // 2
    per = blocks // len(offsets)
    for index, offset in enumerate(offsets):
        there = (place ^ offset) * per
        for block in range(per):
            span = pl.ds(pl.multiple_of((there + block) * size, size), size)
            for rank, part in ((me, mine), (1 - me, other)):
                rows = pl.ds(pl.multiple_of(rank * half, half), half)
                out[rows, span] = half_grad[there + block, rows, :] + part[index, block]


def swap(values, axis="rep", peers=2, offset=1):
    return lax.ppermute(values, axis, [(i, i ^ offset) for i in range(peers)])


def on_device(users, items, user_emb, item_emb, user_deg, item_deg, block_vals, block_row,
              block_col, block_count, trip_user, trip_pos, trip_neg):
    width = user_emb.shape[0]
    slots, size, _ = block_vals.shape
    user_blocks = user_emb.shape[1] // size
    item_blocks = item_emb.shape[1] // size
    trips = trip_user.shape[0]
    half = width // 2
    user_deg = user_deg.reshape(user_blocks, size)
    item_deg = item_deg.reshape(item_blocks, size)

    product_flops = 2 * slots * size * size * width
    product_bytes = slots * size * size * 2
    started = call(begin, shape(8, size), (), [], (), 16 * product_flops, product_bytes)
    ids = call(
        stack_ids, jax.ShapeDtypeStruct((ID_ROWS, trips), jnp.int32),
        [each.reshape(1, trips) for each in (trip_user, trip_pos, trip_neg)] + [started],
        [VMEM, VMEM, VMEM, ANY],
    )
    ids_user = [ids] + [swap(ids, "item", items, o) for o in range(1, items)]
    near = list(range(1, users))
    far = near[::-1]
    ids_item = [ids] + [swap(ids, "user", users, o) for o in far]
    lanes = -(-slots // size) * size

    order_shape = jax.ShapeDtypeStruct((2, lanes), jnp.int32)

    def source_shape(blocks):
        return jax.ShapeDtypeStruct((blocks + 1, width, size), BF16)

    (user_source, item_source, user_scale, item_scale, item_order, user_order) = call(
        prepare,
        [source_shape(user_blocks), source_shape(item_blocks), shape(user_blocks, size),
         shape(item_blocks, size), order_shape, order_shape],
        (block_count, block_row, block_col, user_emb, item_emb, user_deg, item_deg, ids),
        [SMEM, VMEM, VMEM, VMEM, VMEM, VMEM, VMEM, ANY],
        [pltpu.VMEM((8, lanes), jnp.int32)], product_flops, product_bytes,
    )
    item_table = call(
        functools.partial(first_pass, False), shape(item_blocks, width, size),
        (item_order, block_vals, user_source, ids), [SMEM, VMEM, VMEM, ANY], (),
        product_flops, product_bytes,
    )
    ids_here = [*ids_item[1:], *ids_user[1:]]
    user_table = call(
        functools.partial(first_pass, True), shape(user_blocks, width, size),
        (user_order, block_vals, item_source, item_table, *ids_here),
        [SMEM, VMEM, VMEM] + [ANY] * (1 + len(ids_here)), (),
        product_flops, product_bytes,
    )

    hot_flops = 2 * 3 * width * trips * size

    def reduced(rows, table, scale, peer_ids, axis, offsets, after):
        peers, blocks = len(peer_ids), scale.shape[0]
        dealt = call(
            functools.partial(gather, rows, peers), [shape(width, trips)] * peers,
            (table, swap(table), scale, after, *peer_ids), [VMEM] * 3 + [ANY] + [VMEM] * peers,
            [pltpu.VMEM((3 * width, blocks * size), BF16)],
            peers * blocks * hot_flops, 8 * blocks * width * size,
        )
        return [dealt[0]] + [swap(part, axis, peers, o) for part, o in zip(dealt[1:], offsets)]

    item_parts = reduced([1, 2], item_table, item_scale, ids_item, "user", far, ids)
    user_parts = reduced([0], user_table, user_scale, ids_user, "item", list(range(1, items)), item_parts[0])
    user_base, item_base = call(
        gather_base, [shape(width, trips)] * 2, (user_emb, item_emb, ids),
        [VMEM, VMEM, VMEM], (), 4 * width * trips * size * (user_blocks + item_blocks),
        2 * width * size * (user_blocks + item_blocks),
    )
    user_parts.append(user_base)
    item_parts.append(item_base)
    pieces, pushed = call(
        functools.partial(slopes, len(user_parts), len(item_parts)),
        [shape(width + 8, trips), shape(width, trips)],
        (ids, *user_parts, *item_parts), [VMEM] * (1 + len(user_parts) + len(item_parts)),
        moved=4 * width * trips * (len(user_parts) + len(item_parts) + 2),
    )

    arrays = [pieces, swap(pieces)]
    for offset in range(1, items):
        arrays.append(swap(pieces, "item", items, offset))
        arrays.append(lax.ppermute(pieces, ("item", "rep"), [
            (i, i ^ (2 * offset + 1)) for i in range(2 * items)]))
    user_half_grad, item_keep, item_send = call(
        functools.partial(second_items, len(arrays)),
        [shape(user_blocks, width, size)] + [shape(item_blocks, half, size)] * 2,
        (item_order, user_scale, item_scale, block_vals, *arrays),
        [SMEM] + [VMEM] * (3 + len(arrays)),
        [pltpu.VMEM((user_blocks + 1, width, size), BF16),
         pltpu.VMEM((item_blocks, width, size), F32),
         pltpu.VMEM((len(arrays), 3 * width, trips), BF16)],
        product_flops, product_bytes,
    )
    arrays = [pushed] + [swap(pushed, "user", users, o) for o in near]
    item_grad = call(
        functools.partial(scatter_items, users), shape(item_blocks, width, size),
        (item_send, *arrays, ids, *ids_item[:0:-1]), [ANY] + [VMEM] * (2 * users),
        [pltpu.VMEM((users, 3 * width, trips), BF16)], HEAVY, 0,
    )

    per = item_blocks // users
    dealt = call(
        functools.partial(add_deal, [0, *far]), [shape(per, half, size)] * users,
        (item_keep, swap(item_send), item_grad), [VMEM, VMEM, ANY], (), HEAVY,
    )
    item_half_grad, user_back = call(
        second_users, [shape(item_blocks, width, size), shape(user_blocks, width, size)],
        (user_order, item_grad, swap(item_grad), item_scale, user_scale, block_vals, dealt[0]),
        [SMEM] + [VMEM] * 5 + [ANY],
        [pltpu.VMEM((item_blocks + 1, width, size), BF16),
         pltpu.VMEM((user_blocks, width, size), F32)],
        product_flops, product_bytes,
    )
    parts = [dealt[0]] + [swap(part, "user", users, o) for part, o in zip(dealt[1:], far)]
    item_own = call(sum_after, shape(per, half, size), (user_back, *parts),
                    [ANY] + [VMEM] * users,
               moved=4 * (users + 1) * per * half * size)
    item_mine = call(pack, shape(users, per, half, size),
                     (item_own, *[swap(item_own, "user", users, o) for o in near]),
                     [VMEM] * users, (), HEAVY)
    item_other = swap(item_mine)

    user_keep, user_send = call(
        halves_after, [shape(user_blocks, half, size)] * 2, (user_back, item_own), [VMEM, ANY],
        moved=8 * user_blocks * width * size,
    )
    own = call(sum_parts, shape(user_blocks, half, size), (user_keep, swap(user_send)),
               [VMEM, VMEM], moved=12 * user_blocks * half * size)
    mine = call(sum_parts, shape(user_blocks, half, size),
                (own, *[swap(own, "item", items, o) for o in range(1, items)]),
                [VMEM] * items, moved=12 * user_blocks * half * size)
    return call(
        functools.partial(finish, [0, *near]),
        (shape(width, user_blocks * size), shape(width, item_blocks * size)),
        (user_half_grad, mine, swap(mine), item_half_grad, item_mine, item_other),
        [VMEM] * 6, moved=12 * (user_blocks + item_blocks) * width * size,
    )


def solution(mesh):
    return jax.shard_map(
        functools.partial(on_device, mesh.shape["user"], mesh.shape["item"]),
        mesh=mesh,
        in_specs=(
            P(None, ("groups", "user")),
            P(None, ("groups", "item")),
            P(("groups", "user")),
            P(("groups", "item")),
            P(("groups", "user", "item", "rep"), None, None),
            P(("groups", "user", "item", "rep")),
            P(("groups", "user", "item", "rep")),
            P(("groups", "user", "item", "rep")),
            P(("groups", "user", "item", "rep")),
            P(("groups", "user", "item", "rep")),
            P(("groups", "user", "item", "rep")),
        ),
        out_specs=(P(None, ("groups", "user")), P(None, ("groups", "item"))),
        check_vma=False,
    )
```

```python
import functools

import jax
import jax.numpy as jnp
from jax import lax
from jax.experimental import pallas as pl
from jax.experimental.pallas import tpu as pltpu
from jax.sharding import PartitionSpec as P

F32 = jnp.float32
BF16 = jnp.bfloat16
PACK = 4
GROUP = 4
ID_ROWS = 64
HEAVY = 10 ** 11

VMEM = pl.BlockSpec(memory_space=pltpu.VMEM)
SMEM = pl.BlockSpec(memory_space=pltpu.SMEM)
ANY = pl.BlockSpec(memory_space=pl.ANY)
HBM = pl.BlockSpec(memory_space=pltpu.HBM)


def call(kernel, outs, ins, specs, scratch=(), flops=0, moved=0, room=16):
    return pl.pallas_call(
        kernel,
        out_shape=outs,
        in_specs=specs,
        out_specs=jax.tree.map(lambda _: VMEM, outs),
        scratch_shapes=list(scratch),
        cost_estimate=pl.CostEstimate(flops=flops, bytes_accessed=moved, transcendentals=0),
        compiler_params=pltpu.CompilerParams(vmem_limit_bytes=room * 1024 * 1024),
    )(*ins)


def shape(*dims):
    return jax.ShapeDtypeStruct(dims, F32)


def split3(values):
    high = values.astype(BF16)
    rest = values - high.astype(F32)
    middle = rest.astype(BF16)
    low = (rest - middle.astype(F32)).astype(BF16)
    return high, middle, low


def hot(ids, start, tile):
    if len(ids) == 2:
        same = ids[0] == ids[1]
        ids = [jnp.where(same, -1, each) for each in ids]
    ids = [each.astype(jnp.int16) for each in ids]
    place = lax.broadcasted_iota(jnp.int16, (tile, ids[0].shape[1]), 0) + jnp.int16(start)
    chosen = jnp.zeros(place.shape, BF16)
    for each, sign in zip(ids, (1, -1)):
        chosen = jnp.where(place == each, jnp.asarray(sign, BF16), chosen)
    return chosen


def sort_slots(keys, sources, count, blocks):
    lanes = keys.shape[1]
    rows = 2 * blocks
    place = lax.broadcasted_iota(jnp.int32, (1, lanes), 1)
    live = place < count
    mine = (lax.broadcasted_iota(jnp.int32, (rows, lanes), 0) == keys) & live
    mine = jnp.where(mine, 1.0, 0.0)
    earlier = lax.broadcasted_iota(jnp.int32, (lanes, lanes), 0) < lax.broadcasted_iota(
        jnp.int32, (lanes, lanes), 1)
    before = jnp.dot(mine.astype(BF16), jnp.where(earlier, 1.0, 0.0).astype(BF16),
                     preferred_element_type=F32)
    packs = jnp.floor((jnp.sum(mine, axis=1, keepdims=True) + (PACK - 1)) * (1.0 / PACK))
    packs = jnp.broadcast_to(packs, (rows, 128))
    lower = lax.broadcasted_iota(jnp.int32, (rows, rows), 1) < lax.broadcasted_iota(
        jnp.int32, (rows, rows), 0)
    first = jnp.dot(jnp.where(lower, 1.0, 0.0).astype(BF16), packs.astype(BF16),
                    preferred_element_type=F32)
    position = jnp.sum(mine * (first[:, :1] * PACK + before), axis=0, keepdims=True)
    position = jnp.where(live, position.astype(jnp.int32), -1)
    match = lax.broadcasted_iota(jnp.int32, (lanes, lanes), 0) == position
    row = lax.broadcasted_iota(jnp.int32, (16, lanes), 0)
    values = jnp.where(row == 0, place // 16, jnp.where(row == 1, place % 16, jnp.where(
        row == 2, sources, jnp.where(row == 3, keys, jnp.where(row == 4, 1, 0)))))
    values = jnp.where(live, values, 0).astype(F32)
    found = lax.dot_general(values.astype(BF16), jnp.where(match, 1.0, 0.0).astype(BF16),
                            (((1,), (1,)), ((), ())), preferred_element_type=F32)
    found = found.astype(jnp.int32)
    valid = found[4:5] > 0
    total = jnp.broadcast_to(jnp.sum(packs[:, :1], axis=0, keepdims=True), (1, lanes))
    row = lax.broadcasted_iota(jnp.int32, (4, lanes), 0)
    slot = found[0:1] * 16 + found[1:2]
    source = jnp.where(valid, found[2:3], blocks)
    target = jnp.where(valid, found[3:4], 0)
    return jnp.where(row == 0, slot, jnp.where(row == 1, source, jnp.where(
        row == 2, target, total.astype(jnp.int32))))


def multiply_blocks(order, vals, source, total, across):
    _, width, size = source.shape
    total[...] = jnp.zeros_like(total)
    contract = (((1,), (1,)), ((), ())) if across else (((1,), (0,)), ((), ()))

    def group(index, _):
        targets, terms = [], []
        for step in range(GROUP):
            left, right = [], []
            for half in range(2):
                first = ((index * GROUP + step) * 2 + half) * PACK
                places = [first + each for each in range(PACK)]
                left.append(jnp.concatenate([source[order[1, each]] for each in places], axis=1))
                right.append(jnp.concatenate([vals[order[0, each]] for each in places],
                                             axis=1 if across else 0))
                targets.append(order[2, first])
            both = lax.dot_general(
                jnp.concatenate(left, axis=0), jnp.concatenate(right, axis=0 if across else 1),
                contract, preferred_element_type=F32,
            )
            terms += [both[:width, :size], both[width:, size:]]
        for target, term in zip(targets, terms):
            total[target] += term
        return 0

    lax.fori_loop(0, (order[3, 0] + 2 * GROUP - 1) // (2 * GROUP), group, 0)


def begin(out):
    out[...] = jnp.zeros_like(out)


def stack_ids(user, positive, negative, after, out):
    out[...] = jnp.zeros_like(out)
    for row, ids in enumerate((user, positive, negative)):
        out[row:row + 1, :] = ids[...]


def prepare(count, rows, columns, user_emb, item_emb, user_deg, item_deg, after,
            user_source, item_source, user_scale, item_scale, item_order, user_order, keys):
    live = count[0]
    slots = rows.shape[0]
    keys[...] = jnp.zeros_like(keys)
    keys[0:1, 0:slots] = rows[...].reshape(1, slots)
    keys[1:2, 0:slots] = columns[...].reshape(1, slots)
    users, items = keys[0:1, :], keys[1:2, :]
    item_order[...] = sort_slots(items, users, live, item_scale.shape[0])
    user_order[...] = sort_slots(users, items, live, user_scale.shape[0])
    for emb, deg, scale, into in ((user_emb, user_deg, user_scale, user_source),
                                  (item_emb, item_deg, item_scale, item_source)):
        scale[...] = lax.rsqrt(deg[...].astype(F32))
        blocks, size = scale.shape
        for block in range(blocks):
            piece = emb[:, block * size:(block + 1) * size].astype(F32)
            into[block] = (scale[block:block + 1, :] * piece).astype(BF16)
        into[blocks] = jnp.zeros(into.shape[1:], BF16)


def first_pass(across, order, vals, source, *refs):
    multiply_blocks(order, vals, source, refs[-1], across)


def fold(stacked, width):
    return (
        stacked[:width] + stacked[width:2 * width] + stacked[2 * width:3 * width]
    )


def rows_of(ref, rows):
    return [ref[row:row + 1, :] for row in rows]


def pick(table, ids, tile):
    total = None
    for start in range(0, table.shape[1], tile):
        term = jnp.dot(
            table[:, start:start + tile], hot(ids, start, tile),
            preferred_element_type=F32,
        )
        total = term if total is None else total + term
    return total


def gather(rows, peers, mine, other, scale, after, *refs):
    ids, outs, table = refs[:peers], refs[peers:2 * peers], refs[2 * peers]
    blocks, width, size = mine.shape
    for block in range(blocks):
        span = slice(block * size, (block + 1) * size)
        here = scale[block:block + 1, :] * (mine[block] + other[block])
        for part, piece in enumerate(split3(here)):
            table[part * width:(part + 1) * width, span] = piece
    for peer in range(peers):
        outs[peer][...] = fold(pick(table, rows_of(ids[peer], rows), 2 * size), width)


def scatter(pieces, ids, table, blocks, size, put):
    width = table.shape[1] // 3
    tile = 2 * size
    for place, piece in enumerate(pieces):
        for part, value in enumerate(split3(piece[:width, :])):
            table[place, part * width:(part + 1) * width, :] = value
    for start in range(0, blocks * size, tile):
        total = None
        for place, rows in enumerate(ids):
            term = lax.dot_general(
                table[place], hot(rows, start, tile), (((1,), (1,)), ((), ())),
                preferred_element_type=F32,
            )
            total = term if total is None else total + term
        total = fold(total, width)
        for offset in range(0, tile, size):
            put((start + offset) // size, total[:, offset:offset + size])


def scatter_items(peers, after, *refs):
    pieces, ids, out, table = refs[:peers], refs[peers:2 * peers], refs[2 * peers], refs[-1]
    blocks, _, size = out.shape

    def put(block, value):
        out[block] = value

    scatter(pieces, [rows_of(ref, [1, 2]) for ref in ids], table, blocks, size, put)


def gather_base(user_emb, item_emb, ids, user_out, item_out):
    tile = ids.shape[1]
    user_out[...] = pick(user_emb, rows_of(ids, [0]), tile)
    item_out[...] = pick(item_emb, rows_of(ids, [1, 2]), tile)


def add_all(refs):
    total = refs[0][...]
    for ref in refs[1:]:
        total = total + ref[...]
    return total


def slopes(user_parts, item_parts, ids, *refs):
    users, items = refs[:user_parts], refs[user_parts:user_parts + item_parts]
    pieces, pushed = refs[user_parts + item_parts:]
    width = pushed.shape[0]
    user_rows = 0.5 * add_all(users)
    difference = 0.5 * add_all(items)
    margin = jnp.sum(user_rows * difference, axis=0, keepdims=True)
    slope = -jax.nn.sigmoid(-margin)
    pieces[:width, :] = slope * difference
    pieces[width:, :] = jnp.broadcast_to(ids[0:1, :].astype(F32), (8, ids.shape[1]))
    pushed[...] = slope * user_rows


def second_items(parts, order, source_scale, target_scale, vals, *refs):
    pieces = refs[:parts]
    half_grad, out, source, total, table = refs[parts:]
    blocks, width, size = half_grad.shape

    def put(block, grad):
        half_grad[block] = 0.5 * grad
        source[block] = (source_scale[block:block + 1, :] * grad * 0.5).astype(BF16)

    ids = [[piece[width:width + 1, :].astype(jnp.int32)] for piece in pieces]
    scatter(pieces, ids, table, blocks, size, put)
    source[blocks] = jnp.zeros((width, size), BF16)
    multiply_blocks(order, vals, source, total, False)
    for block in range(out.shape[0]):
        out[block] = target_scale[block:block + 1, :] * total[block]


def second_users(order, mine, other, source_scale, target_scale, vals, after,
                 half_grad, out, source, total):
    blocks, width, size = mine.shape
    for block in range(blocks):
        grad = mine[block] + other[block]
        half_grad[block] = 0.5 * grad
        source[block] = (source_scale[block:block + 1, :] * grad * 0.5).astype(BF16)
    source[blocks] = jnp.zeros((width, size), BF16)
    multiply_blocks(order, vals, source, total, True)
    for block in range(out.shape[0]):
        out[block] = target_scale[block:block + 1, :] * total[block]


def add_deal(offsets, keep, received, after, *outs):
    me = lax.axis_index("user")
    per = outs[0].shape[0]
    for out, offset in zip(outs, offsets):
        there = (me ^ offset) * per
        for block in range(per):
            out[block] = keep[there + block] + received[there + block]


def sum_parts(*refs):
    refs[-1][...] = add_all(refs[:-1])


def sum_after(after, *refs):
    sum_parts(*refs)


def pack(*refs):
    for place, ref in enumerate(refs[:-1]):
        refs[-1][place] = ref[...]


def finish(offsets, user_half_grad, user_mine, user_other, item_half_grad, item_mine, item_other,
           user_out, item_out):
    me = lax.axis_index("rep")

    @pl.when(me == 0)
    def _():
        finish_users(user_half_grad, user_other, user_out)
        finish_items(offsets, item_half_grad, item_mine, item_out)

    @pl.when(me != 0)
    def _():
        finish_users(user_half_grad, user_mine, user_out)
        finish_items(offsets, item_half_grad, item_other, item_out)


def finish_users(half_grad, part, out):
    blocks, _, size = half_grad.shape
    for block in range(blocks):
        out[:, block * size:(block + 1) * size] = half_grad[block] + part[block]


def finish_items(offsets, half_grad, part, out):
    place = lax.axis_index("user")
    blocks, _, size = half_grad.shape
    per = blocks // len(offsets)
    for index, offset in enumerate(offsets):
        there = (place ^ offset) * per
        for block in range(per):
            span = pl.ds(pl.multiple_of((there + block) * size, size), size)
            out[:, span] = half_grad[there + block] + part[index, block]


def swap(values, axis="rep", peers=2, offset=1):
    return lax.ppermute(values, axis, [(i, i ^ offset) for i in range(peers)])


def send_core(values, source):
    return lax.ppermute(values, "rep", [(source, 1 - source)])


def swap_core(values, axis, peers, offset, core):
    return lax.ppermute(values, (axis, "rep"), [
        (2 * i + core, 2 * (i ^ offset) + core) for i in range(peers)])


def on_device(users, items, user_emb, item_emb, user_deg, item_deg, block_vals, block_row,
              block_col, block_count, trip_user, trip_pos, trip_neg):
    width = user_emb.shape[0]
    slots, size, _ = block_vals.shape
    user_blocks = user_emb.shape[1] // size
    item_blocks = item_emb.shape[1] // size
    trips = trip_user.shape[0]
    user_deg = user_deg.reshape(user_blocks, size)
    item_deg = item_deg.reshape(item_blocks, size)

    product_flops = 2 * slots * size * size * width
    product_bytes = slots * size * size * 2
    started = call(begin, shape(8, size), (), [], (), 16 * product_flops, product_bytes)
    ids = call(
        stack_ids, jax.ShapeDtypeStruct((ID_ROWS, trips), jnp.int32),
        [each.reshape(1, trips) for each in (trip_user, trip_pos, trip_neg)] + [started],
        [VMEM, VMEM, VMEM, ANY],
    )
    ids_user = [ids] + [swap(ids, "item", items, o) for o in range(1, items)]
    near = list(range(1, users))
    far = near[::-1]
    ids_item = [ids] + [swap(ids, "user", users, o) for o in far]
    lanes = -(-slots // size) * size

    order_shape = jax.ShapeDtypeStruct((4, lanes), jnp.int32)

    def source_shape(blocks):
        return jax.ShapeDtypeStruct((blocks + 1, width, size), BF16)

    (user_source, item_source, user_scale, item_scale, item_order, user_order) = call(
        prepare,
        [source_shape(user_blocks), source_shape(item_blocks), shape(user_blocks, size),
         shape(item_blocks, size), order_shape, order_shape],
        (block_count, block_row, block_col, user_emb, item_emb, user_deg, item_deg, ids),
        [SMEM, VMEM, VMEM, VMEM, VMEM, VMEM, VMEM, ANY],
        [pltpu.VMEM((8, lanes), jnp.int32)], product_flops, product_bytes,
    )
    item_table = call(
        functools.partial(first_pass, False), shape(item_blocks, width, size),
        (item_order, block_vals, user_source, ids), [SMEM, VMEM, VMEM, ANY], (),
        product_flops, product_bytes,
    )
    ids_here = [*ids_item[1:], *ids_user[1:]]
    user_table = call(
        functools.partial(first_pass, True), shape(user_blocks, width, size),
        (user_order, block_vals, item_source, item_table, *ids_here),
        [SMEM, VMEM, VMEM] + [ANY] * (1 + len(ids_here)), (),
        product_flops, product_bytes,
    )

    hot_flops = 2 * 3 * width * trips * size

    def reduced(rows, table, scale, peer_ids, axis, offsets, after):
        peers, blocks = len(peer_ids), scale.shape[0]
        dealt = call(
            functools.partial(gather, rows, peers), [shape(width, trips)] * peers,
            (table, swap(table), scale, after, *peer_ids), [VMEM] * 3 + [ANY] + [VMEM] * peers,
            [pltpu.VMEM((3 * width, blocks * size), BF16)],
            peers * blocks * hot_flops, 8 * blocks * width * size,
        )
        return [dealt[0]] + [swap(part, axis, peers, o) for part, o in zip(dealt[1:], offsets)]

    item_parts = reduced([1, 2], item_table, item_scale, ids_item, "user", far, ids)
    user_parts = reduced([0], user_table, user_scale, ids_user, "item", list(range(1, items)), item_parts[0])
    user_base, item_base = call(
        gather_base, [shape(width, trips)] * 2, (user_emb, item_emb, ids),
        [VMEM, VMEM, VMEM], (), 4 * width * trips * size * (user_blocks + item_blocks),
        2 * width * size * (user_blocks + item_blocks),
    )
    user_parts.append(user_base)
    item_parts.append(item_base)
    pieces, pushed = call(
        functools.partial(slopes, len(user_parts), len(item_parts)),
        [shape(width + 8, trips), shape(width, trips)],
        (ids, *user_parts, *item_parts), [VMEM] * (1 + len(user_parts) + len(item_parts)),
        moved=4 * width * trips * (len(user_parts) + len(item_parts) + 2),
    )

    arrays = [pieces, swap(pieces)]
    for offset in range(1, items):
        arrays.append(swap(pieces, "item", items, offset))
        arrays.append(lax.ppermute(pieces, ("item", "rep"), [
            (i, i ^ (2 * offset + 1)) for i in range(2 * items)]))
    user_half_grad, item_back = call(
        functools.partial(second_items, len(arrays)),
        [shape(user_blocks, width, size), shape(item_blocks, width, size)],
        (item_order, user_scale, item_scale, block_vals, *arrays),
        [SMEM] + [VMEM] * (3 + len(arrays)),
        [pltpu.VMEM((user_blocks + 1, width, size), BF16),
         pltpu.VMEM((item_blocks, width, size), F32),
         pltpu.VMEM((len(arrays), 3 * width, trips), BF16)],
        product_flops, product_bytes,
    )
    arrays = [pushed] + [swap(pushed, "user", users, o) for o in near]
    item_grad = call(
        functools.partial(scatter_items, users), shape(item_blocks, width, size),
        (item_back, *arrays, ids, *ids_item[:0:-1]), [ANY] + [VMEM] * (2 * users),
        [pltpu.VMEM((users, 3 * width, trips), BF16)], HEAVY, 0,
    )

    per = item_blocks // users
    dealt = call(
        functools.partial(add_deal, [0, *far]), [shape(per, width, size)] * users,
        (item_back, send_core(item_back, 1), item_grad), [VMEM, VMEM, ANY], (), HEAVY,
    )
    item_half_grad, user_back = call(
        second_users, [shape(item_blocks, width, size), shape(user_blocks, width, size)],
        (user_order, item_grad, swap(item_grad), item_scale, user_scale, block_vals, dealt[0]),
        [SMEM] + [VMEM] * 5 + [ANY],
        [pltpu.VMEM((item_blocks + 1, width, size), BF16),
         pltpu.VMEM((user_blocks, width, size), F32)],
        product_flops, product_bytes,
    )
    parts = [dealt[0]] + [
        swap_core(part, "user", users, o, 0) for part, o in zip(dealt[1:], far)]
    item_own = call(sum_after, shape(per, width, size), (user_back, *parts),
                    [ANY] + [VMEM] * users, (), HEAVY)
    item_mine = call(
        pack, shape(users, per, width, size),
        (item_own, *[swap_core(item_own, "user", users, o, 0) for o in near]),
        [VMEM] * users, (), HEAVY)
    user_own = call(sum_after, shape(user_blocks, width, size),
                    (item_own, user_back, send_core(user_back, 0)), [ANY, VMEM, VMEM],
                    moved=12 * user_blocks * width * size)
    user_mine = call(
        sum_parts, shape(user_blocks, width, size),
        (user_own, *[swap_core(user_own, "item", items, o, 1) for o in range(1, items)]),
        [VMEM] * items, moved=12 * user_blocks * width * size)
    return call(
        functools.partial(finish, [0, *near]),
        (shape(width, user_blocks * size), shape(width, item_blocks * size)),
        (user_half_grad, user_mine, send_core(user_mine, 1),
         item_half_grad, item_mine, send_core(item_mine, 0)),
        [VMEM] * 6, moved=12 * (user_blocks + item_blocks) * width * size,
    )


def solution(mesh):
    return jax.shard_map(
        functools.partial(on_device, mesh.shape["user"], mesh.shape["item"]),
        mesh=mesh,
        in_specs=(
            P(None, ("groups", "user")),
            P(None, ("groups", "item")),
            P(("groups", "user")),
            P(("groups", "item")),
            P(("groups", "user", "item", "rep"), None, None),
            P(("groups", "user", "item", "rep")),
            P(("groups", "user", "item", "rep")),
            P(("groups", "user", "item", "rep")),
            P(("groups", "user", "item", "rep")),
            P(("groups", "user", "item", "rep")),
            P(("groups", "user", "item", "rep")),
        ),
        out_specs=(P(None, ("groups", "user")), P(None, ("groups", "item"))),
        check_vma=False,
    )
```

```python
import functools

import jax
import jax.numpy as jnp
from jax import lax
from jax.experimental import pallas as pl
from jax.experimental.pallas import tpu as pltpu
from jax.sharding import PartitionSpec as P

F32 = jnp.float32
BF16 = jnp.bfloat16
PACK = 4
GROUP = 4
ID_ROWS = 64
HEAVY = 10 ** 11

VMEM = pl.BlockSpec(memory_space=pltpu.VMEM)
SMEM = pl.BlockSpec(memory_space=pltpu.SMEM)
ANY = pl.BlockSpec(memory_space=pl.ANY)
HBM = pl.BlockSpec(memory_space=pltpu.HBM)


def call(kernel, outs, ins, specs, scratch=(), flops=0, moved=0, room=16):
    return pl.pallas_call(
        kernel,
        out_shape=outs,
        in_specs=specs,
        out_specs=jax.tree.map(lambda _: VMEM, outs),
        scratch_shapes=list(scratch),
        cost_estimate=pl.CostEstimate(flops=flops, bytes_accessed=moved, transcendentals=0),
        compiler_params=pltpu.CompilerParams(vmem_limit_bytes=room * 1024 * 1024),
    )(*ins)


def shape(*dims):
    return jax.ShapeDtypeStruct(dims, F32)


def split3(values):
    high = values.astype(BF16)
    rest = values - high.astype(F32)
    middle = rest.astype(BF16)
    low = (rest - middle.astype(F32)).astype(BF16)
    return high, middle, low


def hot(ids, start, tile):
    if len(ids) == 2:
        same = ids[0] == ids[1]
        ids = [jnp.where(same, -1, each) for each in ids]
    ids = [each.astype(jnp.int16) for each in ids]
    place = lax.broadcasted_iota(jnp.int16, (tile, ids[0].shape[1]), 0) + jnp.int16(start)
    chosen = jnp.zeros(place.shape, BF16)
    for each, sign in zip(ids, (1, -1)):
        chosen = jnp.where(place == each, jnp.asarray(sign, BF16), chosen)
    return chosen


def sort_slots(keys, sources, count, blocks):
    lanes = keys.shape[1]
    rows = 2 * blocks
    place = lax.broadcasted_iota(jnp.int32, (1, lanes), 1)
    live = place < count
    mine = (lax.broadcasted_iota(jnp.int32, (rows, lanes), 0) == keys) & live
    mine = jnp.where(mine, 1.0, 0.0)
    earlier = lax.broadcasted_iota(jnp.int32, (lanes, lanes), 0) < lax.broadcasted_iota(
        jnp.int32, (lanes, lanes), 1)
    before = jnp.dot(mine.astype(BF16), jnp.where(earlier, 1.0, 0.0).astype(BF16),
                     preferred_element_type=F32)
    packs = jnp.floor((jnp.sum(mine, axis=1, keepdims=True) + (PACK - 1)) * (1.0 / PACK))
    packs = jnp.broadcast_to(packs, (rows, 128))
    lower = lax.broadcasted_iota(jnp.int32, (rows, rows), 1) < lax.broadcasted_iota(
        jnp.int32, (rows, rows), 0)
    first = jnp.dot(jnp.where(lower, 1.0, 0.0).astype(BF16), packs.astype(BF16),
                    preferred_element_type=F32)
    position = jnp.sum(mine * (first[:, :1] * PACK + before), axis=0, keepdims=True)
    position = jnp.where(live, position.astype(jnp.int32), -1)
    match = lax.broadcasted_iota(jnp.int32, (lanes, lanes), 0) == position
    row = lax.broadcasted_iota(jnp.int32, (16, lanes), 0)
    values = jnp.where(row == 0, place // 16, jnp.where(row == 1, place % 16, jnp.where(
        row == 2, sources, jnp.where(row == 3, keys, jnp.where(row == 4, 1, 0)))))
    values = jnp.where(live, values, 0).astype(F32)
    found = lax.dot_general(values.astype(BF16), jnp.where(match, 1.0, 0.0).astype(BF16),
                            (((1,), (1,)), ((), ())), preferred_element_type=F32)
    found = found.astype(jnp.int32)
    valid = found[4:5] > 0
    total = jnp.broadcast_to(jnp.sum(packs[:, :1], axis=0, keepdims=True), (1, lanes))
    row = lax.broadcasted_iota(jnp.int32, (4, lanes), 0)
    slot = found[0:1] * 16 + found[1:2]
    source = jnp.where(valid, found[2:3], blocks)
    target = jnp.where(valid, found[3:4], 0)
    return jnp.where(row == 0, slot, jnp.where(row == 1, source, jnp.where(
        row == 2, target, total.astype(jnp.int32))))


def multiply_blocks(order, vals, source, total, across):
    _, width, size = source.shape
    total[...] = jnp.zeros_like(total)
    contract = (((1,), (1,)), ((), ())) if across else (((1,), (0,)), ((), ()))

    def group(index, _):
        targets, terms = [], []
        for step in range(GROUP):
            left, right = [], []
            for half in range(2):
                first = ((index * GROUP + step) * 2 + half) * PACK
                places = [first + each for each in range(PACK)]
                left.append(jnp.concatenate([source[order[1, each]] for each in places], axis=1))
                right.append(jnp.concatenate([vals[order[0, each]] for each in places],
                                             axis=1 if across else 0))
                targets.append(order[2, first])
            both = lax.dot_general(
                jnp.concatenate(left, axis=0), jnp.concatenate(right, axis=0 if across else 1),
                contract, preferred_element_type=F32,
            )
            terms += [both[:width, :size], both[width:, size:]]
        for target, term in zip(targets, terms):
            total[target] += term
        return 0

    lax.fori_loop(0, (order[3, 0] + 2 * GROUP - 1) // (2 * GROUP), group, 0)


def begin(out):
    out[...] = jnp.zeros_like(out)


def stack_ids(user, positive, negative, after, out):
    out[...] = jnp.zeros_like(out)
    for row, ids in enumerate((user, positive, negative)):
        out[row:row + 1, :] = ids[...]


def prepare(count, rows, columns, user_emb, item_emb, user_deg, item_deg, after,
            user_source, item_source, user_scale, item_scale, item_order, user_order, keys):
    live = count[0]
    slots = rows.shape[0]
    keys[...] = jnp.zeros_like(keys)
    keys[0:1, 0:slots] = rows[...].reshape(1, slots)
    keys[1:2, 0:slots] = columns[...].reshape(1, slots)
    users, items = keys[0:1, :], keys[1:2, :]
    item_order[...] = sort_slots(items, users, live, item_scale.shape[0])
    user_order[...] = sort_slots(users, items, live, user_scale.shape[0])
    for emb, deg, scale, into in ((user_emb, user_deg, user_scale, user_source),
                                  (item_emb, item_deg, item_scale, item_source)):
        scale[...] = lax.rsqrt(deg[...].astype(F32))
        blocks, size = scale.shape
        for block in range(blocks):
            piece = emb[:, block * size:(block + 1) * size].astype(F32)
            into[block] = (scale[block:block + 1, :] * piece).astype(BF16)
        into[blocks] = jnp.zeros(into.shape[1:], BF16)


def first_pass(across, order, vals, source, *refs):
    multiply_blocks(order, vals, source, refs[-1], across)


def fold(stacked, width):
    return (
        stacked[:width] + stacked[width:2 * width] + stacked[2 * width:3 * width]
    )


def rows_of(ref, rows):
    return [ref[row:row + 1, :] for row in rows]


def pick(table, ids, tile):
    total = None
    for start in range(0, table.shape[1], tile):
        term = jnp.dot(
            table[:, start:start + tile], hot(ids, start, tile),
            preferred_element_type=F32,
        )
        total = term if total is None else total + term
    return total


def gather(rows, peers, mine, other, scale, after, *refs):
    ids, outs, table = refs[:peers], refs[peers:2 * peers], refs[2 * peers]
    blocks, width, size = mine.shape
    for block in range(blocks):
        span = slice(block * size, (block + 1) * size)
        here = scale[block:block + 1, :] * (mine[block] + other[block])
        for part, piece in enumerate(split3(here)):
            table[part * width:(part + 1) * width, span] = piece
    for peer in range(peers):
        outs[peer][...] = fold(pick(table, rows_of(ids[peer], rows), 2 * size), width)


def scatter(pieces, ids, table, blocks, size, put):
    width = table.shape[1] // 3
    tile = 2 * size
    for place, piece in enumerate(pieces):
        for part, value in enumerate(split3(piece[:width, :])):
            table[place, part * width:(part + 1) * width, :] = value
    for start in range(0, blocks * size, tile):
        total = None
        for place, rows in enumerate(ids):
            term = lax.dot_general(
                table[place], hot(rows, start, tile), (((1,), (1,)), ((), ())),
                preferred_element_type=F32,
            )
            total = term if total is None else total + term
        total = fold(total, width)
        for offset in range(0, tile, size):
            put((start + offset) // size, total[:, offset:offset + size])


def scatter_items(peers, after, *refs):
    pieces, ids, out, table = refs[:peers], refs[peers:2 * peers], refs[2 * peers], refs[-1]
    blocks, _, size = out.shape

    def put(block, value):
        out[block] = value

    scatter(pieces, [rows_of(ref, [1, 2]) for ref in ids], table, blocks, size, put)


def gather_base(user_emb, item_emb, ids, user_out, item_out):
    tile = ids.shape[1]
    user_out[...] = pick(user_emb, rows_of(ids, [0]), tile)
    item_out[...] = pick(item_emb, rows_of(ids, [1, 2]), tile)


def add_all(refs):
    total = refs[0][...]
    for ref in refs[1:]:
        total = total + ref[...]
    return total


def slopes(user_parts, item_parts, ids, *refs):
    users, items = refs[:user_parts], refs[user_parts:user_parts + item_parts]
    pieces, pushed = refs[user_parts + item_parts:]
    width = pushed.shape[0]
    user_rows = 0.5 * add_all(users)
    difference = 0.5 * add_all(items)
    margin = jnp.sum(user_rows * difference, axis=0, keepdims=True)
    slope = -jax.nn.sigmoid(-margin)
    pieces[:width, :] = slope * difference
    pieces[width:, :] = jnp.broadcast_to(ids[0:1, :].astype(F32), (8, ids.shape[1]))
    pushed[...] = slope * user_rows


def halves(total, keep, send):
    me = lax.axis_index("rep")
    half = keep.shape[1]
    for block in range(keep.shape[0]):
        keep[block] = total[block, pl.ds(pl.multiple_of(me * half, half), half), :]
        send[block] = total[block, pl.ds(pl.multiple_of((1 - me) * half, half), half), :]


def second_items(parts, order, source_scale, target_scale, vals, *refs):
    pieces = refs[:parts]
    half_grad, keep, send, source, total, table = refs[parts:]
    blocks, width, size = half_grad.shape

    def put(block, grad):
        half_grad[block] = 0.5 * grad
        source[block] = (source_scale[block:block + 1, :] * grad * 0.5).astype(BF16)

    ids = [[piece[width:width + 1, :].astype(jnp.int32)] for piece in pieces]
    scatter(pieces, ids, table, blocks, size, put)
    source[blocks] = jnp.zeros((width, size), BF16)
    multiply_blocks(order, vals, source, total, False)
    for block in range(total.shape[0]):
        total[block] = target_scale[block:block + 1, :] * total[block]
    halves(total, keep, send)


def second_users(order, mine, other, source_scale, target_scale, vals, after,
                 half_grad, out, source, total):
    blocks, width, size = mine.shape
    for block in range(blocks):
        grad = mine[block] + other[block]
        half_grad[block] = 0.5 * grad
        source[block] = (source_scale[block:block + 1, :] * grad * 0.5).astype(BF16)
    source[blocks] = jnp.zeros((width, size), BF16)
    multiply_blocks(order, vals, source, total, True)
    for block in range(out.shape[0]):
        out[block] = target_scale[block:block + 1, :] * total[block]


def halves_after(total, after, keep, send):
    halves(total, keep, send)


def add_deal(offsets, keep, received, after, *outs):
    me = lax.axis_index("user")
    per = outs[0].shape[0]
    for out, offset in zip(outs, offsets):
        there = (me ^ offset) * per
        for block in range(per):
            out[block] = keep[there + block] + received[there + block]


def sum_parts(*refs):
    refs[-1][...] = add_all(refs[:-1])


def sum_after(after, *refs):
    sum_parts(*refs)


def pack(*refs):
    for place, ref in enumerate(refs[:-1]):
        refs[-1][place] = ref[...]


def finish(offsets, user_half_grad, user_mine, user_other, item_half_grad, item_mine, item_other,
           user_out, item_out):
    finish_users(user_half_grad, user_mine, user_other, user_out)
    finish_items(offsets, item_half_grad, item_mine, item_other, item_out)


def finish_users(half_grad, mine, other, out):
    me = lax.axis_index("rep")
    blocks, width, size = half_grad.shape
    half = width // 2
    for block in range(blocks):
        span = slice(block * size, (block + 1) * size)
        for rank, part in ((me, mine), (1 - me, other)):
            rows = pl.ds(pl.multiple_of(rank * half, half), half)
            out[rows, span] = half_grad[block, rows, :] + part[block]


def finish_items(offsets, half_grad, mine, other, out):
    me = lax.axis_index("rep")
    place = lax.axis_index("user")
    blocks, width, size = half_grad.shape
    half = width // 2
    per = blocks // len(offsets)
    for index, offset in enumerate(offsets):
        there = (place ^ offset) * per
        for block in range(per):
            span = pl.ds(pl.multiple_of((there + block) * size, size), size)
            for rank, part in ((me, mine), (1 - me, other)):
                rows = pl.ds(pl.multiple_of(rank * half, half), half)
                out[rows, span] = half_grad[there + block, rows, :] + part[index, block]


def swap(values, axis="rep", peers=2, offset=1):
    return lax.ppermute(values, axis, [(i, i ^ offset) for i in range(peers)])


def on_device(users, items, user_emb, item_emb, user_deg, item_deg, block_vals, block_row,
              block_col, block_count, trip_user, trip_pos, trip_neg):
    width = user_emb.shape[0]
    slots, size, _ = block_vals.shape
    user_blocks = user_emb.shape[1] // size
    item_blocks = item_emb.shape[1] // size
    trips = trip_user.shape[0]
    half = width // 2
    user_deg = user_deg.reshape(user_blocks, size)
    item_deg = item_deg.reshape(item_blocks, size)

    product_flops = 2 * slots * size * size * width
    product_bytes = slots * size * size * 2
    started = call(begin, shape(8, size), (), [], (), 16 * product_flops, product_bytes)
    ids = call(
        stack_ids, jax.ShapeDtypeStruct((ID_ROWS, trips), jnp.int32),
        [each.reshape(1, trips) for each in (trip_user, trip_pos, trip_neg)] + [started],
        [VMEM, VMEM, VMEM, ANY],
    )
    ids_user = [ids] + [swap(ids, "item", items, o) for o in range(1, items)]
    near = list(range(1, users))
    far = near[::-1]
    ids_item = [ids] + [swap(ids, "user", users, o) for o in far]
    lanes = -(-slots // size) * size

    order_shape = jax.ShapeDtypeStruct((4, lanes), jnp.int32)

    def source_shape(blocks):
        return jax.ShapeDtypeStruct((blocks + 1, width, size), BF16)

    (user_source, item_source, user_scale, item_scale, item_order, user_order) = call(
        prepare,
        [source_shape(user_blocks), source_shape(item_blocks), shape(user_blocks, size),
         shape(item_blocks, size), order_shape, order_shape],
        (block_count, block_row, block_col, user_emb, item_emb, user_deg, item_deg, ids),
        [SMEM, VMEM, VMEM, VMEM, VMEM, VMEM, VMEM, ANY],
        [pltpu.VMEM((8, lanes), jnp.int32)], product_flops, product_bytes,
    )
    item_table = call(
        functools.partial(first_pass, False), shape(item_blocks, width, size),
        (item_order, block_vals, user_source, ids), [SMEM, VMEM, VMEM, ANY], (),
        product_flops, product_bytes,
    )
    ids_here = [*ids_item[1:], *ids_user[1:]]
    user_table = call(
        functools.partial(first_pass, True), shape(user_blocks, width, size),
        (user_order, block_vals, item_source, item_table, *ids_here),
        [SMEM, VMEM, VMEM] + [ANY] * (1 + len(ids_here)), (),
        product_flops, product_bytes,
    )

    hot_flops = 2 * 3 * width * trips * size

    def reduced(rows, table, scale, peer_ids, axis, offsets, after):
        peers, blocks = len(peer_ids), scale.shape[0]
        dealt = call(
            functools.partial(gather, rows, peers), [shape(width, trips)] * peers,
            (table, swap(table), scale, after, *peer_ids), [VMEM] * 3 + [ANY] + [VMEM] * peers,
            [pltpu.VMEM((3 * width, blocks * size), BF16)],
            peers * blocks * hot_flops, 8 * blocks * width * size,
        )
        return [dealt[0]] + [swap(part, axis, peers, o) for part, o in zip(dealt[1:], offsets)]

    item_parts = reduced([1, 2], item_table, item_scale, ids_item, "user", far, ids)
    user_parts = reduced([0], user_table, user_scale, ids_user, "item", list(range(1, items)), item_parts[0])
    user_base, item_base = call(
        gather_base, [shape(width, trips)] * 2, (user_emb, item_emb, ids),
        [VMEM, VMEM, VMEM], (), 4 * width * trips * size * (user_blocks + item_blocks),
        2 * width * size * (user_blocks + item_blocks),
    )
    user_parts.append(user_base)
    item_parts.append(item_base)
    pieces, pushed = call(
        functools.partial(slopes, len(user_parts), len(item_parts)),
        [shape(width + 8, trips), shape(width, trips)],
        (ids, *user_parts, *item_parts), [VMEM] * (1 + len(user_parts) + len(item_parts)),
        moved=4 * width * trips * (len(user_parts) + len(item_parts) + 2),
    )

    arrays = [pieces, swap(pieces)]
    for offset in range(1, items):
        arrays.append(swap(pieces, "item", items, offset))
        arrays.append(lax.ppermute(pieces, ("item", "rep"), [
            (i, i ^ (2 * offset + 1)) for i in range(2 * items)]))
    user_half_grad, item_keep, item_send = call(
        functools.partial(second_items, len(arrays)),
        [shape(user_blocks, width, size)] + [shape(item_blocks, half, size)] * 2,
        (item_order, user_scale, item_scale, block_vals, *arrays),
        [SMEM] + [VMEM] * (3 + len(arrays)),
        [pltpu.VMEM((user_blocks + 1, width, size), BF16),
         pltpu.VMEM((item_blocks, width, size), F32),
         pltpu.VMEM((len(arrays), 3 * width, trips), BF16)],
        product_flops, product_bytes,
    )
    arrays = [pushed] + [swap(pushed, "user", users, o) for o in near]
    item_grad = call(
        functools.partial(scatter_items, users), shape(item_blocks, width, size),
        (item_send, *arrays, ids, *ids_item[:0:-1]), [ANY] + [VMEM] * (2 * users),
        [pltpu.VMEM((users, 3 * width, trips), BF16)], HEAVY, 0,
    )

    per = item_blocks // users
    dealt = call(
        functools.partial(add_deal, [0, *far]), [shape(per, half, size)] * users,
        (item_keep, swap(item_send), item_grad), [VMEM, VMEM, ANY], (), HEAVY,
    )
    item_half_grad, user_back = call(
        second_users, [shape(item_blocks, width, size), shape(user_blocks, width, size)],
        (user_order, item_grad, swap(item_grad), item_scale, user_scale, block_vals, dealt[0]),
        [SMEM] + [VMEM] * 5 + [ANY],
        [pltpu.VMEM((item_blocks + 1, width, size), BF16),
         pltpu.VMEM((user_blocks, width, size), F32)],
        product_flops, product_bytes,
    )
    parts = [dealt[0]] + [swap(part, "user", users, o) for part, o in zip(dealt[1:], far)]
    item_own = call(sum_after, shape(per, half, size), (user_back, *parts),
                    [ANY] + [VMEM] * users,
               moved=4 * (users + 1) * per * half * size)
    item_mine = call(pack, shape(users, per, half, size),
                     (item_own, *[swap(item_own, "user", users, o) for o in near]),
                     [VMEM] * users, moved=8 * item_blocks * half * size)
    item_other = swap(item_mine)

    user_keep, user_send = call(
        halves_after, [shape(user_blocks, half, size)] * 2, (user_back, item_own), [VMEM, ANY],
        moved=8 * user_blocks * width * size,
    )
    own = call(sum_parts, shape(user_blocks, half, size), (user_keep, swap(user_send)),
               [VMEM, VMEM], moved=12 * user_blocks * half * size)
    mine = call(sum_parts, shape(user_blocks, half, size),
                (own, *[swap(own, "item", items, o) for o in range(1, items)]),
                [VMEM] * items, moved=12 * user_blocks * half * size)
    return call(
        functools.partial(finish, [0, *near]),
        (shape(width, user_blocks * size), shape(width, item_blocks * size)),
        (user_half_grad, mine, swap(mine), item_half_grad, item_mine, item_other),
        [VMEM] * 6, moved=12 * (user_blocks + item_blocks) * width * size,
    )


def solution(mesh):
    return jax.shard_map(
        functools.partial(on_device, mesh.shape["user"], mesh.shape["item"]),
        mesh=mesh,
        in_specs=(
            P(None, ("groups", "user")),
            P(None, ("groups", "item")),
            P(("groups", "user")),
            P(("groups", "item")),
            P(("groups", "user", "item", "rep"), None, None),
            P(("groups", "user", "item", "rep")),
            P(("groups", "user", "item", "rep")),
            P(("groups", "user", "item", "rep")),
            P(("groups", "user", "item", "rep")),
            P(("groups", "user", "item", "rep")),
            P(("groups", "user", "item", "rep")),
        ),
        out_specs=(P(None, ("groups", "user")), P(None, ("groups", "item"))),
        check_vma=False,
    )
```

```python
import functools

import jax
import jax.numpy as jnp
from jax import lax
from jax.experimental import pallas as pl
from jax.experimental.pallas import tpu as pltpu
from jax.sharding import PartitionSpec as P

F32 = jnp.float32
BF16 = jnp.bfloat16
PACK = 4
GROUP = 4
ID_ROWS = 64
HEAVY = 10 ** 11

VMEM = pl.BlockSpec(memory_space=pltpu.VMEM)
SMEM = pl.BlockSpec(memory_space=pltpu.SMEM)
ANY = pl.BlockSpec(memory_space=pl.ANY)
HBM = pl.BlockSpec(memory_space=pltpu.HBM)


def call(kernel, outs, ins, specs, scratch=(), flops=0, moved=0, room=16):
    return pl.pallas_call(
        kernel,
        out_shape=outs,
        in_specs=specs,
        out_specs=jax.tree.map(lambda _: VMEM, outs),
        scratch_shapes=list(scratch),
        cost_estimate=pl.CostEstimate(flops=flops, bytes_accessed=moved, transcendentals=0),
        compiler_params=pltpu.CompilerParams(vmem_limit_bytes=room * 1024 * 1024),
    )(*ins)


def shape(*dims):
    return jax.ShapeDtypeStruct(dims, F32)


def split3(values):
    high = values.astype(BF16)
    rest = values - high.astype(F32)
    middle = rest.astype(BF16)
    low = (rest - middle.astype(F32)).astype(BF16)
    return high, middle, low


def hot(ids, start, tile):
    if len(ids) == 2:
        same = ids[0] == ids[1]
        ids = [jnp.where(same, -1, each) for each in ids]
    ids = [each.astype(jnp.int16) for each in ids]
    place = lax.broadcasted_iota(jnp.int16, (tile, ids[0].shape[1]), 0) + jnp.int16(start)
    chosen = jnp.zeros(place.shape, BF16)
    for each, sign in zip(ids, (1, -1)):
        chosen = jnp.where(place == each, jnp.asarray(sign, BF16), chosen)
    return chosen


def sort_slots(keys, sources, count, blocks):
    lanes = keys.shape[1]
    rows = 2 * blocks
    place = lax.broadcasted_iota(jnp.int32, (1, lanes), 1)
    live = place < count
    mine = (lax.broadcasted_iota(jnp.int32, (rows, lanes), 0) == keys) & live
    mine = jnp.where(mine, 1.0, 0.0)
    earlier = lax.broadcasted_iota(jnp.int32, (lanes, lanes), 0) < lax.broadcasted_iota(
        jnp.int32, (lanes, lanes), 1)
    before = jnp.dot(mine.astype(BF16), jnp.where(earlier, 1.0, 0.0).astype(BF16),
                     preferred_element_type=F32)
    packs = jnp.floor((jnp.sum(mine, axis=1, keepdims=True) + (PACK - 1)) * (1.0 / PACK))
    packs = jnp.broadcast_to(packs, (rows, 128))
    lower = lax.broadcasted_iota(jnp.int32, (rows, rows), 1) < lax.broadcasted_iota(
        jnp.int32, (rows, rows), 0)
    first = jnp.dot(jnp.where(lower, 1.0, 0.0).astype(BF16), packs.astype(BF16),
                    preferred_element_type=F32)
    position = jnp.sum(mine * (first[:, :1] * PACK + before), axis=0, keepdims=True)
    position = jnp.where(live, position.astype(jnp.int32), -1)
    match = lax.broadcasted_iota(jnp.int32, (lanes, lanes), 0) == position
    row = lax.broadcasted_iota(jnp.int32, (16, lanes), 0)
    values = jnp.where(row == 0, place // 16, jnp.where(row == 1, place % 16, jnp.where(
        row == 2, sources, jnp.where(row == 3, keys, jnp.where(row == 4, 1, 0)))))
    values = jnp.where(live, values, 0).astype(F32)
    found = lax.dot_general(values.astype(BF16), jnp.where(match, 1.0, 0.0).astype(BF16),
                            (((1,), (1,)), ((), ())), preferred_element_type=F32)
    found = found.astype(jnp.int32)
    valid = found[4:5] > 0
    total = jnp.broadcast_to(jnp.sum(packs[:, :1], axis=0, keepdims=True), (1, lanes))
    row = lax.broadcasted_iota(jnp.int32, (4, lanes), 0)
    slot = found[0:1] * 16 + found[1:2]
    source = jnp.where(valid, found[2:3], blocks)
    target = jnp.where(valid, found[3:4], 0)
    return jnp.where(row == 0, slot, jnp.where(row == 1, source, jnp.where(
        row == 2, target, total.astype(jnp.int32))))


def multiply_blocks(order, vals, source, total, across):
    _, width, size = source.shape
    total[...] = jnp.zeros_like(total)
    contract = (((1,), (1,)), ((), ())) if across else (((1,), (0,)), ((), ()))

    def group(index, _):
        targets, terms = [], []
        for step in range(GROUP):
            left, right = [], []
            for half in range(2):
                first = ((index * GROUP + step) * 2 + half) * PACK
                places = [first + each for each in range(PACK)]
                left.append(jnp.concatenate([source[order[1, each]] for each in places], axis=1))
                right.append(jnp.concatenate([vals[order[0, each]] for each in places],
                                             axis=1 if across else 0))
                targets.append(order[2, first])
            both = lax.dot_general(
                jnp.concatenate(left, axis=0), jnp.concatenate(right, axis=0 if across else 1),
                contract, preferred_element_type=F32,
            )
            terms += [both[:width, :size], both[width:, size:]]
        for target, term in zip(targets, terms):
            total[target] += term
        return 0

    lax.fori_loop(0, (order[3, 0] + 2 * GROUP - 1) // (2 * GROUP), group, 0)


def begin(out):
    out[...] = jnp.zeros_like(out)


def stack_ids(user, positive, negative, after, out):
    out[...] = jnp.zeros_like(out)
    for row, ids in enumerate((user, positive, negative)):
        out[row:row + 1, :] = ids[...]


def pack_ids(places, *refs):
    out = refs[-1]
    out[...] = jnp.zeros_like(out)
    for offset, (index, row) in enumerate(places):
        out[3 * offset:3 * offset + 3, :] = refs[index][row:row + 3, :]


def prepare(count, rows, columns, user_emb, item_emb, user_deg, item_deg, after,
            user_source, item_source, user_scale, item_scale, item_order, user_order, keys):
    live = count[0]
    slots = rows.shape[0]
    keys[...] = jnp.zeros_like(keys)
    keys[0:1, 0:slots] = rows[...].reshape(1, slots)
    keys[1:2, 0:slots] = columns[...].reshape(1, slots)
    users, items = keys[0:1, :], keys[1:2, :]
    item_order[...] = sort_slots(items, users, live, item_scale.shape[0])
    user_order[...] = sort_slots(users, items, live, user_scale.shape[0])
    for emb, deg, scale, into in ((user_emb, user_deg, user_scale, user_source),
                                  (item_emb, item_deg, item_scale, item_source)):
        scale[...] = lax.rsqrt(deg[...].astype(F32))
        blocks, size = scale.shape
        for block in range(blocks):
            piece = emb[:, block * size:(block + 1) * size].astype(F32)
            into[block] = (scale[block:block + 1, :] * piece).astype(BF16)
        into[blocks] = jnp.zeros(into.shape[1:], BF16)


def first_pass(across, order, vals, source, *refs):
    multiply_blocks(order, vals, source, refs[-1], across)


def fold(stacked, width):
    return (
        stacked[:width] + stacked[width:2 * width] + stacked[2 * width:3 * width]
    )


def rows_of(ref, rows):
    return [ref[row:row + 1, :] for row in rows]


def pick(table, ids, tile):
    total = None
    for start in range(0, table.shape[1], tile):
        term = jnp.dot(
            table[:, start:start + tile], hot(ids, start, tile),
            preferred_element_type=F32,
        )
        total = term if total is None else total + term
    return total


def gather(places, count, mine, other, scale, after, *refs):
    ids, outs, table = refs[:count], refs[count:-1], refs[-1]
    blocks, width, size = mine.shape
    for block in range(blocks):
        span = slice(block * size, (block + 1) * size)
        here = scale[block:block + 1, :] * (mine[block] + other[block])
        for part, piece in enumerate(split3(here)):
            table[part * width:(part + 1) * width, span] = piece
    for out, (index, rows) in zip(outs, places):
        out[...] = fold(pick(table, rows_of(ids[index], rows), 2 * size), width)


def scatter(pieces, ids, table, blocks, size, put):
    width = table.shape[1] // 3
    tile = 2 * size
    for place, piece in enumerate(pieces):
        for part, value in enumerate(split3(piece[:width, :])):
            table[place, part * width:(part + 1) * width, :] = value
    for start in range(0, blocks * size, tile):
        total = None
        for place, rows in enumerate(ids):
            term = lax.dot_general(
                table[place], hot(rows, start, tile), (((1,), (1,)), ((), ())),
                preferred_element_type=F32,
            )
            total = term if total is None else total + term
        total = fold(total, width)
        for offset in range(0, tile, size):
            put((start + offset) // size, total[:, offset:offset + size])


def scatter_items(places, after, *refs):
    peers = len(places)
    pieces, ids, out, table = refs[:peers], refs[peers:-2], refs[-2], refs[-1]
    blocks, _, size = out.shape

    def put(block, value):
        out[block] = value

    scatter(pieces, [rows_of(ids[index], rows) for index, rows in places],
            table, blocks, size, put)


def gather_base(user_emb, item_emb, ids, user_out, item_out):
    tile = ids.shape[1]
    user_out[...] = pick(user_emb, rows_of(ids, [0]), tile)
    item_out[...] = pick(item_emb, rows_of(ids, [1, 2]), tile)


def add_all(refs):
    total = refs[0][...]
    for ref in refs[1:]:
        total = total + ref[...]
    return total


def slopes(user_parts, item_parts, ids, *refs):
    users, items = refs[:user_parts], refs[user_parts:user_parts + item_parts]
    pieces, pushed = refs[user_parts + item_parts:]
    width = pushed.shape[0]
    user_rows = 0.5 * add_all(users)
    difference = 0.5 * add_all(items)
    margin = jnp.sum(user_rows * difference, axis=0, keepdims=True)
    slope = -jax.nn.sigmoid(-margin)
    pieces[:width, :] = slope * difference
    pieces[width:, :] = jnp.broadcast_to(ids[0:1, :].astype(F32), (8, ids.shape[1]))
    pushed[...] = slope * user_rows


def halves(total, keep, send):
    me = lax.axis_index("rep")
    half = keep.shape[1]
    for block in range(keep.shape[0]):
        keep[block] = total[block, pl.ds(pl.multiple_of(me * half, half), half), :]
        send[block] = total[block, pl.ds(pl.multiple_of((1 - me) * half, half), half), :]


def second_items(parts, order, source_scale, target_scale, vals, *refs):
    pieces = refs[:parts]
    half_grad, keep, send, source, total, table = refs[parts:]
    blocks, width, size = half_grad.shape

    def put(block, grad):
        half_grad[block] = 0.5 * grad
        source[block] = (source_scale[block:block + 1, :] * grad * 0.5).astype(BF16)

    ids = [[piece[width:width + 1, :].astype(jnp.int32)] for piece in pieces]
    scatter(pieces, ids, table, blocks, size, put)
    source[blocks] = jnp.zeros((width, size), BF16)
    multiply_blocks(order, vals, source, total, False)
    for block in range(total.shape[0]):
        total[block] = target_scale[block:block + 1, :] * total[block]
    halves(total, keep, send)


def second_users(order, mine, other, source_scale, target_scale, vals, after,
                 half_grad, out, source, total):
    blocks, width, size = mine.shape
    for block in range(blocks):
        grad = mine[block] + other[block]
        half_grad[block] = 0.5 * grad
        source[block] = (source_scale[block:block + 1, :] * grad * 0.5).astype(BF16)
    source[blocks] = jnp.zeros((width, size), BF16)
    multiply_blocks(order, vals, source, total, True)
    for block in range(out.shape[0]):
        out[block] = target_scale[block:block + 1, :] * total[block]


def halves_after(total, after, keep, send):
    halves(total, keep, send)


def add_deal(offsets, keep, received, after, *outs):
    me = lax.axis_index("user")
    per = outs[0].shape[0]
    for out, offset in zip(outs, offsets):
        there = (me ^ offset) * per
        for block in range(per):
            out[block] = keep[there + block] + received[there + block]


def sum_parts(*refs):
    refs[-1][...] = add_all(refs[:-1])


def sum_after(after, *refs):
    sum_parts(*refs)


def pack(*refs):
    for place, ref in enumerate(refs[:-1]):
        refs[-1][place] = ref[...]


def finish(offsets, user_half_grad, user_mine, user_other, item_half_grad, item_mine, item_other,
           user_out, item_out):
    finish_users(user_half_grad, user_mine, user_other, user_out)
    finish_items(offsets, item_half_grad, item_mine, item_other, item_out)


def finish_users(half_grad, mine, other, out):
    me = lax.axis_index("rep")
    blocks, width, size = half_grad.shape
    half = width // 2
    for block in range(blocks):
        span = slice(block * size, (block + 1) * size)
        for rank, part in ((me, mine), (1 - me, other)):
            rows = pl.ds(pl.multiple_of(rank * half, half), half)
            out[rows, span] = half_grad[block, rows, :] + part[block]


def finish_items(offsets, half_grad, mine, other, out):
    me = lax.axis_index("rep")
    place = lax.axis_index("user")
    blocks, width, size = half_grad.shape
    half = width // 2
    per = blocks // len(offsets)
    for index, offset in enumerate(offsets):
        there = (place ^ offset) * per
        for block in range(per):
            span = pl.ds(pl.multiple_of((there + block) * size, size), size)
            for rank, part in ((me, mine), (1 - me, other)):
                rows = pl.ds(pl.multiple_of(rank * half, half), half)
                out[rows, span] = half_grad[there + block, rows, :] + part[index, block]


def swap(values, axis="rep", peers=2, offset=1):
    return lax.ppermute(values, axis, [(i, i ^ offset) for i in range(peers)])


def on_device(users, items, user_emb, item_emb, user_deg, item_deg, block_vals, block_row,
              block_col, block_count, trip_user, trip_pos, trip_neg):
    width = user_emb.shape[0]
    slots, size, _ = block_vals.shape
    user_blocks = user_emb.shape[1] // size
    item_blocks = item_emb.shape[1] // size
    trips = trip_user.shape[0]
    half = width // 2
    user_deg = user_deg.reshape(user_blocks, size)
    item_deg = item_deg.reshape(item_blocks, size)

    product_flops = 2 * slots * size * size * width
    product_bytes = slots * size * size * 2
    started = call(begin, shape(8, size), (), [], (), 16 * product_flops, product_bytes)
    ids_shape = jax.ShapeDtypeStruct((ID_ROWS, trips), jnp.int32)
    ids = call(
        stack_ids, ids_shape,
        [each.reshape(1, trips) for each in (trip_user, trip_pos, trip_neg)] + [started],
        [VMEM, VMEM, VMEM, ANY],
    )
    ids_user = [ids] + [swap(ids, "item", items, o) for o in range(1, items)]
    met = sorted(range(1, users), key=lambda offset: (offset != users // 2, -offset))
    back = met[::-1]
    ids_item, held, step = [(0, 0)], [ids], 1
    while step < users:
        packed = ids if step == 1 else call(
            functools.partial(pack_ids, ids_item), ids_shape, held, [VMEM] * len(held))
        held.append(swap(packed, "user", users, step))
        ids_item += [(len(held) - 1, 3 * place) for place in range(step)]
        step *= 2
    lanes = -(-slots // size) * size

    order_shape = jax.ShapeDtypeStruct((4, lanes), jnp.int32)

    def source_shape(blocks):
        return jax.ShapeDtypeStruct((blocks + 1, width, size), BF16)

    (user_source, item_source, user_scale, item_scale, item_order, user_order) = call(
        prepare,
        [source_shape(user_blocks), source_shape(item_blocks), shape(user_blocks, size),
         shape(item_blocks, size), order_shape, order_shape],
        (block_count, block_row, block_col, user_emb, item_emb, user_deg, item_deg, ids),
        [SMEM, VMEM, VMEM, VMEM, VMEM, VMEM, VMEM, ANY],
        [pltpu.VMEM((8, lanes), jnp.int32)], product_flops, product_bytes,
    )
    item_table = call(
        functools.partial(first_pass, False), shape(item_blocks, width, size),
        (item_order, block_vals, user_source, ids), [SMEM, VMEM, VMEM, ANY], (),
        product_flops, product_bytes,
    )
    ids_here = [*held[1:], *ids_user[1:]]
    user_table = call(
        functools.partial(first_pass, True), shape(user_blocks, width, size),
        (user_order, block_vals, item_source, item_table, *ids_here),
        [SMEM, VMEM, VMEM] + [ANY] * (1 + len(ids_here)), (),
        product_flops, product_bytes,
    )

    hot_flops = 2 * 3 * width * trips * size

    def reduced(table, scale, arrays, places, axis, offsets, after):
        peers, blocks = len(places), scale.shape[0]
        dealt = call(
            functools.partial(gather, places, len(arrays)), [shape(width, trips)] * peers,
            (table, swap(table), scale, after, *arrays),
            [VMEM] * 3 + [ANY] + [VMEM] * len(arrays),
            [pltpu.VMEM((3 * width, blocks * size), BF16)],
            peers * blocks * hot_flops, 8 * blocks * width * size,
        )
        return [dealt[0]] + [swap(part, axis, peers, o) for part, o in zip(dealt[1:], offsets)]

    def item_rows(offset):
        index, row = ids_item[offset]
        return index, [row + 1, row + 2]

    item_parts = reduced(item_table, item_scale, held, [item_rows(o) for o in [0, *met]],
                         "user", met, ids)
    user_parts = reduced(user_table, user_scale, ids_user, [(o, [0]) for o in range(items)],
                         "item", list(range(1, items)), item_parts[0])
    user_base, item_base = call(
        gather_base, [shape(width, trips)] * 2, (user_emb, item_emb, ids),
        [VMEM, VMEM, VMEM], (), 4 * width * trips * size * (user_blocks + item_blocks),
        2 * width * size * (user_blocks + item_blocks),
    )
    user_parts.append(user_base)
    item_parts.append(item_base)
    pieces, pushed = call(
        functools.partial(slopes, len(user_parts), len(item_parts)),
        [shape(width + 8, trips), shape(width, trips)],
        (ids, *user_parts, *item_parts), [VMEM] * (1 + len(user_parts) + len(item_parts)),
        moved=4 * width * trips * (len(user_parts) + len(item_parts) + 2),
    )

    arrays = [pieces, swap(pieces)]
    for offset in range(1, items):
        arrays.append(swap(pieces, "item", items, offset))
        arrays.append(lax.ppermute(pieces, ("item", "rep"), [
            (i, i ^ (2 * offset + 1)) for i in range(2 * items)]))
    user_half_grad, item_keep, item_send = call(
        functools.partial(second_items, len(arrays)),
        [shape(user_blocks, width, size)] + [shape(item_blocks, half, size)] * 2,
        (item_order, user_scale, item_scale, block_vals, *arrays),
        [SMEM] + [VMEM] * (3 + len(arrays)),
        [pltpu.VMEM((user_blocks + 1, width, size), BF16),
         pltpu.VMEM((item_blocks, width, size), F32),
         pltpu.VMEM((len(arrays), 3 * width, trips), BF16)],
        product_flops, product_bytes,
    )
    arrays = [pushed] + [swap(pushed, "user", users, o) for o in back]
    item_grad = call(
        functools.partial(scatter_items, [item_rows(o) for o in [0, *back]]),
        shape(item_blocks, width, size),
        (item_send, *arrays, *held), [ANY] + [VMEM] * (users + len(held)),
        [pltpu.VMEM((users, 3 * width, trips), BF16)], HEAVY, 0,
    )

    per = item_blocks // users
    dealt = call(
        functools.partial(add_deal, [0, *met]), [shape(per, half, size)] * users,
        (item_keep, swap(item_send), item_grad), [VMEM, VMEM, ANY], (), HEAVY,
    )
    item_half_grad, user_back = call(
        second_users, [shape(item_blocks, width, size), shape(user_blocks, width, size)],
        (user_order, item_grad, swap(item_grad), item_scale, user_scale, block_vals, dealt[0]),
        [SMEM] + [VMEM] * 5 + [ANY],
        [pltpu.VMEM((item_blocks + 1, width, size), BF16),
         pltpu.VMEM((user_blocks, width, size), F32)],
        product_flops, product_bytes,
    )
    parts = [dealt[0]] + [swap(part, "user", users, o) for part, o in zip(dealt[1:], met)]
    item_own = call(sum_after, shape(per, half, size), (user_back, *parts),
                    [ANY] + [VMEM] * users,
               moved=4 * (users + 1) * per * half * size)
    item_mine = call(pack, shape(users, per, half, size),
                     (item_own, *[swap(item_own, "user", users, o) for o in back]),
                     [VMEM] * users, moved=8 * item_blocks * half * size)
    item_other = swap(item_mine)

    user_keep, user_send = call(
        halves_after, [shape(user_blocks, half, size)] * 2, (user_back, item_own), [VMEM, ANY],
        moved=8 * user_blocks * width * size,
    )
    own = call(sum_parts, shape(user_blocks, half, size), (user_keep, swap(user_send)),
               [VMEM, VMEM], moved=12 * user_blocks * half * size)
    mine = call(sum_parts, shape(user_blocks, half, size),
                (own, *[swap(own, "item", items, o) for o in range(1, items)]),
                [VMEM] * items, moved=12 * user_blocks * half * size)
    return call(
        functools.partial(finish, [0, *back]),
        (shape(width, user_blocks * size), shape(width, item_blocks * size)),
        (user_half_grad, mine, swap(mine), item_half_grad, item_mine, item_other),
        [VMEM] * 6, moved=12 * (user_blocks + item_blocks) * width * size,
    )


def solution(mesh):
    return jax.shard_map(
        functools.partial(on_device, mesh.shape["user"], mesh.shape["item"]),
        mesh=mesh,
        in_specs=(
            P(None, ("groups", "user")),
            P(None, ("groups", "item")),
            P(("groups", "user")),
            P(("groups", "item")),
            P(("groups", "user", "item", "rep"), None, None),
            P(("groups", "user", "item", "rep")),
            P(("groups", "user", "item", "rep")),
            P(("groups", "user", "item", "rep")),
            P(("groups", "user", "item", "rep")),
            P(("groups", "user", "item", "rep")),
            P(("groups", "user", "item", "rep")),
        ),
        out_specs=(P(None, ("groups", "user")), P(None, ("groups", "item"))),
        check_vma=False,
    )
```

```python
import functools

import jax
import jax.numpy as jnp
from jax import lax
from jax.experimental import pallas as pl
from jax.experimental.pallas import tpu as pltpu
from jax.sharding import PartitionSpec as P

F32 = jnp.float32
BF16 = jnp.bfloat16
PACK = 4
GROUP = 4
ID_ROWS = 64
HEAVY = 10 ** 11

VMEM = pl.BlockSpec(memory_space=pltpu.VMEM)
SMEM = pl.BlockSpec(memory_space=pltpu.SMEM)
ANY = pl.BlockSpec(memory_space=pl.ANY)
HBM = pl.BlockSpec(memory_space=pltpu.HBM)


def call(kernel, outs, ins, specs, scratch=(), flops=0, moved=0, room=16):
    return pl.pallas_call(
        kernel,
        out_shape=outs,
        in_specs=specs,
        out_specs=jax.tree.map(lambda _: VMEM, outs),
        scratch_shapes=list(scratch),
        cost_estimate=pl.CostEstimate(flops=flops, bytes_accessed=moved, transcendentals=0),
        compiler_params=pltpu.CompilerParams(vmem_limit_bytes=room * 1024 * 1024),
    )(*ins)


def shape(*dims):
    return jax.ShapeDtypeStruct(dims, F32)


def split3(values):
    high = values.astype(BF16)
    rest = values - high.astype(F32)
    middle = rest.astype(BF16)
    low = (rest - middle.astype(F32)).astype(BF16)
    return high, middle, low


def hot(ids, start, tile):
    if len(ids) == 2:
        same = ids[0] == ids[1]
        ids = [jnp.where(same, -1, each) for each in ids]
    ids = [each.astype(jnp.int16) for each in ids]
    place = lax.broadcasted_iota(jnp.int16, (tile, ids[0].shape[1]), 0) + jnp.int16(start)
    chosen = jnp.zeros(place.shape, BF16)
    for each, sign in zip(ids, (1, -1)):
        chosen = jnp.where(place == each, jnp.asarray(sign, BF16), chosen)
    return chosen


def sort_slots(keys, sources, count, blocks):
    lanes = keys.shape[1]
    rows = 2 * blocks
    place = lax.broadcasted_iota(jnp.int32, (1, lanes), 1)
    live = place < count
    mine = (lax.broadcasted_iota(jnp.int32, (rows, lanes), 0) == keys) & live
    mine = jnp.where(mine, 1.0, 0.0)
    earlier = lax.broadcasted_iota(jnp.int32, (lanes, lanes), 0) < lax.broadcasted_iota(
        jnp.int32, (lanes, lanes), 1)
    before = jnp.dot(mine.astype(BF16), jnp.where(earlier, 1.0, 0.0).astype(BF16),
                     preferred_element_type=F32)
    packs = jnp.floor((jnp.sum(mine, axis=1, keepdims=True) + (PACK - 1)) * (1.0 / PACK))
    packs = jnp.broadcast_to(packs, (rows, 128))
    lower = lax.broadcasted_iota(jnp.int32, (rows, rows), 1) < lax.broadcasted_iota(
        jnp.int32, (rows, rows), 0)
    first = jnp.dot(jnp.where(lower, 1.0, 0.0).astype(BF16), packs.astype(BF16),
                    preferred_element_type=F32)
    position = jnp.sum(mine * (first[:, :1] * PACK + before), axis=0, keepdims=True)
    position = jnp.where(live, position.astype(jnp.int32), -1)
    match = lax.broadcasted_iota(jnp.int32, (lanes, lanes), 0) == position
    row = lax.broadcasted_iota(jnp.int32, (16, lanes), 0)
    values = jnp.where(row == 0, place // 16, jnp.where(row == 1, place % 16, jnp.where(
        row == 2, sources, jnp.where(row == 3, keys, jnp.where(row == 4, 1, 0)))))
    values = jnp.where(live, values, 0).astype(F32)
    found = lax.dot_general(values.astype(BF16), jnp.where(match, 1.0, 0.0).astype(BF16),
                            (((1,), (1,)), ((), ())), preferred_element_type=F32)
    found = found.astype(jnp.int32)
    valid = found[4:5] > 0
    total = jnp.broadcast_to(jnp.sum(packs[:, :1], axis=0, keepdims=True), (1, lanes))
    row = lax.broadcasted_iota(jnp.int32, (4, lanes), 0)
    slot = found[0:1] * 16 + found[1:2]
    source = jnp.where(valid, found[2:3], blocks)
    target = jnp.where(valid, found[3:4], 0)
    return jnp.where(row == 0, slot, jnp.where(row == 1, source, jnp.where(
        row == 2, target, total.astype(jnp.int32))))


def multiply_blocks(order, vals, source, total, across):
    _, width, size = source.shape
    total[...] = jnp.zeros_like(total)
    contract = (((1,), (1,)), ((), ())) if across else (((1,), (0,)), ((), ()))

    def group(index, _):
        targets, terms = [], []
        for step in range(GROUP):
            left, right = [], []
            for half in range(2):
                first = ((index * GROUP + step) * 2 + half) * PACK
                places = [first + each for each in range(PACK)]
                left.append(jnp.concatenate([source[order[1, each]] for each in places], axis=1))
                right.append(jnp.concatenate([vals[order[0, each]] for each in places],
                                             axis=1 if across else 0))
                targets.append(order[2, first])
            both = lax.dot_general(
                jnp.concatenate(left, axis=0), jnp.concatenate(right, axis=0 if across else 1),
                contract, preferred_element_type=F32,
            )
            terms += [both[:width, :size], both[width:, size:]]
        for target, term in zip(targets, terms):
            total[target] += term
        return 0

    lax.fori_loop(0, (order[3, 0] + 2 * GROUP - 1) // (2 * GROUP), group, 0)


def begin(out):
    out[...] = jnp.zeros_like(out)


def stack_ids(user, positive, negative, after, out):
    out[...] = jnp.zeros_like(out)
    for row, ids in enumerate((user, positive, negative)):
        out[row:row + 1, :] = ids[...]


def pack_ids(places, *refs):
    out = refs[-1]
    out[...] = jnp.zeros_like(out)
    for offset, (index, row) in enumerate(places):
        out[3 * offset:3 * offset + 3, :] = refs[index][row:row + 3, :]


def prepare(count, rows, columns, user_emb, item_emb, user_deg, item_deg, after,
            user_source, item_source, user_scale, item_scale, item_order, user_order, keys):
    live = count[0]
    slots = rows.shape[0]
    keys[...] = jnp.zeros_like(keys)
    keys[0:1, 0:slots] = rows[...].reshape(1, slots)
    keys[1:2, 0:slots] = columns[...].reshape(1, slots)
    users, items = keys[0:1, :], keys[1:2, :]
    item_order[...] = sort_slots(items, users, live, item_scale.shape[0])
    user_order[...] = sort_slots(users, items, live, user_scale.shape[0])
    for emb, deg, scale, into in ((user_emb, user_deg, user_scale, user_source),
                                  (item_emb, item_deg, item_scale, item_source)):
        scale[...] = lax.rsqrt(deg[...].astype(F32))
        blocks, size = scale.shape
        for block in range(blocks):
            piece = emb[:, block * size:(block + 1) * size].astype(F32)
            into[block] = (scale[block:block + 1, :] * piece).astype(BF16)
        into[blocks] = jnp.zeros(into.shape[1:], BF16)


def first_pass(across, order, vals, source, *refs):
    multiply_blocks(order, vals, source, refs[-1], across)


def fold(stacked, width):
    return (
        stacked[:width] + stacked[width:2 * width] + stacked[2 * width:3 * width]
    )


def rows_of(ref, rows):
    return [ref[row:row + 1, :] for row in rows]


def pick(table, ids, tile):
    total = None
    for start in range(0, table.shape[1], tile):
        term = jnp.dot(
            table[:, start:start + tile], hot(ids, start, tile),
            preferred_element_type=F32,
        )
        total = term if total is None else total + term
    return total


def gather(places, count, mine, other, scale, after, *refs):
    ids, outs, table = refs[:count], refs[count:-1], refs[-1]
    blocks, width, size = mine.shape
    for block in range(blocks):
        span = slice(block * size, (block + 1) * size)
        here = scale[block:block + 1, :] * (mine[block] + other[block])
        for part, piece in enumerate(split3(here)):
            table[part * width:(part + 1) * width, span] = piece
    for out, (index, rows) in zip(outs, places):
        out[...] = fold(pick(table, rows_of(ids[index], rows), 2 * size), width)


def scatter(pieces, ids, table, blocks, size, put):
    width = table.shape[1] // 3
    tile = 2 * size
    for place, piece in enumerate(pieces):
        for part, value in enumerate(split3(piece[:width, :])):
            table[place, part * width:(part + 1) * width, :] = value
    for start in range(0, blocks * size, tile):
        total = None
        for place, rows in enumerate(ids):
            term = lax.dot_general(
                table[place], hot(rows, start, tile), (((1,), (1,)), ((), ())),
                preferred_element_type=F32,
            )
            total = term if total is None else total + term
        total = fold(total, width)
        for offset in range(0, tile, size):
            put((start + offset) // size, total[:, offset:offset + size])


def scatter_items(places, after, *refs):
    peers = len(places)
    pieces, ids, out, table = refs[:peers], refs[peers:-2], refs[-2], refs[-1]
    blocks, _, size = out.shape

    def put(block, value):
        out[block] = value

    scatter(pieces, [rows_of(ids[index], rows) for index, rows in places],
            table, blocks, size, put)


def gather_base(user_emb, item_emb, ids, user_out, item_out):
    tile = ids.shape[1]
    user_out[...] = pick(user_emb, rows_of(ids, [0]), tile)
    item_out[...] = pick(item_emb, rows_of(ids, [1, 2]), tile)


def add_all(refs):
    total = refs[0][...]
    for ref in refs[1:]:
        total = total + ref[...]
    return total


def slopes(user_parts, item_parts, ids, *refs):
    users, items = refs[:user_parts], refs[user_parts:user_parts + item_parts]
    pieces, pushed = refs[user_parts + item_parts:]
    width = pushed.shape[0]
    user_rows = 0.5 * add_all(users)
    difference = 0.5 * add_all(items)
    margin = jnp.sum(user_rows * difference, axis=0, keepdims=True)
    slope = -jax.nn.sigmoid(-margin)
    pieces[:width, :] = slope * difference
    pieces[width:, :] = jnp.broadcast_to(ids[0:1, :].astype(F32), (8, ids.shape[1]))
    pushed[...] = slope * user_rows


def halves(total, keep, send):
    me = lax.axis_index("rep")
    half = keep.shape[1]
    for block in range(keep.shape[0]):
        keep[block] = total[block, pl.ds(pl.multiple_of(me * half, half), half), :]
        send[block] = total[block, pl.ds(pl.multiple_of((1 - me) * half, half), half), :]


def second_items(parts, order, source_scale, target_scale, vals, *refs):
    pieces = refs[:parts]
    half_grad, keep, send, source, total, table = refs[parts:]
    blocks, width, size = half_grad.shape

    def put(block, grad):
        half_grad[block] = 0.5 * grad
        source[block] = (source_scale[block:block + 1, :] * grad * 0.5).astype(BF16)

    ids = [[piece[width:width + 1, :].astype(jnp.int32)] for piece in pieces]
    scatter(pieces, ids, table, blocks, size, put)
    source[blocks] = jnp.zeros((width, size), BF16)
    multiply_blocks(order, vals, source, total, False)
    for block in range(total.shape[0]):
        total[block] = target_scale[block:block + 1, :] * total[block]
    halves(total, keep, send)


def second_users(order, mine, other, source_scale, target_scale, vals, after,
                 half_grad, out, source, total):
    blocks, width, size = mine.shape
    for block in range(blocks):
        grad = mine[block] + other[block]
        half_grad[block] = 0.5 * grad
        source[block] = (source_scale[block:block + 1, :] * grad * 0.5).astype(BF16)
    source[blocks] = jnp.zeros((width, size), BF16)
    multiply_blocks(order, vals, source, total, True)
    for block in range(out.shape[0]):
        out[block] = target_scale[block:block + 1, :] * total[block]


def halves_after(total, after, keep, send):
    halves(total, keep, send)


def add_deal(offsets, keep, received, after, *outs):
    me = lax.axis_index("user")
    per = outs[0].shape[0]
    for out, offset in zip(outs, offsets):
        there = (me ^ offset) * per
        for block in range(per):
            out[block] = keep[there + block] + received[there + block]


def sum_parts(*refs):
    refs[-1][...] = add_all(refs[:-1])


def sum_after(after, *refs):
    refs[-1][0] = add_all(refs[:-1])


def pack(first, second, out):
    count = first.shape[0]
    out[:count] = first[...]
    out[count:] = second[...]


def finish(places, user_half_grad, user_mine, user_other, item_half_grad, *refs):
    (user_out, item_out), refs = refs[-2:], refs[:-2]
    finish_users(user_half_grad, user_mine, user_other, user_out)
    mine, other = refs[:len(places)], refs[len(places):]
    for offsets, mine_here, other_here in zip(places, mine, other):
        finish_items(offsets, item_half_grad, mine_here, other_here, item_out)


def finish_users(half_grad, mine, other, out):
    me = lax.axis_index("rep")
    blocks, width, size = half_grad.shape
    half = width // 2
    for block in range(blocks):
        span = slice(block * size, (block + 1) * size)
        for rank, part in ((me, mine), (1 - me, other)):
            rows = pl.ds(pl.multiple_of(rank * half, half), half)
            out[rows, span] = half_grad[block, rows, :] + part[block]


def finish_items(offsets, half_grad, mine, other, out):
    me = lax.axis_index("rep")
    place = lax.axis_index("user")
    blocks, width, size = half_grad.shape
    half = width // 2
    per = mine.shape[1]
    for index, offset in enumerate(offsets):
        there = (place ^ offset) * per
        for block in range(per):
            span = pl.ds(pl.multiple_of((there + block) * size, size), size)
            for rank, part in ((me, mine), (1 - me, other)):
                rows = pl.ds(pl.multiple_of(rank * half, half), half)
                out[rows, span] = half_grad[there + block, rows, :] + part[index, block]


def swap(values, axis="rep", peers=2, offset=1):
    return lax.ppermute(values, axis, [(i, i ^ offset) for i in range(peers)])


def on_device(users, items, user_emb, item_emb, user_deg, item_deg, block_vals, block_row,
              block_col, block_count, trip_user, trip_pos, trip_neg):
    width = user_emb.shape[0]
    slots, size, _ = block_vals.shape
    user_blocks = user_emb.shape[1] // size
    item_blocks = item_emb.shape[1] // size
    trips = trip_user.shape[0]
    half = width // 2
    user_deg = user_deg.reshape(user_blocks, size)
    item_deg = item_deg.reshape(item_blocks, size)

    product_flops = 2 * slots * size * size * width
    product_bytes = slots * size * size * 2
    started = call(begin, shape(8, size), (), [], (), 16 * product_flops, product_bytes)
    ids_shape = jax.ShapeDtypeStruct((ID_ROWS, trips), jnp.int32)
    ids = call(
        stack_ids, ids_shape,
        [each.reshape(1, trips) for each in (trip_user, trip_pos, trip_neg)] + [started],
        [VMEM, VMEM, VMEM, ANY],
    )
    ids_user = [ids] + [swap(ids, "item", items, o) for o in range(1, items)]
    met = sorted(range(1, users), key=lambda offset: (offset != users // 2, -offset))
    back = met[::-1]
    ids_item, held, step = [(0, 0)], [ids], 1
    while step < users:
        packed = ids if step == 1 else call(
            functools.partial(pack_ids, ids_item), ids_shape, held, [VMEM] * len(held))
        held.append(swap(packed, "user", users, step))
        ids_item += [(len(held) - 1, 3 * place) for place in range(step)]
        step *= 2
    lanes = -(-slots // size) * size

    order_shape = jax.ShapeDtypeStruct((4, lanes), jnp.int32)

    def source_shape(blocks):
        return jax.ShapeDtypeStruct((blocks + 1, width, size), BF16)

    (user_source, item_source, user_scale, item_scale, item_order, user_order) = call(
        prepare,
        [source_shape(user_blocks), source_shape(item_blocks), shape(user_blocks, size),
         shape(item_blocks, size), order_shape, order_shape],
        (block_count, block_row, block_col, user_emb, item_emb, user_deg, item_deg, ids),
        [SMEM, VMEM, VMEM, VMEM, VMEM, VMEM, VMEM, ANY],
        [pltpu.VMEM((8, lanes), jnp.int32)], product_flops, product_bytes,
    )
    item_table = call(
        functools.partial(first_pass, False), shape(item_blocks, width, size),
        (item_order, block_vals, user_source, ids), [SMEM, VMEM, VMEM, ANY], (),
        product_flops, product_bytes,
    )
    ids_here = [*held[1:], *ids_user[1:]]
    user_table = call(
        functools.partial(first_pass, True), shape(user_blocks, width, size),
        (user_order, block_vals, item_source, item_table, *ids_here),
        [SMEM, VMEM, VMEM] + [ANY] * (1 + len(ids_here)), (),
        product_flops, product_bytes,
    )

    hot_flops = 2 * 3 * width * trips * size

    def reduced(table, scale, arrays, places, axis, offsets, after):
        peers, blocks = len(places), scale.shape[0]
        dealt = call(
            functools.partial(gather, places, len(arrays)), [shape(width, trips)] * peers,
            (table, swap(table), scale, after, *arrays),
            [VMEM] * 3 + [ANY] + [VMEM] * len(arrays),
            [pltpu.VMEM((3 * width, blocks * size), BF16)],
            peers * blocks * hot_flops, 8 * blocks * width * size,
        )
        return [dealt[0]] + [swap(part, axis, peers, o) for part, o in zip(dealt[1:], offsets)]

    def item_rows(offset):
        index, row = ids_item[offset]
        return index, [row + 1, row + 2]

    item_parts = reduced(item_table, item_scale, held, [item_rows(o) for o in [0, *met]],
                         "user", met, ids)
    user_parts = reduced(user_table, user_scale, ids_user, [(o, [0]) for o in range(items)],
                         "item", list(range(1, items)), item_parts[0])
    user_base, item_base = call(
        gather_base, [shape(width, trips)] * 2, (user_emb, item_emb, ids),
        [VMEM, VMEM, VMEM], (), 4 * width * trips * size * (user_blocks + item_blocks),
        2 * width * size * (user_blocks + item_blocks),
    )
    user_parts.append(user_base)
    item_parts.append(item_base)
    pieces, pushed = call(
        functools.partial(slopes, len(user_parts), len(item_parts)),
        [shape(width + 8, trips), shape(width, trips)],
        (ids, *user_parts, *item_parts), [VMEM] * (1 + len(user_parts) + len(item_parts)),
        moved=4 * width * trips * (len(user_parts) + len(item_parts) + 2),
    )

    arrays = [pieces, swap(pieces)]
    for offset in range(1, items):
        arrays.append(swap(pieces, "item", items, offset))
        arrays.append(lax.ppermute(pieces, ("item", "rep"), [
            (i, i ^ (2 * offset + 1)) for i in range(2 * items)]))
    user_half_grad, item_keep, item_send = call(
        functools.partial(second_items, len(arrays)),
        [shape(user_blocks, width, size)] + [shape(item_blocks, half, size)] * 2,
        (item_order, user_scale, item_scale, block_vals, *arrays),
        [SMEM] + [VMEM] * (3 + len(arrays)),
        [pltpu.VMEM((user_blocks + 1, width, size), BF16),
         pltpu.VMEM((item_blocks, width, size), F32),
         pltpu.VMEM((len(arrays), 3 * width, trips), BF16)],
        product_flops, product_bytes,
    )
    arrays = [pushed] + [swap(pushed, "user", users, o) for o in back]
    item_grad = call(
        functools.partial(scatter_items, [item_rows(o) for o in [0, *back]]),
        shape(item_blocks, width, size),
        (item_send, *arrays, *held), [ANY] + [VMEM] * (users + len(held)),
        [pltpu.VMEM((users, 3 * width, trips), BF16)], HEAVY, 0,
    )

    per = item_blocks // users
    dealt = call(
        functools.partial(add_deal, [0, *met]), [shape(per, half, size)] * users,
        (item_keep, swap(item_send), item_grad), [VMEM, VMEM, ANY], (), HEAVY,
    )
    item_half_grad, user_back = call(
        second_users, [shape(item_blocks, width, size), shape(user_blocks, width, size)],
        (user_order, item_grad, swap(item_grad), item_scale, user_scale, block_vals, dealt[0]),
        [SMEM] + [VMEM] * 5 + [ANY],
        [pltpu.VMEM((item_blocks + 1, width, size), BF16),
         pltpu.VMEM((user_blocks, width, size), F32)],
        product_flops, product_bytes,
    )
    parts = [dealt[0]] + [swap(part, "user", users, o) for part, o in zip(dealt[1:], met)]
    item_own = call(sum_after, shape(1, per, half, size), (user_back, *parts),
                    [ANY] + [VMEM] * users,
               moved=4 * (users + 1) * per * half * size)
    known, offsets, step = item_own, [0], users // 2
    item_mine = [(known, offsets)]
    while step >= 1:
        come = swap(known, "user", users, step)
        item_mine = [(known, offsets), (come, [offset ^ step for offset in offsets])]
        offsets = offsets + item_mine[1][1]
        if step > 1:
            known = call(pack, shape(len(offsets), per, half, size), (known, come), [VMEM] * 2,
                         (), HEAVY)
        step //= 2
    item_places = [places for _, places in item_mine]
    item_mine = [part for part, _ in item_mine]
    item_other = [swap(part) for part in item_mine]

    user_keep, user_send = call(
        halves_after, [shape(user_blocks, half, size)] * 2, (user_back, item_own), [VMEM, ANY],
        moved=8 * user_blocks * width * size,
    )
    own = call(sum_parts, shape(user_blocks, half, size), (user_keep, swap(user_send)),
               [VMEM, VMEM], moved=12 * user_blocks * half * size)
    mine = call(sum_parts, shape(user_blocks, half, size),
                (own, *[swap(own, "item", items, o) for o in range(1, items)]),
                [VMEM] * items, moved=12 * user_blocks * half * size)
    return call(
        functools.partial(finish, item_places),
        (shape(width, user_blocks * size), shape(width, item_blocks * size)),
        (user_half_grad, mine, swap(mine), item_half_grad, *item_mine, *item_other),
        [VMEM] * (4 + 2 * len(item_mine)), moved=12 * (user_blocks + item_blocks) * width * size,
    )


def solution(mesh):
    return jax.shard_map(
        functools.partial(on_device, mesh.shape["user"], mesh.shape["item"]),
        mesh=mesh,
        in_specs=(
            P(None, ("groups", "user")),
            P(None, ("groups", "item")),
            P(("groups", "user")),
            P(("groups", "item")),
            P(("groups", "user", "item", "rep"), None, None),
            P(("groups", "user", "item", "rep")),
            P(("groups", "user", "item", "rep")),
            P(("groups", "user", "item", "rep")),
            P(("groups", "user", "item", "rep")),
            P(("groups", "user", "item", "rep")),
            P(("groups", "user", "item", "rep")),
        ),
        out_specs=(P(None, ("groups", "user")), P(None, ("groups", "item"))),
        check_vma=False,
    )
```

```python
import functools

import jax
import jax.numpy as jnp
from jax import lax
from jax.experimental import pallas as pl
from jax.experimental.pallas import tpu as pltpu
from jax.sharding import PartitionSpec as P

F32 = jnp.float32
BF16 = jnp.bfloat16
PACK = 4
GROUP = 8
ID_ROWS = 64
HEAVY = 10 ** 11

VMEM = pl.BlockSpec(memory_space=pltpu.VMEM)
SMEM = pl.BlockSpec(memory_space=pltpu.SMEM)
ANY = pl.BlockSpec(memory_space=pl.ANY)
HBM = pl.BlockSpec(memory_space=pltpu.HBM)


def call(kernel, outs, ins, specs, scratch=(), flops=0, moved=0, room=16):
    return pl.pallas_call(
        kernel,
        out_shape=outs,
        in_specs=specs,
        out_specs=jax.tree.map(lambda _: VMEM, outs),
        scratch_shapes=list(scratch),
        cost_estimate=pl.CostEstimate(flops=flops, bytes_accessed=moved, transcendentals=0),
        compiler_params=pltpu.CompilerParams(vmem_limit_bytes=room * 1024 * 1024),
    )(*ins)


def hold(values, *after, flops=0):
    return pl.pallas_call(
        nothing,
        out_shape=jax.ShapeDtypeStruct(values.shape, values.dtype),
        in_specs=[ANY] * (1 + len(after)),
        out_specs=ANY,
        input_output_aliases={0: 0},
        cost_estimate=pl.CostEstimate(flops=flops, bytes_accessed=0, transcendentals=0),
    )(values, *after)


def shape(*dims):
    return jax.ShapeDtypeStruct(dims, F32)


def split3(values):
    high = values.astype(BF16)
    rest = values - high.astype(F32)
    middle = rest.astype(BF16)
    low = (rest - middle.astype(F32)).astype(BF16)
    return high, middle, low


def hot(ids, start, tile):
    if len(ids) == 2:
        same = ids[0] == ids[1]
        ids = [jnp.where(same, -1, each) for each in ids]
    ids = [each.astype(jnp.int16) for each in ids]
    place = lax.broadcasted_iota(jnp.int16, (tile, ids[0].shape[1]), 0) + jnp.int16(start)
    chosen = jnp.zeros(place.shape, BF16)
    for each, sign in zip(ids, (1, -1)):
        chosen = jnp.where(place == each, jnp.asarray(sign, BF16), chosen)
    return chosen


def sort_slots(keys, sources, count, blocks):
    lanes = keys.shape[1]
    rows = 2 * blocks
    place = lax.broadcasted_iota(jnp.int32, (1, lanes), 1)
    live = place < count
    mine = (lax.broadcasted_iota(jnp.int32, (rows, lanes), 0) == keys) & live
    mine = jnp.where(mine, 1.0, 0.0)
    earlier = lax.broadcasted_iota(jnp.int32, (lanes, lanes), 0) < lax.broadcasted_iota(
        jnp.int32, (lanes, lanes), 1)
    before = jnp.dot(mine.astype(BF16), jnp.where(earlier, 1.0, 0.0).astype(BF16),
                     preferred_element_type=F32)
    packs = jnp.floor((jnp.sum(mine, axis=1, keepdims=True) + (PACK - 1)) * (1.0 / PACK))
    packs = jnp.broadcast_to(packs, (rows, 128))
    lower = lax.broadcasted_iota(jnp.int32, (rows, rows), 1) < lax.broadcasted_iota(
        jnp.int32, (rows, rows), 0)
    first = jnp.dot(jnp.where(lower, 1.0, 0.0).astype(BF16), packs.astype(BF16),
                    preferred_element_type=F32)
    position = jnp.sum(mine * (first[:, :1] * PACK + before), axis=0, keepdims=True)
    position = jnp.where(live, position.astype(jnp.int32), -1)
    match = lax.broadcasted_iota(jnp.int32, (lanes, lanes), 0) == position
    row = lax.broadcasted_iota(jnp.int32, (16, lanes), 0)
    values = jnp.where(row == 0, place // 16, jnp.where(row == 1, place % 16, jnp.where(
        row == 2, sources, jnp.where(row == 3, keys, jnp.where(row == 4, 1, 0)))))
    values = jnp.where(live, values, 0).astype(F32)
    found = lax.dot_general(values.astype(BF16), jnp.where(match, 1.0, 0.0).astype(BF16),
                            (((1,), (1,)), ((), ())), preferred_element_type=F32)
    found = found.astype(jnp.int32)
    valid = found[4:5] > 0
    total = jnp.broadcast_to(jnp.sum(packs[:, :1], axis=0, keepdims=True), (1, lanes))
    row = lax.broadcasted_iota(jnp.int32, (4, lanes), 0)
    slot = found[0:1] * 16 + found[1:2]
    source = jnp.where(valid, found[2:3], blocks)
    target = jnp.where(valid, found[3:4], 0)
    return jnp.where(row == 0, slot, jnp.where(row == 1, source, jnp.where(
        row == 2, target, total.astype(jnp.int32))))


def multiply_blocks(order, vals, source, total, across):
    _, width, size = source.shape
    total[...] = jnp.zeros_like(total)
    contract = (((1,), (1,)), ((), ())) if across else (((1,), (0,)), ((), ()))

    def group(index, _):
        targets, terms = [], []
        for step in range(GROUP):
            left, right = [], []
            for half in range(2):
                first = ((index * GROUP + step) * 2 + half) * PACK
                places = [first + each for each in range(PACK)]
                left.append(jnp.concatenate([source[order[1, each]] for each in places], axis=1))
                right.append(jnp.concatenate([vals[order[0, each]] for each in places],
                                             axis=1 if across else 0))
                targets.append(order[2, first])
            both = lax.dot_general(
                jnp.concatenate(left, axis=0), jnp.concatenate(right, axis=0 if across else 1),
                contract, preferred_element_type=F32,
            )
            terms += [both[:width, :size], both[width:, size:]]
        for target, term in zip(targets, terms):
            total[target] += term
        return 0

    lax.fori_loop(0, (order[3, 0] + 2 * GROUP - 1) // (2 * GROUP), group, 0)


def begin(out):
    out[...] = jnp.zeros_like(out)


def stack_ids(user, positive, negative, after, out):
    out[...] = jnp.zeros_like(out)
    for row, ids in enumerate((user, positive, negative)):
        out[row:row + 1, :] = ids[...]


def pack_ids(places, *refs):
    out = refs[-1]
    out[...] = jnp.zeros_like(out)
    for offset, (index, row) in enumerate(places):
        out[3 * offset:3 * offset + 3, :] = refs[index][row:row + 3, :]


def prepare(count, rows, columns, user_emb, item_emb, user_deg, item_deg, after,
            user_source, item_source, user_scale, item_scale, item_order, user_order, keys):
    live = count[0]
    slots = rows.shape[0]
    keys[...] = jnp.zeros_like(keys)
    keys[0:1, 0:slots] = rows[...].reshape(1, slots)
    keys[1:2, 0:slots] = columns[...].reshape(1, slots)
    users, items = keys[0:1, :], keys[1:2, :]
    item_order[...] = sort_slots(items, users, live, item_scale.shape[0])
    user_order[...] = sort_slots(users, items, live, user_scale.shape[0])
    for emb, deg, scale, into in ((user_emb, user_deg, user_scale, user_source),
                                  (item_emb, item_deg, item_scale, item_source)):
        scale[...] = lax.rsqrt(deg[...].astype(F32))
        blocks, size = scale.shape
        for block in range(blocks):
            piece = emb[:, block * size:(block + 1) * size].astype(F32)
            into[block] = (scale[block:block + 1, :] * piece).astype(BF16)
        into[blocks] = jnp.zeros(into.shape[1:], BF16)


def first_pass(across, order, vals, source, *refs):
    multiply_blocks(order, vals, source, refs[-1], across)


def fold(stacked, width):
    return (
        stacked[:width] + stacked[width:2 * width] + stacked[2 * width:3 * width]
    )


def rows_of(ref, rows):
    return [ref[row:row + 1, :] for row in rows]


def pick(table, ids, tile):
    total = None
    for start in range(0, table.shape[1], tile):
        term = jnp.dot(
            table[:, start:start + tile], hot(ids, start, tile),
            preferred_element_type=F32,
        )
        total = term if total is None else total + term
    return total


def gather(places, count, mine, other, scale, after, *refs):
    ids, outs, table = refs[:count], refs[count:-1], refs[-1]
    blocks, width, size = mine.shape
    for block in range(blocks):
        span = slice(block * size, (block + 1) * size)
        here = scale[block:block + 1, :] * (mine[block] + other[block])
        for part, piece in enumerate(split3(here)):
            table[part * width:(part + 1) * width, span] = piece
    for out, (index, rows) in zip(outs, places):
        out[...] = fold(pick(table, rows_of(ids[index], rows), 2 * size), width)


def scatter(pieces, ids, table, blocks, size, put):
    width = table.shape[1] // 3
    tile = 2 * size
    for place, piece in enumerate(pieces):
        for part, value in enumerate(split3(piece[:width, :])):
            table[place, part * width:(part + 1) * width, :] = value
    for start in range(0, blocks * size, tile):
        total = None
        for place, rows in enumerate(ids):
            term = lax.dot_general(
                table[place], hot(rows, start, tile), (((1,), (1,)), ((), ())),
                preferred_element_type=F32,
            )
            total = term if total is None else total + term
        total = fold(total, width)
        for offset in range(0, tile, size):
            put((start + offset) // size, total[:, offset:offset + size])


def scatter_items(places, after, *refs):
    peers = len(places)
    pieces, ids, out, table = refs[:peers], refs[peers:-2], refs[-2], refs[-1]
    blocks, _, size = out.shape

    def put(block, value):
        out[block] = value

    scatter(pieces, [rows_of(ids[index], rows) for index, rows in places],
            table, blocks, size, put)


def gather_base(user_emb, item_emb, ids, user_out, item_out):
    tile = ids.shape[1]
    user_out[...] = pick(user_emb, rows_of(ids, [0]), tile)
    item_out[...] = pick(item_emb, rows_of(ids, [1, 2]), tile)


def add_all(refs):
    total = refs[0][...]
    for ref in refs[1:]:
        total = total + ref[...]
    return total


def slopes(user_parts, item_parts, ids, *refs):
    users, items = refs[:user_parts], refs[user_parts:user_parts + item_parts]
    pieces, pushed = refs[user_parts + item_parts:]
    width = pushed.shape[0]
    user_rows = 0.5 * add_all(users)
    difference = 0.5 * add_all(items)
    margin = jnp.sum(user_rows * difference, axis=0, keepdims=True)
    slope = -jax.nn.sigmoid(-margin)
    pieces[:width, :] = slope * difference
    pieces[width:, :] = jnp.broadcast_to(ids[0:1, :].astype(F32), (8, ids.shape[1]))
    pushed[...] = slope * user_rows


def halves(total, keep, send):
    me = lax.axis_index("rep")
    half = keep.shape[1]
    for block in range(keep.shape[0]):
        keep[block] = total[block, pl.ds(pl.multiple_of(me * half, half), half), :]
        send[block] = total[block, pl.ds(pl.multiple_of((1 - me) * half, half), half), :]


def second_items(parts, order, source_scale, target_scale, vals, *refs):
    pieces = refs[:parts]
    half_grad, keep, send, source, total, table = refs[parts:]
    blocks, width, size = half_grad.shape

    def put(block, grad):
        half_grad[block] = 0.5 * grad
        source[block] = (source_scale[block:block + 1, :] * grad * 0.5).astype(BF16)

    ids = [[piece[width:width + 1, :].astype(jnp.int32)] for piece in pieces]
    scatter(pieces, ids, table, blocks, size, put)
    source[blocks] = jnp.zeros((width, size), BF16)
    multiply_blocks(order, vals, source, total, False)
    for block in range(total.shape[0]):
        total[block] = target_scale[block:block + 1, :] * total[block]
    halves(total, keep, send)


def second_users(order, mine, other, source_scale, target_scale, vals, after,
                 half_grad, keep, send, source, total):
    blocks, width, size = mine.shape
    for block in range(blocks):
        grad = mine[block] + other[block]
        half_grad[block] = 0.5 * grad
        source[block] = (source_scale[block:block + 1, :] * grad * 0.5).astype(BF16)
    source[blocks] = jnp.zeros((width, size), BF16)
    multiply_blocks(order, vals, source, total, True)
    for block in range(total.shape[0]):
        total[block] = target_scale[block:block + 1, :] * total[block]
    halves(total, keep, send)


def nothing(*refs):
    pass


def add_deal(offsets, keep, received, after, *outs):
    me = lax.axis_index("user")
    per = outs[0].shape[0]
    for out, offset in zip(outs, offsets):
        there = (me ^ offset) * per
        for block in range(per):
            out[block] = keep[there + block] + received[there + block]


def sum_parts(*refs):
    refs[-1][...] = add_all(refs[:-1])


def sum_after(count, *refs):
    sum_parts(*refs[count:])


def pack(*refs):
    for place, ref in enumerate(refs[:-1]):
        refs[-1][place] = ref[...]


def finish(offsets, user_half_grad, user_mine, user_other, item_half_grad, item_mine, item_other,
           user_out, item_out):
    finish_users(user_half_grad, user_mine, user_other, user_out)
    finish_items(offsets, item_half_grad, item_mine, item_other, item_out)


def finish_users(half_grad, mine, other, out):
    me = lax.axis_index("rep")
    blocks, width, size = half_grad.shape
    half = width // 2
    for block in range(blocks):
        span = slice(block * size, (block + 1) * size)
        for rank, part in ((me, mine), (1 - me, other)):
            rows = pl.ds(pl.multiple_of(rank * half, half), half)
            out[rows, span] = half_grad[block, rows, :] + part[block]


def finish_items(offsets, half_grad, mine, other, out):
    me = lax.axis_index("rep")
    place = lax.axis_index("user")
    _, per, half, size = mine.shape
    for index, offset in enumerate(offsets):
        there = (place ^ offset) * per
        for block in range(per):
            span = pl.ds(pl.multiple_of((there + block) * size, size), size)
            for rank, part in ((me, mine), (1 - me, other)):
                rows = pl.ds(pl.multiple_of(rank * half, half), half)
                out[rows, span] = half_grad[there + block, rows, :] + part[index, block]


def swap(values, axis="rep", peers=2, offset=1):
    return lax.ppermute(values, axis, [(i, i ^ offset) for i in range(peers)])


def on_device(users, items, user_emb, item_emb, user_deg, item_deg, block_vals, block_row,
              block_col, block_count, trip_user, trip_pos, trip_neg):
    width = user_emb.shape[0]
    slots, size, _ = block_vals.shape
    user_blocks = user_emb.shape[1] // size
    item_blocks = item_emb.shape[1] // size
    trips = trip_user.shape[0]
    half = width // 2
    user_deg = user_deg.reshape(user_blocks, size)
    item_deg = item_deg.reshape(item_blocks, size)

    product_flops = 2 * slots * size * size * width
    product_bytes = slots * size * size * 2
    started = call(begin, shape(8, size), (), [], (), 16 * product_flops, product_bytes)
    ids_shape = jax.ShapeDtypeStruct((ID_ROWS, trips), jnp.int32)
    ids = call(
        stack_ids, ids_shape,
        [each.reshape(1, trips) for each in (trip_user, trip_pos, trip_neg)] + [started],
        [VMEM, VMEM, VMEM, ANY],
    )
    ids_user = [ids] + [swap(ids, "item", items, o) for o in range(1, items)]
    met = sorted(range(1, users), key=lambda offset: (offset != users // 2, -offset))
    back = met[::-1]
    ids_item, held, step = [(0, 0)], [ids], 1
    while step < users:
        packed = ids if step == 1 else call(
            functools.partial(pack_ids, ids_item), ids_shape, held, [VMEM] * len(held))
        held.append(swap(packed, "user", users, step))
        ids_item += [(len(held) - 1, 3 * place) for place in range(step)]
        step *= 2
    lanes = -(-slots // size) * size

    order_shape = jax.ShapeDtypeStruct((4, lanes), jnp.int32)

    def source_shape(blocks):
        return jax.ShapeDtypeStruct((blocks + 1, width, size), BF16)

    (user_source, item_source, user_scale, item_scale, item_order, user_order) = call(
        prepare,
        [source_shape(user_blocks), source_shape(item_blocks), shape(user_blocks, size),
         shape(item_blocks, size), order_shape, order_shape],
        (block_count, block_row, block_col, user_emb, item_emb, user_deg, item_deg, ids),
        [SMEM, VMEM, VMEM, VMEM, VMEM, VMEM, VMEM, ANY],
        [pltpu.VMEM((8, lanes), jnp.int32)], product_flops, product_bytes,
    )
    item_table = call(
        functools.partial(first_pass, False), shape(item_blocks, width, size),
        (item_order, block_vals, user_source, ids), [SMEM, VMEM, VMEM, ANY], (),
        product_flops, product_bytes,
    )
    ids_here = [*held[1:], *ids_user[1:]]
    user_table = call(
        functools.partial(first_pass, True), shape(user_blocks, width, size),
        (user_order, block_vals, item_source, item_table, *ids_here),
        [SMEM, VMEM, VMEM] + [ANY] * (1 + len(ids_here)), (),
        product_flops, product_bytes,
    )

    hot_flops = 2 * 3 * width * trips * size

    def reduced(table, scale, arrays, places, axis, offsets, after):
        peers, blocks = len(places), scale.shape[0]
        dealt = call(
            functools.partial(gather, places, len(arrays)), [shape(width, trips)] * peers,
            (table, swap(table), scale, after, *arrays),
            [VMEM] * 3 + [ANY] + [VMEM] * len(arrays),
            [pltpu.VMEM((3 * width, blocks * size), BF16)],
            peers * blocks * hot_flops, 8 * blocks * width * size,
        )
        return [dealt[0]] + [swap(part, axis, peers, o) for part, o in zip(dealt[1:], offsets)]

    def item_rows(offset):
        index, row = ids_item[offset]
        return index, [row + 1, row + 2]

    item_parts = reduced(item_table, item_scale, held, [item_rows(o) for o in [0, *met]],
                         "user", met, ids)
    user_parts = reduced(user_table, user_scale, ids_user, [(o, [0]) for o in range(items)],
                         "item", list(range(1, items)), item_parts[0])
    user_base, item_base = call(
        gather_base, [shape(width, trips)] * 2, (user_emb, item_emb, ids),
        [VMEM, VMEM, VMEM], (), 4 * width * trips * size * (user_blocks + item_blocks),
        2 * width * size * (user_blocks + item_blocks),
    )
    user_parts.append(user_base)
    item_parts.append(item_base)
    pieces, pushed = call(
        functools.partial(slopes, len(user_parts), len(item_parts)),
        [shape(width + 8, trips), shape(width, trips)],
        (ids, *user_parts, *item_parts), [VMEM] * (1 + len(user_parts) + len(item_parts)),
        moved=4 * width * trips * (len(user_parts) + len(item_parts) + 2),
    )

    arrays = [pieces, swap(pieces)]
    for offset in range(1, items):
        arrays.append(swap(pieces, "item", items, offset))
        arrays.append(lax.ppermute(pieces, ("item", "rep"), [
            (i, i ^ (2 * offset + 1)) for i in range(2 * items)]))
    user_half_grad, item_keep, item_send = call(
        functools.partial(second_items, len(arrays)),
        [shape(user_blocks, width, size)] + [shape(item_blocks, half, size)] * 2,
        (item_order, user_scale, item_scale, block_vals, *arrays),
        [SMEM] + [VMEM] * (3 + len(arrays)),
        [pltpu.VMEM((user_blocks + 1, width, size), BF16),
         pltpu.VMEM((item_blocks, width, size), F32),
         pltpu.VMEM((len(arrays), 3 * width, trips), BF16)],
        product_flops, product_bytes,
    )
    arrays = [pushed] + [swap(pushed, "user", users, o) for o in back]
    item_grad = call(
        functools.partial(scatter_items, [item_rows(o) for o in [0, *back]]),
        shape(item_blocks, width, size),
        (item_send, *arrays, *held), [ANY] + [VMEM] * (users + len(held)),
        [pltpu.VMEM((users, 3 * width, trips), BF16)], HEAVY, 0,
    )

    per = item_blocks // users
    dealt = call(
        functools.partial(add_deal, [0, *met]), [shape(per, half, size)] * users,
        (item_keep, swap(item_send), item_grad), [VMEM, VMEM, ANY], (), HEAVY,
    )
    item_half_grad, user_keep, user_send = call(
        second_users,
        [shape(item_blocks, width, size)] + [shape(user_blocks, half, size)] * 2,
        (user_order, item_grad, swap(item_grad), item_scale, user_scale, block_vals, dealt[0]),
        [SMEM] + [VMEM] * 5 + [ANY],
        [pltpu.VMEM((item_blocks + 1, width, size), BF16),
         pltpu.VMEM((user_blocks, width, size), F32)],
        product_flops, product_bytes,
    )
    parts = [dealt[0]] + [swap(part, "user", users, o) for part, o in zip(dealt[1:], met)]
    item_own = call(functools.partial(sum_after, 1), shape(per, half, size), (user_keep, *parts),
                    [ANY] + [VMEM] * users,
               moved=4 * (users + 1) * per * half * size)
    item_mine, step = {0: item_own}, users // 2
    while step >= 1:
        for offset, part in list(item_mine.items()):
            item_mine[offset ^ step] = swap(part, "user", users, step)
        if step > 1:
            item_mine[step] = hold(item_mine[step], flops=HEAVY)
        step //= 2
    item_places = list(item_mine)
    item_mine = call(pack, shape(users, per, half, size), tuple(item_mine.values()),
                     [VMEM] * users, moved=8 * item_blocks * half * size)
    user_send = hold(user_send, item_own)

    own = call(sum_parts, shape(user_blocks, half, size), (user_keep, swap(user_send)),
               [VMEM, VMEM], moved=12 * user_blocks * half * size)
    mine = call(functools.partial(sum_after, 1), shape(user_blocks, half, size),
                (item_mine, own, *[swap(own, "item", items, o) for o in range(1, items)]),
                [ANY] + [VMEM] * items, moved=12 * user_blocks * half * size)
    return call(
        functools.partial(finish, item_places),
        (shape(width, user_blocks * size), shape(width, item_blocks * size)),
        (user_half_grad, mine, swap(mine), item_half_grad, item_mine, swap(item_mine)),
        [VMEM] * 6, moved=12 * (user_blocks + item_blocks) * width * size,
    )


def solution(mesh):
    return jax.shard_map(
        functools.partial(on_device, mesh.shape["user"], mesh.shape["item"]),
        mesh=mesh,
        in_specs=(
            P(None, ("groups", "user")),
            P(None, ("groups", "item")),
            P(("groups", "user")),
            P(("groups", "item")),
            P(("groups", "user", "item", "rep"), None, None),
            P(("groups", "user", "item", "rep")),
            P(("groups", "user", "item", "rep")),
            P(("groups", "user", "item", "rep")),
            P(("groups", "user", "item", "rep")),
            P(("groups", "user", "item", "rep")),
            P(("groups", "user", "item", "rep")),
        ),
        out_specs=(P(None, ("groups", "user")), P(None, ("groups", "item"))),
        check_vma=False,
    )
```

```python
import functools

import jax
import jax.numpy as jnp
from jax import lax
from jax.experimental import pallas as pl
from jax.experimental.pallas import tpu as pltpu
from jax.sharding import PartitionSpec as P

F32 = jnp.float32
BF16 = jnp.bfloat16
PACK = 4
GROUP = 8
ID_ROWS = 64
HEAVY = 10 ** 11

VMEM = pl.BlockSpec(memory_space=pltpu.VMEM)
SMEM = pl.BlockSpec(memory_space=pltpu.SMEM)
ANY = pl.BlockSpec(memory_space=pl.ANY)
HBM = pl.BlockSpec(memory_space=pltpu.HBM)


def call(kernel, outs, ins, specs, scratch=(), flops=0, moved=0, room=16):
    return pl.pallas_call(
        kernel,
        out_shape=outs,
        in_specs=specs,
        out_specs=jax.tree.map(lambda _: VMEM, outs),
        scratch_shapes=list(scratch),
        cost_estimate=pl.CostEstimate(flops=flops, bytes_accessed=moved, transcendentals=0),
        compiler_params=pltpu.CompilerParams(vmem_limit_bytes=room * 1024 * 1024),
    )(*ins)


def hold(values, *after, flops=0):
    return call(copy, jax.ShapeDtypeStruct(values.shape, values.dtype), (values, *after),
                [VMEM] + [ANY] * len(after), flops=flops)


def shape(*dims):
    return jax.ShapeDtypeStruct(dims, F32)


def split3(values):
    high = values.astype(BF16)
    rest = values - high.astype(F32)
    middle = rest.astype(BF16)
    low = (rest - middle.astype(F32)).astype(BF16)
    return high, middle, low


def hot(ids, start, tile):
    if len(ids) == 2:
        same = ids[0] == ids[1]
        ids = [jnp.where(same, -1, each) for each in ids]
    ids = [each.astype(jnp.int16) for each in ids]
    place = lax.broadcasted_iota(jnp.int16, (tile, ids[0].shape[1]), 0) + jnp.int16(start)
    chosen = jnp.zeros(place.shape, BF16)
    for each, sign in zip(ids, (1, -1)):
        chosen = jnp.where(place == each, jnp.asarray(sign, BF16), chosen)
    return chosen


def sort_slots(keys, sources, count, blocks):
    lanes = keys.shape[1]
    rows = 2 * blocks
    place = lax.broadcasted_iota(jnp.int32, (1, lanes), 1)
    live = place < count
    mine = (lax.broadcasted_iota(jnp.int32, (rows, lanes), 0) == keys) & live
    mine = jnp.where(mine, 1.0, 0.0)
    earlier = lax.broadcasted_iota(jnp.int32, (lanes, lanes), 0) < lax.broadcasted_iota(
        jnp.int32, (lanes, lanes), 1)
    before = jnp.dot(mine.astype(BF16), jnp.where(earlier, 1.0, 0.0).astype(BF16),
                     preferred_element_type=F32)
    packs = jnp.floor((jnp.sum(mine, axis=1, keepdims=True) + (PACK - 1)) * (1.0 / PACK))
    packs = jnp.broadcast_to(packs, (rows, 128))
    lower = lax.broadcasted_iota(jnp.int32, (rows, rows), 1) < lax.broadcasted_iota(
        jnp.int32, (rows, rows), 0)
    first = jnp.dot(jnp.where(lower, 1.0, 0.0).astype(BF16), packs.astype(BF16),
                    preferred_element_type=F32)
    position = jnp.sum(mine * (first[:, :1] * PACK + before), axis=0, keepdims=True)
    position = jnp.where(live, position.astype(jnp.int32), -1)
    match = lax.broadcasted_iota(jnp.int32, (lanes, lanes), 0) == position
    row = lax.broadcasted_iota(jnp.int32, (16, lanes), 0)
    values = jnp.where(row == 0, place // 16, jnp.where(row == 1, place % 16, jnp.where(
        row == 2, sources, jnp.where(row == 3, keys, jnp.where(row == 4, 1, 0)))))
    values = jnp.where(live, values, 0).astype(F32)
    found = lax.dot_general(values.astype(BF16), jnp.where(match, 1.0, 0.0).astype(BF16),
                            (((1,), (1,)), ((), ())), preferred_element_type=F32)
    found = found.astype(jnp.int32)
    valid = found[4:5] > 0
    total = jnp.broadcast_to(jnp.sum(packs[:, :1], axis=0, keepdims=True), (1, lanes))
    row = lax.broadcasted_iota(jnp.int32, (4, lanes), 0)
    slot = found[0:1] * 16 + found[1:2]
    source = jnp.where(valid, found[2:3], blocks)
    target = jnp.where(valid, found[3:4], 0)
    return jnp.where(row == 0, slot, jnp.where(row == 1, source, jnp.where(
        row == 2, target, total.astype(jnp.int32))))


def multiply_blocks(order, vals, source, total, across):
    _, width, size = source.shape
    total[...] = jnp.zeros_like(total)
    contract = (((1,), (1,)), ((), ())) if across else (((1,), (0,)), ((), ()))

    def group(index, _):
        targets, terms = [], []
        for step in range(GROUP):
            left, right = [], []
            for half in range(2):
                first = ((index * GROUP + step) * 2 + half) * PACK
                places = [first + each for each in range(PACK)]
                left.append(jnp.concatenate([source[order[1, each]] for each in places], axis=1))
                right.append(jnp.concatenate([vals[order[0, each]] for each in places],
                                             axis=1 if across else 0))
                targets.append(order[2, first])
            both = lax.dot_general(
                jnp.concatenate(left, axis=0), jnp.concatenate(right, axis=0 if across else 1),
                contract, preferred_element_type=F32,
            )
            terms += [both[:width, :size], both[width:, size:]]
        for target, term in zip(targets, terms):
            total[target] += term
        return 0

    lax.fori_loop(0, (order[3, 0] + 2 * GROUP - 1) // (2 * GROUP), group, 0)


def begin(out):
    out[...] = jnp.zeros_like(out)


def stack_ids(user, positive, negative, after, out):
    out[...] = jnp.zeros_like(out)
    for row, ids in enumerate((user, positive, negative)):
        out[row:row + 1, :] = ids[...]


def pack_ids(places, *refs):
    out = refs[-1]
    out[...] = jnp.zeros_like(out)
    for offset, (index, row) in enumerate(places):
        out[3 * offset:3 * offset + 3, :] = refs[index][row:row + 3, :]


def prepare(count, rows, columns, user_emb, item_emb, user_deg, item_deg, after,
            user_source, item_source, user_scale, item_scale, item_order, user_order, keys):
    live = count[0]
    slots = rows.shape[0]
    keys[...] = jnp.zeros_like(keys)
    keys[0:1, 0:slots] = rows[...].reshape(1, slots)
    keys[1:2, 0:slots] = columns[...].reshape(1, slots)
    users, items = keys[0:1, :], keys[1:2, :]
    item_order[...] = sort_slots(items, users, live, item_scale.shape[0])
    user_order[...] = sort_slots(users, items, live, user_scale.shape[0])
    for emb, deg, scale, into in ((user_emb, user_deg, user_scale, user_source),
                                  (item_emb, item_deg, item_scale, item_source)):
        scale[...] = lax.rsqrt(deg[...].astype(F32))
        blocks, size = scale.shape
        for block in range(blocks):
            piece = emb[:, block * size:(block + 1) * size].astype(F32)
            into[block] = (scale[block:block + 1, :] * piece).astype(BF16)
        into[blocks] = jnp.zeros(into.shape[1:], BF16)


def first_pass(across, order, vals, source, *refs):
    multiply_blocks(order, vals, source, refs[-1], across)


def fold(stacked, width):
    return (
        stacked[:width] + stacked[width:2 * width] + stacked[2 * width:3 * width]
    )


def rows_of(ref, rows):
    return [ref[row:row + 1, :] for row in rows]


def pick(table, ids, tile):
    total = None
    for start in range(0, table.shape[1], tile):
        term = jnp.dot(
            table[:, start:start + tile], hot(ids, start, tile),
            preferred_element_type=F32,
        )
        total = term if total is None else total + term
    return total


def gather(places, count, mine, other, scale, after, *refs):
    ids, outs, table = refs[:count], refs[count:-1], refs[-1]
    blocks, width, size = mine.shape
    for block in range(blocks):
        span = slice(block * size, (block + 1) * size)
        here = scale[block:block + 1, :] * (mine[block] + other[block])
        for part, piece in enumerate(split3(here)):
            table[part * width:(part + 1) * width, span] = piece
    for out, (index, rows) in zip(outs, places):
        out[...] = fold(pick(table, rows_of(ids[index], rows), 2 * size), width)


def scatter(pieces, ids, table, blocks, size, put):
    width = table.shape[1] // 3
    tile = 2 * size
    for place, piece in enumerate(pieces):
        for part, value in enumerate(split3(piece[:width, :])):
            table[place, part * width:(part + 1) * width, :] = value
    for start in range(0, blocks * size, tile):
        total = None
        for place, rows in enumerate(ids):
            term = lax.dot_general(
                table[place], hot(rows, start, tile), (((1,), (1,)), ((), ())),
                preferred_element_type=F32,
            )
            total = term if total is None else total + term
        total = fold(total, width)
        for offset in range(0, tile, size):
            put((start + offset) // size, total[:, offset:offset + size])


def scatter_items(places, after, *refs):
    peers = len(places)
    pieces, ids, out, table = refs[:peers], refs[peers:-2], refs[-2], refs[-1]
    blocks, _, size = out.shape

    def put(block, value):
        out[block] = value

    scatter(pieces, [rows_of(ids[index], rows) for index, rows in places],
            table, blocks, size, put)


def gather_base(user_emb, item_emb, ids, user_out, item_out):
    tile = ids.shape[1]
    user_out[...] = pick(user_emb, rows_of(ids, [0]), tile)
    item_out[...] = pick(item_emb, rows_of(ids, [1, 2]), tile)


def add_all(refs):
    total = refs[0][...]
    for ref in refs[1:]:
        total = total + ref[...]
    return total


def slopes(user_parts, item_parts, ids, *refs):
    users, items = refs[:user_parts], refs[user_parts:user_parts + item_parts]
    pieces, pushed = refs[user_parts + item_parts:]
    width = pushed.shape[0]
    user_rows = 0.5 * add_all(users)
    difference = 0.5 * add_all(items)
    margin = jnp.sum(user_rows * difference, axis=0, keepdims=True)
    slope = -jax.nn.sigmoid(-margin)
    pieces[:width, :] = slope * difference
    pieces[width:, :] = jnp.broadcast_to(ids[0:1, :].astype(F32), (8, ids.shape[1]))
    pushed[...] = slope * user_rows


def halves(total, keep, send):
    me = lax.axis_index("rep")
    half = keep.shape[1]
    for block in range(keep.shape[0]):
        keep[block] = total[block, pl.ds(pl.multiple_of(me * half, half), half), :]
        send[block] = total[block, pl.ds(pl.multiple_of((1 - me) * half, half), half), :]


def second_items(parts, order, source_scale, target_scale, vals, *refs):
    pieces = refs[:parts]
    half_grad, keep, send, source, total, table = refs[parts:]
    blocks, width, size = half_grad.shape

    def put(block, grad):
        half_grad[block] = 0.5 * grad
        source[block] = (source_scale[block:block + 1, :] * grad * 0.5).astype(BF16)

    ids = [[piece[width:width + 1, :].astype(jnp.int32)] for piece in pieces]
    scatter(pieces, ids, table, blocks, size, put)
    source[blocks] = jnp.zeros((width, size), BF16)
    multiply_blocks(order, vals, source, total, False)
    for block in range(total.shape[0]):
        total[block] = target_scale[block:block + 1, :] * total[block]
    halves(total, keep, send)


def second_users(order, mine, other, source_scale, target_scale, vals, after,
                 half_grad, keep, send, source, total):
    blocks, width, size = mine.shape
    for block in range(blocks):
        grad = mine[block] + other[block]
        half_grad[block] = 0.5 * grad
        source[block] = (source_scale[block:block + 1, :] * grad * 0.5).astype(BF16)
    source[blocks] = jnp.zeros((width, size), BF16)
    multiply_blocks(order, vals, source, total, True)
    for block in range(total.shape[0]):
        total[block] = target_scale[block:block + 1, :] * total[block]
    halves(total, keep, send)


def copy(values, *refs):
    refs[-1][...] = values[...]


def add_deal(offsets, keep, received, after, *outs):
    me = lax.axis_index("user")
    per = outs[0].shape[0]
    for out, offset in zip(outs, offsets):
        there = (me ^ offset) * per
        for block in range(per):
            out[block] = keep[there + block] + received[there + block]


def sum_parts(*refs):
    refs[-1][...] = add_all(refs[:-1])


def sum_after(count, *refs):
    sum_parts(*refs[count:])


def pack(*refs):
    for place, ref in enumerate(refs[:-1]):
        refs[-1][place] = ref[...]


def finish(offsets, user_half_grad, user_mine, user_other, item_half_grad, item_mine, item_other,
           user_out, item_out):
    finish_users(user_half_grad, user_mine, user_other, user_out)
    finish_items(offsets, item_half_grad, item_mine, item_other, item_out)


def finish_users(half_grad, mine, other, out):
    me = lax.axis_index("rep")
    blocks, width, size = half_grad.shape
    half = width // 2
    for block in range(blocks):
        span = slice(block * size, (block + 1) * size)
        for rank, part in ((me, mine), (1 - me, other)):
            rows = pl.ds(pl.multiple_of(rank * half, half), half)
            out[rows, span] = half_grad[block, rows, :] + part[block]


def finish_items(offsets, half_grad, mine, other, out):
    me = lax.axis_index("rep")
    place = lax.axis_index("user")
    _, per, half, size = mine.shape
    for index, offset in enumerate(offsets):
        there = (place ^ offset) * per
        for block in range(per):
            span = pl.ds(pl.multiple_of((there + block) * size, size), size)
            for rank, part in ((me, mine), (1 - me, other)):
                rows = pl.ds(pl.multiple_of(rank * half, half), half)
                out[rows, span] = half_grad[there + block, rows, :] + part[index, block]


def swap(values, axis="rep", peers=2, offset=1):
    return lax.ppermute(values, axis, [(i, i ^ offset) for i in range(peers)])


def on_device(users, items, user_emb, item_emb, user_deg, item_deg, block_vals, block_row,
              block_col, block_count, trip_user, trip_pos, trip_neg):
    width = user_emb.shape[0]
    slots, size, _ = block_vals.shape
    user_blocks = user_emb.shape[1] // size
    item_blocks = item_emb.shape[1] // size
    trips = trip_user.shape[0]
    half = width // 2
    user_deg = user_deg.reshape(user_blocks, size)
    item_deg = item_deg.reshape(item_blocks, size)

    product_flops = 2 * slots * size * size * width
    product_bytes = slots * size * size * 2
    started = call(begin, shape(8, size), (), [], (), 16 * product_flops, product_bytes)
    ids_shape = jax.ShapeDtypeStruct((ID_ROWS, trips), jnp.int32)
    ids = call(
        stack_ids, ids_shape,
        [each.reshape(1, trips) for each in (trip_user, trip_pos, trip_neg)] + [started],
        [VMEM, VMEM, VMEM, ANY],
    )
    ids_user = [ids] + [swap(ids, "item", items, o) for o in range(1, items)]
    met = sorted(range(1, users), key=lambda offset: (offset != users // 2, -offset))
    back = met[::-1]
    ids_item, held, step = [(0, 0)], [ids], 1
    while step < users:
        packed = ids if step == 1 else call(
            functools.partial(pack_ids, ids_item), ids_shape, held, [VMEM] * len(held))
        held.append(swap(packed, "user", users, step))
        ids_item += [(len(held) - 1, 3 * place) for place in range(step)]
        step *= 2
    lanes = -(-slots // size) * size

    order_shape = jax.ShapeDtypeStruct((4, lanes), jnp.int32)

    def source_shape(blocks):
        return jax.ShapeDtypeStruct((blocks + 1, width, size), BF16)

    (user_source, item_source, user_scale, item_scale, item_order, user_order) = call(
        prepare,
        [source_shape(user_blocks), source_shape(item_blocks), shape(user_blocks, size),
         shape(item_blocks, size), order_shape, order_shape],
        (block_count, block_row, block_col, user_emb, item_emb, user_deg, item_deg, ids),
        [SMEM, VMEM, VMEM, VMEM, VMEM, VMEM, VMEM, ANY],
        [pltpu.VMEM((8, lanes), jnp.int32)], product_flops, product_bytes,
    )
    item_table = call(
        functools.partial(first_pass, False), shape(item_blocks, width, size),
        (item_order, block_vals, user_source, ids), [SMEM, VMEM, VMEM, ANY], (),
        product_flops, product_bytes,
    )
    ids_here = [*held[1:], *ids_user[1:]]
    user_table = call(
        functools.partial(first_pass, True), shape(user_blocks, width, size),
        (user_order, block_vals, item_source, item_table, *ids_here),
        [SMEM, VMEM, VMEM] + [ANY] * (1 + len(ids_here)), (),
        product_flops, product_bytes,
    )

    hot_flops = 2 * 3 * width * trips * size

    def reduced(table, scale, arrays, places, axis, offsets, after):
        peers, blocks = len(places), scale.shape[0]
        dealt = call(
            functools.partial(gather, places, len(arrays)), [shape(width, trips)] * peers,
            (table, swap(table), scale, after, *arrays),
            [VMEM] * 3 + [ANY] + [VMEM] * len(arrays),
            [pltpu.VMEM((3 * width, blocks * size), BF16)],
            peers * blocks * hot_flops, 8 * blocks * width * size,
        )
        return [dealt[0]] + [swap(part, axis, peers, o) for part, o in zip(dealt[1:], offsets)]

    def item_rows(offset):
        index, row = ids_item[offset]
        return index, [row + 1, row + 2]

    item_parts = reduced(item_table, item_scale, held, [item_rows(o) for o in [0, *met]],
                         "user", met, ids)
    user_parts = reduced(user_table, user_scale, ids_user, [(o, [0]) for o in range(items)],
                         "item", list(range(1, items)), item_parts[0])
    user_base, item_base = call(
        gather_base, [shape(width, trips)] * 2, (user_emb, item_emb, ids),
        [VMEM, VMEM, VMEM], (), 4 * width * trips * size * (user_blocks + item_blocks),
        2 * width * size * (user_blocks + item_blocks),
    )
    user_parts.append(user_base)
    item_parts.append(item_base)
    pieces, pushed = call(
        functools.partial(slopes, len(user_parts), len(item_parts)),
        [shape(width + 8, trips), shape(width, trips)],
        (ids, *user_parts, *item_parts), [VMEM] * (1 + len(user_parts) + len(item_parts)),
        moved=4 * width * trips * (len(user_parts) + len(item_parts) + 2),
    )

    arrays = [pieces, swap(pieces)]
    for offset in range(1, items):
        arrays.append(swap(pieces, "item", items, offset))
        arrays.append(lax.ppermute(pieces, ("item", "rep"), [
            (i, i ^ (2 * offset + 1)) for i in range(2 * items)]))
    user_half_grad, item_keep, item_send = call(
        functools.partial(second_items, len(arrays)),
        [shape(user_blocks, width, size)] + [shape(item_blocks, half, size)] * 2,
        (item_order, user_scale, item_scale, block_vals, *arrays),
        [SMEM] + [VMEM] * (3 + len(arrays)),
        [pltpu.VMEM((user_blocks + 1, width, size), BF16),
         pltpu.VMEM((item_blocks, width, size), F32),
         pltpu.VMEM((len(arrays), 3 * width, trips), BF16)],
        product_flops, product_bytes,
    )
    arrays = [pushed] + [swap(pushed, "user", users, o) for o in back]
    item_grad = call(
        functools.partial(scatter_items, [item_rows(o) for o in [0, *back]]),
        shape(item_blocks, width, size),
        (item_send, *arrays, *held), [ANY] + [VMEM] * (users + len(held)),
        [pltpu.VMEM((users, 3 * width, trips), BF16)], HEAVY, 0,
    )

    per = item_blocks // users
    dealt = call(
        functools.partial(add_deal, [0, *met]), [shape(per, half, size)] * users,
        (item_keep, swap(item_send), item_grad), [VMEM, VMEM, ANY], (), HEAVY,
    )
    item_half_grad, user_keep, user_send = call(
        second_users,
        [shape(item_blocks, width, size)] + [shape(user_blocks, half, size)] * 2,
        (user_order, item_grad, swap(item_grad), item_scale, user_scale, block_vals, dealt[0]),
        [SMEM] + [VMEM] * 5 + [ANY],
        [pltpu.VMEM((item_blocks + 1, width, size), BF16),
         pltpu.VMEM((user_blocks, width, size), F32)],
        product_flops, product_bytes,
    )
    parts = [dealt[0]] + [swap(part, "user", users, o) for part, o in zip(dealt[1:], met)]
    item_own = call(functools.partial(sum_after, 1), shape(per, half, size), (user_keep, *parts),
                    [ANY] + [VMEM] * users,
               moved=4 * (users + 1) * per * half * size)
    item_mine, step = {0: item_own}, users // 2
    while step >= 1:
        for offset, part in list(item_mine.items()):
            item_mine[offset ^ step] = swap(part, "user", users, step)
        if step > 1:
            item_mine[step] = hold(item_mine[step], flops=HEAVY)
        step //= 2
    item_places = list(item_mine)
    item_mine = call(pack, shape(users, per, half, size), tuple(item_mine.values()),
                     [VMEM] * users, moved=8 * item_blocks * half * size)
    user_send = hold(user_send, item_own)

    own = call(sum_parts, shape(user_blocks, half, size), (user_keep, swap(user_send)),
               [VMEM, VMEM], moved=12 * user_blocks * half * size)
    mine = call(functools.partial(sum_after, 1), shape(user_blocks, half, size),
                (item_mine, own, *[swap(own, "item", items, o) for o in range(1, items)]),
                [ANY] + [VMEM] * items, moved=12 * user_blocks * half * size)
    return call(
        functools.partial(finish, item_places),
        (shape(width, user_blocks * size), shape(width, item_blocks * size)),
        (user_half_grad, mine, swap(mine), item_half_grad, item_mine, swap(item_mine)),
        [VMEM] * 6, moved=12 * (user_blocks + item_blocks) * width * size,
    )


def solution(mesh):
    return jax.shard_map(
        functools.partial(on_device, mesh.shape["user"], mesh.shape["item"]),
        mesh=mesh,
        in_specs=(
            P(None, ("groups", "user")),
            P(None, ("groups", "item")),
            P(("groups", "user")),
            P(("groups", "item")),
            P(("groups", "user", "item", "rep"), None, None),
            P(("groups", "user", "item", "rep")),
            P(("groups", "user", "item", "rep")),
            P(("groups", "user", "item", "rep")),
            P(("groups", "user", "item", "rep")),
            P(("groups", "user", "item", "rep")),
            P(("groups", "user", "item", "rep")),
        ),
        out_specs=(P(None, ("groups", "user")), P(None, ("groups", "item"))),
        check_vma=False,
    )
```

```python
import functools

import jax
import jax.numpy as jnp
from jax import lax
from jax.experimental import pallas as pl
from jax.experimental.pallas import tpu as pltpu
from jax.sharding import PartitionSpec as P

F32 = jnp.float32
BF16 = jnp.bfloat16
PACK = 4
GROUP = 8
HEAVY = 10 ** 11

VMEM = pl.BlockSpec(memory_space=pltpu.VMEM)
SMEM = pl.BlockSpec(memory_space=pltpu.SMEM)
ANY = pl.BlockSpec(memory_space=pl.ANY)
HBM = pl.BlockSpec(memory_space=pltpu.HBM)


def call(kernel, outs, ins, specs, scratch=(), flops=0, moved=0, room=16):
    return pl.pallas_call(
        kernel,
        out_shape=outs,
        in_specs=specs,
        out_specs=jax.tree.map(lambda _: VMEM, outs),
        scratch_shapes=list(scratch),
        cost_estimate=pl.CostEstimate(flops=flops, bytes_accessed=moved, transcendentals=0),
        compiler_params=pltpu.CompilerParams(vmem_limit_bytes=room * 1024 * 1024),
    )(*ins)


def hold(values, *after, flops=0):
    return call(copy, jax.ShapeDtypeStruct(values.shape, values.dtype), (values, *after),
                [VMEM] + [ANY] * len(after), flops=flops)


def shape(*dims):
    return jax.ShapeDtypeStruct(dims, F32)


def split3(values):
    high = values.astype(BF16)
    rest = values - high.astype(F32)
    middle = rest.astype(BF16)
    low = (rest - middle.astype(F32)).astype(BF16)
    return high, middle, low


def hot(ids, start, tile):
    if len(ids) == 2:
        same = ids[0] == ids[1]
        ids = [jnp.where(same, -1, each) for each in ids]
    ids = [each.astype(jnp.int16) for each in ids]
    place = lax.broadcasted_iota(jnp.int16, (tile, ids[0].shape[1]), 0) + jnp.int16(start)
    chosen = jnp.zeros(place.shape, BF16)
    for each, sign in zip(ids, (1, -1)):
        chosen = jnp.where(place == each, jnp.asarray(sign, BF16), chosen)
    return chosen


def sort_slots(keys, sources, count, blocks):
    lanes = keys.shape[1]
    rows = 2 * blocks
    place = lax.broadcasted_iota(jnp.int32, (1, lanes), 1)
    live = place < count
    mine = (lax.broadcasted_iota(jnp.int32, (rows, lanes), 0) == keys) & live
    mine = jnp.where(mine, 1.0, 0.0)
    earlier = lax.broadcasted_iota(jnp.int32, (lanes, lanes), 0) < lax.broadcasted_iota(
        jnp.int32, (lanes, lanes), 1)
    before = jnp.dot(mine.astype(BF16), jnp.where(earlier, 1.0, 0.0).astype(BF16),
                     preferred_element_type=F32)
    packs = jnp.floor((jnp.sum(mine, axis=1, keepdims=True) + (PACK - 1)) * (1.0 / PACK))
    packs = jnp.broadcast_to(packs, (rows, 128))
    lower = lax.broadcasted_iota(jnp.int32, (rows, rows), 1) < lax.broadcasted_iota(
        jnp.int32, (rows, rows), 0)
    first = jnp.dot(jnp.where(lower, 1.0, 0.0).astype(BF16), packs.astype(BF16),
                    preferred_element_type=F32)
    position = jnp.sum(mine * (first[:, :1] * PACK + before), axis=0, keepdims=True)
    position = jnp.where(live, position.astype(jnp.int32), -1)
    match = lax.broadcasted_iota(jnp.int32, (lanes, lanes), 0) == position
    row = lax.broadcasted_iota(jnp.int32, (16, lanes), 0)
    values = jnp.where(row == 0, place // 16, jnp.where(row == 1, place % 16, jnp.where(
        row == 2, sources, jnp.where(row == 3, keys, jnp.where(row == 4, 1, 0)))))
    values = jnp.where(live, values, 0).astype(F32)
    found = lax.dot_general(values.astype(BF16), jnp.where(match, 1.0, 0.0).astype(BF16),
                            (((1,), (1,)), ((), ())), preferred_element_type=F32)
    found = found.astype(jnp.int32)
    valid = found[4:5] > 0
    total = jnp.broadcast_to(jnp.sum(packs[:, :1], axis=0, keepdims=True), (1, lanes))
    row = lax.broadcasted_iota(jnp.int32, (4, lanes), 0)
    slot = found[0:1] * 16 + found[1:2]
    source = jnp.where(valid, found[2:3], blocks)
    target = jnp.where(valid, found[3:4], 0)
    return jnp.where(row == 0, slot, jnp.where(row == 1, source, jnp.where(
        row == 2, target, total.astype(jnp.int32))))


def multiply_blocks(order, vals, source, total, across):
    _, width, size = source.shape
    total[...] = jnp.zeros_like(total)
    contract = (((1,), (1,)), ((), ())) if across else (((1,), (0,)), ((), ()))

    def group(index, _):
        targets, terms = [], []
        for step in range(GROUP):
            left, right = [], []
            for half in range(2):
                first = ((index * GROUP + step) * 2 + half) * PACK
                places = [first + each for each in range(PACK)]
                left.append(jnp.concatenate([source[order[1, each]] for each in places], axis=1))
                right.append(jnp.concatenate([vals[order[0, each]] for each in places],
                                             axis=1 if across else 0))
                targets.append(order[2, first])
            both = lax.dot_general(
                jnp.concatenate(left, axis=0), jnp.concatenate(right, axis=0 if across else 1),
                contract, preferred_element_type=F32,
            )
            terms += [both[:width, :size], both[width:, size:]]
        for target, term in zip(targets, terms):
            total[target] += term
        return 0

    lax.fori_loop(0, (order[3, 0] + 2 * GROUP - 1) // (2 * GROUP), group, 0)


def begin(out):
    out[...] = jnp.zeros_like(out)


def stack_ids(user, positive, negative, after, out):
    out[...] = jnp.zeros_like(out)
    for row, ids in enumerate((user, positive, negative)):
        out[row:row + 1, :] = ids[...]


def pack_ids(places, *refs):
    out = refs[-1]
    out[...] = jnp.zeros_like(out)
    for offset, (index, row) in enumerate(places):
        out[3 * offset:3 * offset + 3, :] = refs[index][row:row + 3, :]


def prepare(count, rows, columns, user_emb, item_emb, user_deg, item_deg, after,
            user_source, item_source, user_scale, item_scale, item_order, user_order, keys):
    live = count[0]
    slots = rows.shape[0]
    keys[...] = jnp.zeros_like(keys)
    keys[0:1, 0:slots] = rows[...].reshape(1, slots)
    keys[1:2, 0:slots] = columns[...].reshape(1, slots)
    users, items = keys[0:1, :], keys[1:2, :]
    item_order[...] = sort_slots(items, users, live, item_scale.shape[0])
    user_order[...] = sort_slots(users, items, live, user_scale.shape[0])
    for emb, deg, scale, into in ((user_emb, user_deg, user_scale, user_source),
                                  (item_emb, item_deg, item_scale, item_source)):
        scale[...] = lax.rsqrt(deg[...].astype(F32))
        blocks, size = scale.shape
        for block in range(blocks):
            piece = emb[:, block * size:(block + 1) * size].astype(F32)
            into[block] = (scale[block:block + 1, :] * piece).astype(BF16)
        into[blocks] = jnp.zeros(into.shape[1:], BF16)


def first_pass(across, order, vals, source, *refs):
    multiply_blocks(order, vals, source, refs[-1], across)


def fold(stacked, width):
    return (
        stacked[:width] + stacked[width:2 * width] + stacked[2 * width:3 * width]
    )


def rows_of(ref, rows):
    return [ref[row:row + 1, :] for row in rows]


def pick(table, ids, tile):
    total = None
    for start in range(0, table.shape[1], tile):
        term = jnp.dot(
            table[:, start:start + tile], hot(ids, start, tile),
            preferred_element_type=F32,
        )
        total = term if total is None else total + term
    return total


def gather(places, count, mine, other, scale, after, *refs):
    ids, outs, table = refs[:count], refs[count:-1], refs[-1]
    blocks, width, size = mine.shape
    for block in range(blocks):
        span = slice(block * size, (block + 1) * size)
        here = scale[block:block + 1, :] * (mine[block] + other[block])
        for part, piece in enumerate(split3(here)):
            table[part * width:(part + 1) * width, span] = piece
    for out, (index, rows) in zip(outs, places):
        out[...] = fold(pick(table, rows_of(ids[index], rows), 2 * size), width)


def scatter(pieces, ids, table, blocks, size, put):
    width = table.shape[1] // 3
    tile = 2 * size
    for place, piece in enumerate(pieces):
        for part, value in enumerate(split3(piece[:width, :])):
            table[place, part * width:(part + 1) * width, :] = value
    for start in range(0, blocks * size, tile):
        total = None
        for place, rows in enumerate(ids):
            term = lax.dot_general(
                table[place], hot(rows, start, tile), (((1,), (1,)), ((), ())),
                preferred_element_type=F32,
            )
            total = term if total is None else total + term
        total = fold(total, width)
        for offset in range(0, tile, size):
            put((start + offset) // size, total[:, offset:offset + size])


def scatter_items(places, after, *refs):
    peers = len(places)
    pieces, ids, out, table = refs[:peers], refs[peers:-2], refs[-2], refs[-1]
    blocks, _, size = out.shape

    def put(block, value):
        out[block] = value

    scatter(pieces, [rows_of(ids[index], rows) for index, rows in places],
            table, blocks, size, put)


def gather_base(user_emb, item_emb, ids, user_out, item_out):
    tile = ids.shape[1]
    user_out[...] = pick(user_emb, rows_of(ids, [0]), tile)
    item_out[...] = pick(item_emb, rows_of(ids, [1, 2]), tile)


def add_all(refs):
    total = refs[0][...]
    for ref in refs[1:]:
        total = total + ref[...]
    return total


def slopes(user_parts, item_parts, ids, *refs):
    users, items = refs[:user_parts], refs[user_parts:user_parts + item_parts]
    pieces, pushed = refs[user_parts + item_parts:]
    width = pushed.shape[0]
    user_rows = 0.5 * add_all(users)
    difference = 0.5 * add_all(items)
    margin = jnp.sum(user_rows * difference, axis=0, keepdims=True)
    slope = -jax.nn.sigmoid(-margin)
    pieces[:width, :] = slope * difference
    pieces[width:, :] = jnp.broadcast_to(ids[0:1, :].astype(F32), (8, ids.shape[1]))
    pushed[...] = slope * user_rows


def halves(total, keep, send):
    me = lax.axis_index("rep")
    half = keep.shape[1]
    for block in range(keep.shape[0]):
        keep[block] = total[block, pl.ds(pl.multiple_of(me * half, half), half), :]
        send[block] = total[block, pl.ds(pl.multiple_of((1 - me) * half, half), half), :]


def second_items(parts, order, source_scale, target_scale, vals, *refs):
    pieces = refs[:parts]
    half_grad, keep, send, source, total, table = refs[parts:]
    blocks, width, size = half_grad.shape

    def put(block, grad):
        half_grad[block] = 0.5 * grad
        source[block] = (source_scale[block:block + 1, :] * grad * 0.5).astype(BF16)

    ids = [[piece[width:width + 1, :].astype(jnp.int32)] for piece in pieces]
    scatter(pieces, ids, table, blocks, size, put)
    source[blocks] = jnp.zeros((width, size), BF16)
    multiply_blocks(order, vals, source, total, False)
    for block in range(total.shape[0]):
        total[block] = target_scale[block:block + 1, :] * total[block]
    halves(total, keep, send)


def second_users(order, mine, other, source_scale, target_scale, vals, after,
                 half_grad, keep, send, source, total):
    blocks, width, size = mine.shape
    for block in range(blocks):
        grad = mine[block] + other[block]
        half_grad[block] = 0.5 * grad
        source[block] = (source_scale[block:block + 1, :] * grad * 0.5).astype(BF16)
    source[blocks] = jnp.zeros((width, size), BF16)
    multiply_blocks(order, vals, source, total, True)
    for block in range(total.shape[0]):
        total[block] = target_scale[block:block + 1, :] * total[block]
    halves(total, keep, send)


def copy(values, *refs):
    refs[-1][...] = values[...]


def add_deal(offsets, keep, received, after, *outs):
    me = lax.axis_index("user")
    per = outs[0].shape[0]
    for out, offset in zip(outs, offsets):
        there = (me ^ offset) * per
        for block in range(per):
            out[block] = keep[there + block] + received[there + block]


def sum_parts(*refs):
    refs[-1][...] = add_all(refs[:-1])


def sum_after(count, *refs):
    sum_parts(*refs[count:])


def pack(*refs):
    for place, ref in enumerate(refs[:-1]):
        refs[-1][place] = ref[...]


def finish(offsets, user_half_grad, user_mine, user_other, item_half_grad, item_mine, item_other,
           user_out, item_out):
    finish_users(user_half_grad, user_mine, user_other, user_out)
    finish_items(offsets, item_half_grad, item_mine, item_other, item_out)


def finish_users(half_grad, mine, other, out):
    me = lax.axis_index("rep")
    blocks, width, size = half_grad.shape
    half = width // 2
    for block in range(blocks):
        span = slice(block * size, (block + 1) * size)
        for rank, part in ((me, mine), (1 - me, other)):
            rows = pl.ds(pl.multiple_of(rank * half, half), half)
            out[rows, span] = half_grad[block, rows, :] + part[block]


def finish_items(offsets, half_grad, mine, other, out):
    me = lax.axis_index("rep")
    place = lax.axis_index("user")
    _, per, half, size = mine.shape
    for index, offset in enumerate(offsets):
        there = (place ^ offset) * per
        for block in range(per):
            span = pl.ds(pl.multiple_of((there + block) * size, size), size)
            for rank, part in ((me, mine), (1 - me, other)):
                rows = pl.ds(pl.multiple_of(rank * half, half), half)
                out[rows, span] = half_grad[there + block, rows, :] + part[index, block]


def swap(values, axis="rep", peers=2, offset=1):
    return lax.ppermute(values, axis, [(i, i ^ offset) for i in range(peers)])


def on_device(users, items, user_emb, item_emb, user_deg, item_deg, block_vals, block_row,
              block_col, block_count, trip_user, trip_pos, trip_neg):
    width = user_emb.shape[0]
    slots, size, _ = block_vals.shape
    user_blocks = user_emb.shape[1] // size
    item_blocks = item_emb.shape[1] // size
    trips = trip_user.shape[0]
    half = width // 2
    user_deg = user_deg.reshape(user_blocks, size)
    item_deg = item_deg.reshape(item_blocks, size)

    product_flops = 2 * slots * size * size * width
    product_bytes = slots * size * size * 2
    started = call(begin, shape(8, size), (), [], (), 16 * product_flops, product_bytes)
    id_rows = max(16, -(-3 * users // 16) * 8)
    ids_shape = jax.ShapeDtypeStruct((id_rows, trips), jnp.int32)
    ids = call(
        stack_ids, ids_shape,
        [each.reshape(1, trips) for each in (trip_user, trip_pos, trip_neg)] + [started],
        [VMEM, VMEM, VMEM, ANY],
    )
    ids_user = [ids] + [swap(ids, "item", items, o) for o in range(1, items)]
    met = sorted(range(1, users), key=lambda offset: (offset != users // 2, -offset))
    back = met[::-1]
    ids_item, held, step = [(0, 0)], [ids], 1
    while step < users:
        packed = ids if step == 1 else call(
            functools.partial(pack_ids, ids_item), ids_shape, held, [VMEM] * len(held))
        held.append(swap(packed, "user", users, step))
        ids_item += [(len(held) - 1, 3 * place) for place in range(step)]
        step *= 2
    lanes = -(-slots // size) * size

    order_shape = jax.ShapeDtypeStruct((4, lanes), jnp.int32)

    def source_shape(blocks):
        return jax.ShapeDtypeStruct((blocks + 1, width, size), BF16)

    (user_source, item_source, user_scale, item_scale, item_order, user_order) = call(
        prepare,
        [source_shape(user_blocks), source_shape(item_blocks), shape(user_blocks, size),
         shape(item_blocks, size), order_shape, order_shape],
        (block_count, block_row, block_col, user_emb, item_emb, user_deg, item_deg, ids),
        [SMEM, VMEM, VMEM, VMEM, VMEM, VMEM, VMEM, ANY],
        [pltpu.VMEM((8, lanes), jnp.int32)], product_flops, product_bytes,
    )
    item_table = call(
        functools.partial(first_pass, False), shape(item_blocks, width, size),
        (item_order, block_vals, user_source, ids), [SMEM, VMEM, VMEM, ANY], (),
        product_flops, product_bytes,
    )
    user_table = call(
        functools.partial(first_pass, True), shape(user_blocks, width, size),
        (user_order, block_vals, item_source, item_table), [SMEM, VMEM, VMEM, ANY], (),
        HEAVY, product_bytes,
    )

    hot_flops = 2 * 3 * width * trips * size

    def reduced(table, scale, arrays, places, axis, offsets, after):
        peers, blocks = len(places), scale.shape[0]
        dealt = call(
            functools.partial(gather, places, len(arrays)), [shape(width, trips)] * peers,
            (table, swap(table), scale, after, *arrays),
            [VMEM] * 3 + [ANY] + [VMEM] * len(arrays),
            [pltpu.VMEM((3 * width, blocks * size), BF16)],
            HEAVY if axis == "user" else 0, 8 * blocks * width * size,
        )
        return [dealt[0]] + [swap(part, axis, peers, o) for part, o in zip(dealt[1:], offsets)]

    def item_rows(offset):
        index, row = ids_item[offset]
        return index, [row + 1, row + 2]

    item_parts = reduced(item_table, item_scale, held, [item_rows(o) for o in [0, *met]],
                         "user", met, ids)
    user_parts = reduced(user_table, user_scale, ids_user, [(o, [0]) for o in range(items)],
                         "item", list(range(1, items)), item_parts[0])
    user_base, item_base = call(
        gather_base, [shape(width, trips)] * 2, (user_emb, item_emb, ids),
        [VMEM, VMEM, VMEM], (), 4 * width * trips * size * (user_blocks + item_blocks),
        2 * width * size * (user_blocks + item_blocks),
    )
    user_parts.append(user_base)
    item_parts.append(item_base)
    pieces, pushed = call(
        functools.partial(slopes, len(user_parts), len(item_parts)),
        [shape(width + 8, trips), shape(width, trips)],
        (ids, *user_parts, *item_parts), [VMEM] * (1 + len(user_parts) + len(item_parts)),
        moved=4 * width * trips * (len(user_parts) + len(item_parts) + 2),
    )

    arrays = [pieces, swap(pieces)]
    for offset in range(1, items):
        arrays.append(swap(pieces, "item", items, offset))
        arrays.append(lax.ppermute(pieces, ("item", "rep"), [
            (i, i ^ (2 * offset + 1)) for i in range(2 * items)]))
    user_half_grad, item_keep, item_send = call(
        functools.partial(second_items, len(arrays)),
        [shape(user_blocks, width, size)] + [shape(item_blocks, half, size)] * 2,
        (item_order, user_scale, item_scale, block_vals, *arrays),
        [SMEM] + [VMEM] * (3 + len(arrays)),
        [pltpu.VMEM((user_blocks + 1, width, size), BF16),
         pltpu.VMEM((item_blocks, width, size), F32),
         pltpu.VMEM((len(arrays), 3 * width, trips), BF16)],
        product_flops, product_bytes,
    )
    arrays = [pushed] + [swap(pushed, "user", users, o) for o in back]
    item_grad = call(
        functools.partial(scatter_items, [item_rows(o) for o in [0, *back]]),
        shape(item_blocks, width, size),
        (item_send, *arrays, *held), [ANY] + [VMEM] * (users + len(held)),
        [pltpu.VMEM((users, 3 * width, trips), BF16)], HEAVY, 0,
    )

    per = item_blocks // users
    dealt = call(
        functools.partial(add_deal, [0, *met]), [shape(per, half, size)] * users,
        (item_keep, swap(item_send), item_grad), [VMEM, VMEM, ANY], (), HEAVY,
    )
    item_half_grad, user_keep, user_send = call(
        second_users,
        [shape(item_blocks, width, size)] + [shape(user_blocks, half, size)] * 2,
        (user_order, item_grad, swap(item_grad), item_scale, user_scale, block_vals, dealt[0]),
        [SMEM] + [VMEM] * 5 + [ANY],
        [pltpu.VMEM((item_blocks + 1, width, size), BF16),
         pltpu.VMEM((user_blocks, width, size), F32)],
        product_flops, product_bytes,
    )
    parts = [dealt[0]] + [swap(part, "user", users, o) for part, o in zip(dealt[1:], met)]
    item_own = call(functools.partial(sum_after, 1), shape(per, half, size), (user_keep, *parts),
                    [ANY] + [VMEM] * users,
               moved=4 * (users + 1) * per * half * size)
    item_mine, step = {0: item_own}, 1
    while step < users:
        for offset, part in list(item_mine.items()):
            item_mine[offset ^ step] = swap(part, "user", users, step)
        if 2 * step < users:
            item_mine[step] = hold(item_mine[step], flops=HEAVY)
        step *= 2
    item_places = list(item_mine)
    item_mine = call(pack, shape(users, per, half, size), tuple(item_mine.values()),
                     [VMEM] * users, moved=8 * item_blocks * half * size)
    user_send = hold(user_send, item_own)

    own = call(sum_parts, shape(user_blocks, half, size), (user_keep, swap(user_send)),
               [VMEM, VMEM], moved=12 * user_blocks * half * size)
    mine = call(functools.partial(sum_after, 1), shape(user_blocks, half, size),
                (item_mine, own, *[swap(own, "item", items, o) for o in range(1, items)]),
                [ANY] + [VMEM] * items, moved=12 * user_blocks * half * size)
    return call(
        functools.partial(finish, item_places),
        (shape(width, user_blocks * size), shape(width, item_blocks * size)),
        (user_half_grad, mine, swap(mine), item_half_grad, item_mine, swap(item_mine)),
        [VMEM] * 6, moved=12 * (user_blocks + item_blocks) * width * size,
    )


def solution(mesh):
    return jax.shard_map(
        functools.partial(on_device, mesh.shape["user"], mesh.shape["item"]),
        mesh=mesh,
        in_specs=(
            P(None, ("groups", "user")),
            P(None, ("groups", "item")),
            P(("groups", "user")),
            P(("groups", "item")),
            P(("groups", "user", "item", "rep"), None, None),
            P(("groups", "user", "item", "rep")),
            P(("groups", "user", "item", "rep")),
            P(("groups", "user", "item", "rep")),
            P(("groups", "user", "item", "rep")),
            P(("groups", "user", "item", "rep")),
            P(("groups", "user", "item", "rep")),
        ),
        out_specs=(P(None, ("groups", "user")), P(None, ("groups", "item"))),
        check_vma=False,
    )
```

```python
import functools

import jax
import jax.numpy as jnp
from jax import lax
from jax.experimental import pallas as pl
from jax.experimental.pallas import tpu as pltpu
from jax.sharding import PartitionSpec as P

F32 = jnp.float32
BF16 = jnp.bfloat16
PACK = 4
GROUP = 8
HEAVY = 10 ** 11

VMEM = pl.BlockSpec(memory_space=pltpu.VMEM)
SMEM = pl.BlockSpec(memory_space=pltpu.SMEM)
ANY = pl.BlockSpec(memory_space=pl.ANY)
HBM = pl.BlockSpec(memory_space=pltpu.HBM)


def call(kernel, outs, ins, specs, scratch=(), flops=0, moved=0, room=16):
    return pl.pallas_call(
        kernel,
        out_shape=outs,
        in_specs=specs,
        out_specs=jax.tree.map(lambda _: VMEM, outs),
        scratch_shapes=list(scratch),
        cost_estimate=pl.CostEstimate(flops=flops, bytes_accessed=moved, transcendentals=0),
        compiler_params=pltpu.CompilerParams(vmem_limit_bytes=room * 1024 * 1024),
    )(*ins)


def hold(values, *after, flops=0):
    return call(copy, jax.ShapeDtypeStruct(values.shape, values.dtype), (values, *after),
                [VMEM] + [ANY] * len(after), flops=flops)


def shape(*dims):
    return jax.ShapeDtypeStruct(dims, F32)


def split3(values):
    high = values.astype(BF16)
    rest = values - high.astype(F32)
    middle = rest.astype(BF16)
    low = (rest - middle.astype(F32)).astype(BF16)
    return high, middle, low


def hot(ids, start, tile):
    if len(ids) == 2:
        same = ids[0] == ids[1]
        ids = [jnp.where(same, -1, each) for each in ids]
    ids = [each.astype(jnp.int16) for each in ids]
    place = lax.broadcasted_iota(jnp.int16, (tile, ids[0].shape[1]), 0) + jnp.int16(start)
    chosen = jnp.zeros(place.shape, BF16)
    for each, sign in zip(ids, (1, -1)):
        chosen = jnp.where(place == each, jnp.asarray(sign, BF16), chosen)
    return chosen


def sort_slots(keys, sources, count, blocks):
    lanes = keys.shape[1]
    rows = 2 * blocks
    place = lax.broadcasted_iota(jnp.int32, (1, lanes), 1)
    live = place < count
    mine = (lax.broadcasted_iota(jnp.int32, (rows, lanes), 0) == keys) & live
    mine = jnp.where(mine, 1.0, 0.0)
    earlier = lax.broadcasted_iota(jnp.int32, (lanes, lanes), 0) < lax.broadcasted_iota(
        jnp.int32, (lanes, lanes), 1)
    before = jnp.dot(mine.astype(BF16), jnp.where(earlier, 1.0, 0.0).astype(BF16),
                     preferred_element_type=F32)
    packs = jnp.floor((jnp.sum(mine, axis=1, keepdims=True) + (PACK - 1)) * (1.0 / PACK))
    packs = jnp.broadcast_to(packs, (rows, 128))
    lower = lax.broadcasted_iota(jnp.int32, (rows, rows), 1) < lax.broadcasted_iota(
        jnp.int32, (rows, rows), 0)
    first = jnp.dot(jnp.where(lower, 1.0, 0.0).astype(BF16), packs.astype(BF16),
                    preferred_element_type=F32)
    position = jnp.sum(mine * (first[:, :1] * PACK + before), axis=0, keepdims=True)
    position = jnp.where(live, position.astype(jnp.int32), -1)
    match = lax.broadcasted_iota(jnp.int32, (lanes, lanes), 0) == position
    row = lax.broadcasted_iota(jnp.int32, (16, lanes), 0)
    values = jnp.where(row == 0, place // 16, jnp.where(row == 1, place % 16, jnp.where(
        row == 2, sources, jnp.where(row == 3, keys, jnp.where(row == 4, 1, 0)))))
    values = jnp.where(live, values, 0).astype(F32)
    found = lax.dot_general(values.astype(BF16), jnp.where(match, 1.0, 0.0).astype(BF16),
                            (((1,), (1,)), ((), ())), preferred_element_type=F32)
    found = found.astype(jnp.int32)
    valid = found[4:5] > 0
    total = jnp.broadcast_to(jnp.sum(packs[:, :1], axis=0, keepdims=True), (1, lanes))
    row = lax.broadcasted_iota(jnp.int32, (4, lanes), 0)
    slot = found[0:1] * 16 + found[1:2]
    source = jnp.where(valid, found[2:3], blocks)
    target = jnp.where(valid, found[3:4], 0)
    return jnp.where(row == 0, slot, jnp.where(row == 1, source, jnp.where(
        row == 2, target, total.astype(jnp.int32))))


def multiply_blocks(order, vals, source, total, across):
    _, width, size = source.shape
    total[...] = jnp.zeros_like(total)
    contract = (((1,), (1,)), ((), ())) if across else (((1,), (0,)), ((), ()))

    def group(index, _):
        targets, terms = [], []
        for step in range(GROUP):
            left, right = [], []
            for half in range(2):
                first = ((index * GROUP + step) * 2 + half) * PACK
                places = [first + each for each in range(PACK)]
                left.append(jnp.concatenate([source[order[1, each]] for each in places], axis=1))
                right.append(jnp.concatenate([vals[order[0, each]] for each in places],
                                             axis=1 if across else 0))
                targets.append(order[2, first])
            both = lax.dot_general(
                jnp.concatenate(left, axis=0), jnp.concatenate(right, axis=0 if across else 1),
                contract, preferred_element_type=F32,
            )
            terms += [both[:width, :size], both[width:, size:]]
        for target, term in zip(targets, terms):
            total[target] += term
        return 0

    lax.fori_loop(0, (order[3, 0] + 2 * GROUP - 1) // (2 * GROUP), group, 0)


def begin(out):
    out[...] = jnp.zeros_like(out)


def stack_ids(user, positive, negative, after, out):
    out[...] = jnp.zeros_like(out)
    for row, ids in enumerate((user, positive, negative)):
        out[row:row + 1, :] = ids[...]


def pack_ids(places, *refs):
    out = refs[-1]
    out[...] = jnp.zeros_like(out)
    for offset, (index, row) in enumerate(places):
        out[3 * offset:3 * offset + 3, :] = refs[index][row:row + 3, :]


def prepare(count, rows, columns, user_emb, item_emb, user_deg, item_deg, after,
            user_source, item_source, user_scale, item_scale, item_order, user_order, keys):
    live = count[0]
    slots = rows.shape[0]
    keys[...] = jnp.zeros_like(keys)
    keys[0:1, 0:slots] = rows[...].reshape(1, slots)
    keys[1:2, 0:slots] = columns[...].reshape(1, slots)
    users, items = keys[0:1, :], keys[1:2, :]
    item_order[...] = sort_slots(items, users, live, item_scale.shape[0])
    user_order[...] = sort_slots(users, items, live, user_scale.shape[0])
    for emb, deg, scale, into in ((user_emb, user_deg, user_scale, user_source),
                                  (item_emb, item_deg, item_scale, item_source)):
        scale[...] = lax.rsqrt(deg[...].astype(F32))
        blocks, size = scale.shape
        for block in range(blocks):
            piece = emb[:, block * size:(block + 1) * size].astype(F32)
            into[block] = (scale[block:block + 1, :] * piece).astype(BF16)
        into[blocks] = jnp.zeros(into.shape[1:], BF16)


def first_pass(across, order, vals, source, *refs):
    multiply_blocks(order, vals, source, refs[-1], across)


def fold(stacked, width):
    return (
        stacked[:width] + stacked[width:2 * width] + stacked[2 * width:3 * width]
    )


def rows_of(ref, rows):
    return [ref[row:row + 1, :] for row in rows]


def pick(table, ids, tile):
    total = None
    for start in range(0, table.shape[1], tile):
        term = jnp.dot(
            table[:, start:start + tile], hot(ids, start, tile),
            preferred_element_type=F32,
        )
        total = term if total is None else total + term
    return total


def gather(places, count, mine, other, scale, after, *refs):
    ids, outs, table = refs[:count], refs[count:-1], refs[-1]
    blocks, width, size = mine.shape
    for block in range(blocks):
        span = slice(block * size, (block + 1) * size)
        here = scale[block:block + 1, :] * (mine[block] + other[block])
        for part, piece in enumerate(split3(here)):
            table[part * width:(part + 1) * width, span] = piece
    for out, (index, rows) in zip(outs, places):
        out[...] = fold(pick(table, rows_of(ids[index], rows), 2 * size), width)


def scatter(pieces, ids, table, blocks, size, put):
    width = table.shape[1] // 3
    tile = 2 * size
    for place, piece in enumerate(pieces):
        for part, value in enumerate(split3(piece[:width, :])):
            table[place, part * width:(part + 1) * width, :] = value
    for start in range(0, blocks * size, tile):
        total = None
        for place, rows in enumerate(ids):
            term = lax.dot_general(
                table[place], hot(rows, start, tile), (((1,), (1,)), ((), ())),
                preferred_element_type=F32,
            )
            total = term if total is None else total + term
        total = fold(total, width)
        for offset in range(0, tile, size):
            put((start + offset) // size, total[:, offset:offset + size])


def scatter_items(places, after, *refs):
    peers = len(places)
    pieces, ids, out, table = refs[:peers], refs[peers:-2], refs[-2], refs[-1]
    blocks, _, size = out.shape

    def put(block, value):
        out[block] = value

    scatter(pieces, [rows_of(ids[index], rows) for index, rows in places],
            table, blocks, size, put)


def gather_base(user_emb, item_emb, ids, user_out, item_out):
    tile = ids.shape[1]
    user_out[...] = pick(user_emb, rows_of(ids, [0]), tile)
    item_out[...] = pick(item_emb, rows_of(ids, [1, 2]), tile)


def add_all(refs):
    total = refs[0][...]
    for ref in refs[1:]:
        total = total + ref[...]
    return total


def slopes(user_parts, item_parts, ids, *refs):
    users, items = refs[:user_parts], refs[user_parts:user_parts + item_parts]
    pieces, pushed = refs[user_parts + item_parts:]
    width = pushed.shape[0]
    user_rows = 0.5 * add_all(users)
    difference = 0.5 * add_all(items)
    margin = jnp.sum(user_rows * difference, axis=0, keepdims=True)
    slope = -jax.nn.sigmoid(-margin)
    pieces[:width, :] = slope * difference
    pieces[width:, :] = jnp.broadcast_to(ids[0:1, :].astype(F32), (8, ids.shape[1]))
    pushed[...] = slope * user_rows


def halves(total, keep, send):
    me = lax.axis_index("rep")
    half = keep.shape[1]
    for block in range(keep.shape[0]):
        keep[block] = total[block, pl.ds(pl.multiple_of(me * half, half), half), :]
        send[block] = total[block, pl.ds(pl.multiple_of((1 - me) * half, half), half), :]


def second_items(parts, order, source_scale, target_scale, vals, *refs):
    pieces = refs[:parts]
    half_grad, keep, send, source, total, table = refs[parts:]
    blocks, width, size = half_grad.shape

    def put(block, grad):
        half_grad[block] = 0.5 * grad
        source[block] = (source_scale[block:block + 1, :] * grad * 0.5).astype(BF16)

    ids = [[piece[width:width + 1, :].astype(jnp.int32)] for piece in pieces]
    scatter(pieces, ids, table, blocks, size, put)
    source[blocks] = jnp.zeros((width, size), BF16)
    multiply_blocks(order, vals, source, total, False)
    for block in range(total.shape[0]):
        total[block] = target_scale[block:block + 1, :] * total[block]
    halves(total, keep, send)


def second_users(order, mine, other, source_scale, target_scale, vals, after,
                 half_grad, keep, send, source, total):
    blocks, width, size = mine.shape
    for block in range(blocks):
        grad = mine[block] + other[block]
        half_grad[block] = 0.5 * grad
        source[block] = (source_scale[block:block + 1, :] * grad * 0.5).astype(BF16)
    source[blocks] = jnp.zeros((width, size), BF16)
    multiply_blocks(order, vals, source, total, True)
    for block in range(total.shape[0]):
        total[block] = target_scale[block:block + 1, :] * total[block]
    halves(total, keep, send)


def copy(values, *refs):
    refs[-1][...] = values[...]


def add_deal(offsets, keep, received, after, *outs):
    me = lax.axis_index("user")
    per = outs[0].shape[0]
    for out, offset in zip(outs, offsets):
        there = (me ^ offset) * per
        for block in range(per):
            out[block] = keep[there + block] + received[there + block]


def sum_parts(*refs):
    refs[-1][...] = add_all(refs[:-1])


def sum_after(count, *refs):
    sum_parts(*refs[count:])


def pack(*refs):
    for place, ref in enumerate(refs[:-1]):
        refs[-1][place] = ref[...]


def finish(offsets, user_half_grad, user_mine, user_other, item_half_grad, item_mine, item_other,
           user_out, item_out):
    finish_users(user_half_grad, user_mine, user_other, user_out)
    finish_items(offsets, item_half_grad, item_mine, item_other, item_out)


def finish_users(half_grad, mine, other, out):
    me = lax.axis_index("rep")
    blocks, width, size = half_grad.shape
    half = width // 2
    for block in range(blocks):
        span = slice(block * size, (block + 1) * size)
        for rank, part in ((me, mine), (1 - me, other)):
            rows = pl.ds(pl.multiple_of(rank * half, half), half)
            out[rows, span] = half_grad[block, rows, :] + part[block]


def finish_items(offsets, half_grad, mine, other, out):
    me = lax.axis_index("rep")
    place = lax.axis_index("user")
    _, per, half, size = mine.shape
    for index, offset in enumerate(offsets):
        there = (place ^ offset) * per
        for block in range(per):
            span = pl.ds(pl.multiple_of((there + block) * size, size), size)
            for rank, part in ((me, mine), (1 - me, other)):
                rows = pl.ds(pl.multiple_of(rank * half, half), half)
                out[rows, span] = half_grad[there + block, rows, :] + part[index, block]


def swap(values, axis="rep", peers=2, offset=1):
    return lax.ppermute(values, axis, [(i, i ^ offset) for i in range(peers)])


def on_device(users, items, user_emb, item_emb, user_deg, item_deg, block_vals, block_row,
              block_col, block_count, trip_user, trip_pos, trip_neg):
    width = user_emb.shape[0]
    slots, size, _ = block_vals.shape
    user_blocks = user_emb.shape[1] // size
    item_blocks = item_emb.shape[1] // size
    trips = trip_user.shape[0]
    half = width // 2
    user_deg = user_deg.reshape(user_blocks, size)
    item_deg = item_deg.reshape(item_blocks, size)

    product_flops = 2 * slots * size * size * width
    product_bytes = slots * size * size * 2
    started = call(begin, shape(8, size), (), [], (), 16 * product_flops, product_bytes)
    id_rows = max(16, -(-3 * users // 16) * 8)
    ids_shape = jax.ShapeDtypeStruct((id_rows, trips), jnp.int32)
    ids = call(
        stack_ids, ids_shape,
        [each.reshape(1, trips) for each in (trip_user, trip_pos, trip_neg)] + [started],
        [VMEM, VMEM, VMEM, ANY],
    )
    ids_user = [ids] + [swap(ids, "item", items, o) for o in range(1, items)]
    met = sorted(range(1, users), key=lambda offset: (offset != users // 2, -offset))
    back = met[::-1]
    ids_item, held, step = [(0, 0)], [ids], 1
    while step < users:
        packed = ids if step == 1 else call(
            functools.partial(pack_ids, ids_item), ids_shape, held, [VMEM] * len(held))
        held.append(swap(packed, "user", users, step))
        ids_item += [(len(held) - 1, 3 * place) for place in range(step)]
        step *= 2
    lanes = -(-slots // size) * size

    order_shape = jax.ShapeDtypeStruct((4, lanes), jnp.int32)

    def source_shape(blocks):
        return jax.ShapeDtypeStruct((blocks + 1, width, size), BF16)

    (user_source, item_source, user_scale, item_scale, item_order, user_order) = call(
        prepare,
        [source_shape(user_blocks), source_shape(item_blocks), shape(user_blocks, size),
         shape(item_blocks, size), order_shape, order_shape],
        (block_count, block_row, block_col, user_emb, item_emb, user_deg, item_deg, ids),
        [SMEM, VMEM, VMEM, VMEM, VMEM, VMEM, VMEM, ANY],
        [pltpu.VMEM((8, lanes), jnp.int32)], product_flops, product_bytes,
    )
    item_table = call(
        functools.partial(first_pass, False), shape(item_blocks, width, size),
        (item_order, block_vals, user_source, ids), [SMEM, VMEM, VMEM, ANY], (),
        product_flops, product_bytes,
    )
    user_table = call(
        functools.partial(first_pass, True), shape(user_blocks, width, size),
        (user_order, block_vals, item_source, item_table, *ids_user[1:]),
        [SMEM, VMEM, VMEM] + [ANY] * items, (),
        HEAVY, product_bytes,
    )

    hot_flops = 2 * 3 * width * trips * size

    def reduced(table, scale, arrays, places, axis, offsets, after):
        peers, blocks = len(places), scale.shape[0]
        dealt = call(
            functools.partial(gather, places, len(arrays)), [shape(width, trips)] * peers,
            (table, swap(table), scale, after, *arrays),
            [VMEM] * 3 + [ANY] + [VMEM] * len(arrays),
            [pltpu.VMEM((3 * width, blocks * size), BF16)],
            HEAVY if axis == "user" else 0, 8 * blocks * width * size,
        )
        return [dealt[0]] + [swap(part, axis, peers, o) for part, o in zip(dealt[1:], offsets)]

    def item_rows(offset):
        index, row = ids_item[offset]
        return index, [row + 1, row + 2]

    item_parts = reduced(item_table, item_scale, held, [item_rows(o) for o in [0, *met]],
                         "user", met, ids)
    user_parts = reduced(user_table, user_scale, ids_user, [(o, [0]) for o in range(items)],
                         "item", list(range(1, items)), item_parts[0])
    user_base, item_base = call(
        gather_base, [shape(width, trips)] * 2, (user_emb, item_emb, ids),
        [VMEM, VMEM, VMEM], (), 4 * width * trips * size * (user_blocks + item_blocks),
        2 * width * size * (user_blocks + item_blocks),
    )
    user_parts.append(user_base)
    item_parts.append(item_base)
    pieces, pushed = call(
        functools.partial(slopes, len(user_parts), len(item_parts)),
        [shape(width + 8, trips), shape(width, trips)],
        (ids, *user_parts, *item_parts), [VMEM] * (1 + len(user_parts) + len(item_parts)),
        moved=4 * width * trips * (len(user_parts) + len(item_parts) + 2),
    )

    arrays = [pieces, swap(pieces)]
    for offset in range(1, items):
        arrays.append(swap(pieces, "item", items, offset))
        arrays.append(lax.ppermute(pieces, ("item", "rep"), [
            (i, i ^ (2 * offset + 1)) for i in range(2 * items)]))
    user_half_grad, item_keep, item_send = call(
        functools.partial(second_items, len(arrays)),
        [shape(user_blocks, width, size)] + [shape(item_blocks, half, size)] * 2,
        (item_order, user_scale, item_scale, block_vals, *arrays),
        [SMEM] + [VMEM] * (3 + len(arrays)),
        [pltpu.VMEM((user_blocks + 1, width, size), BF16),
         pltpu.VMEM((item_blocks, width, size), F32),
         pltpu.VMEM((len(arrays), 3 * width, trips), BF16)],
        product_flops, product_bytes,
    )
    arrays = [pushed] + [swap(pushed, "user", users, o) for o in back]
    item_grad = call(
        functools.partial(scatter_items, [item_rows(o) for o in [0, *back]]),
        shape(item_blocks, width, size),
        (item_send, *arrays, *held), [ANY] + [VMEM] * (users + len(held)),
        [pltpu.VMEM((users, 3 * width, trips), BF16)], HEAVY, 0,
    )

    per = item_blocks // users
    dealt = call(
        functools.partial(add_deal, [0, *met]), [shape(per, half, size)] * users,
        (item_keep, swap(item_send), item_grad), [VMEM, VMEM, ANY], (), HEAVY,
    )
    item_half_grad, user_keep, user_send = call(
        second_users,
        [shape(item_blocks, width, size)] + [shape(user_blocks, half, size)] * 2,
        (user_order, item_grad, swap(item_grad), item_scale, user_scale, block_vals, dealt[0]),
        [SMEM] + [VMEM] * 5 + [ANY],
        [pltpu.VMEM((item_blocks + 1, width, size), BF16),
         pltpu.VMEM((user_blocks, width, size), F32)],
        product_flops, product_bytes,
    )
    parts = [dealt[0]] + [swap(part, "user", users, o) for part, o in zip(dealt[1:], met)]
    item_own = call(functools.partial(sum_after, 1), shape(per, half, size), (user_keep, *parts),
                    [ANY] + [VMEM] * users,
               moved=4 * (users + 1) * per * half * size)
    item_mine, step = {0: item_own}, 1
    while step < users:
        for offset, part in list(item_mine.items()):
            item_mine[offset ^ step] = swap(part, "user", users, step)
        if 2 * step < users:
            item_mine[step] = hold(item_mine[step], flops=HEAVY)
        step *= 2
    item_places = list(item_mine)
    item_mine = call(pack, shape(users, per, half, size), tuple(item_mine.values()),
                     [VMEM] * users, moved=8 * item_blocks * half * size)
    user_send = hold(user_send, item_own)

    own = call(sum_parts, shape(user_blocks, half, size), (user_keep, swap(user_send)),
               [VMEM, VMEM], moved=12 * user_blocks * half * size)
    mine = call(functools.partial(sum_after, 1), shape(user_blocks, half, size),
                (item_mine, own, *[swap(own, "item", items, o) for o in range(1, items)]),
                [ANY] + [VMEM] * items, moved=12 * user_blocks * half * size)
    return call(
        functools.partial(finish, item_places),
        (shape(width, user_blocks * size), shape(width, item_blocks * size)),
        (user_half_grad, mine, swap(mine), item_half_grad, item_mine, swap(item_mine)),
        [VMEM] * 6, moved=12 * (user_blocks + item_blocks) * width * size,
    )


def solution(mesh):
    return jax.shard_map(
        functools.partial(on_device, mesh.shape["user"], mesh.shape["item"]),
        mesh=mesh,
        in_specs=(
            P(None, ("groups", "user")),
            P(None, ("groups", "item")),
            P(("groups", "user")),
            P(("groups", "item")),
            P(("groups", "user", "item", "rep"), None, None),
            P(("groups", "user", "item", "rep")),
            P(("groups", "user", "item", "rep")),
            P(("groups", "user", "item", "rep")),
            P(("groups", "user", "item", "rep")),
            P(("groups", "user", "item", "rep")),
            P(("groups", "user", "item", "rep")),
        ),
        out_specs=(P(None, ("groups", "user")), P(None, ("groups", "item"))),
        check_vma=False,
    )
```

```python
import functools

import jax
import jax.numpy as jnp
from jax import lax
from jax.experimental import pallas as pl
from jax.experimental.pallas import tpu as pltpu
from jax.sharding import PartitionSpec as P

F32 = jnp.float32
BF16 = jnp.bfloat16
PACK = 4
GROUP = 8
HEAVY = 10 ** 11
MEDIUM = 24 * 10 ** 8

VMEM = pl.BlockSpec(memory_space=pltpu.VMEM)
SMEM = pl.BlockSpec(memory_space=pltpu.SMEM)
ANY = pl.BlockSpec(memory_space=pl.ANY)
HBM = pl.BlockSpec(memory_space=pltpu.HBM)


def call(kernel, outs, ins, specs, scratch=(), flops=0, moved=0, room=16):
    return pl.pallas_call(
        kernel,
        out_shape=outs,
        in_specs=specs,
        out_specs=jax.tree.map(lambda _: VMEM, outs),
        scratch_shapes=list(scratch),
        cost_estimate=pl.CostEstimate(flops=flops, bytes_accessed=moved, transcendentals=0),
        compiler_params=pltpu.CompilerParams(vmem_limit_bytes=room * 1024 * 1024),
    )(*ins)


def hold(values, *after, flops=0):
    return call(copy, jax.ShapeDtypeStruct(values.shape, values.dtype), (values, *after),
                [VMEM] + [ANY] * len(after), flops=flops)


def shape(*dims):
    return jax.ShapeDtypeStruct(dims, F32)


def split3(values):
    high = values.astype(BF16)
    rest = values - high.astype(F32)
    middle = rest.astype(BF16)
    low = (rest - middle.astype(F32)).astype(BF16)
    return high, middle, low


def hot(ids, start, tile):
    if len(ids) == 2:
        same = ids[0] == ids[1]
        ids = [jnp.where(same, -1, each) for each in ids]
    ids = [each.astype(jnp.int16) for each in ids]
    place = lax.broadcasted_iota(jnp.int16, (tile, ids[0].shape[1]), 0) + jnp.int16(start)
    chosen = jnp.zeros(place.shape, BF16)
    for each, sign in zip(ids, (1, -1)):
        chosen = jnp.where(place == each, jnp.asarray(sign, BF16), chosen)
    return chosen


def sort_slots(keys, sources, count, blocks):
    lanes = keys.shape[1]
    rows = 2 * blocks
    place = lax.broadcasted_iota(jnp.int32, (1, lanes), 1)
    live = place < count
    mine = (lax.broadcasted_iota(jnp.int32, (rows, lanes), 0) == keys) & live
    mine = jnp.where(mine, 1.0, 0.0)
    earlier = lax.broadcasted_iota(jnp.int32, (lanes, lanes), 0) < lax.broadcasted_iota(
        jnp.int32, (lanes, lanes), 1)
    before = jnp.dot(mine.astype(BF16), jnp.where(earlier, 1.0, 0.0).astype(BF16),
                     preferred_element_type=F32)
    packs = jnp.floor((jnp.sum(mine, axis=1, keepdims=True) + (PACK - 1)) * (1.0 / PACK))
    packs = jnp.broadcast_to(packs, (rows, 128))
    lower = lax.broadcasted_iota(jnp.int32, (rows, rows), 1) < lax.broadcasted_iota(
        jnp.int32, (rows, rows), 0)
    first = jnp.dot(jnp.where(lower, 1.0, 0.0).astype(BF16), packs.astype(BF16),
                    preferred_element_type=F32)
    position = jnp.sum(mine * (first[:, :1] * PACK + before), axis=0, keepdims=True)
    position = jnp.where(live, position.astype(jnp.int32), -1)
    match = lax.broadcasted_iota(jnp.int32, (lanes, lanes), 0) == position
    row = lax.broadcasted_iota(jnp.int32, (16, lanes), 0)
    values = jnp.where(row == 0, place // 16, jnp.where(row == 1, place % 16, jnp.where(
        row == 2, sources, jnp.where(row == 3, keys, jnp.where(row == 4, 1, 0)))))
    values = jnp.where(live, values, 0).astype(F32)
    found = lax.dot_general(values.astype(BF16), jnp.where(match, 1.0, 0.0).astype(BF16),
                            (((1,), (1,)), ((), ())), preferred_element_type=F32)
    found = found.astype(jnp.int32)
    valid = found[4:5] > 0
    total = jnp.broadcast_to(jnp.sum(packs[:, :1], axis=0, keepdims=True), (1, lanes))
    row = lax.broadcasted_iota(jnp.int32, (4, lanes), 0)
    slot = found[0:1] * 16 + found[1:2]
    source = jnp.where(valid, found[2:3], blocks)
    target = jnp.where(valid, found[3:4], 0)
    return jnp.where(row == 0, slot, jnp.where(row == 1, source, jnp.where(
        row == 2, target, total.astype(jnp.int32))))


def multiply_blocks(order, vals, source, total, across):
    _, width, size = source.shape
    total[...] = jnp.zeros_like(total)
    contract = (((1,), (1,)), ((), ())) if across else (((1,), (0,)), ((), ()))

    def group(index, _):
        targets, terms = [], []
        for step in range(GROUP):
            left, right = [], []
            for half in range(2):
                first = ((index * GROUP + step) * 2 + half) * PACK
                places = [first + each for each in range(PACK)]
                left.append(jnp.concatenate([source[order[1, each]] for each in places], axis=1))
                right.append(jnp.concatenate([vals[order[0, each]] for each in places],
                                             axis=1 if across else 0))
                targets.append(order[2, first])
            both = lax.dot_general(
                jnp.concatenate(left, axis=0), jnp.concatenate(right, axis=0 if across else 1),
                contract, preferred_element_type=F32,
            )
            terms += [both[:width, :size], both[width:, size:]]
        for target, term in zip(targets, terms):
            total[target] += term
        return 0

    lax.fori_loop(0, (order[3, 0] + 2 * GROUP - 1) // (2 * GROUP), group, 0)


def begin(out):
    out[...] = jnp.zeros_like(out)


def stack_ids(user, positive, negative, after, out):
    out[...] = jnp.zeros_like(out)
    for row, ids in enumerate((user, positive, negative)):
        out[row:row + 1, :] = ids[...]


def pack_ids(places, *refs):
    out = refs[-1]
    out[...] = jnp.zeros_like(out)
    for offset, (index, row) in enumerate(places):
        out[3 * offset:3 * offset + 3, :] = refs[index][row:row + 3, :]


def prepare(count, rows, columns, user_emb, item_emb, user_deg, item_deg, after,
            user_source, item_source, user_scale, item_scale, item_order, user_order, keys):
    live = count[0]
    slots = rows.shape[0]
    keys[...] = jnp.zeros_like(keys)
    keys[0:1, 0:slots] = rows[...].reshape(1, slots)
    keys[1:2, 0:slots] = columns[...].reshape(1, slots)
    users, items = keys[0:1, :], keys[1:2, :]
    item_order[...] = sort_slots(items, users, live, item_scale.shape[0])
    user_order[...] = sort_slots(users, items, live, user_scale.shape[0])
    for emb, deg, scale, into in ((user_emb, user_deg, user_scale, user_source),
                                  (item_emb, item_deg, item_scale, item_source)):
        scale[...] = lax.rsqrt(deg[...].astype(F32))
        blocks, size = scale.shape
        for block in range(blocks):
            piece = emb[:, block * size:(block + 1) * size].astype(F32)
            into[block] = (scale[block:block + 1, :] * piece).astype(BF16)
        into[blocks] = jnp.zeros(into.shape[1:], BF16)


def first_pass(across, order, vals, source, *refs):
    multiply_blocks(order, vals, source, refs[-1], across)


def fold(stacked, width):
    return (
        stacked[:width] + stacked[width:2 * width] + stacked[2 * width:3 * width]
    )


def rows_of(ref, rows):
    return [ref[row:row + 1, :] for row in rows]


def pick(table, ids, tile):
    total = None
    for start in range(0, table.shape[1], tile):
        term = jnp.dot(
            table[:, start:start + tile], hot(ids, start, tile),
            preferred_element_type=F32,
        )
        total = term if total is None else total + term
    return total


def gather(places, count, mine, other, scale, after, *refs):
    ids, outs, table = refs[:count], refs[count:-1], refs[-1]
    blocks, width, size = mine.shape
    for block in range(blocks):
        span = slice(block * size, (block + 1) * size)
        here = scale[block:block + 1, :] * (mine[block] + other[block])
        for part, piece in enumerate(split3(here)):
            table[part * width:(part + 1) * width, span] = piece
    for out, (index, rows) in zip(outs, places):
        out[...] = fold(pick(table, rows_of(ids[index], rows), 2 * size), width)


def scatter(pieces, ids, table, blocks, size, put):
    width = table.shape[1] // 3
    tile = 2 * size
    for place, piece in enumerate(pieces):
        for part, value in enumerate(split3(piece[:width, :])):
            table[place, part * width:(part + 1) * width, :] = value
    for start in range(0, blocks * size, tile):
        total = None
        for place, rows in enumerate(ids):
            term = lax.dot_general(
                table[place], hot(rows, start, tile), (((1,), (1,)), ((), ())),
                preferred_element_type=F32,
            )
            total = term if total is None else total + term
        total = fold(total, width)
        for offset in range(0, tile, size):
            put((start + offset) // size, total[:, offset:offset + size])


def scatter_items(places, after, *refs):
    peers = len(places)
    pieces, ids, out, table = refs[:peers], refs[peers:-2], refs[-2], refs[-1]
    blocks, _, size = out.shape

    def put(block, value):
        out[block] = value

    scatter(pieces, [rows_of(ids[index], rows) for index, rows in places],
            table, blocks, size, put)


def gather_base(user_emb, item_emb, ids, user_out, item_out):
    tile = ids.shape[1]
    user_out[...] = pick(user_emb, rows_of(ids, [0]), tile)
    item_out[...] = pick(item_emb, rows_of(ids, [1, 2]), tile)


def add_all(refs):
    total = refs[0][...]
    for ref in refs[1:]:
        total = total + ref[...]
    return total


def slopes(user_parts, item_parts, ids, *refs):
    users, items = refs[:user_parts], refs[user_parts:user_parts + item_parts]
    pieces, pushed = refs[user_parts + item_parts:]
    width = pushed.shape[0]
    user_rows = 0.5 * add_all(users)
    difference = 0.5 * add_all(items)
    margin = jnp.sum(user_rows * difference, axis=0, keepdims=True)
    slope = -jax.nn.sigmoid(-margin)
    pieces[:width, :] = slope * difference
    pieces[width:, :] = jnp.broadcast_to(ids[0:1, :].astype(F32), (8, ids.shape[1]))
    pushed[...] = slope * user_rows


def halves(total, keep, send):
    me = lax.axis_index("rep")
    half = keep.shape[1]
    for block in range(keep.shape[0]):
        keep[block] = total[block, pl.ds(pl.multiple_of(me * half, half), half), :]
        send[block] = total[block, pl.ds(pl.multiple_of((1 - me) * half, half), half), :]


def second_items(parts, order, source_scale, target_scale, vals, *refs):
    pieces = refs[:parts]
    half_grad, keep, send, source, total, table = refs[parts:]
    blocks, width, size = half_grad.shape

    def put(block, grad):
        half_grad[block] = 0.5 * grad
        source[block] = (source_scale[block:block + 1, :] * grad * 0.5).astype(BF16)

    ids = [[piece[width:width + 1, :].astype(jnp.int32)] for piece in pieces]
    scatter(pieces, ids, table, blocks, size, put)
    source[blocks] = jnp.zeros((width, size), BF16)
    multiply_blocks(order, vals, source, total, False)
    for block in range(total.shape[0]):
        total[block] = target_scale[block:block + 1, :] * total[block]
    halves(total, keep, send)


def second_users(order, mine, other, source_scale, target_scale, vals, after,
                 half_grad, keep, send, source, total):
    blocks, width, size = mine.shape
    for block in range(blocks):
        grad = mine[block] + other[block]
        half_grad[block] = 0.5 * grad
        source[block] = (source_scale[block:block + 1, :] * grad * 0.5).astype(BF16)
    source[blocks] = jnp.zeros((width, size), BF16)
    multiply_blocks(order, vals, source, total, True)
    for block in range(total.shape[0]):
        total[block] = target_scale[block:block + 1, :] * total[block]
    halves(total, keep, send)


def copy(values, *refs):
    refs[-1][...] = values[...]


def add_deal(offsets, keep, received, after, *outs):
    me = lax.axis_index("user")
    per = outs[0].shape[0]
    for out, offset in zip(outs, offsets):
        there = (me ^ offset) * per
        for block in range(per):
            out[block] = keep[there + block] + received[there + block]


def sum_parts(*refs):
    refs[-1][...] = add_all(refs[:-1])


def sum_after(count, *refs):
    sum_parts(*refs[count:])


def pack(*refs):
    for place, ref in enumerate(refs[:-1]):
        refs[-1][place] = ref[...]


def finish(offsets, user_half_grad, user_mine, user_other, item_half_grad, item_mine, item_other,
           user_out, item_out):
    finish_users(user_half_grad, user_mine, user_other, user_out)
    finish_items(offsets, item_half_grad, item_mine, item_other, item_out)


def finish_users(half_grad, mine, other, out):
    me = lax.axis_index("rep")
    blocks, width, size = half_grad.shape
    half = width // 2
    for block in range(blocks):
        span = slice(block * size, (block + 1) * size)
        for rank, part in ((me, mine), (1 - me, other)):
            rows = pl.ds(pl.multiple_of(rank * half, half), half)
            out[rows, span] = half_grad[block, rows, :] + part[block]


def finish_items(offsets, half_grad, mine, other, out):
    me = lax.axis_index("rep")
    place = lax.axis_index("user")
    _, per, half, size = mine.shape
    for index, offset in enumerate(offsets):
        there = (place ^ offset) * per
        for block in range(per):
            span = pl.ds(pl.multiple_of((there + block) * size, size), size)
            for rank, part in ((me, mine), (1 - me, other)):
                rows = pl.ds(pl.multiple_of(rank * half, half), half)
                out[rows, span] = half_grad[there + block, rows, :] + part[index, block]


def swap(values, axis="rep", peers=2, offset=1):
    return lax.ppermute(values, axis, [(i, i ^ offset) for i in range(peers)])


def on_device(users, items, user_emb, item_emb, user_deg, item_deg, block_vals, block_row,
              block_col, block_count, trip_user, trip_pos, trip_neg):
    width = user_emb.shape[0]
    slots, size, _ = block_vals.shape
    user_blocks = user_emb.shape[1] // size
    item_blocks = item_emb.shape[1] // size
    trips = trip_user.shape[0]
    half = width // 2
    user_deg = user_deg.reshape(user_blocks, size)
    item_deg = item_deg.reshape(item_blocks, size)

    product_flops = 2 * slots * size * size * width
    product_bytes = slots * size * size * 2
    started = call(begin, shape(8, size), (), [], (), 16 * product_flops, product_bytes)
    id_rows = max(16, -(-3 * users // 16) * 8)
    ids_shape = jax.ShapeDtypeStruct((id_rows, trips), jnp.int32)
    ids = call(
        stack_ids, ids_shape,
        [each.reshape(1, trips) for each in (trip_user, trip_pos, trip_neg)] + [started],
        [VMEM, VMEM, VMEM, ANY],
    )
    ids_user = [ids] + [swap(ids, "item", items, o) for o in range(1, items)]
    met = sorted(range(1, users), key=lambda offset: (offset != users // 2, -offset))
    back = met[::-1]
    ids_item, held, step = [(0, 0)], [ids], 1
    while step < users:
        packed = ids if step == 1 else call(
            functools.partial(pack_ids, ids_item), ids_shape, held, [VMEM] * len(held))
        held.append(swap(packed, "user", users, step))
        ids_item += [(len(held) - 1, 3 * place) for place in range(step)]
        step *= 2
    lanes = -(-slots // size) * size

    order_shape = jax.ShapeDtypeStruct((4, lanes), jnp.int32)

    def source_shape(blocks):
        return jax.ShapeDtypeStruct((blocks + 1, width, size), BF16)

    (user_source, item_source, user_scale, item_scale, item_order, user_order) = call(
        prepare,
        [source_shape(user_blocks), source_shape(item_blocks), shape(user_blocks, size),
         shape(item_blocks, size), order_shape, order_shape],
        (block_count, block_row, block_col, user_emb, item_emb, user_deg, item_deg, ids),
        [SMEM, VMEM, VMEM, VMEM, VMEM, VMEM, VMEM, ANY],
        [pltpu.VMEM((8, lanes), jnp.int32)], product_flops, product_bytes,
    )
    item_table = call(
        functools.partial(first_pass, False), shape(item_blocks, width, size),
        (item_order, block_vals, user_source, ids), [SMEM, VMEM, VMEM, ANY], (),
        product_flops, product_bytes,
    )
    user_table = call(
        functools.partial(first_pass, True), shape(user_blocks, width, size),
        (user_order, block_vals, item_source, item_table, *ids_user[1:]),
        [SMEM, VMEM, VMEM] + [ANY] * items, (),
        HEAVY, product_bytes,
    )

    hot_flops = 2 * 3 * width * trips * size

    def reduced(table, scale, arrays, places, axis, offsets, after):
        peers, blocks = len(places), scale.shape[0]
        dealt = call(
            functools.partial(gather, places, len(arrays)), [shape(width, trips)] * peers,
            (table, swap(table), scale, after, *arrays),
            [VMEM] * 3 + [ANY] + [VMEM] * len(arrays),
            [pltpu.VMEM((3 * width, blocks * size), BF16)],
            HEAVY if axis == "user" else 0, 8 * blocks * width * size,
        )
        return [dealt[0]] + [swap(part, axis, peers, o) for part, o in zip(dealt[1:], offsets)]

    def item_rows(offset):
        index, row = ids_item[offset]
        return index, [row + 1, row + 2]

    item_parts = reduced(item_table, item_scale, held, [item_rows(o) for o in [0, *met]],
                         "user", met, ids)
    user_parts = reduced(user_table, user_scale, ids_user, [(o, [0]) for o in range(items)],
                         "item", list(range(1, items)), item_parts[0])
    user_base, item_base = call(
        gather_base, [shape(width, trips)] * 2, (user_emb, item_emb, ids),
        [VMEM, VMEM, VMEM], (), 4 * width * trips * size * (user_blocks + item_blocks),
        2 * width * size * (user_blocks + item_blocks),
    )
    user_parts.append(user_base)
    item_parts.append(item_base)
    pieces, pushed = call(
        functools.partial(slopes, len(user_parts), len(item_parts)),
        [shape(width + 8, trips), shape(width, trips)],
        (ids, *user_parts, *item_parts), [VMEM] * (1 + len(user_parts) + len(item_parts)),
        moved=4 * width * trips * (len(user_parts) + len(item_parts) + 2),
    )

    arrays = [pieces, swap(pieces)]
    for offset in range(1, items):
        arrays.append(swap(pieces, "item", items, offset))
        arrays.append(lax.ppermute(pieces, ("item", "rep"), [
            (i, i ^ (2 * offset + 1)) for i in range(2 * items)]))
    user_half_grad, item_keep, item_send = call(
        functools.partial(second_items, len(arrays)),
        [shape(user_blocks, width, size)] + [shape(item_blocks, half, size)] * 2,
        (item_order, user_scale, item_scale, block_vals, *arrays),
        [SMEM] + [VMEM] * (3 + len(arrays)),
        [pltpu.VMEM((user_blocks + 1, width, size), BF16),
         pltpu.VMEM((item_blocks, width, size), F32),
         pltpu.VMEM((len(arrays), 3 * width, trips), BF16)],
        product_flops, product_bytes,
    )
    arrays = [pushed] + [swap(pushed, "user", users, o) for o in back]
    item_grad = call(
        functools.partial(scatter_items, [item_rows(o) for o in [0, *back]]),
        shape(item_blocks, width, size),
        (item_send, *arrays, *held), [ANY] + [VMEM] * (users + len(held)),
        [pltpu.VMEM((users, 3 * width, trips), BF16)], HEAVY, 0,
    )

    per = item_blocks // users
    dealt = call(
        functools.partial(add_deal, [0, *met]), [shape(per, half, size)] * users,
        (item_keep, swap(item_send), item_grad), [VMEM, VMEM, ANY], (), HEAVY,
    )
    item_half_grad, user_keep, user_send = call(
        second_users,
        [shape(item_blocks, width, size)] + [shape(user_blocks, half, size)] * 2,
        (user_order, item_grad, swap(item_grad), item_scale, user_scale, block_vals, dealt[0]),
        [SMEM] + [VMEM] * 5 + [ANY],
        [pltpu.VMEM((item_blocks + 1, width, size), BF16),
         pltpu.VMEM((user_blocks, width, size), F32)],
        product_flops, product_bytes,
    )
    parts = [dealt[0]] + [swap(part, "user", users, o) for part, o in zip(dealt[1:], met)]
    item_own = call(functools.partial(sum_after, 1), shape(per, half, size), (user_keep, *parts),
                    [ANY] + [VMEM] * users,
               moved=4 * (users + 1) * per * half * size)
    user_send = hold(user_send, item_own)

    own = call(sum_parts, shape(user_blocks, half, size), (user_keep, swap(user_send)),
               [VMEM, VMEM], moved=12 * user_blocks * half * size)
    late = hold(item_own, own)
    item_mine = {0: item_own}
    for offset in [users - 1, *range(1, users - 1)] if users > 1 else []:
        part = item_own if offset == users - 1 else late
        item_mine[offset] = swap(part, "user", users, offset)
    if users > 2:
        item_mine[users - 1] = hold(item_mine[users - 1], flops=MEDIUM)
    item_places = list(item_mine)
    item_mine = call(pack, shape(users, per, half, size), tuple(item_mine.values()),
                     [VMEM] * users, moved=8 * item_blocks * half * size)
    mine = call(functools.partial(sum_after, 1), shape(user_blocks, half, size),
                (item_mine, own, *[swap(own, "item", items, o) for o in range(1, items)]),
                [ANY] + [VMEM] * items, moved=12 * user_blocks * half * size)
    return call(
        functools.partial(finish, item_places),
        (shape(width, user_blocks * size), shape(width, item_blocks * size)),
        (user_half_grad, mine, swap(mine), item_half_grad, item_mine, swap(item_mine)),
        [VMEM] * 6, moved=12 * (user_blocks + item_blocks) * width * size,
    )


def solution(mesh):
    return jax.shard_map(
        functools.partial(on_device, mesh.shape["user"], mesh.shape["item"]),
        mesh=mesh,
        in_specs=(
            P(None, ("groups", "user")),
            P(None, ("groups", "item")),
            P(("groups", "user")),
            P(("groups", "item")),
            P(("groups", "user", "item", "rep"), None, None),
            P(("groups", "user", "item", "rep")),
            P(("groups", "user", "item", "rep")),
            P(("groups", "user", "item", "rep")),
            P(("groups", "user", "item", "rep")),
            P(("groups", "user", "item", "rep")),
            P(("groups", "user", "item", "rep")),
        ),
        out_specs=(P(None, ("groups", "user")), P(None, ("groups", "item"))),
        check_vma=False,
    )
```

```python
import functools

import jax
import jax.numpy as jnp
from jax import lax
from jax.experimental import pallas as pl
from jax.experimental.pallas import tpu as pltpu
from jax.sharding import PartitionSpec as P

F32 = jnp.float32
BF16 = jnp.bfloat16
PACK = 4
GROUP = 8
HEAVY = 10 ** 11
MEDIUM = 24 * 10 ** 8

VMEM = pl.BlockSpec(memory_space=pltpu.VMEM)
SMEM = pl.BlockSpec(memory_space=pltpu.SMEM)
ANY = pl.BlockSpec(memory_space=pl.ANY)
HBM = pl.BlockSpec(memory_space=pltpu.HBM)


def call(kernel, outs, ins, specs, scratch=(), flops=0, moved=0, room=16):
    return pl.pallas_call(
        kernel,
        out_shape=outs,
        in_specs=specs,
        out_specs=jax.tree.map(lambda _: VMEM, outs),
        scratch_shapes=list(scratch),
        cost_estimate=pl.CostEstimate(flops=flops, bytes_accessed=moved, transcendentals=0),
        compiler_params=pltpu.CompilerParams(vmem_limit_bytes=room * 1024 * 1024),
    )(*ins)


def hold(values, *after, flops=0):
    return call(copy, jax.ShapeDtypeStruct(values.shape, values.dtype), (values, *after),
                [VMEM] + [ANY] * len(after), flops=flops)


def shape(*dims):
    return jax.ShapeDtypeStruct(dims, F32)


def split3(values):
    high = values.astype(BF16)
    rest = values - high.astype(F32)
    middle = rest.astype(BF16)
    low = (rest - middle.astype(F32)).astype(BF16)
    return high, middle, low


def hot(ids, start, tile):
    if len(ids) == 2:
        same = ids[0] == ids[1]
        ids = [jnp.where(same, -1, each) for each in ids]
    ids = [each.astype(jnp.int16) for each in ids]
    place = lax.broadcasted_iota(jnp.int16, (tile, ids[0].shape[1]), 0) + jnp.int16(start)
    chosen = jnp.zeros(place.shape, BF16)
    for each, sign in zip(ids, (1, -1)):
        chosen = jnp.where(place == each, jnp.asarray(sign, BF16), chosen)
    return chosen


def sort_slots(keys, sources, count, blocks):
    lanes = keys.shape[1]
    rows = 2 * blocks
    place = lax.broadcasted_iota(jnp.int32, (1, lanes), 1)
    live = place < count
    mine = (lax.broadcasted_iota(jnp.int32, (rows, lanes), 0) == keys) & live
    mine = jnp.where(mine, 1.0, 0.0)
    earlier = lax.broadcasted_iota(jnp.int32, (lanes, lanes), 0) < lax.broadcasted_iota(
        jnp.int32, (lanes, lanes), 1)
    before = jnp.dot(mine.astype(BF16), jnp.where(earlier, 1.0, 0.0).astype(BF16),
                     preferred_element_type=F32)
    packs = jnp.floor((jnp.sum(mine, axis=1, keepdims=True) + (PACK - 1)) * (1.0 / PACK))
    packs = jnp.broadcast_to(packs, (rows, 128))
    lower = lax.broadcasted_iota(jnp.int32, (rows, rows), 1) < lax.broadcasted_iota(
        jnp.int32, (rows, rows), 0)
    first = jnp.dot(jnp.where(lower, 1.0, 0.0).astype(BF16), packs.astype(BF16),
                    preferred_element_type=F32)
    position = jnp.sum(mine * (first[:, :1] * PACK + before), axis=0, keepdims=True)
    position = jnp.where(live, position.astype(jnp.int32), -1)
    match = lax.broadcasted_iota(jnp.int32, (lanes, lanes), 0) == position
    row = lax.broadcasted_iota(jnp.int32, (16, lanes), 0)
    values = jnp.where(row == 0, place // 16, jnp.where(row == 1, place % 16, jnp.where(
        row == 2, sources, jnp.where(row == 3, keys, jnp.where(row == 4, 1, 0)))))
    values = jnp.where(live, values, 0).astype(F32)
    found = lax.dot_general(values.astype(BF16), jnp.where(match, 1.0, 0.0).astype(BF16),
                            (((1,), (1,)), ((), ())), preferred_element_type=F32)
    found = found.astype(jnp.int32)
    valid = found[4:5] > 0
    total = jnp.broadcast_to(jnp.sum(packs[:, :1], axis=0, keepdims=True), (1, lanes))
    row = lax.broadcasted_iota(jnp.int32, (4, lanes), 0)
    slot = found[0:1] * 16 + found[1:2]
    source = jnp.where(valid, found[2:3], blocks)
    target = jnp.where(valid, found[3:4], 0)
    return jnp.where(row == 0, slot, jnp.where(row == 1, source, jnp.where(
        row == 2, target, total.astype(jnp.int32))))


def multiply_blocks(order, vals, source, total, across):
    _, width, size = source.shape
    total[...] = jnp.zeros_like(total)
    contract = (((1,), (1,)), ((), ())) if across else (((1,), (0,)), ((), ()))

    def group(index, _):
        targets, terms = [], []
        for step in range(GROUP):
            left, right = [], []
            for half in range(2):
                first = ((index * GROUP + step) * 2 + half) * PACK
                places = [first + each for each in range(PACK)]
                left.append(jnp.concatenate([source[order[1, each]] for each in places], axis=1))
                right.append(jnp.concatenate([vals[order[0, each]] for each in places],
                                             axis=1 if across else 0))
                targets.append(order[2, first])
            both = lax.dot_general(
                jnp.concatenate(left, axis=0), jnp.concatenate(right, axis=0 if across else 1),
                contract, preferred_element_type=F32,
            )
            terms += [both[:width, :size], both[width:, size:]]
        for target, term in zip(targets, terms):
            total[target] += term
        return 0

    lax.fori_loop(0, (order[3, 0] + 2 * GROUP - 1) // (2 * GROUP), group, 0)


def begin(out):
    out[...] = jnp.zeros_like(out)


def stack_ids(user, positive, negative, after, out):
    out[...] = jnp.zeros_like(out)
    for row, ids in enumerate((user, positive, negative)):
        out[row:row + 1, :] = ids[...]


def pack_ids(places, *refs):
    out = refs[-1]
    out[...] = jnp.zeros_like(out)
    for offset, (index, row) in enumerate(places):
        out[3 * offset:3 * offset + 3, :] = refs[index][row:row + 3, :]


def prepare(count, rows, columns, user_emb, item_emb, user_deg, item_deg, after,
            user_source, item_source, user_scale, item_scale, item_order, user_order, keys):
    live = count[0]
    slots = rows.shape[0]
    keys[...] = jnp.zeros_like(keys)
    keys[0:1, 0:slots] = rows[...].reshape(1, slots)
    keys[1:2, 0:slots] = columns[...].reshape(1, slots)
    users, items = keys[0:1, :], keys[1:2, :]
    item_order[...] = sort_slots(items, users, live, item_scale.shape[0])
    user_order[...] = sort_slots(users, items, live, user_scale.shape[0])
    for emb, deg, scale, into in ((user_emb, user_deg, user_scale, user_source),
                                  (item_emb, item_deg, item_scale, item_source)):
        scale[...] = lax.rsqrt(deg[...].astype(F32))
        blocks, size = scale.shape
        for block in range(blocks):
            piece = emb[:, block * size:(block + 1) * size].astype(F32)
            into[block] = (scale[block:block + 1, :] * piece).astype(BF16)
        into[blocks] = jnp.zeros(into.shape[1:], BF16)


def first_pass(across, order, vals, source, *refs):
    multiply_blocks(order, vals, source, refs[-1], across)


def fold(stacked, width):
    return (
        stacked[:width] + stacked[width:2 * width] + stacked[2 * width:3 * width]
    )


def rows_of(ref, rows):
    return [ref[row:row + 1, :] for row in rows]


def pick(table, ids, tile):
    total = None
    for start in range(0, table.shape[1], tile):
        term = jnp.dot(
            table[:, start:start + tile], hot(ids, start, tile),
            preferred_element_type=F32,
        )
        total = term if total is None else total + term
    return total


def gather(places, count, mine, other, scale, after, *refs):
    ids, outs, table = refs[:count], refs[count:-1], refs[-1]
    blocks, width, size = mine.shape
    for block in range(blocks):
        span = slice(block * size, (block + 1) * size)
        here = scale[block:block + 1, :] * (mine[block] + other[block])
        for part, piece in enumerate(split3(here)):
            table[part * width:(part + 1) * width, span] = piece
    for out, (index, rows) in zip(outs, places):
        out[...] = fold(pick(table, rows_of(ids[index], rows), 2 * size), width)


def scatter(pieces, ids, table, blocks, size, put):
    width = table.shape[1] // 3
    tile = 2 * size
    for place, piece in enumerate(pieces):
        for part, value in enumerate(split3(piece[:width, :])):
            table[place, part * width:(part + 1) * width, :] = value
    for start in range(0, blocks * size, tile):
        total = None
        for place, rows in enumerate(ids):
            term = lax.dot_general(
                table[place], hot(rows, start, tile), (((1,), (1,)), ((), ())),
                preferred_element_type=F32,
            )
            total = term if total is None else total + term
        total = fold(total, width)
        for offset in range(0, tile, size):
            put((start + offset) // size, total[:, offset:offset + size])


def scatter_items(places, after, *refs):
    peers = len(places)
    pieces, ids, out, table = refs[:peers], refs[peers:-2], refs[-2], refs[-1]
    blocks, _, size = out.shape

    def put(block, value):
        out[block] = value

    scatter(pieces, [rows_of(ids[index], rows) for index, rows in places],
            table, blocks, size, put)


def gather_base(user_emb, item_emb, ids, after, user_out, item_out):
    tile = ids.shape[1]
    user_out[...] = pick(user_emb, rows_of(ids, [0]), tile)
    item_out[...] = pick(item_emb, rows_of(ids, [1, 2]), tile)


def add_all(refs):
    total = refs[0][...]
    for ref in refs[1:]:
        total = total + ref[...]
    return total


def slopes(user_parts, item_parts, ids, *refs):
    users, items = refs[:user_parts], refs[user_parts:user_parts + item_parts]
    pieces, pushed = refs[user_parts + item_parts:]
    width = pushed.shape[0]
    user_rows = 0.5 * add_all(users)
    difference = 0.5 * add_all(items)
    margin = jnp.sum(user_rows * difference, axis=0, keepdims=True)
    slope = -jax.nn.sigmoid(-margin)
    pieces[:width, :] = slope * difference
    pieces[width:, :] = jnp.broadcast_to(ids[0:1, :].astype(F32), (8, ids.shape[1]))
    pushed[...] = slope * user_rows


def halves(total, keep, send):
    me = lax.axis_index("rep")
    half = keep.shape[1]
    for block in range(keep.shape[0]):
        keep[block] = total[block, pl.ds(pl.multiple_of(me * half, half), half), :]
        send[block] = total[block, pl.ds(pl.multiple_of((1 - me) * half, half), half), :]


def second_items(parts, order, source_scale, target_scale, vals, *refs):
    pieces = refs[:parts]
    half_grad, keep, send, source, total, table = refs[parts:]
    blocks, width, size = half_grad.shape

    def put(block, grad):
        half_grad[block] = 0.5 * grad
        source[block] = (source_scale[block:block + 1, :] * grad * 0.5).astype(BF16)

    ids = [[piece[width:width + 1, :].astype(jnp.int32)] for piece in pieces]
    scatter(pieces, ids, table, blocks, size, put)
    source[blocks] = jnp.zeros((width, size), BF16)
    multiply_blocks(order, vals, source, total, False)
    for block in range(total.shape[0]):
        total[block] = target_scale[block:block + 1, :] * total[block]
    halves(total, keep, send)


def second_users(order, mine, other, source_scale, target_scale, vals, after,
                 half_grad, keep, send, source, total):
    blocks, width, size = mine.shape
    for block in range(blocks):
        grad = mine[block] + other[block]
        half_grad[block] = 0.5 * grad
        source[block] = (source_scale[block:block + 1, :] * grad * 0.5).astype(BF16)
    source[blocks] = jnp.zeros((width, size), BF16)
    multiply_blocks(order, vals, source, total, True)
    for block in range(total.shape[0]):
        total[block] = target_scale[block:block + 1, :] * total[block]
    halves(total, keep, send)


def copy(values, *refs):
    refs[-1][...] = values[...]


def add_deal(offsets, keep, received, after, *outs):
    me = lax.axis_index("user")
    per = outs[0].shape[0]
    for out, offset in zip(outs, offsets):
        there = (me ^ offset) * per
        for block in range(per):
            out[block] = keep[there + block] + received[there + block]


def sum_parts(*refs):
    refs[-1][...] = add_all(refs[:-1])


def sum_after(count, *refs):
    sum_parts(*refs[count:])


def pack(*refs):
    for place, ref in enumerate(refs[:-1]):
        refs[-1][place] = ref[...]


def finish(offsets, user_half_grad, user_mine, user_other, item_half_grad, item_mine, item_other,
           user_out, item_out):
    finish_users(user_half_grad, user_mine, user_other, user_out)
    finish_items(offsets, item_half_grad, item_mine, item_other, item_out)


def finish_users(half_grad, mine, other, out):
    me = lax.axis_index("rep")
    blocks, width, size = half_grad.shape
    half = width // 2
    for block in range(blocks):
        span = slice(block * size, (block + 1) * size)
        for rank, part in ((me, mine), (1 - me, other)):
            rows = pl.ds(pl.multiple_of(rank * half, half), half)
            out[rows, span] = half_grad[block, rows, :] + part[block]


def finish_items(offsets, half_grad, mine, other, out):
    me = lax.axis_index("rep")
    place = lax.axis_index("user")
    _, per, half, size = mine.shape
    for index, offset in enumerate(offsets):
        there = (place ^ offset) * per
        for block in range(per):
            span = pl.ds(pl.multiple_of((there + block) * size, size), size)
            for rank, part in ((me, mine), (1 - me, other)):
                rows = pl.ds(pl.multiple_of(rank * half, half), half)
                out[rows, span] = half_grad[there + block, rows, :] + part[index, block]


def swap(values, axis="rep", peers=2, offset=1):
    return lax.ppermute(values, axis, [(i, i ^ offset) for i in range(peers)])


def on_device(users, items, user_emb, item_emb, user_deg, item_deg, block_vals, block_row,
              block_col, block_count, trip_user, trip_pos, trip_neg):
    width = user_emb.shape[0]
    slots, size, _ = block_vals.shape
    user_blocks = user_emb.shape[1] // size
    item_blocks = item_emb.shape[1] // size
    trips = trip_user.shape[0]
    half = width // 2
    user_deg = user_deg.reshape(user_blocks, size)
    item_deg = item_deg.reshape(item_blocks, size)

    product_flops = 2 * slots * size * size * width
    product_bytes = slots * size * size * 2
    started = call(begin, shape(8, size), (), [], (), 16 * product_flops, product_bytes)
    id_rows = max(16, -(-3 * users // 16) * 8)
    ids_shape = jax.ShapeDtypeStruct((id_rows, trips), jnp.int32)
    ids = call(
        stack_ids, ids_shape,
        [each.reshape(1, trips) for each in (trip_user, trip_pos, trip_neg)] + [started],
        [VMEM, VMEM, VMEM, ANY],
    )
    ids_user = [ids] + [swap(ids, "item", items, o) for o in range(1, items)]
    met = sorted(range(1, users), key=lambda offset: (offset != users // 2, -offset))
    back = met[::-1]
    ids_item, held, step = [(0, 0)], [ids], 1
    while step < users:
        packed = ids if step == 1 else call(
            functools.partial(pack_ids, ids_item), ids_shape, held, [VMEM] * len(held))
        held.append(swap(packed, "user", users, step))
        ids_item += [(len(held) - 1, 3 * place) for place in range(step)]
        step *= 2
    lanes = -(-slots // size) * size

    order_shape = jax.ShapeDtypeStruct((4, lanes), jnp.int32)

    def source_shape(blocks):
        return jax.ShapeDtypeStruct((blocks + 1, width, size), BF16)

    (user_source, item_source, user_scale, item_scale, item_order, user_order) = call(
        prepare,
        [source_shape(user_blocks), source_shape(item_blocks), shape(user_blocks, size),
         shape(item_blocks, size), order_shape, order_shape],
        (block_count, block_row, block_col, user_emb, item_emb, user_deg, item_deg, ids),
        [SMEM, VMEM, VMEM, VMEM, VMEM, VMEM, VMEM, ANY],
        [pltpu.VMEM((8, lanes), jnp.int32)], product_flops, product_bytes,
    )
    item_table = call(
        functools.partial(first_pass, False), shape(item_blocks, width, size),
        (item_order, block_vals, user_source, ids), [SMEM, VMEM, VMEM, ANY], (),
        product_flops, product_bytes,
    )
    user_table = call(
        functools.partial(first_pass, True), shape(user_blocks, width, size),
        (user_order, block_vals, item_source, item_table, *ids_user[1:]),
        [SMEM, VMEM, VMEM] + [ANY] * items, (),
        HEAVY, product_bytes,
    )

    hot_flops = 2 * 3 * width * trips * size

    def picked(table, other, scale, arrays, places, after, flops):
        return call(
            functools.partial(gather, places, len(arrays)), [shape(width, trips)] * len(places),
            (table, other, scale, after, *arrays),
            [VMEM] * 3 + [ANY] + [VMEM] * len(arrays),
            [pltpu.VMEM((3 * width, scale.shape[0] * size), BF16)], flops,
        )

    def item_rows(offset):
        index, row = ids_item[offset]
        return index, [row + 1, row + 2]

    other = swap(item_table)
    first = picked(item_table, other, item_scale, held, [item_rows(o) for o in met[:1]], ids, 0)
    rest = picked(item_table, other, item_scale, held, [item_rows(o) for o in [0, *met[1:]]],
                  first[0] if first else ids, HEAVY)
    item_parts = [rest[0]]
    for offset, part in zip(met, [*first, *rest[1:]]):
        come = swap(part, "user", users, offset)
        item_parts.append(hold(come, flops=MEDIUM) if offset == met[0] else come)
    dealt = picked(user_table, swap(user_table), user_scale, ids_user,
                   [(o, [0]) for o in range(items)], rest[0], 0)
    user_parts = [dealt[0]] + [
        swap(part, "item", items, o) for o, part in zip(range(1, items), dealt[1:])]
    user_base, item_base = call(
        gather_base, [shape(width, trips)] * 2, (user_emb, item_emb, ids, dealt[0]),
        [VMEM, VMEM, VMEM, ANY], (), 4 * width * trips * size * (user_blocks + item_blocks),
        2 * width * size * (user_blocks + item_blocks),
    )
    user_parts.append(user_base)
    item_parts.append(item_base)
    pieces, pushed = call(
        functools.partial(slopes, len(user_parts), len(item_parts)),
        [shape(width + 8, trips), shape(width, trips)],
        (ids, *user_parts, *item_parts), [VMEM] * (1 + len(user_parts) + len(item_parts)),
        moved=4 * width * trips * (len(user_parts) + len(item_parts) + 2),
    )

    arrays = [pieces, swap(pieces)]
    for offset in range(1, items):
        arrays.append(swap(pieces, "item", items, offset))
        arrays.append(lax.ppermute(pieces, ("item", "rep"), [
            (i, i ^ (2 * offset + 1)) for i in range(2 * items)]))
    user_half_grad, item_keep, item_send = call(
        functools.partial(second_items, len(arrays)),
        [shape(user_blocks, width, size)] + [shape(item_blocks, half, size)] * 2,
        (item_order, user_scale, item_scale, block_vals, *arrays),
        [SMEM] + [VMEM] * (3 + len(arrays)),
        [pltpu.VMEM((user_blocks + 1, width, size), BF16),
         pltpu.VMEM((item_blocks, width, size), F32),
         pltpu.VMEM((len(arrays), 3 * width, trips), BF16)],
        product_flops, product_bytes,
    )
    arrays = [pushed] + [swap(pushed, "user", users, o) for o in back]
    item_grad = call(
        functools.partial(scatter_items, [item_rows(o) for o in [0, *back]]),
        shape(item_blocks, width, size),
        (item_send, *arrays, *held), [ANY] + [VMEM] * (users + len(held)),
        [pltpu.VMEM((users, 3 * width, trips), BF16)], HEAVY, 0,
    )

    per = item_blocks // users
    dealt = call(
        functools.partial(add_deal, [0, *met]), [shape(per, half, size)] * users,
        (item_keep, swap(item_send), item_grad), [VMEM, VMEM, ANY], (), HEAVY,
    )
    item_half_grad, user_keep, user_send = call(
        second_users,
        [shape(item_blocks, width, size)] + [shape(user_blocks, half, size)] * 2,
        (user_order, item_grad, swap(item_grad), item_scale, user_scale, block_vals, dealt[0]),
        [SMEM] + [VMEM] * 5 + [ANY],
        [pltpu.VMEM((item_blocks + 1, width, size), BF16),
         pltpu.VMEM((user_blocks, width, size), F32)],
        product_flops, product_bytes,
    )
    parts = [dealt[0]] + [swap(part, "user", users, o) for part, o in zip(dealt[1:], met)]
    item_own = call(functools.partial(sum_after, 1), shape(per, half, size), (user_keep, *parts),
                    [ANY] + [VMEM] * users,
               moved=4 * (users + 1) * per * half * size)
    user_send = hold(user_send, item_own)

    own = call(sum_parts, shape(user_blocks, half, size), (user_keep, swap(user_send)),
               [VMEM, VMEM], moved=12 * user_blocks * half * size)
    late = hold(item_own, own)
    item_mine = {0: item_own}
    for offset in [users - 1, *range(1, users - 1)] if users > 1 else []:
        part = item_own if offset == users - 1 else late
        item_mine[offset] = swap(part, "user", users, offset)
    if users > 2:
        item_mine[users - 1] = hold(item_mine[users - 1], flops=MEDIUM)
    item_places = list(item_mine)
    item_mine = call(pack, shape(users, per, half, size), tuple(item_mine.values()),
                     [VMEM] * users, moved=8 * item_blocks * half * size)
    mine = call(functools.partial(sum_after, 1), shape(user_blocks, half, size),
                (item_mine, own, *[swap(own, "item", items, o) for o in range(1, items)]),
                [ANY] + [VMEM] * items, moved=12 * user_blocks * half * size)
    return call(
        functools.partial(finish, item_places),
        (shape(width, user_blocks * size), shape(width, item_blocks * size)),
        (user_half_grad, mine, swap(mine), item_half_grad, item_mine, swap(item_mine)),
        [VMEM] * 6, moved=12 * (user_blocks + item_blocks) * width * size,
    )


def solution(mesh):
    return jax.shard_map(
        functools.partial(on_device, mesh.shape["user"], mesh.shape["item"]),
        mesh=mesh,
        in_specs=(
            P(None, ("groups", "user")),
            P(None, ("groups", "item")),
            P(("groups", "user")),
            P(("groups", "item")),
            P(("groups", "user", "item", "rep"), None, None),
            P(("groups", "user", "item", "rep")),
            P(("groups", "user", "item", "rep")),
            P(("groups", "user", "item", "rep")),
            P(("groups", "user", "item", "rep")),
            P(("groups", "user", "item", "rep")),
            P(("groups", "user", "item", "rep")),
        ),
        out_specs=(P(None, ("groups", "user")), P(None, ("groups", "item"))),
        check_vma=False,
    )
```

```python
import functools

import jax
import jax.numpy as jnp
from jax import lax
from jax.experimental import pallas as pl
from jax.experimental.pallas import tpu as pltpu
from jax.sharding import PartitionSpec as P

F32 = jnp.float32
BF16 = jnp.bfloat16
PACK = 4
GROUP = 8
HEAVY = 10 ** 11
MEDIUM = 24 * 10 ** 8

VMEM = pl.BlockSpec(memory_space=pltpu.VMEM)
SMEM = pl.BlockSpec(memory_space=pltpu.SMEM)
ANY = pl.BlockSpec(memory_space=pl.ANY)
HBM = pl.BlockSpec(memory_space=pltpu.HBM)


def call(kernel, outs, ins, specs, scratch=(), flops=0, moved=0, room=16):
    return pl.pallas_call(
        kernel,
        out_shape=outs,
        in_specs=specs,
        out_specs=jax.tree.map(lambda _: VMEM, outs),
        scratch_shapes=list(scratch),
        cost_estimate=pl.CostEstimate(flops=flops, bytes_accessed=moved, transcendentals=0),
        compiler_params=pltpu.CompilerParams(vmem_limit_bytes=room * 1024 * 1024),
    )(*ins)


def hold(values, *after, flops=0):
    return call(copy, jax.ShapeDtypeStruct(values.shape, values.dtype), (values, *after),
                [VMEM] + [ANY] * len(after), flops=flops)


def shape(*dims):
    return jax.ShapeDtypeStruct(dims, F32)


def split3(values):
    high = values.astype(BF16)
    rest = values - high.astype(F32)
    middle = rest.astype(BF16)
    low = (rest - middle.astype(F32)).astype(BF16)
    return high, middle, low


def hot(ids, start, tile):
    if len(ids) == 2:
        same = ids[0] == ids[1]
        ids = [jnp.where(same, -1, each) for each in ids]
    ids = [each.astype(jnp.int16) for each in ids]
    place = lax.broadcasted_iota(jnp.int16, (tile, ids[0].shape[1]), 0) + jnp.int16(start)
    chosen = jnp.zeros(place.shape, BF16)
    for each, sign in zip(ids, (1, -1)):
        chosen = jnp.where(place == each, jnp.asarray(sign, BF16), chosen)
    return chosen


def sort_slots(keys, sources, count, blocks):
    lanes = keys.shape[1]
    rows = 2 * blocks
    place = lax.broadcasted_iota(jnp.int32, (1, lanes), 1)
    live = place < count
    mine = (lax.broadcasted_iota(jnp.int32, (rows, lanes), 0) == keys) & live
    mine = jnp.where(mine, 1.0, 0.0)
    earlier = lax.broadcasted_iota(jnp.int32, (lanes, lanes), 0) < lax.broadcasted_iota(
        jnp.int32, (lanes, lanes), 1)
    before = jnp.dot(mine.astype(BF16), jnp.where(earlier, 1.0, 0.0).astype(BF16),
                     preferred_element_type=F32)
    packs = jnp.floor((jnp.sum(mine, axis=1, keepdims=True) + (PACK - 1)) * (1.0 / PACK))
    packs = jnp.broadcast_to(packs, (rows, 128))
    lower = lax.broadcasted_iota(jnp.int32, (rows, rows), 1) < lax.broadcasted_iota(
        jnp.int32, (rows, rows), 0)
    first = jnp.dot(jnp.where(lower, 1.0, 0.0).astype(BF16), packs.astype(BF16),
                    preferred_element_type=F32)
    position = jnp.sum(mine * (first[:, :1] * PACK + before), axis=0, keepdims=True)
    position = jnp.where(live, position.astype(jnp.int32), -1)
    match = lax.broadcasted_iota(jnp.int32, (lanes, lanes), 0) == position
    row = lax.broadcasted_iota(jnp.int32, (16, lanes), 0)
    values = jnp.where(row == 0, place // 16, jnp.where(row == 1, place % 16, jnp.where(
        row == 2, sources, jnp.where(row == 3, keys, jnp.where(row == 4, 1, 0)))))
    values = jnp.where(live, values, 0).astype(F32)
    found = lax.dot_general(values.astype(BF16), jnp.where(match, 1.0, 0.0).astype(BF16),
                            (((1,), (1,)), ((), ())), preferred_element_type=F32)
    found = found.astype(jnp.int32)
    valid = found[4:5] > 0
    total = jnp.broadcast_to(jnp.sum(packs[:, :1], axis=0, keepdims=True), (1, lanes))
    row = lax.broadcasted_iota(jnp.int32, (4, lanes), 0)
    slot = found[0:1] * 16 + found[1:2]
    source = jnp.where(valid, found[2:3], blocks)
    target = jnp.where(valid, found[3:4], 0)
    return jnp.where(row == 0, slot, jnp.where(row == 1, source, jnp.where(
        row == 2, target, total.astype(jnp.int32))))


def multiply_blocks(order, vals, source, total, across):
    _, width, size = source.shape
    total[...] = jnp.zeros_like(total)
    contract = (((1,), (1,)), ((), ())) if across else (((1,), (0,)), ((), ()))

    def group(index, _):
        targets, terms = [], []
        for step in range(GROUP):
            left, right = [], []
            for half in range(2):
                first = ((index * GROUP + step) * 2 + half) * PACK
                places = [first + each for each in range(PACK)]
                left.append(jnp.concatenate([source[order[1, each]] for each in places], axis=1))
                right.append(jnp.concatenate([vals[order[0, each]] for each in places],
                                             axis=1 if across else 0))
                targets.append(order[2, first])
            both = lax.dot_general(
                jnp.concatenate(left, axis=0), jnp.concatenate(right, axis=0 if across else 1),
                contract, preferred_element_type=F32,
            )
            terms += [both[:width, :size], both[width:, size:]]
        for target, term in zip(targets, terms):
            total[target] += term
        return 0

    lax.fori_loop(0, (order[3, 0] + 2 * GROUP - 1) // (2 * GROUP), group, 0)


def begin(out):
    out[...] = jnp.zeros_like(out)


def stack_ids(user, positive, negative, after, out):
    out[...] = jnp.zeros_like(out)
    for row, ids in enumerate((user, positive, negative)):
        out[row:row + 1, :] = ids[...]


def pack_ids(places, *refs):
    out = refs[-1]
    out[...] = jnp.zeros_like(out)
    for offset, (index, row) in enumerate(places):
        out[3 * offset:3 * offset + 3, :] = refs[index][row:row + 3, :]


def prepare(count, rows, columns, user_emb, item_emb, user_deg, item_deg, after,
            user_source, item_source, user_scale, item_scale, item_order, user_order, keys):
    live = count[0]
    slots = rows.shape[0]
    keys[...] = jnp.zeros_like(keys)
    keys[0:1, 0:slots] = rows[...].reshape(1, slots)
    keys[1:2, 0:slots] = columns[...].reshape(1, slots)
    users, items = keys[0:1, :], keys[1:2, :]
    item_order[...] = sort_slots(items, users, live, item_scale.shape[0])
    user_order[...] = sort_slots(users, items, live, user_scale.shape[0])
    for emb, deg, scale, into in ((user_emb, user_deg, user_scale, user_source),
                                  (item_emb, item_deg, item_scale, item_source)):
        scale[...] = lax.rsqrt(deg[...].astype(F32))
        blocks, size = scale.shape
        for block in range(blocks):
            piece = emb[:, block * size:(block + 1) * size].astype(F32)
            into[block] = (scale[block:block + 1, :] * piece).astype(BF16)
        into[blocks] = jnp.zeros(into.shape[1:], BF16)


def first_pass(across, order, vals, source, *refs):
    multiply_blocks(order, vals, source, refs[-1], across)


def fold(stacked, width):
    return (
        stacked[:width] + stacked[width:2 * width] + stacked[2 * width:3 * width]
    )


def rows_of(ref, rows):
    return [ref[row:row + 1, :] for row in rows]


def pick(table, ids, tile):
    total = None
    for start in range(0, table.shape[1], tile):
        term = jnp.dot(
            table[:, start:start + tile], hot(ids, start, tile),
            preferred_element_type=F32,
        )
        total = term if total is None else total + term
    return total


def gather(places, count, mine, other, scale, after, *refs):
    ids, outs, table = refs[:count], refs[count:-1], refs[-1]
    blocks, width, size = mine.shape
    for block in range(blocks):
        span = slice(block * size, (block + 1) * size)
        here = scale[block:block + 1, :] * (mine[block] + other[block])
        for part, piece in enumerate(split3(here)):
            table[part * width:(part + 1) * width, span] = piece
    for out, (index, rows) in zip(outs, places):
        out[...] = fold(pick(table, rows_of(ids[index], rows), 2 * size), width)


def scatter(pieces, ids, table, blocks, size, put):
    width = table.shape[1] // 3
    tile = 2 * size
    for place, piece in enumerate(pieces):
        for part, value in enumerate(split3(piece[:width, :])):
            table[place, part * width:(part + 1) * width, :] = value
    for start in range(0, blocks * size, tile):
        total = None
        for place, rows in enumerate(ids):
            term = lax.dot_general(
                table[place], hot(rows, start, tile), (((1,), (1,)), ((), ())),
                preferred_element_type=F32,
            )
            total = term if total is None else total + term
        total = fold(total, width)
        for offset in range(0, tile, size):
            put((start + offset) // size, total[:, offset:offset + size])


def scatter_items(places, after, *refs):
    peers = len(places)
    pieces, ids, out, table = refs[:peers], refs[peers:-2], refs[-2], refs[-1]
    blocks, _, size = out.shape

    def put(block, value):
        out[block] = value

    scatter(pieces, [rows_of(ids[index], rows) for index, rows in places],
            table, blocks, size, put)


def gather_base(user_emb, item_emb, ids, user_out, item_out):
    tile = ids.shape[1]
    user_out[...] = pick(user_emb, rows_of(ids, [0]), tile)
    item_out[...] = pick(item_emb, rows_of(ids, [1, 2]), tile)


def add_all(refs):
    total = refs[0][...]
    for ref in refs[1:]:
        total = total + ref[...]
    return total


def slopes(user_parts, item_parts, ids, *refs):
    users, items = refs[:user_parts], refs[user_parts:user_parts + item_parts]
    pieces, pushed = refs[user_parts + item_parts:]
    width = pushed.shape[0]
    user_rows = 0.5 * add_all(users)
    difference = 0.5 * add_all(items)
    margin = jnp.sum(user_rows * difference, axis=0, keepdims=True)
    slope = -jax.nn.sigmoid(-margin)
    pieces[:width, :] = slope * difference
    pieces[width:, :] = jnp.broadcast_to(ids[0:1, :].astype(F32), (8, ids.shape[1]))
    pushed[...] = slope * user_rows


def halves(total, keep, send):
    me = lax.axis_index("rep")
    half = keep.shape[1]
    for block in range(keep.shape[0]):
        keep[block] = total[block, pl.ds(pl.multiple_of(me * half, half), half), :]
        send[block] = total[block, pl.ds(pl.multiple_of((1 - me) * half, half), half), :]


def second_items(parts, order, source_scale, target_scale, vals, *refs):
    pieces = refs[:parts]
    half_grad, keep, send, source, total, table = refs[-6:]
    blocks, width, size = half_grad.shape

    def put(block, grad):
        half_grad[block] = 0.5 * grad
        source[block] = (source_scale[block:block + 1, :] * grad * 0.5).astype(BF16)

    ids = [[piece[width:width + 1, :].astype(jnp.int32)] for piece in pieces]
    scatter(pieces, ids, table, blocks, size, put)
    source[blocks] = jnp.zeros((width, size), BF16)
    multiply_blocks(order, vals, source, total, False)
    for block in range(total.shape[0]):
        total[block] = target_scale[block:block + 1, :] * total[block]
    halves(total, keep, send)


def second_users(order, mine, other, source_scale, target_scale, vals, after,
                 half_grad, keep, send, source, total):
    blocks, width, size = mine.shape
    for block in range(blocks):
        grad = mine[block] + other[block]
        half_grad[block] = 0.5 * grad
        source[block] = (source_scale[block:block + 1, :] * grad * 0.5).astype(BF16)
    source[blocks] = jnp.zeros((width, size), BF16)
    multiply_blocks(order, vals, source, total, True)
    for block in range(total.shape[0]):
        total[block] = target_scale[block:block + 1, :] * total[block]
    halves(total, keep, send)


def copy(values, *refs):
    refs[-1][...] = values[...]


def add_deal(offsets, keep, received, after, *outs):
    me = lax.axis_index("user")
    per = outs[0].shape[0]
    for out, offset in zip(outs, offsets):
        there = (me ^ offset) * per
        for block in range(per):
            out[block] = keep[there + block] + received[there + block]


def sum_parts(*refs):
    refs[-1][...] = add_all(refs[:-1])


def sum_after(count, *refs):
    sum_parts(*refs[count:])


def pack(*refs):
    for place, ref in enumerate(refs[:-1]):
        refs[-1][place] = ref[...]


def finish(offsets, user_half_grad, user_mine, user_other, item_half_grad, item_mine, item_other,
           user_out, item_out):
    finish_users(user_half_grad, user_mine, user_other, user_out)
    finish_items(offsets, item_half_grad, item_mine, item_other, item_out)


def finish_users(half_grad, mine, other, out):
    me = lax.axis_index("rep")
    blocks, width, size = half_grad.shape
    half = width // 2
    for block in range(blocks):
        span = slice(block * size, (block + 1) * size)
        for rank, part in ((me, mine), (1 - me, other)):
            rows = pl.ds(pl.multiple_of(rank * half, half), half)
            out[rows, span] = half_grad[block, rows, :] + part[block]


def finish_items(offsets, half_grad, mine, other, out):
    me = lax.axis_index("rep")
    place = lax.axis_index("user")
    _, per, half, size = mine.shape
    for index, offset in enumerate(offsets):
        there = (place ^ offset) * per
        for block in range(per):
            span = pl.ds(pl.multiple_of((there + block) * size, size), size)
            for rank, part in ((me, mine), (1 - me, other)):
                rows = pl.ds(pl.multiple_of(rank * half, half), half)
                out[rows, span] = half_grad[there + block, rows, :] + part[index, block]


def swap(values, axis="rep", peers=2, offset=1):
    return lax.ppermute(values, axis, [(i, i ^ offset) for i in range(peers)])


def on_device(users, items, user_emb, item_emb, user_deg, item_deg, block_vals, block_row,
              block_col, block_count, trip_user, trip_pos, trip_neg):
    width = user_emb.shape[0]
    slots, size, _ = block_vals.shape
    user_blocks = user_emb.shape[1] // size
    item_blocks = item_emb.shape[1] // size
    trips = trip_user.shape[0]
    half = width // 2
    user_deg = user_deg.reshape(user_blocks, size)
    item_deg = item_deg.reshape(item_blocks, size)

    product_flops = 2 * slots * size * size * width
    product_bytes = slots * size * size * 2
    started = call(begin, shape(8, size), (), [], (), 16 * product_flops, product_bytes)
    id_rows = max(16, -(-3 * users // 16) * 8)
    ids_shape = jax.ShapeDtypeStruct((id_rows, trips), jnp.int32)
    ids = call(
        stack_ids, ids_shape,
        [each.reshape(1, trips) for each in (trip_user, trip_pos, trip_neg)] + [started],
        [VMEM, VMEM, VMEM, ANY],
    )
    ids_user = [ids] + [swap(ids, "item", items, o) for o in range(1, items)]
    met = sorted(range(1, users), key=lambda offset: (offset != users // 2, -offset))
    back = met[::-1]
    ids_item, held, step = [(0, 0)], [ids], 1
    while step < users:
        packed = ids if step == 1 else call(
            functools.partial(pack_ids, ids_item), ids_shape, held, [VMEM] * len(held))
        held.append(swap(packed, "user", users, step))
        ids_item += [(len(held) - 1, 3 * place) for place in range(step)]
        step *= 2
    lanes = -(-slots // size) * size

    order_shape = jax.ShapeDtypeStruct((4, lanes), jnp.int32)

    def source_shape(blocks):
        return jax.ShapeDtypeStruct((blocks + 1, width, size), BF16)

    (user_source, item_source, user_scale, item_scale, item_order, user_order) = call(
        prepare,
        [source_shape(user_blocks), source_shape(item_blocks), shape(user_blocks, size),
         shape(item_blocks, size), order_shape, order_shape],
        (block_count, block_row, block_col, user_emb, item_emb, user_deg, item_deg, ids),
        [SMEM, VMEM, VMEM, VMEM, VMEM, VMEM, VMEM, ANY],
        [pltpu.VMEM((8, lanes), jnp.int32)], product_flops, product_bytes,
    )
    item_table = call(
        functools.partial(first_pass, False), shape(item_blocks, width, size),
        (item_order, block_vals, user_source, ids), [SMEM, VMEM, VMEM, ANY], (),
        product_flops, product_bytes,
    )
    user_table = call(
        functools.partial(first_pass, True), shape(user_blocks, width, size),
        (user_order, block_vals, item_source, item_table, *ids_user[1:]),
        [SMEM, VMEM, VMEM] + [ANY] * items, (),
        HEAVY, product_bytes,
    )

    hot_flops = 2 * 3 * width * trips * size

    def reduced(table, scale, arrays, places, axis, offsets, after):
        peers, blocks = len(places), scale.shape[0]
        dealt = call(
            functools.partial(gather, places, len(arrays)), [shape(width, trips)] * peers,
            (table, swap(table), scale, after, *arrays),
            [VMEM] * 3 + [ANY] + [VMEM] * len(arrays),
            [pltpu.VMEM((3 * width, blocks * size), BF16)],
            HEAVY if axis == "user" else 0, 8 * blocks * width * size,
        )
        return [dealt[0]] + [swap(part, axis, peers, o) for part, o in zip(dealt[1:], offsets)]

    def item_rows(offset):
        index, row = ids_item[offset]
        return index, [row + 1, row + 2]

    item_parts = reduced(item_table, item_scale, held, [item_rows(o) for o in [0, *met]],
                         "user", met, ids)
    user_parts = reduced(user_table, user_scale, ids_user, [(o, [0]) for o in range(items)],
                         "item", list(range(1, items)), item_parts[0])
    user_base, item_base = call(
        gather_base, [shape(width, trips)] * 2, (user_emb, item_emb, ids),
        [VMEM, VMEM, VMEM], (), 4 * width * trips * size * (user_blocks + item_blocks),
        2 * width * size * (user_blocks + item_blocks),
    )
    user_parts.append(user_base)
    item_parts.append(item_base)
    pieces, pushed = call(
        functools.partial(slopes, len(user_parts), len(item_parts)),
        [shape(width + 8, trips), shape(width, trips)],
        (ids, *user_parts, *item_parts), [VMEM] * (1 + len(user_parts) + len(item_parts)),
        moved=4 * width * trips * (len(user_parts) + len(item_parts) + 2),
    )

    arrays = [pieces, swap(pieces)]
    for offset in range(1, items):
        arrays.append(swap(pieces, "item", items, offset))
        arrays.append(lax.ppermute(pieces, ("item", "rep"), [
            (i, i ^ (2 * offset + 1)) for i in range(2 * items)]))
    shared, step = {0: pushed}, 1
    while step < users:
        for offset, part in list(shared.items()):
            shared[offset ^ step] = swap(part, "user", users, step)
        if 2 * step < users:
            shared[step] = hold(shared[step], flops=0)
        step *= 2
    user_half_grad, item_keep, item_send = call(
        functools.partial(second_items, len(arrays)),
        [shape(user_blocks, width, size)] + [shape(item_blocks, half, size)] * 2,
        (item_order, user_scale, item_scale, block_vals, *arrays, *list(shared.values())[1:2]),
        [SMEM] + [VMEM] * (3 + len(arrays)) + [ANY] * min(1, users - 1),
        [pltpu.VMEM((user_blocks + 1, width, size), BF16),
         pltpu.VMEM((item_blocks, width, size), F32),
         pltpu.VMEM((len(arrays), 3 * width, trips), BF16)],
        product_flops, product_bytes,
    )
    item_grad = call(
        functools.partial(scatter_items, [item_rows(o) for o in shared]),
        shape(item_blocks, width, size),
        (item_send, *shared.values(), *held), [ANY] + [VMEM] * (users + len(held)),
        [pltpu.VMEM((users, 3 * width, trips), BF16)], HEAVY, 0,
    )

    per = item_blocks // users
    dealt = call(
        functools.partial(add_deal, [0, *met]), [shape(per, half, size)] * users,
        (item_keep, swap(item_send), item_grad), [VMEM, VMEM, ANY], (), HEAVY,
    )
    item_half_grad, user_keep, user_send = call(
        second_users,
        [shape(item_blocks, width, size)] + [shape(user_blocks, half, size)] * 2,
        (user_order, item_grad, swap(item_grad), item_scale, user_scale, block_vals, dealt[0]),
        [SMEM] + [VMEM] * 5 + [ANY],
        [pltpu.VMEM((item_blocks + 1, width, size), BF16),
         pltpu.VMEM((user_blocks, width, size), F32)],
        product_flops, product_bytes,
    )
    parts = [dealt[0]] + [swap(part, "user", users, o) for part, o in zip(dealt[1:], met)]
    item_own = call(functools.partial(sum_after, 1), shape(per, half, size), (user_keep, *parts),
                    [ANY] + [VMEM] * users,
               moved=4 * (users + 1) * per * half * size)
    user_send = hold(user_send, item_own)

    own = call(sum_parts, shape(user_blocks, half, size), (user_keep, swap(user_send)),
               [VMEM, VMEM], moved=12 * user_blocks * half * size)
    late = hold(item_own, own)
    item_mine = {0: item_own}
    for offset in [users - 1, *range(1, users - 1)] if users > 1 else []:
        part = item_own if offset == users - 1 else late
        item_mine[offset] = swap(part, "user", users, offset)
    if users > 2:
        item_mine[users - 1] = hold(item_mine[users - 1], flops=MEDIUM)
    item_places = list(item_mine)
    item_mine = call(pack, shape(users, per, half, size), tuple(item_mine.values()),
                     [VMEM] * users, moved=8 * item_blocks * half * size)
    mine = call(functools.partial(sum_after, 1), shape(user_blocks, half, size),
                (item_mine, own, *[swap(own, "item", items, o) for o in range(1, items)]),
                [ANY] + [VMEM] * items, moved=12 * user_blocks * half * size)
    return call(
        functools.partial(finish, item_places),
        (shape(width, user_blocks * size), shape(width, item_blocks * size)),
        (user_half_grad, mine, swap(mine), item_half_grad, item_mine, swap(item_mine)),
        [VMEM] * 6, moved=12 * (user_blocks + item_blocks) * width * size,
    )


def solution(mesh):
    return jax.shard_map(
        functools.partial(on_device, mesh.shape["user"], mesh.shape["item"]),
        mesh=mesh,
        in_specs=(
            P(None, ("groups", "user")),
            P(None, ("groups", "item")),
            P(("groups", "user")),
            P(("groups", "item")),
            P(("groups", "user", "item", "rep"), None, None),
            P(("groups", "user", "item", "rep")),
            P(("groups", "user", "item", "rep")),
            P(("groups", "user", "item", "rep")),
            P(("groups", "user", "item", "rep")),
            P(("groups", "user", "item", "rep")),
            P(("groups", "user", "item", "rep")),
        ),
        out_specs=(P(None, ("groups", "user")), P(None, ("groups", "item"))),
        check_vma=False,
    )
```

```python
import functools

import jax
import jax.numpy as jnp
from jax import lax
from jax.experimental import pallas as pl
from jax.experimental.pallas import tpu as pltpu
from jax.sharding import PartitionSpec as P

F32 = jnp.float32
BF16 = jnp.bfloat16
PACK = 4
GROUP = 8
HEAVY = 10 ** 11
MEDIUM = 24 * 10 ** 8

VMEM = pl.BlockSpec(memory_space=pltpu.VMEM)
SMEM = pl.BlockSpec(memory_space=pltpu.SMEM)
ANY = pl.BlockSpec(memory_space=pl.ANY)
HBM = pl.BlockSpec(memory_space=pltpu.HBM)


def call(kernel, outs, ins, specs, scratch=(), flops=0, moved=0, room=16):
    return pl.pallas_call(
        kernel,
        out_shape=outs,
        in_specs=specs,
        out_specs=jax.tree.map(lambda _: VMEM, outs),
        scratch_shapes=list(scratch),
        cost_estimate=pl.CostEstimate(flops=flops, bytes_accessed=moved, transcendentals=0),
        compiler_params=pltpu.CompilerParams(vmem_limit_bytes=room * 1024 * 1024),
    )(*ins)


def hold(values, *after, flops=0):
    return call(copy, jax.ShapeDtypeStruct(values.shape, values.dtype), (values, *after),
                [VMEM] + [ANY] * len(after), flops=flops)


def shape(*dims):
    return jax.ShapeDtypeStruct(dims, F32)


def split3(values):
    high = values.astype(BF16)
    rest = values - high.astype(F32)
    middle = rest.astype(BF16)
    low = (rest - middle.astype(F32)).astype(BF16)
    return high, middle, low


def hot(ids, start, tile):
    if len(ids) == 2:
        same = ids[0] == ids[1]
        ids = [jnp.where(same, -1, each) for each in ids]
    ids = [each.astype(jnp.int16) for each in ids]
    place = lax.broadcasted_iota(jnp.int16, (tile, ids[0].shape[1]), 0) + jnp.int16(start)
    chosen = jnp.zeros(place.shape, BF16)
    for each, sign in zip(ids, (1, -1)):
        chosen = jnp.where(place == each, jnp.asarray(sign, BF16), chosen)
    return chosen


def sort_slots(keys, sources, count, blocks):
    lanes = keys.shape[1]
    rows = 2 * blocks
    place = lax.broadcasted_iota(jnp.int32, (1, lanes), 1)
    live = place < count
    mine = (lax.broadcasted_iota(jnp.int32, (rows, lanes), 0) == keys) & live
    mine = jnp.where(mine, 1.0, 0.0)
    earlier = lax.broadcasted_iota(jnp.int32, (lanes, lanes), 0) < lax.broadcasted_iota(
        jnp.int32, (lanes, lanes), 1)
    before = jnp.dot(mine.astype(BF16), jnp.where(earlier, 1.0, 0.0).astype(BF16),
                     preferred_element_type=F32)
    packs = jnp.floor((jnp.sum(mine, axis=1, keepdims=True) + (PACK - 1)) * (1.0 / PACK))
    packs = jnp.broadcast_to(packs, (rows, 128))
    lower = lax.broadcasted_iota(jnp.int32, (rows, rows), 1) < lax.broadcasted_iota(
        jnp.int32, (rows, rows), 0)
    first = jnp.dot(jnp.where(lower, 1.0, 0.0).astype(BF16), packs.astype(BF16),
                    preferred_element_type=F32)
    position = jnp.sum(mine * (first[:, :1] * PACK + before), axis=0, keepdims=True)
    position = jnp.where(live, position.astype(jnp.int32), -1)
    match = lax.broadcasted_iota(jnp.int32, (lanes, lanes), 0) == position
    row = lax.broadcasted_iota(jnp.int32, (16, lanes), 0)
    values = jnp.where(row == 0, place // 16, jnp.where(row == 1, place % 16, jnp.where(
        row == 2, sources, jnp.where(row == 3, keys, jnp.where(row == 4, 1, 0)))))
    values = jnp.where(live, values, 0).astype(F32)
    found = lax.dot_general(values.astype(BF16), jnp.where(match, 1.0, 0.0).astype(BF16),
                            (((1,), (1,)), ((), ())), preferred_element_type=F32)
    found = found.astype(jnp.int32)
    valid = found[4:5] > 0
    total = jnp.broadcast_to(jnp.sum(packs[:, :1], axis=0, keepdims=True), (1, lanes))
    row = lax.broadcasted_iota(jnp.int32, (4, lanes), 0)
    slot = found[0:1] * 16 + found[1:2]
    source = jnp.where(valid, found[2:3], blocks)
    target = jnp.where(valid, found[3:4], 0)
    return jnp.where(row == 0, slot, jnp.where(row == 1, source, jnp.where(
        row == 2, target, total.astype(jnp.int32))))


def multiply_blocks(order, vals, source, total, across):
    _, width, size = source.shape
    total[...] = jnp.zeros_like(total)
    contract = (((1,), (1,)), ((), ())) if across else (((1,), (0,)), ((), ()))

    def group(index, _):
        targets, terms = [], []
        for step in range(GROUP):
            left, right = [], []
            for half in range(2):
                first = ((index * GROUP + step) * 2 + half) * PACK
                places = [first + each for each in range(PACK)]
                left.append(jnp.concatenate([source[order[1, each]] for each in places], axis=1))
                right.append(jnp.concatenate([vals[order[0, each]] for each in places],
                                             axis=1 if across else 0))
                targets.append(order[2, first])
            both = lax.dot_general(
                jnp.concatenate(left, axis=0), jnp.concatenate(right, axis=0 if across else 1),
                contract, preferred_element_type=F32,
            )
            terms += [both[:width, :size], both[width:, size:]]
        for target, term in zip(targets, terms):
            total[target] += term
        return 0

    lax.fori_loop(0, (order[3, 0] + 2 * GROUP - 1) // (2 * GROUP), group, 0)


def begin(out):
    out[...] = jnp.zeros_like(out)


def stack_ids(user, positive, negative, after, out):
    out[...] = jnp.zeros_like(out)
    for row, ids in enumerate((user, positive, negative)):
        out[row:row + 1, :] = ids[...]


def pack_ids(places, *refs):
    out = refs[-1]
    out[...] = jnp.zeros_like(out)
    for offset, (index, row) in enumerate(places):
        out[3 * offset:3 * offset + 3, :] = refs[index][row:row + 3, :]


def prepare(count, rows, columns, user_emb, item_emb, user_deg, item_deg, after,
            user_source, item_source, user_scale, item_scale, item_order, user_order, keys):
    live = count[0]
    slots = rows.shape[0]
    keys[...] = jnp.zeros_like(keys)
    keys[0:1, 0:slots] = rows[...].reshape(1, slots)
    keys[1:2, 0:slots] = columns[...].reshape(1, slots)
    users, items = keys[0:1, :], keys[1:2, :]
    item_order[...] = sort_slots(items, users, live, item_scale.shape[0])
    user_order[...] = sort_slots(users, items, live, user_scale.shape[0])
    for emb, deg, scale, into in ((user_emb, user_deg, user_scale, user_source),
                                  (item_emb, item_deg, item_scale, item_source)):
        scale[...] = lax.rsqrt(deg[...].astype(F32))
        blocks, size = scale.shape
        for block in range(blocks):
            piece = emb[:, block * size:(block + 1) * size].astype(F32)
            into[block] = (scale[block:block + 1, :] * piece).astype(BF16)
        into[blocks] = jnp.zeros(into.shape[1:], BF16)


def first_pass(across, order, vals, source, *refs):
    multiply_blocks(order, vals, source, refs[-1], across)


def fold(stacked, width):
    return (
        stacked[:width] + stacked[width:2 * width] + stacked[2 * width:3 * width]
    )


def rows_of(ref, rows):
    return [ref[row:row + 1, :] for row in rows]


def pick(table, ids, tile):
    total = None
    for start in range(0, table.shape[1], tile):
        term = jnp.dot(
            table[:, start:start + tile], hot(ids, start, tile),
            preferred_element_type=F32,
        )
        total = term if total is None else total + term
    return total


def gather(places, count, mine, other, scale, after, *refs):
    ids, outs, table = refs[:count], refs[count:-1], refs[-1]
    blocks, width, size = mine.shape
    for block in range(blocks):
        span = slice(block * size, (block + 1) * size)
        here = scale[block:block + 1, :] * (mine[block] + other[block])
        for part, piece in enumerate(split3(here)):
            table[part * width:(part + 1) * width, span] = piece
    for out, (index, rows) in zip(outs, places):
        out[...] = fold(pick(table, rows_of(ids[index], rows), 2 * size), width)


def scatter(pieces, ids, table, blocks, size, put):
    width = table.shape[1] // 3
    tile = 2 * size
    for place, piece in enumerate(pieces):
        for part, value in enumerate(split3(piece[:width, :])):
            table[place, part * width:(part + 1) * width, :] = value
    for start in range(0, blocks * size, tile):
        total = None
        for place, rows in enumerate(ids):
            term = lax.dot_general(
                table[place], hot(rows, start, tile), (((1,), (1,)), ((), ())),
                preferred_element_type=F32,
            )
            total = term if total is None else total + term
        total = fold(total, width)
        for offset in range(0, tile, size):
            put((start + offset) // size, total[:, offset:offset + size])


def scatter_items(places, after, *refs):
    peers = len(places)
    pieces, ids, out, table = refs[:peers], refs[peers:-2], refs[-2], refs[-1]
    blocks, _, size = out.shape

    def put(block, value):
        out[block] = value

    scatter(pieces, [rows_of(ids[index], rows) for index, rows in places],
            table, blocks, size, put)


def gather_base(user_emb, item_emb, ids, user_out, item_out):
    tile = ids.shape[1]
    user_out[...] = pick(user_emb, rows_of(ids, [0]), tile)
    item_out[...] = pick(item_emb, rows_of(ids, [1, 2]), tile)


def add_all(refs):
    total = refs[0][...]
    for ref in refs[1:]:
        total = total + ref[...]
    return total


def slopes(user_parts, item_parts, ids, *refs):
    users, items = refs[:user_parts], refs[user_parts:user_parts + item_parts]
    pieces, pushed = refs[user_parts + item_parts:]
    width = pushed.shape[0]
    user_rows = 0.5 * add_all(users)
    difference = 0.5 * add_all(items)
    margin = jnp.sum(user_rows * difference, axis=0, keepdims=True)
    slope = -jax.nn.sigmoid(-margin)
    pieces[:width, :] = slope * difference
    pieces[width:, :] = jnp.broadcast_to(ids[0:1, :].astype(F32), (8, ids.shape[1]))
    pushed[...] = slope * user_rows


def halves(total, keep, send):
    me = lax.axis_index("rep")
    half = keep.shape[1]
    for block in range(keep.shape[0]):
        keep[block] = total[block, pl.ds(pl.multiple_of(me * half, half), half), :]
        send[block] = total[block, pl.ds(pl.multiple_of((1 - me) * half, half), half), :]


def second_items(parts, order, source_scale, target_scale, vals, *refs):
    pieces = refs[:parts]
    half_grad, keep, send, source, total, table = refs[parts:]
    blocks, width, size = half_grad.shape

    def put(block, grad):
        half_grad[block] = 0.5 * grad
        source[block] = (source_scale[block:block + 1, :] * grad * 0.5).astype(BF16)

    ids = [[piece[width:width + 1, :].astype(jnp.int32)] for piece in pieces]
    scatter(pieces, ids, table, blocks, size, put)
    source[blocks] = jnp.zeros((width, size), BF16)
    multiply_blocks(order, vals, source, total, False)
    for block in range(total.shape[0]):
        total[block] = target_scale[block:block + 1, :] * total[block]
    halves(total, keep, send)


def second_users(order, mine, other, source_scale, target_scale, vals, after,
                 half_grad, keep, send, source, total):
    blocks, width, size = mine.shape
    for block in range(blocks):
        grad = mine[block] + other[block]
        half_grad[block] = 0.5 * grad
        source[block] = (source_scale[block:block + 1, :] * grad * 0.5).astype(BF16)
    source[blocks] = jnp.zeros((width, size), BF16)
    multiply_blocks(order, vals, source, total, True)
    for block in range(total.shape[0]):
        total[block] = target_scale[block:block + 1, :] * total[block]
    halves(total, keep, send)


def copy(values, *refs):
    refs[-1][...] = values[...]


def add_deal(offsets, keep, received, after, *outs):
    me = lax.axis_index("user")
    per = outs[0].shape[0]
    for out, offset in zip(outs, offsets):
        there = (me ^ offset) * per
        for block in range(per):
            out[block] = keep[there + block] + received[there + block]


def sum_parts(*refs):
    refs[-1][...] = add_all(refs[:-1])


def sum_after(count, *refs):
    sum_parts(*refs[count:])


def pack(*refs):
    for place, ref in enumerate(refs[:-1]):
        refs[-1][place] = ref[...]


def finish_users(half_grad, mine, other, after, out):
    me = lax.axis_index("rep")
    blocks, width, size = half_grad.shape
    half = width // 2
    for block in range(blocks):
        span = slice(block * size, (block + 1) * size)
        for rank, part in ((me, mine), (1 - me, other)):
            rows = pl.ds(pl.multiple_of(rank * half, half), half)
            out[rows, span] = half_grad[block, rows, :] + part[block]


def finish_items(offsets, half_grad, mine, other, out):
    me = lax.axis_index("rep")
    place = lax.axis_index("user")
    _, per, half, size = mine.shape
    for index, offset in enumerate(offsets):
        there = (place ^ offset) * per
        for block in range(per):
            span = pl.ds(pl.multiple_of((there + block) * size, size), size)
            for rank, part in ((me, mine), (1 - me, other)):
                rows = pl.ds(pl.multiple_of(rank * half, half), half)
                out[rows, span] = half_grad[there + block, rows, :] + part[index, block]


def swap(values, axis="rep", peers=2, offset=1):
    return lax.ppermute(values, axis, [(i, i ^ offset) for i in range(peers)])


def on_device(users, items, user_emb, item_emb, user_deg, item_deg, block_vals, block_row,
              block_col, block_count, trip_user, trip_pos, trip_neg):
    width = user_emb.shape[0]
    slots, size, _ = block_vals.shape
    user_blocks = user_emb.shape[1] // size
    item_blocks = item_emb.shape[1] // size
    trips = trip_user.shape[0]
    half = width // 2
    user_deg = user_deg.reshape(user_blocks, size)
    item_deg = item_deg.reshape(item_blocks, size)

    product_flops = 2 * slots * size * size * width
    product_bytes = slots * size * size * 2
    started = call(begin, shape(8, size), (), [], (), 16 * product_flops, product_bytes)
    id_rows = max(16, -(-3 * users // 16) * 8)
    ids_shape = jax.ShapeDtypeStruct((id_rows, trips), jnp.int32)
    ids = call(
        stack_ids, ids_shape,
        [each.reshape(1, trips) for each in (trip_user, trip_pos, trip_neg)] + [started],
        [VMEM, VMEM, VMEM, ANY],
    )
    ids_user = [ids] + [swap(ids, "item", items, o) for o in range(1, items)]
    met = sorted(range(1, users), key=lambda offset: (offset != users // 2, -offset))
    back = met[::-1]
    ids_item, held, step = [(0, 0)], [ids], 1
    while step < users:
        packed = ids if step == 1 else call(
            functools.partial(pack_ids, ids_item), ids_shape, held, [VMEM] * len(held))
        held.append(swap(packed, "user", users, step))
        ids_item += [(len(held) - 1, 3 * place) for place in range(step)]
        step *= 2
    lanes = -(-slots // size) * size

    order_shape = jax.ShapeDtypeStruct((4, lanes), jnp.int32)

    def source_shape(blocks):
        return jax.ShapeDtypeStruct((blocks + 1, width, size), BF16)

    (user_source, item_source, user_scale, item_scale, item_order, user_order) = call(
        prepare,
        [source_shape(user_blocks), source_shape(item_blocks), shape(user_blocks, size),
         shape(item_blocks, size), order_shape, order_shape],
        (block_count, block_row, block_col, user_emb, item_emb, user_deg, item_deg, ids),
        [SMEM, VMEM, VMEM, VMEM, VMEM, VMEM, VMEM, ANY],
        [pltpu.VMEM((8, lanes), jnp.int32)], product_flops, product_bytes,
    )
    item_table = call(
        functools.partial(first_pass, False), shape(item_blocks, width, size),
        (item_order, block_vals, user_source, ids), [SMEM, VMEM, VMEM, ANY], (),
        product_flops, product_bytes,
    )
    user_table = call(
        functools.partial(first_pass, True), shape(user_blocks, width, size),
        (user_order, block_vals, item_source, item_table, *ids_user[1:]),
        [SMEM, VMEM, VMEM] + [ANY] * items, (),
        HEAVY, product_bytes,
    )

    hot_flops = 2 * 3 * width * trips * size

    def reduced(table, scale, arrays, places, axis, offsets, after):
        peers, blocks = len(places), scale.shape[0]
        dealt = call(
            functools.partial(gather, places, len(arrays)), [shape(width, trips)] * peers,
            (table, swap(table), scale, after, *arrays),
            [VMEM] * 3 + [ANY] + [VMEM] * len(arrays),
            [pltpu.VMEM((3 * width, blocks * size), BF16)],
            HEAVY if axis == "user" else 0, 8 * blocks * width * size,
        )
        return [dealt[0]] + [swap(part, axis, peers, o) for part, o in zip(dealt[1:], offsets)]

    def item_rows(offset):
        index, row = ids_item[offset]
        return index, [row + 1, row + 2]

    item_parts = reduced(item_table, item_scale, held, [item_rows(o) for o in [0, *met]],
                         "user", met, ids)
    user_parts = reduced(user_table, user_scale, ids_user, [(o, [0]) for o in range(items)],
                         "item", list(range(1, items)), item_parts[0])
    user_base, item_base = call(
        gather_base, [shape(width, trips)] * 2, (user_emb, item_emb, ids),
        [VMEM, VMEM, VMEM], (), 4 * width * trips * size * (user_blocks + item_blocks),
        2 * width * size * (user_blocks + item_blocks),
    )
    user_parts.append(user_base)
    item_parts.append(item_base)
    pieces, pushed = call(
        functools.partial(slopes, len(user_parts), len(item_parts)),
        [shape(width + 8, trips), shape(width, trips)],
        (ids, *user_parts, *item_parts), [VMEM] * (1 + len(user_parts) + len(item_parts)),
        moved=4 * width * trips * (len(user_parts) + len(item_parts) + 2),
    )

    arrays = [pieces, swap(pieces)]
    for offset in range(1, items):
        arrays.append(swap(pieces, "item", items, offset))
        arrays.append(lax.ppermute(pieces, ("item", "rep"), [
            (i, i ^ (2 * offset + 1)) for i in range(2 * items)]))
    user_half_grad, item_keep, item_send = call(
        functools.partial(second_items, len(arrays)),
        [shape(user_blocks, width, size)] + [shape(item_blocks, half, size)] * 2,
        (item_order, user_scale, item_scale, block_vals, *arrays),
        [SMEM] + [VMEM] * (3 + len(arrays)),
        [pltpu.VMEM((user_blocks + 1, width, size), BF16),
         pltpu.VMEM((item_blocks, width, size), F32),
         pltpu.VMEM((len(arrays), 3 * width, trips), BF16)],
        product_flops, product_bytes,
    )
    arrays = [pushed] + [swap(pushed, "user", users, o) for o in back]
    item_grad = call(
        functools.partial(scatter_items, [item_rows(o) for o in [0, *back]]),
        shape(item_blocks, width, size),
        (item_send, *arrays, *held), [ANY] + [VMEM] * (users + len(held)),
        [pltpu.VMEM((users, 3 * width, trips), BF16)], HEAVY, 0,
    )

    per = item_blocks // users
    dealt = call(
        functools.partial(add_deal, [0, *met]), [shape(per, half, size)] * users,
        (item_keep, swap(item_send), item_grad), [VMEM, VMEM, ANY], (), HEAVY,
    )
    item_half_grad, user_keep, user_send = call(
        second_users,
        [shape(item_blocks, width, size)] + [shape(user_blocks, half, size)] * 2,
        (user_order, item_grad, swap(item_grad), item_scale, user_scale, block_vals, dealt[0]),
        [SMEM] + [VMEM] * 5 + [ANY],
        [pltpu.VMEM((item_blocks + 1, width, size), BF16),
         pltpu.VMEM((user_blocks, width, size), F32)],
        product_flops, product_bytes,
    )
    parts = [dealt[0]] + [swap(part, "user", users, o) for part, o in zip(dealt[1:], met)]
    item_own = call(functools.partial(sum_after, 1), shape(per, half, size), (user_keep, *parts),
                    [ANY] + [VMEM] * users,
               moved=4 * (users + 1) * per * half * size)
    user_send = hold(user_send, item_own)

    own = call(sum_parts, shape(user_blocks, half, size), (user_keep, swap(user_send)),
               [VMEM, VMEM], moved=12 * user_blocks * half * size)
    late = hold(item_own, own)
    item_mine = {0: item_own}
    for offset in [users - 1, *range(1, users - 1)] if users > 1 else []:
        part = item_own if offset == users - 1 else late
        item_mine[offset] = swap(part, "user", users, offset)
    if users > 2:
        item_mine[users - 1] = hold(item_mine[users - 1], flops=MEDIUM)
    item_places = list(item_mine)
    item_mine = call(pack, shape(users, per, half, size), tuple(item_mine.values()),
                     [VMEM] * users, moved=8 * item_blocks * half * size)
    mine = call(functools.partial(sum_after, 1), shape(user_blocks, half, size),
                (item_mine, own, *[swap(own, "item", items, o) for o in range(1, items)]),
                [ANY] + [VMEM] * items, moved=12 * user_blocks * half * size)
    grad_item = call(
        functools.partial(finish_items, item_places), shape(width, item_blocks * size),
        (item_half_grad, item_mine, swap(item_mine)), [VMEM] * 3,
        moved=12 * item_blocks * width * size,
    )
    grad_user = call(
        finish_users, shape(width, user_blocks * size),
        (user_half_grad, mine, swap(mine), item_mine), [VMEM] * 3 + [ANY],
        moved=12 * user_blocks * width * size,
    )
    return (grad_user, grad_item)


def solution(mesh):
    return jax.shard_map(
        functools.partial(on_device, mesh.shape["user"], mesh.shape["item"]),
        mesh=mesh,
        in_specs=(
            P(None, ("groups", "user")),
            P(None, ("groups", "item")),
            P(("groups", "user")),
            P(("groups", "item")),
            P(("groups", "user", "item", "rep"), None, None),
            P(("groups", "user", "item", "rep")),
            P(("groups", "user", "item", "rep")),
            P(("groups", "user", "item", "rep")),
            P(("groups", "user", "item", "rep")),
            P(("groups", "user", "item", "rep")),
            P(("groups", "user", "item", "rep")),
        ),
        out_specs=(P(None, ("groups", "user")), P(None, ("groups", "item"))),
        check_vma=False,
    )
```
